32 devices in a mesh: rep: 4 (over y, x), fsdp: 8 (over z, core).
Axes of the slice: x: 2, y: 2, z: 4, core: 2. Of those that a mesh axis runs over, the one named last changes fastest.
Arguments:
- images: bfloat16 [8, 1376, 1024], P('rep', 'fsdp'), may hold values from -6 to 6
- cotangent: bfloat16 [8, 1376, 1024], P('rep', 'fsdp'), may hold values from -6 to 6
- attn_norm_gain: bfloat16 [2, 1024], P(None, 'fsdp'), may hold values from 0.5 to 1.5
- attn_norm_bias: bfloat16 [2, 1024], P(None, 'fsdp'), may hold values from -1.5 to 1.5
- heads_weight: bfloat16 [2, 1024, 3072], P(None, 'fsdp'), may hold values from -0.1875 to 0.1875
- query_bias: bfloat16 [2, 1024], P(None, 'fsdp'), may hold values from -2.5 to 2.5
- value_bias: bfloat16 [2, 1024], P(None, 'fsdp'), may hold values from -2.5 to 2.5
- output_weight: bfloat16 [2, 1024, 1024], P(None, 'fsdp'), may hold values from -1.5 to 1.5
- output_bias: bfloat16 [2, 1024], P(None, 'fsdp'), may hold values from -1.5 to 1.5
- attn_layerscale: bfloat16 [2, 1024], P(None, 'fsdp'), may hold values from 0.29882812 to 1.5
- mlp_norm_gain: bfloat16 [2, 1024], P(None, 'fsdp'), may hold values from 0.5 to 1.5
- mlp_norm_bias: bfloat16 [2, 1024], P(None, 'fsdp'), may hold values from -1.5 to 1.5
- expand_weight: bfloat16 [2, 1024, 4096], P(None, 'fsdp'), may hold values from -0.1875 to 0.1875
- expand_bias: bfloat16 [2, 4096], P(None, 'fsdp'), may hold values from -2.5 to 2.5
- shrink_weight: bfloat16 [2, 4096, 1024], P(None, 'fsdp'), may hold values from -0.125 to 0.125
- shrink_bias: bfloat16 [2, 1024], P(None, 'fsdp'), may hold values from -1.5 to 1.5
- mlp_layerscale: bfloat16 [2, 1024], P(None, 'fsdp'), may hold values from 0.29882812 to 1.5
Outputs:
- activations: bfloat16 [8, 1376, 1024], P('rep', 'fsdp')
- grad_images: float32 [8, 1376, 1024], P('rep', 'fsdp')
- grad_attn_norm_gain: float32 [2, 1024], P(None, 'fsdp')
- grad_attn_norm_bias: float32 [2, 1024], P(None, 'fsdp')
- grad_heads_weight: float32 [2, 1024, 3072], P(None, 'fsdp')
- grad_query_bias: float32 [2, 1024], P(None, 'fsdp')
- grad_value_bias: float32 [2, 1024], P(None, 'fsdp')
- grad_output_weight: float32 [2, 1024, 1024], P(None, 'fsdp')
- grad_output_bias: float32 [2, 1024], P(None, 'fsdp')
- grad_attn_layerscale: float32 [2, 1024], P(None, 'fsdp')
- grad_mlp_norm_gain: float32 [2, 1024], P(None, 'fsdp')
- grad_mlp_norm_bias: float32 [2, 1024], P(None, 'fsdp')
- grad_expand_weight: float32 [2, 1024, 4096], P(None, 'fsdp')
- grad_expand_bias: float32 [2, 4096], P(None, 'fsdp')
- grad_shrink_weight: float32 [2, 4096, 1024], P(None, 'fsdp')
- grad_shrink_bias: float32 [2, 1024], P(None, 'fsdp')
- grad_mlp_layerscale: float32 [2, 1024], P(None, 'fsdp')
The draws below stay inside these ranges and needn't reach their ends.
All inputs are finite; a program needn't handle non-finite values.
Results may differ from the reference program's by a relative error of at most 0.035.
Values may be sent and summed in bfloat16 or wider, within the bound.
A program may use at most 384 MiB of HBM per device.

```python
import math
import jax
import jax.numpy as jnp
from jax import lax

D = 1024
HEADS = 16
FF = 4096
SEQ = 1376
LAYERS = 2
IMAGES = 8


def block_scale(rng, extent, split, least, top_value):
    def one(position, blocks):
        draws = jax.random.uniform(jax.random.fold_in(jax.random.fold_in(rng, 6), position), (blocks,), jnp.float32, least / len(split), top_value / len(split))
        return jnp.repeat(jnp.exp(draws), extent[position] // blocks).reshape((-1,) + (1,) * (len(extent) - position - 1))

    loudness = one(*split[0])
    for cut in split[1:]:
        loudness = loudness * one(*cut)
    return loudness


def scatter_about(rng, extent, scale, most, split=(), held_as=jnp.bfloat16):
    loudness = block_scale(rng, extent, split, -0.22, 0.18) if split else 1.0
    array = jax.random.normal(rng, extent, jnp.float32) * scale * loudness
    return jnp.minimum(jnp.maximum(array, -most), most).astype(held_as)


def setup_inputs(seed: int = 0) -> dict:
    streams_of = jax.random.split(jax.random.key(seed), 18)
    return {
        "images": scatter_about(streams_of[0], (IMAGES, SEQ, D), 1.0, 6.0, ((0, 4), (1, 8))),
        "cotangent": scatter_about(streams_of[1], (IMAGES, SEQ, D), 1.0, 6.0, ((0, 4), (1, 8))),
        "attn_norm_gain": jnp.clip(1.0 + 0.1 * jax.random.normal(streams_of[2], (LAYERS, D), jnp.float32), 0.5, 1.5).astype(jnp.bfloat16),
        "attn_norm_bias": scatter_about(streams_of[3], (LAYERS, D), 0.3, 1.5, ((1, 8),)),
        "heads_weight": scatter_about(streams_of[4], (LAYERS, D, 3 * D), D ** -0.5, 0.1875, ((1, 8),)),
        "query_bias": scatter_about(streams_of[5], (LAYERS, D), 0.5, 2.5, ((1, 8),)),
        "value_bias": scatter_about(streams_of[6], (LAYERS, D), 0.5, 2.5, ((1, 8),)),
        "output_weight": scatter_about(streams_of[7], (LAYERS, D, D), (D // 64) ** -0.5, 1.5, ((1, 8),)),
        "output_bias": scatter_about(streams_of[8], (LAYERS, D), 0.3, 1.5, ((1, 8),)),
        "attn_layerscale": jnp.clip(jnp.exp(math.log(1.5) - 1.6133518 * jax.random.uniform(streams_of[9], (LAYERS, D), jnp.float32) ** block_scale(streams_of[9], (LAYERS, D), ((1, 8),), -0.2, 0.2)), 0.29882812, 1.5).astype(jnp.bfloat16),
        "mlp_norm_gain": jnp.clip(1.0 + 0.1 * jax.random.normal(streams_of[10], (LAYERS, D), jnp.float32), 0.5, 1.5).astype(jnp.bfloat16),
        "mlp_norm_bias": scatter_about(streams_of[11], (LAYERS, D), 0.3, 1.5, ((1, 8),)),
        "expand_weight": scatter_about(streams_of[12], (LAYERS, D, FF), D ** -0.5, 0.1875, ((1, 8),)),
        "expand_bias": scatter_about(streams_of[13], (LAYERS, FF), 0.5, 2.5, ((1, 8),)),
        "shrink_weight": scatter_about(streams_of[14], (LAYERS, FF, D), (FF // 2) ** -0.5, 0.125, ((1, 8),)),
        "shrink_bias": scatter_about(streams_of[15], (LAYERS, D), 0.3, 1.5, ((1, 8),)),
        "mlp_layerscale": jnp.clip(jnp.exp(math.log(1.5) - 1.6133518 * jax.random.uniform(streams_of[16], (LAYERS, D), jnp.float32) ** block_scale(streams_of[16], (LAYERS, D), ((1, 8),), -0.2, 0.2)), 0.29882812, 1.5).astype(jnp.bfloat16),
    }


@jax.custom_vjp
def low(v):
    return lax.optimization_barrier(v.astype(jnp.bfloat16)).astype(jnp.float32)

@jax.custom_vjp
def low_back(v):
    return v

def low_keep(v):
    return (low(v), None)

def low_pass(kept, grad):
    return (grad,)

def back_keep(v):
    return (v, None)

def back_low(kept, grad):
    return (low(grad),)
low.defvjp(low_keep, low_pass)
low_back.defvjp(back_keep, back_low)
epsilon = 1e-06

def layer_norm(values_in, norm_gain, norm_shift):
    centre = lax.optimization_barrier(jnp.mean(values_in, -1, keepdims=True))
    centered = values_in - centre
    spread = lax.optimization_barrier(jnp.mean(centered * centered, -1, keepdims=True))
    return centered * lax.rsqrt(spread + epsilon) * norm_gain + norm_shift

def product(left, right):
    return jnp.dot(left, right, precision=lax.Precision.HIGHEST)

def block(tok_rows, layer_params):
    attn_norm_gain, attn_norm_bias, heads_weight, query_bias, value_bias, output_weight, output_bias, attn_layerscale, mlp_norm_gain, mlp_norm_bias, expand_weight, expand_bias, shrink_weight, shrink_bias, mlp_layerscale = layer_params
    width = tok_rows.shape[1]
    head_dim = width // HEADS
    normed = low(layer_norm(tok_rows, attn_norm_gain, attn_norm_bias))
    bias_row = jnp.concatenate([query_bias, jnp.zeros_like(query_bias), value_bias])
    projected = low_back(low(product(normed, heads_weight) + bias_row))
    queries = projected[:, :width].reshape(-1, HEADS, head_dim)
    key_heads = projected[:, width:2 * width].reshape(-1, HEADS, head_dim)
    value_heads = projected[:, 2 * width:].reshape(-1, HEADS, head_dim)
    scores = jnp.einsum('qhd,khd->hqk', queries, key_heads, precision=lax.Precision.HIGHEST)
    scores = low_back(scores * head_dim ** (-0.5))
    weights = low(jax.nn.softmax(scores, -1))
    attended = jnp.einsum('hqk,khd->qhd', weights, value_heads, precision=lax.Precision.HIGHEST)
    attended = low_back(low(attended.reshape(-1, width)))
    branch = low_back(product(attended, output_weight) + output_bias)
    middle = tok_rows + attn_layerscale * branch
    normed_two = low(layer_norm(middle, mlp_norm_gain, mlp_norm_bias))
    hidden = low_back(product(normed_two, expand_weight) + expand_bias)
    activated = low(jax.nn.gelu(hidden, approximate=False))
    mlp_out = low_back(product(activated, shrink_weight) + shrink_bias)
    return middle + mlp_layerscale * mlp_out

def reference(images, cotangent, attn_norm_gain, attn_norm_bias, heads_weight, query_bias, value_bias, output_weight, output_bias, attn_layerscale, mlp_norm_gain, mlp_norm_bias, expand_weight, expand_bias, shrink_weight, shrink_bias, mlp_layerscale):
    params = tuple((param.astype(jnp.float32) for param in (attn_norm_gain, attn_norm_bias, heads_weight, query_bias, value_bias, output_weight, output_bias, attn_layerscale, mlp_norm_gain, mlp_norm_bias, expand_weight, expand_bias, shrink_weight, shrink_bias, mlp_layerscale)))

    def forward(tok_rows, all_params):
        for layer_idx in range(LAYERS):
            tok_rows = block(tok_rows, tuple((param[layer_idx] for param in all_params)))
        return tok_rows

    def scan_step(totals, scan_item):
        image_rows, image_cot = scan_item
        result, pullback = jax.vjp(forward, image_rows.astype(jnp.float32), params)
        grad_rows, grad_params = pullback(image_cot.astype(jnp.float32))
        totals = tuple((first + second for first, second in zip(totals, grad_params)))
        return (totals, (result.astype(jnp.bfloat16), grad_rows))
    zero_grads = tuple((jnp.zeros_like(param) for param in params))
    totals, (activations, grad_images) = lax.scan(scan_step, zero_grads, (images, cotangent))
    return (activations, grad_images) + totals
```

```python
import functools
import math

import jax
import jax.numpy as jnp
from jax import lax
from jax.experimental import pallas as pl
from jax.experimental.pallas import tpu as pltpu
from jax.sharding import PartitionSpec as P

HEADS = 16
LAYERS = 2
SMALL = (0, 1, 3, 4, 6, 7, 8, 9, 11, 13, 14)
MIB = 1 << 20

epsilon = 1e-06


def layer_norm(values_in, norm_gain, norm_shift):
    centre = jnp.mean(values_in, -1, keepdims=True)
    centered = values_in - centre
    spread = jnp.mean(centered * centered, -1, keepdims=True)
    return centered * lax.rsqrt(spread + epsilon) * norm_gain + norm_shift


def norm_back(values_in, norm_gain, norm_shift, grad):
    unused, pullback = jax.vjp(layer_norm, values_in, norm_gain, norm_shift)
    return pullback(grad)


def widen(tensor):
    return tensor.astype(jnp.float32)


def low(tensor):
    return tensor.astype(jnp.bfloat16)


def forward_dot(left, weight):
    return jnp.dot(left, weight, preferred_element_type=jnp.float32)


def weight_dot(left, grad):
    return lax.dot_general(left, grad, (((0,), (0,)), ((), ())), preferred_element_type=jnp.float32)


def input_dot(grad, weight):
    return lax.dot_general(
        grad, weight, (((1,), (1,)), ((), ())), preferred_element_type=jnp.float32
    )


def column_sum(grad):
    return jnp.sum(widen(grad), 0)


def pick(tensor, index, axis):
    return lax.dynamic_index_in_dim(tensor, index, axis, keepdims=False)


def swap(tensor, axis, offset):
    count = lax.axis_size(axis)
    return lax.ppermute(tensor, axis, [(i, i ^ offset) for i in range(count)])


def position():
    owner = lax.axis_index("fsdp")
    return owner // 2, owner % 2, lax.axis_index("rep")


def scalars(*values):
    return jnp.stack(values).astype(jnp.int32)


def estimate(microseconds, moved):
    return pl.CostEstimate(flops=1000, bytes_accessed=1000, transcendentals=0)


def params():
    return pltpu.CompilerParams(vmem_limit_bytes=60 * MIB)


def after(tensor, *earlier):
    return lax.optimization_barrier((tensor,) + earlier)[0]


def by_core(own, got, axis):
    core = position()[1]
    return jnp.where(
        core == 0, jnp.stack([own, got], axis), jnp.stack([got, own], axis)
    )


def columns_kernel(blocks, where_ref, *refs):
    ins, (own_ref, other_ref) = refs[:-2], refs[-2:]
    for side in range(2):

        @pl.when(where_ref[1] == side)
        def _():
            for out_ref, parity in ((own_ref, side), (other_ref, 1 - side)):
                start = 0
                for ref, block in zip(ins, blocks):
                    for i in range(parity, ref.shape[2] // block, 2):
                        out_ref[0, :, start : start + block] = ref[0, :, i * block : (i + 1) * block]
                        start += block


def column_pieces(shards):
    plane, core, member = position()
    owners, count = lax.axis_size("fsdp"), lax.axis_size("rep")
    rows = shards[0].shape[1] // count
    blocks = tuple(
        size // owners for size in (shards[0].shape[2] // 3, shards[1].shape[2])
    )
    columns = sum(shard.shape[2] for shard in shards) // 2
    shape = jax.ShapeDtypeStruct((LAYERS, rows, columns), jnp.bfloat16)
    out = pl.BlockSpec((1, rows, columns), lambda layer, where: (layer, 0, 0))
    own, other = pl.pallas_call(
        functools.partial(columns_kernel, blocks),
        out_shape=[shape, shape],
        grid_spec=pltpu.PrefetchScalarGridSpec(
            num_scalar_prefetch=1,
            grid=(LAYERS,),
            in_specs=[
                pl.BlockSpec((1, rows, shard.shape[2]), lambda layer, where: (layer, where[0], 0))
                for shard in shards
            ],
            out_specs=[out, out],
        ),
        compiler_params=params(),
        cost_estimate=estimate(0, 4 * LAYERS * rows * columns * 2),
    )(scalars(member, core), *shards)
    both = by_core(own, swap(other, "fsdp", 1), 1)
    split = shards[0].shape[2] // 2
    both = both.reshape(LAYERS, 2 * rows, columns)
    return both[..., :split], both[..., split:]


def place_kernel(half_rows, blocks, parts, where_ref, *refs):
    count = len(parts)
    pieces, outs, (in_sems, out_sems) = refs[:count], refs[count : -count - 2], refs[-2:]
    held = refs[-count - 2 : -2]
    plane, member = where_ref[0], where_ref[1]
    arrivals = []
    for i in range(count):
        arrivals.append(pltpu.make_async_copy(pieces[i], held[i], in_sems.at[i]))
        arrivals[-1].start()
    copies = []
    for i, (k, halves) in enumerate(parts):
        arrivals[i].wait()
        for j in range(pieces[0].shape[0]):
            for b, (row, rows, column, columns, put) in enumerate(blocks):
                if row // half_rows not in halves:
                    continue
                first = row - halves[0] * half_rows
                copy = pltpu.make_async_copy(
                    held[i].at[j, first : first + rows, column : column + columns],
                    put(outs, j ^ plane, k ^ member),
                    out_sems.at[b, i, j],
                )
                copy.start()
                copies.append(copy)
    for copy in copies:
        copy.wait()


def place(pieces, parts, shapes, blocks):
    plane, core, member = position()
    planes = pieces[0].shape[0]
    outs = pl.pallas_call(
        functools.partial(place_kernel, pieces[0].shape[1] // 2, blocks, parts),
        out_shape=[jax.ShapeDtypeStruct(shape, pieces[0].dtype) for shape in shapes],
        in_specs=[pl.BlockSpec(memory_space=pltpu.SMEM)]
        + [pl.BlockSpec(memory_space=pl.ANY)] * len(pieces),
        out_specs=[pl.BlockSpec(memory_space=pl.ANY)] * len(shapes),
        scratch_shapes=[pltpu.VMEM(piece.shape, piece.dtype) for piece in pieces]
        + [
            pltpu.SemaphoreType.DMA((len(pieces),)),
            pltpu.SemaphoreType.DMA((len(blocks), len(pieces), planes)),
        ],
        compiler_params=params(),
        cost_estimate=estimate(0, 4 * sum(piece.size for piece in pieces)),
    )(scalars(plane, member), *pieces)
    return [out.reshape(-1, out.shape[-1]) for out in outs]


def put_pair(side):
    return lambda outs, plane, member: outs[0].at[plane, side, member]


def place_first(pieces, parts, count, split):
    planes, rows, columns = pieces[0].shape
    half, rest = rows // 2, columns - split

    def put(side):
        return lambda outs, plane, member: outs[1].at[
            plane, member, :, side * rest : (side + 1) * rest
        ]

    shapes = [(planes, 2, count, half, split), (planes, count, half, 2 * rest)]
    blocks = [(side * half, half, 0, split, put_pair(side)) for side in range(2)]
    blocks += [(side * half, half, split, rest, put(side)) for side in range(2)]
    return place(pieces, parts, shapes, blocks)


def place_second(pieces, parts, count):
    planes, rows, columns = pieces[0].shape
    half, fine, width = rows // 2, rows // 4, columns // 2

    def put(side):
        return lambda outs, plane, member: outs[1].at[plane, member, side]

    shapes = [(planes, 2, count, fine, columns), (planes, count, 2, half, width)]
    blocks = [(side * fine, fine, 0, columns, put_pair(side)) for side in range(2)]
    blocks += [(half, half, side * width, width, put(side)) for side in range(2)]
    return place(pieces, parts, shapes, blocks)


def gather_planes(piece, *earlier, beside=()):
    column, sent, step = piece[None], list(earlier), lax.axis_size("fsdp") // 4
    while step:
        got = swap(after(column, *sent[-1:], *(beside if len(sent) > len(earlier) else ())), "fsdp", 2 * step)
        sent.append(got)
        column = jnp.stack([column, got], 1).reshape((-1,) + piece.shape)
        step //= 2
    return column, sent[len(earlier) :]


def gather_neighbours(column, earlier):
    held = {0: [column]}
    for bit in range(lax.axis_size("rep").bit_length() - 1):
        held[1 << bit] = [swap(after(column, *earlier), "rep", 1 << bit)]
    return held, [held[k][0] for k in held if k]


def gather_members(held, beside):
    count, rows = lax.axis_size("rep"), held[0][0].shape[1] // 2
    earlier = [held[k][0] for k in held if k] + list(beside)
    for level in range(1, count.bit_length() - 1):
        sent = []
        for k in range(1, count):
            if bin(k).count("1") != level + 1:
                continue
            held[k] = []
            for half, last in ((0, k & -k), (1, 1 << (k.bit_length() - 1))):
                source = held[k ^ last]
                if len(source) == 1:
                    source = source[0][:, half * rows : (half + 1) * rows]
                else:
                    source = source[half]
                held[k].append(swap(after(source, *earlier), "rep", last))
            sent += held[k]
        earlier = sent
    arrays, parts = [], []
    for k in range(count):
        for half, array in enumerate(held[k]):
            arrays.append(array)
            parts.append((k, (0, 1) if len(held[k]) == 1 else (half,)))
    return arrays, parts, earlier


def message_pieces(shards):
    heads, expand = column_pieces((shards[2], shards[10]))
    pieces = []
    for layer in range(LAYERS):
        output, shrink = quarter(shards[5][layer]), quarter(shards[12][layer])
        half = output.shape[1] // 2
        packed = jnp.concatenate([output[:, :half], output[:, half:]], 0)
        pieces.append(jnp.concatenate([heads[layer], packed], 1))
        half = shrink.shape[0] // 2
        packed = jnp.concatenate([shrink[:half], shrink[half:]], 1)
        pieces.append(jnp.concatenate([expand[layer], packed], 0))
    return pieces


def quarter(param):
    rows = param.shape[0] // lax.axis_size("rep")
    return lax.dynamic_slice_in_dim(param, lax.axis_index("rep") * rows, rows, 0)


def gather_small(all_params, token):
    packed = after(jnp.concatenate([all_params[i] for i in SMALL], 1), token)
    whole, owner, step = packed[None], lax.axis_index("fsdp"), 1
    while step < lax.axis_size("fsdp"):
        got = swap(whole, "fsdp", step)
        whole = jnp.where(
            (owner // step) % 2 == 0,
            jnp.concatenate([whole, got], 0),
            jnp.concatenate([got, whole], 0),
        )
        step *= 2
    vectors, start = [], 0
    for i in SMALL:
        size = all_params[i].shape[1]
        vectors.append(
            jnp.moveaxis(whole[:, :, start : start + size], 0, 1).reshape(LAYERS, -1)
        )
        start += size
    return vectors


def link_orders():
    bits = list(range(lax.axis_size("rep").bit_length() - 1))
    return [bits, bits[::-1]]


def divide(blocks, shapes, bits, outs):
    for side in range(len(shapes)):
        high, later = shapes[side]
        for i in range(high):
            for j in range(later):
                base = 2 * i * later + j
                for out_ref, index in (
                    (outs[2 * side], base + bits[side] * later),
                    (outs[2 * side + 1], base + (1 - bits[side]) * later),
                ):
                    for row, column, block in blocks(side, index):
                        out_ref[
                            0, i, j, row : row + block.shape[0], column : column + block.shape[1]
                        ] = block


def block_grad_kernel(shapes, where_ref, left_ref, grad_ref, more_ref, other_ref, *refs):
    outs, held, extra = refs[:-2], refs[-2], refs[-1]
    held[...] = low(weight_dot(left_ref[...], grad_ref[...])).reshape(held.shape)
    extra[...] = low(weight_dot(more_ref[...], other_ref[...])).reshape(extra.shape)
    rows, half, tall = held.shape[2], held.shape[3] // 2, extra.shape[1] // 2

    def blocks(side, index):
        return [
            (p * rows, 0, held[p, index, :, side * half : (side + 1) * half]) for p in range(2)
        ] + [(2 * rows, 0, extra[index, side * tall : (side + 1) * tall])]

    divide(blocks, shapes, (where_ref[0], where_ref[1]), outs)


def mixed_grad_kernel(shapes, where_ref, left_ref, grad_ref, more_ref, other_ref, *refs):
    outs, held, extra = refs[:4], refs[4], refs[5]
    held[...] = low(weight_dot(left_ref[...], grad_ref[...])).reshape(held.shape)
    extra[...] = low(weight_dot(more_ref[...], other_ref[...])).reshape(extra.shape)
    rows, rest = held.shape[2], extra.shape[2] // 2
    half = (held.shape[3] + rest) // 2

    def blocks(side, index):
        if side == 0:
            return [(p * rows, 0, held[p, index, :, :half]) for p in range(2)]
        return [(p * rows, 0, held[p, index, :, half:]) for p in range(2)] + [
            (p * rows, half - rest, extra[index, :, p * rest : (p + 1) * rest]) for p in range(2)
        ]

    divide(blocks, shapes, (where_ref[0], where_ref[1]), outs)


def grad_call(kernel, arrays, widths, rows, columns, scratch, orders):
    planes, count = lax.axis_size("fsdp") // 2, lax.axis_size("rep")
    member = lax.axis_index("rep")
    shapes = tuple((count >> (order[0] + 1), 1 << order[0]) for order in orders)
    tokens = arrays[0].shape[0]
    specs = []
    for array, width in zip(arrays, widths):
        if width is None:
            specs.append(pl.BlockSpec(array.shape, lambda z, where: (0, 0)))
        else:
            specs.append(pl.BlockSpec((tokens, width), lambda z, where: (0, z)))
    out_shapes, out_specs = [], []
    for high, later in shapes:
        block = (high, later, rows, columns // len(orders))
        out_specs += [pl.BlockSpec((1,) + block, lambda z, where: (z, 0, 0, 0, 0))] * 2
        out_shapes += [jax.ShapeDtypeStruct((planes,) + block, jnp.bfloat16)] * 2
    return pl.pallas_call(
        functools.partial(kernel, shapes),
        out_shape=out_shapes,
        grid_spec=pltpu.PrefetchScalarGridSpec(
            num_scalar_prefetch=1,
            grid=(planes,),
            in_specs=specs,
            out_specs=out_specs,
            scratch_shapes=[pltpu.VMEM(size, jnp.bfloat16) for size in scratch],
        ),
        compiler_params=params(),
        cost_estimate=estimate(5, 0),
    )(scalars(*[(member >> order[0]) & 1 for order in orders]), *arrays)


def block_grad(left, grad, more, other, orders):
    planes, count = lax.axis_size("fsdp") // 2, lax.axis_size("rep")
    widths = left.shape[1] // planes, more.shape[1] // planes
    columns = grad.shape[1]
    rows, tall = widths[0] // (2 * count), widths[1] // count
    return grad_call(
        block_grad_kernel, (left, grad, more, other), (widths[0], None, widths[1], None),
        2 * rows + tall // 2, columns,
        [(2, count, rows, columns), (count, tall, other.shape[1])], orders,
    )


def mixed_grad(left, grad, more, other, orders):
    planes, count = lax.axis_size("fsdp") // 2, lax.axis_size("rep")
    widths = left.shape[1] // planes, more.shape[1] // planes
    columns, rest = grad.shape[1], other.shape[1]
    rows = widths[1] // count
    if widths[1] % 128:
        first = low(weight_dot(left, grad)).reshape(planes, 2, count, rows, columns)
        second = low(weight_dot(more, other)).reshape(planes, count, rows, 2, rest // 2)
        total = jnp.concatenate([jnp.swapaxes(first, 1, 2), jnp.swapaxes(second, 2, 3)], 4)
        total = total.reshape(planes, count, 2 * rows, -1)
        half, member = total.shape[3] // 2, lax.axis_index("rep")
        top = count // 2
        left_part = total[..., :half].reshape(planes, top, 2, 1, 2 * rows, half)
        right_part = total[..., half:].reshape(planes, 1, 2, top, 2 * rows, half)
        sides = member % 2, member // top
        return [
            pick(part, side if kept else 1 - side, 2)
            for part, side in zip((left_part, right_part), sides)
            for kept in (True, False)
        ]
    return grad_call(
        mixed_grad_kernel, (left, grad, more, other), (widths[0], None, widths[1], None),
        2 * rows, columns + rest // 2,
        [(2, count, rows, columns), (count, rows, rest)], orders,
    )


def split_kernel(where_ref, *refs):
    count = len(refs) // 4
    for n in range(count):
        bit = where_ref[n]
        keep_in, got_ref = refs[2 * n], refs[2 * n + 1]
        keep_ref, send_ref = refs[2 * (count + n)], refs[2 * (count + n) + 1]
        keep_ref[0] = low(widen(keep_in[0, bit]) + widen(got_ref[0, bit]))
        send_ref[0] = low(widen(keep_in[0, 1 - bit]) + widen(got_ref[0, 1 - bit]))


def add_split(pairs, later, sides, rows):
    if len({pair[0].size // n for pair, n in zip(pairs, later)}) > 1:
        return [
            out
            for pair, n, side in zip(pairs, later, sides)
            for out in add_split([pair], [n], [side], rows)
        ]
    arrays, in_specs, out_specs, out_shapes = [], [], [], []
    for pair, n in zip(pairs, later):
        columns = pair[0].shape[-1]
        for array in pair:
            arrays.append(array.reshape(-1, 2, n, rows, columns))
            in_specs.append(
                pl.BlockSpec((1, 2, n, rows, columns), lambda i, where: (i, 0, 0, 0, 0))
            )
            out_specs.append(pl.BlockSpec((1, n, rows, columns), lambda i, where: (i, 0, 0, 0)))
            out_shapes.append(
                jax.ShapeDtypeStruct((arrays[-1].shape[0], n, rows, columns), jnp.bfloat16)
            )
    return pl.pallas_call(
        split_kernel,
        out_shape=out_shapes,
        grid_spec=pltpu.PrefetchScalarGridSpec(
            num_scalar_prefetch=1,
            grid=(arrays[0].shape[0],),
            in_specs=in_specs,
            out_specs=out_specs,
        ),
        compiler_params=params(),
        cost_estimate=estimate(0, sum(array.size for array in arrays) * 3),
    )(scalars(*sides), *arrays)


def merge_kernel(where_ref, *refs):
    arrays, (keep_ref, send_ref) = refs[:-2], refs[-2:]
    half = arrays[0].shape[-1]
    for out_ref, bit in ((keep_ref, where_ref[0]), (send_ref, 1 - where_ref[0])):
        start = 0
        for n in range(0, len(arrays), 4):
            left_ref, left_got, right_ref, right_got = arrays[n : n + 4]
            rows = slice(start, start + left_ref.shape[2])
            out_ref[0, rows, :half] = low(widen(left_ref[0, bit]) + widen(left_got[0, bit]))
            out_ref[0, rows, half:] = low(widen(right_ref[0, bit]) + widen(right_got[0, bit]))
            start += left_ref.shape[2]


def add_merge(messages, side):
    half = messages[0][0].shape[-1]
    arrays, specs, total = [], [], 0
    for message in messages:
        rows = message[0].shape[-2]
        arrays += [array.reshape(-1, 2, rows, half) for array in message]
        specs += [pl.BlockSpec((1, 2, rows, half), lambda i, where: (i, 0, 0, 0))] * 4
        total += rows
    high = arrays[0].shape[0]
    given = pl.BlockSpec((1, total, 2 * half), lambda i, where: (i, 0, 0))
    shape = jax.ShapeDtypeStruct((high, total, 2 * half), jnp.bfloat16)
    return pl.pallas_call(
        merge_kernel,
        out_shape=[shape, shape],
        grid_spec=pltpu.PrefetchScalarGridSpec(
            num_scalar_prefetch=1,
            grid=(high,),
            in_specs=specs,
            out_specs=[given, given],
        ),
        compiler_params=params(),
        cost_estimate=estimate(0, sum(array.size for array in arrays) * 3),
    )(scalars(side), *arrays)


def reduce_members(arrays):
    member, lanes = lax.axis_index("rep"), range(2)
    rows, orders = arrays[0].shape[-2], link_orders()
    bits = [sorted(order) for order in orders]
    keeps, sends = list(arrays[::2]), list(arrays[1::2])
    for n in range(len(orders[0])):
        gots = [swap(sends[i], "rep", 1 << orders[i][n]) for i in lanes]
        for i in lanes:
            bits[i].remove(orders[i][n])
        token = yield sends, gots
        gots = [after(got, token) for got in gots]
        if n + 1 < len(orders[0]):
            later = [1 << bits[i].index(orders[i][n + 1]) for i in lanes]
            sides = [(member >> orders[i][n + 1]) & 1 for i in lanes]
            outs = add_split(list(zip(keeps, gots)), later, sides, rows)
            keeps, sends = list(outs[::2]), list(outs[1::2])
    return [keeps[0], gots[0], keeps[1], gots[1]]


def reduce_planes(messages):
    plane, planes = position()[0], lax.axis_size("fsdp") // 2
    rows = sum(message[0].shape[-2] for message in messages)
    keep, send = add_merge(messages, plane % 2)
    step = 1
    while True:
        got = swap(send, "fsdp", 2 * step)
        token = yield [send], [got]
        got = after(got, token)
        step *= 2
        if step == planes:
            return low(widen(keep) + widen(got)).reshape(rows, -1)
        keep, send = add_split([(keep, got)], [1], [(plane // step) % 2], rows)


def finish_columns(total, columns):
    core = position()[1]
    rows = total.shape[0] // 2
    part = total[:, :columns].reshape(2, rows, columns)
    got = swap(pick(part, 1 - core, 0), "fsdp", 1)
    part = jnp.concatenate([pick(part, core, 0), got], 0)
    return jnp.concatenate([part, total[:, columns:]], 1)


def spread(own, low_last):
    pieces = [own]
    for k in range(1, lax.axis_size("rep")):
        last = k & -k if low_last else 1 << (k.bit_length() - 1)
        pieces.append(swap(pieces[k ^ last], "rep", last))
    return pieces


def column_out(out_ref, block, side, ref, start):
    rows = out_ref.shape[2]
    for i in range(out_ref.shape[3] // block):
        first = start if i % 2 == side else start + rows
        out_ref[0, 0, :, i * block : (i + 1) * block] = widen(
            ref[first : first + rows, (i // 2) * block : (i // 2 + 1) * block]
        )


def early_out_kernel(block, where_ref, *refs):
    expand_out, shrink_out = refs[-2:]
    for k, ref in enumerate(refs[:-4]):
        for side in range(2):

            @pl.when((pl.program_id(0) == k) & (where_ref[1] == side))
            def _():
                column_out(expand_out, block, side, ref, 0)

        @pl.when(pl.program_id(0) == k)
        def _():
            rows, columns = shrink_out.shape[2] // 2, shrink_out.shape[3]
            start = ref.shape[0] - rows
            shrink_out[0, 0, :rows] = widen(ref[start:, :columns])
            shrink_out[0, 0, rows:] = widen(ref[start:, columns:])


def late_out_kernel(block, where_ref, *refs):
    heads_out, output_out = refs[-2:]
    for k, ref in enumerate(refs[:-4]):
        for side in range(2):

            @pl.when((pl.program_id(0) == k) & (where_ref[1] == side))
            def _():
                column_out(heads_out, block, side, ref, 0)

        @pl.when(pl.program_id(0) == k)
        def _():
            rows, half = output_out.shape[2], output_out.shape[3] // 2
            start = ref.shape[1] - half
            output_out[0, 0, :, :half] = widen(ref[:rows, start:])
            output_out[0, 0, :, half:] = widen(ref[rows:, start:])


def write_out(kernel, layer, pieces, sizes, earlier):
    plane, core, member = position()
    count = len(pieces)
    shapes = [(LAYERS, count) + size for size in sizes]
    if earlier is None:
        earlier = [jnp.zeros((8, 128), jnp.float32)] * len(sizes)
        aliases = {}
    else:
        earlier = [array.reshape(shape) for array, shape in zip(earlier, shapes)]
        aliases = {1 + count + i: i for i in range(len(sizes))}
    return pl.pallas_call(
        kernel,
        out_shape=[jax.ShapeDtypeStruct(shape, jnp.float32) for shape in shapes],
        grid_spec=pltpu.PrefetchScalarGridSpec(
            num_scalar_prefetch=1,
            grid=(count,),
            in_specs=[pl.BlockSpec(piece.shape, lambda k, where: (0, 0)) for piece in pieces]
            + [pl.BlockSpec(memory_space=pl.ANY)] * len(sizes),
            out_specs=[
                pl.BlockSpec((1, 1) + size, lambda k, where: (layer, k ^ where[0], 0, 0))
                for size in sizes
            ],
        ),
        input_output_aliases=aliases,
        compiler_params=params(),
        cost_estimate=estimate(0, count * pieces[0].size * 6),
    )(scalars(member, core), *pieces, *earlier)


def reduce_small(grads):
    owners, count = lax.axis_size("fsdp"), lax.axis_size("rep")
    total = jnp.concatenate([g.reshape(LAYERS, owners, -1) for g in grads], 2)
    owner = lax.axis_index("fsdp")
    step = owners // 2
    while step:
        total = total.reshape(LAYERS, 2, step, -1)
        mine = (owner // step) % 2
        total = pick(total, mine, 1) + swap(pick(total, 1 - mine, 1), "fsdp", step)
        step //= 2
    step = 1
    while step < count:
        total = total + swap(total, "rep", step)
        step *= 2
    total = total.reshape(LAYERS, -1)
    outs, start = [], 0
    for g in grads:
        size = g.shape[1] // owners
        outs.append(total[:, start : start + size])
        start += size
    return outs


def other_half(rows):
    return swap(rows, "fsdp", lax.axis_size("fsdp") // 2)


def image_side():
    return lax.axis_index("fsdp") // (lax.axis_size("fsdp") // 2)


def regroup(blocks):
    side = image_side()
    return pick(blocks, side, 0), other_half(pick(blocks, 1 - side, 0))


def ungroup(rows, got):
    own, got = rows[: rows.shape[0] // 2], got.astype(rows.dtype)
    return jnp.where(image_side() == 0, jnp.stack([own, got]), jnp.stack([got, own]))


def chips_per_image():
    return lax.axis_size("fsdp") // 4


def share_rows(local_kv):
    shared = [local_kv]
    for k in range(1, chips_per_image()):
        low_bit = k & -k
        shared.append(swap(shared[k ^ low_bit], "fsdp", 2 * low_bit))
    return shared


def collect_rows(own, others):
    chips = chips_per_image()
    if chips == 2:
        got = swap(others, "fsdp", 2)
        return low(widen(own) + widen(got)), got
    total = jnp.concatenate([own, others], 1)
    while chips > 1:
        rows = total.shape[1] // 2
        got = swap(total[:, rows:], "fsdp", chips)
        total = low(widen(total[:, :rows]) + widen(got))
        chips //= 2
    return total, got


def both_cores(rows):
    return jnp.concatenate([rows, swap(rows, "fsdp", 1)], 0)


def one_head(tensor, head):
    half = tensor.shape[1] // 2
    lane = lax.broadcasted_iota(jnp.int32, tensor.shape, 1)
    keep = lane < half if head == 0 else lane >= half
    return jnp.where(keep, tensor, jnp.zeros_like(tensor))


def join(refs, held):
    start = 0
    for ref in refs:
        held[start : start + ref.shape[0], :] = ref[...]
        start += ref.shape[0]
    return held[...]


def attend_kernel(factor, parts, query_ref, *refs):
    out_ref, log_ref, held_keys, held_values = refs[2 * parts :]
    keys, values = join(refs[:parts], held_keys), join(refs[parts : 2 * parts], held_values)
    results, logs = [], []
    for head in range(2):
        scores = input_dot(one_head(query_ref[...], head), keys)
        largest = jnp.max(scores, -1, keepdims=True)
        weights = jnp.exp2((scores - largest) * factor)
        total = jnp.sum(weights, -1, keepdims=True)
        results.append(forward_dot(low(weights), values) / total)
        logs.append(largest * factor + jnp.log2(total))
    out_ref[...] = low(one_head(results[0], 0) + one_head(results[1], 1))
    shape = log_ref.shape
    log_ref[...] = one_head(jnp.broadcast_to(logs[0], shape), 0) + one_head(
        jnp.broadcast_to(logs[1], shape), 1
    )


def pair_block(rows, start):
    return pl.BlockSpec((rows, 128), lambda i: (0, start + i))


def kv_parts(projected, others):
    pairs = projected.shape[1] // 384
    if projected.shape[0] % 16:
        others = [jnp.concatenate([projected[:, 128 * pairs :]] + others, 0)]
        parts = []
    else:
        parts = [(projected, pairs, 2 * pairs)]
    return parts + [(other, 0, pairs) for other in others]


def kv_specs(parts, first=0):
    keys = [pair_block(array.shape[0], first + start) for array, start, unused in parts]
    values = [pair_block(array.shape[0], first + start) for array, unused, start in parts]
    rows = sum(array.shape[0] for array, unused, more in parts)
    held = [pltpu.VMEM((rows, 128), jnp.bfloat16)] * 2
    return keys + values, [array for array, unused, more in parts] * 2, held


def attend(projected, others, head_size):
    tokens, width = projected.shape[0], projected.shape[1] // 3
    pairs = width // 128
    parts = kv_parts(projected, others)
    specs, arrays, held = kv_specs(parts)
    factor = head_size ** (-0.5) * math.log2(math.e)
    return pl.pallas_call(
        functools.partial(attend_kernel, factor, len(parts)),
        out_shape=[
            jax.ShapeDtypeStruct((tokens, width), jnp.bfloat16),
            jax.ShapeDtypeStruct((tokens, width), jnp.float32),
        ],
        grid=(pairs,),
        in_specs=[pair_block(tokens, 0)] + specs,
        out_specs=[pair_block(tokens, 0), pair_block(tokens, 0)],
        scratch_shapes=held,
        compiler_params=params(),
        cost_estimate=estimate(18, 0),
    )(projected, *arrays)


def attend_back_kernel(factor, scale, parts, query_ref, *refs):
    log_ref, grad_ref, dq_ref, own_ref, others_ref, held_keys, held_values = refs[2 * parts :]
    keys, values = join(refs[:parts], held_keys), join(refs[parts : 2 * parts], held_values)
    d_query, d_key, d_value = [], 0.0, 0.0
    for head in range(2):
        query = one_head(query_ref[...], head)
        grad = one_head(grad_ref[...], head)
        half = query.shape[1] // 2
        log_total = log_ref[:, head * half : head * half + 1]
        probs = jnp.exp2(input_dot(query, keys) * factor - log_total)
        products = probs * input_dot(grad, values)
        d_scores = low(products - probs * jnp.sum(products, -1, keepdims=True))
        d_query.append(forward_dot(d_scores, keys))
        d_key = d_key + weight_dot(d_scores, query)
        d_value = d_value + weight_dot(low(probs), grad)
    dq_ref[...] = low((one_head(d_query[0], 0) + one_head(d_query[1], 1)) * scale)
    rows = own_ref.shape[1]
    for i, total in enumerate((low(d_key * scale), low(d_value))):
        own_ref[i] = total[:rows]
        others_ref[i] = total[rows:]


def attend_back(projected, others, log_total, d_attended, head_size, first, pairs):
    tokens, width = d_attended.shape[0], 128 * pairs
    parts = kv_parts(projected, others)
    specs, arrays, held = kv_specs(parts, first)
    rows = held[0].shape[0]
    scale = head_size ** (-0.5)
    own, taken = pair_block(tokens, 0), pair_block(tokens, first)
    return pl.pallas_call(
        functools.partial(attend_back_kernel, scale * math.log2(math.e), scale, len(parts)),
        out_shape=[
            jax.ShapeDtypeStruct((tokens, width), jnp.bfloat16),
            jax.ShapeDtypeStruct((2, tokens, width), jnp.bfloat16),
            jax.ShapeDtypeStruct((2, rows - tokens, width), jnp.bfloat16),
        ],
        grid=(pairs,),
        in_specs=[taken] + specs + [taken, taken],
        out_specs=[
            own,
            pl.BlockSpec((2, tokens, 128), lambda i: (0, 0, i)),
            pl.BlockSpec((2, rows - tokens, 128), lambda i: (0, 0, i)),
        ],
        scratch_shapes=held,
        compiler_params=params(),
        cost_estimate=estimate(8 * pairs, 0),
    )(projected, *arrays, log_total, d_attended)


def add_tile(part, own_ref, other_ref, total_ref):
    @pl.when(pl.program_id(0) == 0)
    def _():
        total_ref[...] = part

    @pl.when(pl.program_id(0) > 0)
    def _():
        total_ref[...] += part

    @pl.when(pl.program_id(0) == pl.num_programs(0) - 1)
    def _():
        half = own_ref.shape[0]
        own_ref[...] = total_ref[:half]
        other_ref[...] = low(total_ref[half:])


def expand_kernel(
    rows_ref, expand_ref, bias_ref, shrink_ref, active_ref, slope_ref, own_ref, other_ref, total_ref
):
    hidden = forward_dot(rows_ref[...], expand_ref[...]) + bias_ref[...]
    normal = 0.5 + 0.5 * lax.erf(hidden * math.sqrt(0.5))
    density = jnp.exp2(hidden * hidden * (-0.5 * math.log2(math.e)))
    slope_ref[...] = low(normal + hidden * density * (1.0 / math.sqrt(2.0 * math.pi)))
    active = low(hidden * normal)
    active_ref[...] = active
    add_tile(forward_dot(active, shrink_ref[...]), own_ref, other_ref, total_ref)


def feed_forward(rows_in, expand, expand_bias, shrink):
    tokens, width = rows_in.shape
    units = expand.shape[1]
    tile = 512
    whole = pl.BlockSpec((tokens, width), lambda i: (0, 0))
    half = pl.BlockSpec((tokens // 2, width), lambda i: (0, 0))
    part = pl.BlockSpec((tokens, tile), lambda i: (0, i))
    return pl.pallas_call(
        expand_kernel,
        out_shape=[
            jax.ShapeDtypeStruct((tokens, units), jnp.bfloat16),
            jax.ShapeDtypeStruct((tokens, units), jnp.bfloat16),
            jax.ShapeDtypeStruct((tokens // 2, width), jnp.float32),
            jax.ShapeDtypeStruct((tokens // 2, width), jnp.bfloat16),
        ],
        grid=(units // tile,),
        in_specs=[
            whole,
            pl.BlockSpec((width, tile), lambda i: (0, i)),
            pl.BlockSpec((1, tile), lambda i: (0, i)),
            pl.BlockSpec((tile, width), lambda i: (i, 0)),
        ],
        out_specs=[part, part, half, half],
        scratch_shapes=[pltpu.VMEM((tokens, width), jnp.float32)],
        compiler_params=params(),
        cost_estimate=estimate(14, 0),
    )(rows_in, expand, expand_bias[None], shrink)


def shrink_kernel(
    grad_ref, shrink_ref, slope_ref, expand_ref, hidden_ref, bias_ref, own_ref, other_ref, total_ref
):
    d_hidden = low(input_dot(grad_ref[...], shrink_ref[...]) * widen(slope_ref[...]))
    hidden_ref[...] = d_hidden
    bias_ref[...] = jnp.sum(widen(d_hidden), 0, keepdims=True)
    add_tile(input_dot(d_hidden, expand_ref[...]), own_ref, other_ref, total_ref)


def feed_back(d_mlp, shrink, slope, expand):
    tokens, width = d_mlp.shape
    units = expand.shape[1]
    tile = 512
    whole = pl.BlockSpec((tokens, width), lambda i: (0, 0))
    half = pl.BlockSpec((tokens // 2, width), lambda i: (0, 0))
    part = pl.BlockSpec((tokens, tile), lambda i: (0, i))
    return pl.pallas_call(
        shrink_kernel,
        out_shape=[
            jax.ShapeDtypeStruct((tokens, units), jnp.bfloat16),
            jax.ShapeDtypeStruct((1, units), jnp.float32),
            jax.ShapeDtypeStruct((tokens // 2, width), jnp.float32),
            jax.ShapeDtypeStruct((tokens // 2, width), jnp.bfloat16),
        ],
        grid=(units // tile,),
        in_specs=[
            whole,
            pl.BlockSpec((tile, width), lambda i: (i, 0)),
            part,
            pl.BlockSpec((width, tile), lambda i: (0, i)),
        ],
        out_specs=[part, pl.BlockSpec((1, tile), lambda i: (0, i)), half, half],
        scratch_shapes=[pltpu.VMEM((tokens, width), jnp.float32)],
        compiler_params=params(),
        cost_estimate=estimate(9, 0),
    )(d_mlp, shrink, slope, expand)


def core_half(vector):
    core = position()[1]
    return pick(widen(vector).reshape(lax.axis_size("fsdp") // 2, 2, -1), core, 1).reshape(-1)


def core_fill(half):
    parts = half.reshape(lax.axis_size("fsdp") // 2, -1)
    return by_core(parts, jnp.zeros_like(parts), 1).reshape(-1)


def normed_rows(tok_rows, gathered):
    return both_cores(low(layer_norm(tok_rows, widen(gathered[0]), widen(gathered[1]))))


def project(normed, gathered, token):
    heads_weight, query_bias, value_bias = gathered[2], gathered[3], gathered[4]
    width = normed.shape[1]
    bias_row = jnp.concatenate(
        [core_half(query_bias), jnp.zeros((width // 2,), jnp.float32), core_half(value_bias)]
    )
    projected = low(forward_dot(normed, heads_weight) + bias_row)
    return projected, share_rows(after(projected[:, width // 2 :], token))[1:]


def forward_layer(tok_rows, normed, projected, others, gathered, beside, neighbours, planes):
    (
        attn_norm_gain,
        attn_norm_bias,
        heads_weight,
        query_bias,
        value_bias,
        output_weight,
        output_bias,
        attn_layerscale,
        mlp_norm_gain,
        mlp_norm_bias,
        expand_weight,
        expand_bias,
        shrink_weight,
        shrink_bias,
        mlp_layerscale,
    ) = gathered
    tokens, width = tok_rows.shape
    attended, log_total = attend(projected, others, width // HEADS)
    attended = after(attended, *beside)
    got = swap(low(forward_dot(attended[tokens:], output_weight)), "fsdp", 1)
    branch = forward_dot(attended[:tokens], output_weight) + widen(got) + widen(output_bias)
    middle = tok_rows + widen(attn_layerscale) * branch
    normed_two = low(layer_norm(middle, widen(mlp_norm_gain), widen(mlp_norm_bias)))
    normed_two = both_cores(after(normed_two, *planes[:1]))
    activated, slope, own_sum, other_sum = feed_forward(
        normed_two, expand_weight, core_half(expand_bias), shrink_weight
    )
    other_sum = after(other_sum, *neighbours, *planes[1:])
    mlp_out = own_sum + widen(swap(other_sum, "fsdp", 1)) + widen(shrink_bias)
    result = middle + widen(mlp_layerscale) * mlp_out
    saved = (
        tok_rows,
        normed,
        projected,
        others,
        log_total,
        attended,
        branch,
        middle,
        normed_two,
        slope,
        activated,
        mlp_out,
    )
    return (result, saved)


class Later:
    def __init__(self):
        self.running, self.done, self.sends, self.gots = {}, {}, {}, {}

    def begin(self, name, kernel, arrays):
        self.running[name] = reduce_members(kernel(*arrays, link_orders()))
        self.step(name, None)

    def join(self, name, parts, token):
        for part in parts:
            while part in self.running:
                self.step(part, token)
        self.running[name] = reduce_planes([self.done[part] for part in parts])
        self.step(name, None)

    def step(self, name, token):
        try:
            self.sends[name], self.gots[name] = self.running[name].send(token)
        except StopIteration as end:
            self.done[name] = end.value
            self.sends[name] = self.gots[name] = []
            del self.running[name]

    def sent(self, value, *names):
        return after(value, *[array for name in names for array in self.sends[name]])

    def came(self, value, *names):
        return after(value, *[array for name in names for array in self.gots[name]])


def backward_layer(d_result, saved, gathered, later, new, old, activation_got):
    (
        attn_norm_gain,
        attn_norm_bias,
        heads_weight,
        query_bias,
        value_bias,
        output_weight,
        output_bias,
        attn_layerscale,
        mlp_norm_gain,
        mlp_norm_bias,
        expand_weight,
        expand_bias,
        shrink_weight,
        shrink_bias,
        mlp_layerscale,
    ) = gathered
    (
        tok_rows,
        normed,
        projected,
        others,
        log_total,
        attended,
        branch,
        middle,
        normed_two,
        slope,
        activated,
        mlp_out,
    ) = saved
    tokens, width = tok_rows.shape
    d_mlp = low(d_result * widen(mlp_layerscale))
    d_mlp_both = both_cores(d_mlp)
    g_mlp_scale = jnp.sum(d_result * mlp_out, 0)
    g_shrink_bias = column_sum(d_mlp)
    d_hidden, g_expand_bias, own_sum, other_sum = feed_back(
        d_mlp_both, shrink_weight, slope, expand_weight
    )
    block, mixed, block_planes, mixed_planes = new
    if old:
        other_sum = later.came(other_sum, old[0])
        later.join(old[2], [old[0]], other_sum)
        d_hidden = later.sent(d_hidden, old[2])
    got = swap(other_sum, "fsdp", 1)
    later.begin(block, block_grad, (normed_two, d_hidden, activated, d_mlp_both))
    own_sum = later.sent(own_sum, block)
    if old:
        own_sum = later.came(own_sum, old[1])
        later.step(old[1], own_sum)
        own_sum = later.sent(own_sum, old[1])
    d_middle_norm, g_mlp_gain, g_mlp_shift = norm_back(
        middle, widen(mlp_norm_gain), widen(mlp_norm_bias), own_sum + widen(got)
    )
    d_middle = d_result + d_middle_norm
    d_branch = low(d_middle * widen(attn_layerscale))
    d_branch_both = both_cores(d_branch)
    g_attn_scale = jnp.sum(d_middle * branch, 0)
    g_output_bias = column_sum(d_branch)
    d_attended = low(input_dot(d_branch_both, output_weight))
    pairs = d_attended.shape[1] // 128

    def back(first):
        return attend_back(
            projected, others, log_total, d_attended, width // HEADS, first, pairs // 2
        )

    first_query, d_own, d_others = back(0)
    first_kv, first_got = collect_rows(d_own, d_others)
    if old:
        d_attended = later.came(d_attended, old[1], old[2])
        later.join(old[3], [old[1]], first_query)
        later.step(old[2], first_query)
        d_attended = later.sent(d_attended, old[3], old[2])
    else:
        d_attended = after(d_attended, activation_got)
    second_query, d_own, d_others = back(pairs // 2)
    d_others = after(d_others, first_got)
    second_kv, second_got = collect_rows(d_own, d_others)
    second_query = later.came(second_query, block)
    later.step(block, second_query)
    second_query = later.sent(second_query, block)
    if old:
        later.step(old[3], second_query)
    d_query = jnp.concatenate([first_query, second_query], 1)
    d_key = jnp.concatenate([first_kv[0], second_kv[0]], 1)
    d_value = jnp.concatenate([first_kv[1], second_kv[1]], 1)
    d_projected = jnp.concatenate([d_query, d_key, d_value], 1)
    g_query_bias = column_sum(d_query)
    g_value_bias = column_sum(d_value)
    got = swap(low(input_dot(d_projected[tokens:], heads_weight)), "fsdp", 1)
    later.begin(mixed, mixed_grad, (normed, d_projected, attended, d_branch_both))
    d_projected = later.sent(d_projected, mixed)
    if old:
        later.join(block_planes, [block], d_projected)
        d_projected = later.sent(d_projected, block_planes)
    d_normed = input_dot(d_projected[:tokens], heads_weight) + widen(got)
    d_rows_norm, g_attn_gain, g_attn_shift = norm_back(
        tok_rows, widen(attn_norm_gain), widen(attn_norm_bias), d_normed
    )
    d_rows = d_middle + d_rows_norm
    small_grads = (
        g_attn_gain,
        g_attn_shift,
        core_fill(g_query_bias),
        core_fill(g_value_bias),
        g_output_bias,
        g_attn_scale,
        g_mlp_gain,
        g_mlp_shift,
        core_fill(g_expand_bias),
        g_shrink_bias,
        g_mlp_scale,
    )
    return (d_rows, small_grads)


def local(images, cotangent, *all_params):
    owners, count = lax.axis_size("fsdp"), lax.axis_size("rep")
    pieces = message_pieces(all_params)
    column, planes = gather_planes(pieces[0])
    own, got = regroup(after(images, planes[0]))
    tok_rows = widen(jnp.concatenate([own, got], 0))
    column = after(column, got)
    next_column, next_planes = gather_planes(pieces[1], got)
    small = gather_small(all_params, got)
    held, neighbours = gather_neighbours(column, [])
    saved_layers, fetched = [], []
    for layer in range(LAYERS):
        gathered = [None] * len(all_params)
        for i, vector in zip(SMALL, small):
            gathered[i] = vector[layer]
        normed = normed_rows(tok_rows, gathered)
        arrays, parts, earlier = gather_members(held, [])
        arrays[0] = after(arrays[0], next_planes[-1])
        gathered[2], gathered[5] = place_first(
            arrays, parts, count, all_params[2].shape[2] // 2
        )
        projected, others = project(normed, gathered, next_planes[-1])
        held, neighbours = gather_neighbours(next_column, earlier)
        if layer + 1 < LAYERS:
            column, planes = gather_planes(pieces[2 * layer + 2], others[-1])
            beside = planes[:1]
        else:
            own, got = regroup(after(cotangent, others[-1]))
            d_rows = widen(jnp.concatenate([own, got], 0))
            beside, planes, neighbours, next_planes = [got], [], [], []
        arrays, parts, earlier = gather_members(held, [])
        arrays[0] = after(arrays[0], *planes[-1:])
        if layer + 1 < LAYERS:
            next_column, next_planes = gather_planes(pieces[2 * layer + 3], planes[-1])
            held, neighbours = gather_neighbours(column, earlier)
        gathered[10], gathered[12] = place_second(arrays, parts, count)
        fetched.append(tuple(gathered))
        tok_rows, saved = forward_layer(
            tok_rows, normed, projected, others, gathered, beside, neighbours, next_planes
        )
        saved_layers.append(saved)
    activation_rows = low(tok_rows)
    small_grads = [None] * LAYERS
    outs = {}

    def size(i):
        return (all_params[i].shape[1] // count, all_params[i].shape[2])

    def block_piece(later, layer):
        total = later.done[layer, 2]
        half = total.shape[0] // 2
        return jnp.concatenate([finish_columns(total[:half], total.shape[1]), total[half:]], 0)

    def mixed_piece(later, layer):
        return finish_columns(later.done[layer, 3], size(2)[1] // 2)

    def write_block(layer, pieces):
        outs["block"] = write_out(
            functools.partial(early_out_kernel, size(10)[1] // owners),
            layer, pieces, [size(10), size(12)], outs.get("block"),
        )

    def write_mixed(layer, pieces):
        outs["mixed"] = write_out(
            functools.partial(late_out_kernel, size(2)[1] // 3 // owners),
            layer, pieces, [size(2), size(5)], outs.get("mixed"),
        )

    later = Later()
    for layer in reversed(range(LAYERS)):
        new = [(layer, n) for n in range(4)]
        old = [(layer + 1, n) for n in range(4)] if layer + 1 < LAYERS else None
        if not old:
            activation_got = other_half(activation_rows[activation_rows.shape[0] // 2 :])
        d_rows, small_grads[layer] = backward_layer(
            d_rows, saved_layers[layer], fetched[layer], later, new, old, activation_got
        )
    activations = ungroup(activation_rows, activation_got)
    image_got = other_half(low(d_rows[d_rows.shape[0] // 2 :]))
    d_images = ungroup(d_rows, image_got)
    for name in (old[2], old[3]):
        while name in later.running:
            later.step(name, d_rows)
    first = block_piece(later, layer + 1)
    rows = first.shape[0]
    first = after(jnp.concatenate([first, mixed_piece(later, layer + 1)], 0), d_rows)
    later.step(new[1], d_rows)
    pieces = spread(later.sent(first, new[1]), True)
    write_block(layer + 1, [piece[:rows] for piece in pieces])
    write_mixed(layer + 1, [piece[rows:] for piece in pieces])
    later.join(new[3], [new[1]], d_rows)
    for name in (new[3], new[2]):
        while name in later.running:
            later.step(name, image_got)
    write_block(layer, spread(block_piece(later, layer), False))
    write_mixed(layer, spread(mixed_piece(later, layer), False))
    stacked = [None] * len(all_params)
    for i, out in zip((10, 12, 2, 5), list(outs["block"]) + list(outs["mixed"])):
        stacked[i] = out.reshape(all_params[i].shape)
    reduced = reduce_small(
        [jnp.stack([grads[n] for grads in small_grads]) for n in range(len(SMALL))]
    )
    for i, vector in zip(SMALL, reduced):
        stacked[i] = vector
    return (activations, d_images) + tuple(stacked)


def solution(mesh):
    in_specs = (
        P("rep", "fsdp", None),
        P("rep", "fsdp", None),
        P(None, "fsdp"),
        P(None, "fsdp"),
        P(None, "fsdp", None),
        P(None, "fsdp"),
        P(None, "fsdp"),
        P(None, "fsdp", None),
        P(None, "fsdp"),
        P(None, "fsdp"),
        P(None, "fsdp"),
        P(None, "fsdp"),
        P(None, "fsdp", None),
        P(None, "fsdp"),
        P(None, "fsdp", None),
        P(None, "fsdp"),
        P(None, "fsdp"),
    )
    out_specs = (
        P("rep", "fsdp", None),
        P("rep", "fsdp", None),
        P(None, "fsdp"),
        P(None, "fsdp"),
        P(None, "fsdp", None),
        P(None, "fsdp"),
        P(None, "fsdp"),
        P(None, "fsdp", None),
        P(None, "fsdp"),
        P(None, "fsdp"),
        P(None, "fsdp"),
        P(None, "fsdp"),
        P(None, "fsdp", None),
        P(None, "fsdp"),
        P(None, "fsdp", None),
        P(None, "fsdp"),
        P(None, "fsdp"),
    )
    return jax.shard_map(local, mesh=mesh, in_specs=in_specs, out_specs=out_specs, check_vma=False)
```

```python
import functools
import math

import jax
import jax.numpy as jnp
from jax import lax
from jax.experimental import pallas as pl
from jax.experimental.pallas import tpu as pltpu
from jax.sharding import PartitionSpec as P

HEADS = 16
LAYERS = 2
SMALL = (0, 1, 3, 4, 6, 7, 8, 9, 11, 13, 14)
MIB = 1 << 20

epsilon = 1e-06


def layer_norm(values_in, norm_gain, norm_shift):
    centre = jnp.mean(values_in, -1, keepdims=True)
    centered = values_in - centre
    spread = jnp.mean(centered * centered, -1, keepdims=True)
    return centered * lax.rsqrt(spread + epsilon) * norm_gain + norm_shift


def norm_back(values_in, norm_gain, norm_shift, grad):
    unused, pullback = jax.vjp(layer_norm, values_in, norm_gain, norm_shift)
    return pullback(grad)


def widen(tensor):
    return tensor.astype(jnp.float32)


def low(tensor):
    return tensor.astype(jnp.bfloat16)


def forward_dot(left, weight):
    return jnp.dot(left, weight, preferred_element_type=jnp.float32)


def weight_dot(left, grad):
    return lax.dot_general(left, grad, (((0,), (0,)), ((), ())), preferred_element_type=jnp.float32)


def input_dot(grad, weight):
    return lax.dot_general(
        grad, weight, (((1,), (1,)), ((), ())), preferred_element_type=jnp.float32
    )


def column_sum(grad):
    return jnp.sum(widen(grad), 0)


def pick(tensor, index, axis):
    return lax.dynamic_index_in_dim(tensor, index, axis, keepdims=False)


def swap(tensor, axis, offset):
    count = lax.axis_size(axis)
    return lax.ppermute(tensor, axis, [(i, i ^ offset) for i in range(count)])


def position():
    owner = lax.axis_index("fsdp")
    return owner // 2, owner % 2, lax.axis_index("rep")


def scalars(*values):
    return jnp.stack(values).astype(jnp.int32)


def estimate(microseconds, moved):
    return pl.CostEstimate(flops=1000, bytes_accessed=1000, transcendentals=0)


def params(mib):
    return pltpu.CompilerParams(vmem_limit_bytes=mib * MIB)


def after(tensor, *earlier):
    return lax.optimization_barrier((tensor,) + earlier)[0]


def by_core(own, got, axis):
    core = position()[1]
    return jnp.where(
        core == 0, jnp.stack([own, got], axis), jnp.stack([got, own], axis)
    )


def columns_kernel(blocks, where_ref, *refs):
    ins, (own_ref, other_ref) = refs[:-2], refs[-2:]
    for side in range(2):

        @pl.when(where_ref[1] == side)
        def _():
            for out_ref, parity in ((own_ref, side), (other_ref, 1 - side)):
                start = 0
                for ref, block in zip(ins, blocks):
                    for i in range(parity, ref.shape[2] // block, 2):
                        out_ref[0, :, start : start + block] = ref[0, :, i * block : (i + 1) * block]
                        start += block


def column_pieces(shards):
    plane, core, member = position()
    owners, count = lax.axis_size("fsdp"), lax.axis_size("rep")
    rows = shards[0].shape[1] // count
    blocks = tuple(
        size // owners for size in (shards[0].shape[2] // 3, shards[1].shape[2])
    )
    columns = sum(shard.shape[2] for shard in shards) // 2
    shape = jax.ShapeDtypeStruct((LAYERS, rows, columns), jnp.bfloat16)
    out = pl.BlockSpec((1, rows, columns), lambda layer, where: (layer, 0, 0))
    own, other = pl.pallas_call(
        functools.partial(columns_kernel, blocks),
        out_shape=[shape, shape],
        grid_spec=pltpu.PrefetchScalarGridSpec(
            num_scalar_prefetch=1,
            grid=(LAYERS,),
            in_specs=[
                pl.BlockSpec((1, rows, shard.shape[2]), lambda layer, where: (layer, where[0], 0))
                for shard in shards
            ],
            out_specs=[out, out],
        ),
        cost_estimate=estimate(0, 4 * LAYERS * rows * columns * 2),
    )(scalars(member, core), *shards)
    both = by_core(own, swap(other, "fsdp", 1), 1)
    split = shards[0].shape[2] // 2
    both = both.reshape(LAYERS, 2 * rows, columns)
    return both[..., :split], both[..., split:]


def place_kernel(half_rows, blocks, parts, where_ref, *refs):
    count = len(parts)
    pieces, outs, (in_sems, out_sems) = refs[:count], refs[count : -count - 2], refs[-2:]
    held = refs[-count - 2 : -2]
    plane, member = where_ref[0], where_ref[1]
    arrivals = []
    for i in range(count):
        arrivals.append(pltpu.make_async_copy(pieces[i], held[i], in_sems.at[i]))
        arrivals[-1].start()
    copies = []
    for i, (k, halves) in enumerate(parts):
        arrivals[i].wait()
        for j in range(pieces[0].shape[0]):
            for b, (row, rows, column, columns, put) in enumerate(blocks):
                if row // half_rows not in halves:
                    continue
                first = row - halves[0] * half_rows
                copy = pltpu.make_async_copy(
                    held[i].at[j, first : first + rows, column : column + columns],
                    put(outs, j ^ plane, k ^ member),
                    out_sems.at[b, i, j],
                )
                copy.start()
                copies.append(copy)
    for copy in copies:
        copy.wait()


def place(pieces, parts, shapes, blocks):
    plane, core, member = position()
    planes = pieces[0].shape[0]
    outs = pl.pallas_call(
        functools.partial(place_kernel, pieces[0].shape[1] // 2, blocks, parts),
        out_shape=[jax.ShapeDtypeStruct(shape, pieces[0].dtype) for shape in shapes],
        in_specs=[pl.BlockSpec(memory_space=pltpu.SMEM)]
        + [pl.BlockSpec(memory_space=pl.ANY)] * len(pieces),
        out_specs=[pl.BlockSpec(memory_space=pl.ANY)] * len(shapes),
        scratch_shapes=[pltpu.VMEM(piece.shape, piece.dtype) for piece in pieces]
        + [
            pltpu.SemaphoreType.DMA((len(pieces),)),
            pltpu.SemaphoreType.DMA((len(blocks), len(pieces), planes)),
        ],
        compiler_params=params(20),
        cost_estimate=estimate(0, 4 * sum(piece.size for piece in pieces)),
    )(scalars(plane, member), *pieces)
    return [out.reshape(-1, out.shape[-1]) for out in outs]


def put_pair(side):
    return lambda outs, plane, member: outs[0].at[plane, side, member]


def place_first(pieces, parts, count, split):
    planes, rows, columns = pieces[0].shape
    half, rest = rows // 2, columns - split

    def put(side):
        return lambda outs, plane, member: outs[1].at[
            plane, member, :, side * rest : (side + 1) * rest
        ]

    shapes = [(planes, 2, count, half, split), (planes, count, half, 2 * rest)]
    blocks = [(side * half, half, 0, split, put_pair(side)) for side in range(2)]
    blocks += [(side * half, half, split, rest, put(side)) for side in range(2)]
    return place(pieces, parts, shapes, blocks)


def place_second(pieces, parts, count):
    planes, rows, columns = pieces[0].shape
    half, fine, width = rows // 2, rows // 4, columns // 2

    def put(side):
        return lambda outs, plane, member: outs[1].at[plane, member, side]

    shapes = [(planes, 2, count, fine, columns), (planes, count, 2, half, width)]
    blocks = [(side * fine, fine, 0, columns, put_pair(side)) for side in range(2)]
    blocks += [(half, half, side * width, width, put(side)) for side in range(2)]
    return place(pieces, parts, shapes, blocks)


def gather_planes(piece, *earlier, beside=()):
    column, sent, step = piece[None], list(earlier), lax.axis_size("fsdp") // 4
    while step:
        got = swap(after(column, *sent[-1:], *(beside if len(sent) > len(earlier) else ())), "fsdp", 2 * step)
        sent.append(got)
        column = jnp.stack([column, got], 1).reshape((-1,) + piece.shape)
        step //= 2
    return column, sent[len(earlier) :]


def gather_neighbours(column, earlier):
    held = {0: [column]}
    for bit in range(lax.axis_size("rep").bit_length() - 1):
        held[1 << bit] = [swap(after(column, *earlier), "rep", 1 << bit)]
    return held, [held[k][0] for k in held if k]


def gather_members(held, beside):
    count, rows = lax.axis_size("rep"), held[0][0].shape[1] // 2
    earlier = [held[k][0] for k in held if k] + list(beside)
    for level in range(1, count.bit_length() - 1):
        sent = []
        for k in range(1, count):
            if bin(k).count("1") != level + 1:
                continue
            held[k] = []
            for half, last in ((0, k & -k), (1, 1 << (k.bit_length() - 1))):
                source = held[k ^ last]
                if len(source) == 1:
                    source = source[0][:, half * rows : (half + 1) * rows]
                else:
                    source = source[half]
                held[k].append(swap(after(source, *earlier), "rep", last))
            sent += held[k]
        earlier = sent
    arrays, parts = [], []
    for k in range(count):
        for half, array in enumerate(held[k]):
            arrays.append(array)
            parts.append((k, (0, 1) if len(held[k]) == 1 else (half,)))
    return arrays, parts, earlier


def message_pieces(shards):
    heads, expand = column_pieces((shards[2], shards[10]))
    pieces = []
    for layer in range(LAYERS):
        output, shrink = quarter(shards[5][layer]), quarter(shards[12][layer])
        half = output.shape[1] // 2
        packed = jnp.concatenate([output[:, :half], output[:, half:]], 0)
        pieces.append(jnp.concatenate([heads[layer], packed], 1))
        half = shrink.shape[0] // 2
        packed = jnp.concatenate([shrink[:half], shrink[half:]], 1)
        pieces.append(jnp.concatenate([expand[layer], packed], 0))
    return pieces


def quarter(param):
    rows = param.shape[0] // lax.axis_size("rep")
    return lax.dynamic_slice_in_dim(param, lax.axis_index("rep") * rows, rows, 0)


def gather_small(all_params, token):
    packed = after(jnp.concatenate([all_params[i] for i in SMALL], 1), token)
    whole, owner, step = packed[None], lax.axis_index("fsdp"), 1
    while step < lax.axis_size("fsdp"):
        got = swap(whole, "fsdp", step)
        whole = jnp.where(
            (owner // step) % 2 == 0,
            jnp.concatenate([whole, got], 0),
            jnp.concatenate([got, whole], 0),
        )
        step *= 2
    vectors, start = [], 0
    for i in SMALL:
        size = all_params[i].shape[1]
        vectors.append(
            jnp.moveaxis(whole[:, :, start : start + size], 0, 1).reshape(LAYERS, -1)
        )
        start += size
    return vectors


def link_orders():
    bits = list(range(lax.axis_size("rep").bit_length() - 1))
    return [bits, bits[::-1]]


def divide(blocks, shapes, bits, outs):
    for side in range(len(shapes)):
        high, later = shapes[side]
        for i in range(high):
            for j in range(later):
                base = 2 * i * later + j
                for out_ref, index in (
                    (outs[2 * side], base + bits[side] * later),
                    (outs[2 * side + 1], base + (1 - bits[side]) * later),
                ):
                    for row, column, block in blocks(side, index):
                        out_ref[
                            0, i, j, row : row + block.shape[0], column : column + block.shape[1]
                        ] = block


def block_grad_kernel(shapes, where_ref, left_ref, grad_ref, more_ref, other_ref, *refs):
    outs, held, extra = refs[:-2], refs[-2], refs[-1]
    held[...] = low(weight_dot(left_ref[...], grad_ref[...])).reshape(held.shape)
    extra[...] = low(weight_dot(more_ref[...], other_ref[...])).reshape(extra.shape)
    rows, half, tall = held.shape[2], held.shape[3] // 2, extra.shape[1] // 2

    def blocks(side, index):
        return [
            (p * rows, 0, held[p, index, :, side * half : (side + 1) * half]) for p in range(2)
        ] + [(2 * rows, 0, extra[index, side * tall : (side + 1) * tall])]

    divide(blocks, shapes, (where_ref[0], where_ref[1]), outs)


def mixed_grad_kernel(shapes, where_ref, left_ref, grad_ref, more_ref, other_ref, *refs):
    outs, held, extra = refs[:4], refs[4], refs[5]
    held[...] = low(weight_dot(left_ref[...], grad_ref[...])).reshape(held.shape)
    extra[...] = low(weight_dot(more_ref[...], other_ref[...])).reshape(extra.shape)
    rows, rest = held.shape[2], extra.shape[2] // 2
    half = (held.shape[3] + rest) // 2

    def blocks(side, index):
        if side == 0:
            return [(p * rows, 0, held[p, index, :, :half]) for p in range(2)]
        return [(p * rows, 0, held[p, index, :, half:]) for p in range(2)] + [
            (p * rows, half - rest, extra[index, :, p * rest : (p + 1) * rest]) for p in range(2)
        ]

    divide(blocks, shapes, (where_ref[0], where_ref[1]), outs)


def grad_call(kernel, arrays, widths, rows, columns, scratch, orders):
    planes, count = lax.axis_size("fsdp") // 2, lax.axis_size("rep")
    member = lax.axis_index("rep")
    shapes = tuple((count >> (order[0] + 1), 1 << order[0]) for order in orders)
    tokens = arrays[0].shape[0]
    specs = []
    for array, width in zip(arrays, widths):
        if width is None:
            specs.append(pl.BlockSpec(array.shape, lambda z, where: (0, 0)))
        else:
            specs.append(pl.BlockSpec((tokens, width), lambda z, where: (0, z)))
    out_shapes, out_specs = [], []
    for high, later in shapes:
        block = (high, later, rows, columns // len(orders))
        out_specs += [pl.BlockSpec((1,) + block, lambda z, where: (z, 0, 0, 0, 0))] * 2
        out_shapes += [jax.ShapeDtypeStruct((planes,) + block, jnp.bfloat16)] * 2
    return pl.pallas_call(
        functools.partial(kernel, shapes),
        out_shape=out_shapes,
        grid_spec=pltpu.PrefetchScalarGridSpec(
            num_scalar_prefetch=1,
            grid=(planes,),
            in_specs=specs,
            out_specs=out_specs,
            scratch_shapes=[pltpu.VMEM(size, jnp.bfloat16) for size in scratch],
        ),
        compiler_params=params(40),
        cost_estimate=estimate(5, 0),
    )(scalars(*[(member >> order[0]) & 1 for order in orders]), *arrays)


def block_grad(left, grad, more, other, orders):
    planes, count = lax.axis_size("fsdp") // 2, lax.axis_size("rep")
    widths = left.shape[1] // planes, more.shape[1] // planes
    columns = grad.shape[1]
    rows, tall = widths[0] // (2 * count), widths[1] // count
    return grad_call(
        block_grad_kernel, (left, grad, more, other), (widths[0], None, widths[1], None),
        2 * rows + tall // 2, columns,
        [(2, count, rows, columns), (count, tall, other.shape[1])], orders,
    )


def mixed_grad(left, grad, more, other, orders):
    planes, count = lax.axis_size("fsdp") // 2, lax.axis_size("rep")
    widths = left.shape[1] // planes, more.shape[1] // planes
    columns, rest = grad.shape[1], other.shape[1]
    rows = widths[1] // count
    if widths[1] % 128:
        first = low(weight_dot(left, grad)).reshape(planes, 2, count, rows, columns)
        second = low(weight_dot(more, other)).reshape(planes, count, rows, 2, rest // 2)
        total = jnp.concatenate([jnp.swapaxes(first, 1, 2), jnp.swapaxes(second, 2, 3)], 4)
        total = total.reshape(planes, count, 2 * rows, -1)
        half, member = total.shape[3] // 2, lax.axis_index("rep")
        top = count // 2
        left_part = total[..., :half].reshape(planes, top, 2, 1, 2 * rows, half)
        right_part = total[..., half:].reshape(planes, 1, 2, top, 2 * rows, half)
        sides = member % 2, member // top
        return [
            pick(part, side if kept else 1 - side, 2)
            for part, side in zip((left_part, right_part), sides)
            for kept in (True, False)
        ]
    return grad_call(
        mixed_grad_kernel, (left, grad, more, other), (widths[0], None, widths[1], None),
        2 * rows, columns + rest // 2,
        [(2, count, rows, columns), (count, rows, rest)], orders,
    )


def split_kernel(where_ref, *refs):
    count = len(refs) // 4
    for n in range(count):
        bit = where_ref[n]
        keep_in, got_ref = refs[2 * n], refs[2 * n + 1]
        keep_ref, send_ref = refs[2 * (count + n)], refs[2 * (count + n) + 1]
        keep_ref[0] = low(widen(keep_in[0, bit]) + widen(got_ref[0, bit]))
        send_ref[0] = low(widen(keep_in[0, 1 - bit]) + widen(got_ref[0, 1 - bit]))


def add_split(pairs, later, sides, rows):
    if len({pair[0].size // n for pair, n in zip(pairs, later)}) > 1:
        return [
            out
            for pair, n, side in zip(pairs, later, sides)
            for out in add_split([pair], [n], [side], rows)
        ]
    arrays, in_specs, out_specs, out_shapes = [], [], [], []
    for pair, n in zip(pairs, later):
        columns = pair[0].shape[-1]
        for array in pair:
            arrays.append(array.reshape(-1, 2, n, rows, columns))
            in_specs.append(
                pl.BlockSpec((1, 2, n, rows, columns), lambda i, where: (i, 0, 0, 0, 0))
            )
            out_specs.append(pl.BlockSpec((1, n, rows, columns), lambda i, where: (i, 0, 0, 0)))
            out_shapes.append(
                jax.ShapeDtypeStruct((arrays[-1].shape[0], n, rows, columns), jnp.bfloat16)
            )
    return pl.pallas_call(
        split_kernel,
        out_shape=out_shapes,
        grid_spec=pltpu.PrefetchScalarGridSpec(
            num_scalar_prefetch=1,
            grid=(arrays[0].shape[0],),
            in_specs=in_specs,
            out_specs=out_specs,
        ),
        compiler_params=params(24),
        cost_estimate=estimate(0, sum(array.size for array in arrays) * 3),
    )(scalars(*sides), *arrays)


def merge_kernel(where_ref, *refs):
    arrays, (keep_ref, send_ref) = refs[:-2], refs[-2:]
    half = arrays[0].shape[-1]
    for out_ref, bit in ((keep_ref, where_ref[0]), (send_ref, 1 - where_ref[0])):
        start = 0
        for n in range(0, len(arrays), 4):
            left_ref, left_got, right_ref, right_got = arrays[n : n + 4]
            rows = slice(start, start + left_ref.shape[2])
            out_ref[0, rows, :half] = low(widen(left_ref[0, bit]) + widen(left_got[0, bit]))
            out_ref[0, rows, half:] = low(widen(right_ref[0, bit]) + widen(right_got[0, bit]))
            start += left_ref.shape[2]


def add_merge(messages, side):
    half = messages[0][0].shape[-1]
    arrays, specs, total = [], [], 0
    for message in messages:
        rows = message[0].shape[-2]
        arrays += [array.reshape(-1, 2, rows, half) for array in message]
        specs += [pl.BlockSpec((1, 2, rows, half), lambda i, where: (i, 0, 0, 0))] * 4
        total += rows
    high = arrays[0].shape[0]
    given = pl.BlockSpec((1, total, 2 * half), lambda i, where: (i, 0, 0))
    shape = jax.ShapeDtypeStruct((high, total, 2 * half), jnp.bfloat16)
    return pl.pallas_call(
        merge_kernel,
        out_shape=[shape, shape],
        grid_spec=pltpu.PrefetchScalarGridSpec(
            num_scalar_prefetch=1,
            grid=(high,),
            in_specs=specs,
            out_specs=[given, given],
        ),
        compiler_params=params(24),
        cost_estimate=estimate(0, sum(array.size for array in arrays) * 3),
    )(scalars(side), *arrays)


def reduce_members(arrays):
    member, lanes = lax.axis_index("rep"), range(2)
    rows, orders = arrays[0].shape[-2], link_orders()
    bits = [sorted(order) for order in orders]
    keeps, sends = list(arrays[::2]), list(arrays[1::2])
    for n in range(len(orders[0])):
        gots = [swap(sends[i], "rep", 1 << orders[i][n]) for i in lanes]
        for i in lanes:
            bits[i].remove(orders[i][n])
        token = yield sends, gots
        gots = [after(got, token) for got in gots]
        if n + 1 < len(orders[0]):
            later = [1 << bits[i].index(orders[i][n + 1]) for i in lanes]
            sides = [(member >> orders[i][n + 1]) & 1 for i in lanes]
            outs = add_split(list(zip(keeps, gots)), later, sides, rows)
            keeps, sends = list(outs[::2]), list(outs[1::2])
    return [keeps[0], gots[0], keeps[1], gots[1]]


def reduce_planes(messages):
    plane, planes = position()[0], lax.axis_size("fsdp") // 2
    rows = sum(message[0].shape[-2] for message in messages)
    keep, send = add_merge(messages, plane % 2)
    step = 1
    while True:
        got = swap(send, "fsdp", 2 * step)
        token = yield [send], [got]
        got = after(got, token)
        step *= 2
        if step == planes:
            return low(widen(keep) + widen(got)).reshape(rows, -1)
        keep, send = add_split([(keep, got)], [1], [(plane // step) % 2], rows)


def finish_columns(total, columns):
    core = position()[1]
    rows = total.shape[0] // 2
    part = total[:, :columns].reshape(2, rows, columns)
    got = swap(pick(part, 1 - core, 0), "fsdp", 1)
    part = jnp.concatenate([pick(part, core, 0), got], 0)
    return jnp.concatenate([part, total[:, columns:]], 1)


def spread(own, low_last):
    pieces = [own]
    for k in range(1, lax.axis_size("rep")):
        last = k & -k if low_last else 1 << (k.bit_length() - 1)
        pieces.append(swap(pieces[k ^ last], "rep", last))
    return pieces


def column_out(out_ref, block, side, ref, start):
    rows = out_ref.shape[2]
    for i in range(out_ref.shape[3] // block):
        first = start if i % 2 == side else start + rows
        out_ref[0, 0, :, i * block : (i + 1) * block] = widen(
            ref[first : first + rows, (i // 2) * block : (i // 2 + 1) * block]
        )


def early_out_kernel(block, where_ref, *refs):
    expand_out, shrink_out = refs[-2:]
    for k, ref in enumerate(refs[:-4]):
        for side in range(2):

            @pl.when((pl.program_id(0) == k) & (where_ref[1] == side))
            def _():
                column_out(expand_out, block, side, ref, 0)

        @pl.when(pl.program_id(0) == k)
        def _():
            rows, columns = shrink_out.shape[2] // 2, shrink_out.shape[3]
            start = ref.shape[0] - rows
            shrink_out[0, 0, :rows] = widen(ref[start:, :columns])
            shrink_out[0, 0, rows:] = widen(ref[start:, columns:])


def late_out_kernel(block, where_ref, *refs):
    heads_out, output_out = refs[-2:]
    for k, ref in enumerate(refs[:-4]):
        for side in range(2):

            @pl.when((pl.program_id(0) == k) & (where_ref[1] == side))
            def _():
                column_out(heads_out, block, side, ref, 0)

        @pl.when(pl.program_id(0) == k)
        def _():
            rows, half = output_out.shape[2], output_out.shape[3] // 2
            start = ref.shape[1] - half
            output_out[0, 0, :, :half] = widen(ref[:rows, start:])
            output_out[0, 0, :, half:] = widen(ref[rows:, start:])


def write_out(kernel, layer, pieces, sizes, earlier):
    plane, core, member = position()
    count = len(pieces)
    shapes = [(LAYERS, count) + size for size in sizes]
    if earlier is None:
        earlier = [jnp.zeros((8, 128), jnp.float32)] * len(sizes)
        aliases = {}
    else:
        earlier = [array.reshape(shape) for array, shape in zip(earlier, shapes)]
        aliases = {1 + count + i: i for i in range(len(sizes))}
    return pl.pallas_call(
        kernel,
        out_shape=[jax.ShapeDtypeStruct(shape, jnp.float32) for shape in shapes],
        grid_spec=pltpu.PrefetchScalarGridSpec(
            num_scalar_prefetch=1,
            grid=(count,),
            in_specs=[pl.BlockSpec(piece.shape, lambda k, where: (0, 0)) for piece in pieces]
            + [pl.BlockSpec(memory_space=pl.ANY)] * len(sizes),
            out_specs=[
                pl.BlockSpec((1, 1) + size, lambda k, where: (layer, k ^ where[0], 0, 0))
                for size in sizes
            ],
        ),
        input_output_aliases=aliases,
        compiler_params=params(24),
        cost_estimate=estimate(0, count * pieces[0].size * 6),
    )(scalars(member, core), *pieces, *earlier)


def reduce_small(grads, earlier):
    owners, count = lax.axis_size("fsdp"), lax.axis_size("rep")
    total = jnp.concatenate([g.reshape(LAYERS, owners, -1) for g in grads], 2)
    total = after(total, *earlier)
    owner = lax.axis_index("fsdp")
    step = owners // 2
    while step:
        total = total.reshape(LAYERS, 2, step, -1)
        mine = (owner // step) % 2
        total = pick(total, mine, 1) + swap(pick(total, 1 - mine, 1), "fsdp", step)
        step //= 2
    step = 1
    while step < count:
        total = total + swap(total, "rep", step)
        step *= 2
    total = total.reshape(LAYERS, -1)
    outs, start = [], 0
    for g in grads:
        size = g.shape[1] // owners
        outs.append(total[:, start : start + size])
        start += size
    return outs


def other_half(rows):
    return swap(rows, "fsdp", lax.axis_size("fsdp") // 2)


def image_side():
    return lax.axis_index("fsdp") // (lax.axis_size("fsdp") // 2)


def regroup(blocks):
    side = image_side()
    return pick(blocks, side, 0), other_half(pick(blocks, 1 - side, 0))


def ungroup(rows, got):
    own, got = rows[: rows.shape[0] // 2], got.astype(rows.dtype)
    return jnp.where(image_side() == 0, jnp.stack([own, got]), jnp.stack([got, own]))


def chips_per_image():
    return lax.axis_size("fsdp") // 4


def share_rows(local_kv):
    shared = [local_kv]
    for k in range(1, chips_per_image()):
        low_bit = k & -k
        shared.append(swap(shared[k ^ low_bit], "fsdp", 2 * low_bit))
    return shared


def collect_rows(own, others):
    chips = chips_per_image()
    if chips == 2:
        got = swap(others, "fsdp", 2)
        return low(widen(own) + widen(got)), got
    total = jnp.concatenate([own, others], 1)
    while chips > 1:
        rows = total.shape[1] // 2
        got = swap(total[:, rows:], "fsdp", chips)
        total = low(widen(total[:, :rows]) + widen(got))
        chips //= 2
    return total, got


def both_cores(rows):
    return jnp.concatenate([rows, swap(rows, "fsdp", 1)], 0)


def one_head(tensor, head):
    half = tensor.shape[1] // 2
    lane = lax.broadcasted_iota(jnp.int32, tensor.shape, 1)
    keep = lane < half if head == 0 else lane >= half
    return jnp.where(keep, tensor, jnp.zeros_like(tensor))


def join(refs, held):
    start = 0
    for ref in refs:
        held[start : start + ref.shape[0], :] = ref[...]
        start += ref.shape[0]
    return held[...]


def attend_kernel(factor, parts, query_ref, *refs):
    out_ref, log_ref, held_keys, held_values = refs[2 * parts :]
    keys, values = join(refs[:parts], held_keys), join(refs[parts : 2 * parts], held_values)
    results, logs = [], []
    for head in range(2):
        scores = input_dot(one_head(query_ref[...], head), keys)
        largest = jnp.max(scores, -1, keepdims=True)
        weights = jnp.exp2((scores - largest) * factor)
        total = jnp.sum(weights, -1, keepdims=True)
        results.append(forward_dot(low(weights), values) / total)
        logs.append(largest * factor + jnp.log2(total))
    out_ref[...] = low(one_head(results[0], 0) + one_head(results[1], 1))
    shape = log_ref.shape
    log_ref[...] = one_head(jnp.broadcast_to(logs[0], shape), 0) + one_head(
        jnp.broadcast_to(logs[1], shape), 1
    )


def pair_block(rows, start):
    return pl.BlockSpec((rows, 128), lambda i: (0, start + i))


def kv_parts(projected, others):
    pairs = projected.shape[1] // 384
    if projected.shape[0] % 16:
        others = [jnp.concatenate([projected[:, 128 * pairs :]] + others, 0)]
        parts = []
    else:
        parts = [(projected, pairs, 2 * pairs)]
    return parts + [(other, 0, pairs) for other in others]


def kv_specs(parts, first=0):
    keys = [pair_block(array.shape[0], first + start) for array, start, unused in parts]
    values = [pair_block(array.shape[0], first + start) for array, unused, start in parts]
    rows = sum(array.shape[0] for array, unused, more in parts)
    held = [pltpu.VMEM((rows, 128), jnp.bfloat16)] * 2
    return keys + values, [array for array, unused, more in parts] * 2, held


def attend(projected, others, head_size):
    tokens, width = projected.shape[0], projected.shape[1] // 3
    pairs = width // 128
    parts = kv_parts(projected, others)
    specs, arrays, held = kv_specs(parts)
    factor = head_size ** (-0.5) * math.log2(math.e)
    return pl.pallas_call(
        functools.partial(attend_kernel, factor, len(parts)),
        out_shape=[
            jax.ShapeDtypeStruct((tokens, width), jnp.bfloat16),
            jax.ShapeDtypeStruct((tokens, width), jnp.float32),
        ],
        grid=(pairs,),
        in_specs=[pair_block(tokens, 0)] + specs,
        out_specs=[pair_block(tokens, 0), pair_block(tokens, 0)],
        scratch_shapes=held,
        compiler_params=params(56),
        cost_estimate=estimate(18, 0),
    )(projected, *arrays)


def attend_back_kernel(factor, scale, parts, query_ref, *refs):
    log_ref, grad_ref, dq_ref, own_ref, others_ref, held_keys, held_values = refs[2 * parts :]
    keys, values = join(refs[:parts], held_keys), join(refs[parts : 2 * parts], held_values)
    d_query, d_key, d_value = [], 0.0, 0.0
    for head in range(2):
        query = one_head(query_ref[...], head)
        grad = one_head(grad_ref[...], head)
        half = query.shape[1] // 2
        log_total = log_ref[:, head * half : head * half + 1]
        probs = jnp.exp2(input_dot(query, keys) * factor - log_total)
        products = probs * input_dot(grad, values)
        d_scores = low(products - probs * jnp.sum(products, -1, keepdims=True))
        d_query.append(forward_dot(d_scores, keys))
        d_key = d_key + weight_dot(d_scores, query)
        d_value = d_value + weight_dot(low(probs), grad)
    dq_ref[...] = low((one_head(d_query[0], 0) + one_head(d_query[1], 1)) * scale)
    rows = own_ref.shape[1]
    for i, total in enumerate((low(d_key * scale), low(d_value))):
        own_ref[i] = total[:rows]
        others_ref[i] = total[rows:]


def attend_back(projected, others, log_total, d_attended, head_size, first, pairs):
    tokens, width = d_attended.shape[0], 128 * pairs
    parts = kv_parts(projected, others)
    specs, arrays, held = kv_specs(parts, first)
    rows = held[0].shape[0]
    scale = head_size ** (-0.5)
    own, taken = pair_block(tokens, 0), pair_block(tokens, first)
    return pl.pallas_call(
        functools.partial(attend_back_kernel, scale * math.log2(math.e), scale, len(parts)),
        out_shape=[
            jax.ShapeDtypeStruct((tokens, width), jnp.bfloat16),
            jax.ShapeDtypeStruct((2, tokens, width), jnp.bfloat16),
            jax.ShapeDtypeStruct((2, rows - tokens, width), jnp.bfloat16),
        ],
        grid=(pairs,),
        in_specs=[taken] + specs + [taken, taken],
        out_specs=[
            own,
            pl.BlockSpec((2, tokens, 128), lambda i: (0, 0, i)),
            pl.BlockSpec((2, rows - tokens, 128), lambda i: (0, 0, i)),
        ],
        scratch_shapes=held,
        compiler_params=params(60),
        cost_estimate=estimate(8 * pairs, 0),
    )(projected, *arrays, log_total, d_attended)


def add_tile(part, own_ref, other_ref, total_ref):
    @pl.when(pl.program_id(0) == 0)
    def _():
        total_ref[...] = part

    @pl.when(pl.program_id(0) > 0)
    def _():
        total_ref[...] += part

    @pl.when(pl.program_id(0) == pl.num_programs(0) - 1)
    def _():
        half = own_ref.shape[0]
        own_ref[...] = total_ref[:half]
        other_ref[...] = low(total_ref[half:])


def expand_kernel(
    rows_ref, expand_ref, bias_ref, shrink_ref, active_ref, slope_ref, own_ref, other_ref, total_ref
):
    hidden = forward_dot(rows_ref[...], expand_ref[...]) + bias_ref[...]
    normal = 0.5 + 0.5 * lax.erf(hidden * math.sqrt(0.5))
    density = jnp.exp2(hidden * hidden * (-0.5 * math.log2(math.e)))
    slope_ref[...] = low(normal + hidden * density * (1.0 / math.sqrt(2.0 * math.pi)))
    active = low(hidden * normal)
    active_ref[...] = active
    add_tile(forward_dot(active, shrink_ref[...]), own_ref, other_ref, total_ref)


def feed_forward(rows_in, expand, expand_bias, shrink):
    tokens, width = rows_in.shape
    units = expand.shape[1]
    tile = 512
    whole = pl.BlockSpec((tokens, width), lambda i: (0, 0))
    half = pl.BlockSpec((tokens // 2, width), lambda i: (0, 0))
    part = pl.BlockSpec((tokens, tile), lambda i: (0, i))
    return pl.pallas_call(
        expand_kernel,
        out_shape=[
            jax.ShapeDtypeStruct((tokens, units), jnp.bfloat16),
            jax.ShapeDtypeStruct((tokens, units), jnp.bfloat16),
            jax.ShapeDtypeStruct((tokens // 2, width), jnp.float32),
            jax.ShapeDtypeStruct((tokens // 2, width), jnp.bfloat16),
        ],
        grid=(units // tile,),
        in_specs=[
            whole,
            pl.BlockSpec((width, tile), lambda i: (0, i)),
            pl.BlockSpec((1, tile), lambda i: (0, i)),
            pl.BlockSpec((tile, width), lambda i: (i, 0)),
        ],
        out_specs=[part, part, half, half],
        scratch_shapes=[pltpu.VMEM((tokens, width), jnp.float32)],
        compiler_params=params(32),
        cost_estimate=estimate(14, 0),
    )(rows_in, expand, expand_bias[None], shrink)


def shrink_kernel(
    grad_ref, shrink_ref, slope_ref, expand_ref, hidden_ref, bias_ref, own_ref, other_ref, total_ref
):
    d_hidden = low(input_dot(grad_ref[...], shrink_ref[...]) * widen(slope_ref[...]))
    hidden_ref[...] = d_hidden
    bias_ref[...] = jnp.sum(widen(d_hidden), 0, keepdims=True)
    add_tile(input_dot(d_hidden, expand_ref[...]), own_ref, other_ref, total_ref)


def feed_back(d_mlp, shrink, slope, expand):
    tokens, width = d_mlp.shape
    units = expand.shape[1]
    tile = 512
    whole = pl.BlockSpec((tokens, width), lambda i: (0, 0))
    half = pl.BlockSpec((tokens // 2, width), lambda i: (0, 0))
    part = pl.BlockSpec((tokens, tile), lambda i: (0, i))
    return pl.pallas_call(
        shrink_kernel,
        out_shape=[
            jax.ShapeDtypeStruct((tokens, units), jnp.bfloat16),
            jax.ShapeDtypeStruct((1, units), jnp.float32),
            jax.ShapeDtypeStruct((tokens // 2, width), jnp.float32),
            jax.ShapeDtypeStruct((tokens // 2, width), jnp.bfloat16),
        ],
        grid=(units // tile,),
        in_specs=[
            whole,
            pl.BlockSpec((tile, width), lambda i: (i, 0)),
            part,
            pl.BlockSpec((width, tile), lambda i: (0, i)),
        ],
        out_specs=[part, pl.BlockSpec((1, tile), lambda i: (0, i)), half, half],
        scratch_shapes=[pltpu.VMEM((tokens, width), jnp.float32)],
        compiler_params=params(32),
        cost_estimate=estimate(9, 0),
    )(d_mlp, shrink, slope, expand)


def core_half(vector):
    core = position()[1]
    return pick(widen(vector).reshape(lax.axis_size("fsdp") // 2, 2, -1), core, 1).reshape(-1)


def core_fill(half):
    parts = half.reshape(lax.axis_size("fsdp") // 2, -1)
    return by_core(parts, jnp.zeros_like(parts), 1).reshape(-1)


def normed_rows(tok_rows, gathered):
    return both_cores(low(layer_norm(tok_rows, widen(gathered[0]), widen(gathered[1]))))


def project(normed, gathered, token):
    heads_weight, query_bias, value_bias = gathered[2], gathered[3], gathered[4]
    width = normed.shape[1]
    bias_row = jnp.concatenate(
        [core_half(query_bias), jnp.zeros((width // 2,), jnp.float32), core_half(value_bias)]
    )
    projected = low(forward_dot(normed, heads_weight) + bias_row)
    return projected, share_rows(after(projected[:, width // 2 :], token))[1:]


def forward_layer(tok_rows, normed, projected, others, gathered, beside, neighbours, planes):
    (
        attn_norm_gain,
        attn_norm_bias,
        heads_weight,
        query_bias,
        value_bias,
        output_weight,
        output_bias,
        attn_layerscale,
        mlp_norm_gain,
        mlp_norm_bias,
        expand_weight,
        expand_bias,
        shrink_weight,
        shrink_bias,
        mlp_layerscale,
    ) = gathered
    tokens, width = tok_rows.shape
    attended, log_total = attend(projected, others, width // HEADS)
    attended = after(attended, *beside)
    got = swap(low(forward_dot(attended[tokens:], output_weight)), "fsdp", 1)
    branch = forward_dot(attended[:tokens], output_weight) + widen(got) + widen(output_bias)
    middle = tok_rows + widen(attn_layerscale) * branch
    normed_two = low(layer_norm(middle, widen(mlp_norm_gain), widen(mlp_norm_bias)))
    normed_two = both_cores(after(normed_two, *planes[:1]))
    activated, slope, own_sum, other_sum = feed_forward(
        normed_two, expand_weight, core_half(expand_bias), shrink_weight
    )
    other_sum = after(other_sum, *neighbours, *planes[1:])
    mlp_out = own_sum + widen(swap(other_sum, "fsdp", 1)) + widen(shrink_bias)
    result = middle + widen(mlp_layerscale) * mlp_out
    saved = (
        tok_rows,
        normed,
        projected,
        others,
        log_total,
        attended,
        branch,
        middle,
        normed_two,
        slope,
        activated,
        mlp_out,
    )
    return (result, saved)


class Later:
    def __init__(self):
        self.running, self.done, self.sends, self.gots = {}, {}, {}, {}

    def begin(self, name, kernel, arrays):
        self.running[name] = reduce_members(kernel(*arrays, link_orders()))
        self.step(name, None)

    def join(self, name, parts, token):
        for part in parts:
            while part in self.running:
                self.step(part, token)
        self.running[name] = reduce_planes([self.done[part] for part in parts])
        self.step(name, None)

    def step(self, name, token):
        try:
            self.sends[name], self.gots[name] = self.running[name].send(token)
        except StopIteration as end:
            self.done[name] = end.value
            self.sends[name] = self.gots[name] = []
            del self.running[name]

    def sent(self, value, *names):
        return after(value, *[array for name in names for array in self.sends[name]])

    def came(self, value, *names):
        return after(value, *[array for name in names for array in self.gots[name]])


def backward_layer(d_result, saved, gathered, later, new, old, activation_got):
    (
        attn_norm_gain,
        attn_norm_bias,
        heads_weight,
        query_bias,
        value_bias,
        output_weight,
        output_bias,
        attn_layerscale,
        mlp_norm_gain,
        mlp_norm_bias,
        expand_weight,
        expand_bias,
        shrink_weight,
        shrink_bias,
        mlp_layerscale,
    ) = gathered
    (
        tok_rows,
        normed,
        projected,
        others,
        log_total,
        attended,
        branch,
        middle,
        normed_two,
        slope,
        activated,
        mlp_out,
    ) = saved
    tokens, width = tok_rows.shape
    d_mlp = low(d_result * widen(mlp_layerscale))
    d_mlp_both = both_cores(d_mlp)
    g_mlp_scale = jnp.sum(d_result * mlp_out, 0)
    g_shrink_bias = column_sum(d_mlp)
    d_hidden, g_expand_bias, own_sum, other_sum = feed_back(
        d_mlp_both, shrink_weight, slope, expand_weight
    )
    block, mixed, block_planes, mixed_planes = new
    if old:
        other_sum = later.came(other_sum, old[0])
        later.join(old[2], [old[0]], other_sum)
        d_hidden = later.sent(d_hidden, old[2])
    got = swap(other_sum, "fsdp", 1)
    later.begin(block, block_grad, (normed_two, d_hidden, activated, d_mlp_both))
    own_sum = later.sent(own_sum, block)
    if not old:
        own_sum = after(own_sum, activation_got)
    if old:
        own_sum = later.came(own_sum, old[1])
        later.step(old[1], own_sum)
        own_sum = later.sent(own_sum, old[1])
    d_middle_norm, g_mlp_gain, g_mlp_shift = norm_back(
        middle, widen(mlp_norm_gain), widen(mlp_norm_bias), own_sum + widen(got)
    )
    d_middle = d_result + d_middle_norm
    d_branch = low(d_middle * widen(attn_layerscale))
    d_branch_both = both_cores(d_branch)
    g_attn_scale = jnp.sum(d_middle * branch, 0)
    g_output_bias = column_sum(d_branch)
    d_attended = low(input_dot(d_branch_both, output_weight))
    pairs = d_attended.shape[1] // 128

    def back(first):
        return attend_back(
            projected, others, log_total, d_attended, width // HEADS, first, pairs // 2
        )

    first_query, d_own, d_others = back(0)
    first_kv, first_got = collect_rows(d_own, d_others)
    if old:
        d_attended = later.came(d_attended, old[2])
        later.step(old[2], first_query)
        d_attended = later.sent(d_attended, old[2])
    second_query, d_own, d_others = back(pairs // 2)
    d_others = after(d_others, first_got)
    second_kv, second_got = collect_rows(d_own, d_others)
    second_query = later.came(second_query, block)
    later.step(block, second_query)
    second_query = later.sent(second_query, block)
    if old:
        second_query = later.came(second_query, old[1])
        later.join(old[3], [old[1]], second_query)
        second_query = later.sent(second_query, old[3])
    d_query = jnp.concatenate([first_query, second_query], 1)
    d_key = jnp.concatenate([first_kv[0], second_kv[0]], 1)
    d_value = jnp.concatenate([first_kv[1], second_kv[1]], 1)
    d_projected = jnp.concatenate([d_query, d_key, d_value], 1)
    g_query_bias = column_sum(d_query)
    g_value_bias = column_sum(d_value)
    got = swap(low(input_dot(d_projected[tokens:], heads_weight)), "fsdp", 1)
    later.begin(mixed, mixed_grad, (normed, d_projected, attended, d_branch_both))
    d_projected = later.sent(d_projected, mixed)
    if old:
        later.join(block_planes, [block], d_projected)
        d_projected = later.sent(d_projected, block_planes)
    d_normed = input_dot(d_projected[:tokens], heads_weight) + widen(got)
    d_rows_norm, g_attn_gain, g_attn_shift = norm_back(
        tok_rows, widen(attn_norm_gain), widen(attn_norm_bias), d_normed
    )
    d_rows = d_middle + d_rows_norm
    small_grads = (
        g_attn_gain,
        g_attn_shift,
        core_fill(g_query_bias),
        core_fill(g_value_bias),
        g_output_bias,
        g_attn_scale,
        g_mlp_gain,
        g_mlp_shift,
        core_fill(g_expand_bias),
        g_shrink_bias,
        g_mlp_scale,
    )
    return (d_rows, small_grads)


def local(images, cotangent, *all_params):
    owners, count = lax.axis_size("fsdp"), lax.axis_size("rep")
    pieces = message_pieces(all_params)
    column, planes = gather_planes(pieces[0])
    own, got = regroup(after(images, planes[0]))
    tok_rows = widen(jnp.concatenate([own, got], 0))
    column = after(column, got)
    next_column, next_planes = gather_planes(pieces[1], got)
    small = gather_small(all_params, got)
    held, neighbours = gather_neighbours(column, [])
    saved_layers, fetched = [], []
    for layer in range(LAYERS):
        gathered = [None] * len(all_params)
        for i, vector in zip(SMALL, small):
            gathered[i] = vector[layer]
        normed = normed_rows(tok_rows, gathered)
        arrays, parts, earlier = gather_members(held, [])
        arrays[0] = after(arrays[0], next_planes[-1])
        gathered[2], gathered[5] = place_first(
            arrays, parts, count, all_params[2].shape[2] // 2
        )
        projected, others = project(normed, gathered, next_planes[-1])
        held, neighbours = gather_neighbours(next_column, earlier)
        if layer + 1 < LAYERS:
            column, planes = gather_planes(pieces[2 * layer + 2], others[-1])
            beside = planes[:1]
        else:
            own, got = regroup(after(cotangent, others[-1]))
            d_rows = widen(jnp.concatenate([own, got], 0))
            beside, planes, neighbours, next_planes = [got], [], [], []
        arrays, parts, earlier = gather_members(held, [])
        arrays[0] = after(arrays[0], *planes[-1:])
        if layer + 1 < LAYERS:
            next_column, next_planes = gather_planes(pieces[2 * layer + 3], planes[-1])
            held, neighbours = gather_neighbours(column, earlier)
        gathered[10], gathered[12] = place_second(arrays, parts, count)
        fetched.append(tuple(gathered))
        tok_rows, saved = forward_layer(
            tok_rows, normed, projected, others, gathered, beside, neighbours, next_planes
        )
        saved_layers.append(saved)
    activation_rows = low(tok_rows)
    small_grads = [None] * LAYERS
    outs = {}

    def size(i):
        return (all_params[i].shape[1] // count, all_params[i].shape[2])

    def block_piece(later, layer):
        total = later.done[layer, 2]
        half = total.shape[0] // 2
        return jnp.concatenate([finish_columns(total[:half], total.shape[1]), total[half:]], 0)

    def mixed_piece(later, layer):
        return finish_columns(later.done[layer, 3], size(2)[1] // 2)

    def write_block(layer, pieces):
        outs["block"] = write_out(
            functools.partial(early_out_kernel, size(10)[1] // owners),
            layer, pieces, [size(10), size(12)], outs.get("block"),
        )

    def write_mixed(layer, pieces):
        outs["mixed"] = write_out(
            functools.partial(late_out_kernel, size(2)[1] // 3 // owners),
            layer, pieces, [size(2), size(5)], outs.get("mixed"),
        )

    later = Later()
    for layer in reversed(range(LAYERS)):
        new = [(layer, n) for n in range(4)]
        old = [(layer + 1, n) for n in range(4)] if layer + 1 < LAYERS else None
        if not old:
            activation_got = other_half(activation_rows[activation_rows.shape[0] // 2 :])
        d_rows, small_grads[layer] = backward_layer(
            d_rows, saved_layers[layer], fetched[layer], later, new, old, activation_got
        )
    activations = ungroup(activation_rows, activation_got)
    image_got = other_half(low(d_rows[d_rows.shape[0] // 2 :]))
    d_images = ungroup(d_rows, image_got)
    for name in (old[2], old[3]):
        while name in later.running:
            later.step(name, d_rows)
    first = block_piece(later, layer + 1)
    rows = first.shape[0]
    first = after(jnp.concatenate([first, mixed_piece(later, layer + 1)], 0), d_rows)
    later.step(new[1], d_rows)
    pieces = spread(later.sent(first, new[1]), True)
    write_block(layer + 1, [piece[:rows] for piece in pieces])
    write_mixed(layer + 1, [piece[rows:] for piece in pieces])
    last_sends = later.sends[new[1]]
    later.join(new[3], [new[1]], d_rows)
    while new[3] in later.running:
        later.step(new[3], d_rows)
    while new[2] in later.running:
        later.step(new[2], image_got)
    write_block(layer, spread(block_piece(later, layer), False))
    write_mixed(layer, spread(mixed_piece(later, layer), False))
    stacked = [None] * len(all_params)
    for i, out in zip((10, 12, 2, 5), list(outs["block"]) + list(outs["mixed"])):
        stacked[i] = out.reshape(all_params[i].shape)
    reduced = reduce_small(
        [jnp.stack([grads[n] for grads in small_grads]) for n in range(len(SMALL))], last_sends
    )
    for i, vector in zip(SMALL, reduced):
        stacked[i] = vector
    return (activations, d_images) + tuple(stacked)


def solution(mesh):
    in_specs = (
        P("rep", "fsdp", None),
        P("rep", "fsdp", None),
        P(None, "fsdp"),
        P(None, "fsdp"),
        P(None, "fsdp", None),
        P(None, "fsdp"),
        P(None, "fsdp"),
        P(None, "fsdp", None),
        P(None, "fsdp"),
        P(None, "fsdp"),
        P(None, "fsdp"),
        P(None, "fsdp"),
        P(None, "fsdp", None),
        P(None, "fsdp"),
        P(None, "fsdp", None),
        P(None, "fsdp"),
        P(None, "fsdp"),
    )
    out_specs = (
        P("rep", "fsdp", None),
        P("rep", "fsdp", None),
        P(None, "fsdp"),
        P(None, "fsdp"),
        P(None, "fsdp", None),
        P(None, "fsdp"),
        P(None, "fsdp"),
        P(None, "fsdp", None),
        P(None, "fsdp"),
        P(None, "fsdp"),
        P(None, "fsdp"),
        P(None, "fsdp"),
        P(None, "fsdp", None),
        P(None, "fsdp"),
        P(None, "fsdp", None),
        P(None, "fsdp"),
        P(None, "fsdp"),
    )
    return jax.shard_map(local, mesh=mesh, in_specs=in_specs, out_specs=out_specs, check_vma=False)
```

```python
import functools
import math

import jax
import jax.numpy as jnp
from jax import lax
from jax.experimental import pallas as pl
from jax.experimental.pallas import tpu as pltpu
from jax.sharding import PartitionSpec as P

HEADS = 16
LAYERS = 2
SMALL = (0, 1, 3, 4, 6, 7, 8, 9, 11, 13, 14)
MIB = 1 << 20

epsilon = 1e-06


def layer_norm(values_in, norm_gain, norm_shift):
    centre = jnp.mean(values_in, -1, keepdims=True)
    centered = values_in - centre
    spread = jnp.mean(centered * centered, -1, keepdims=True)
    return centered * lax.rsqrt(spread + epsilon) * norm_gain + norm_shift


def norm_back(values_in, norm_gain, norm_shift, grad):
    unused, pullback = jax.vjp(layer_norm, values_in, norm_gain, norm_shift)
    return pullback(grad)


def widen(tensor):
    return tensor.astype(jnp.float32)


def low(tensor):
    return tensor.astype(jnp.bfloat16)


def forward_dot(left, weight):
    return jnp.dot(left, weight, preferred_element_type=jnp.float32)


def weight_dot(left, grad):
    return lax.dot_general(left, grad, (((0,), (0,)), ((), ())), preferred_element_type=jnp.float32)


def input_dot(grad, weight):
    return lax.dot_general(
        grad, weight, (((1,), (1,)), ((), ())), preferred_element_type=jnp.float32
    )


def column_sum(grad):
    return jnp.sum(widen(grad), 0)


def pick(tensor, index, axis):
    return lax.dynamic_index_in_dim(tensor, index, axis, keepdims=False)


def swap(tensor, axis, offset):
    count = lax.axis_size(axis)
    return lax.ppermute(tensor, axis, [(i, i ^ offset) for i in range(count)])


def position():
    owner = lax.axis_index("fsdp")
    return owner // 2, owner % 2, lax.axis_index("rep")


def scalars(*values):
    return jnp.stack(values).astype(jnp.int32)


def estimate(microseconds, moved):
    return pl.CostEstimate(flops=1000, bytes_accessed=1000, transcendentals=0)


def params(mib):
    return pltpu.CompilerParams(vmem_limit_bytes=mib * MIB)


def after(tensor, *earlier):
    return lax.optimization_barrier((tensor,) + earlier)[0]


def by_core(own, got, axis):
    core = position()[1]
    return jnp.where(
        core == 0, jnp.stack([own, got], axis), jnp.stack([got, own], axis)
    )


def columns_kernel(blocks, where_ref, *refs):
    ins, (own_ref, other_ref) = refs[:-2], refs[-2:]
    for side in range(2):

        @pl.when(where_ref[1] == side)
        def _():
            for out_ref, parity in ((own_ref, side), (other_ref, 1 - side)):
                start = 0
                for ref, block in zip(ins, blocks):
                    for i in range(parity, ref.shape[2] // block, 2):
                        out_ref[0, :, start : start + block] = ref[0, :, i * block : (i + 1) * block]
                        start += block


def column_pieces(shards):
    plane, core, member = position()
    owners, count = lax.axis_size("fsdp"), lax.axis_size("rep")
    rows = shards[0].shape[1] // count
    blocks = tuple(
        size // owners for size in (shards[0].shape[2] // 3, shards[1].shape[2])
    )
    columns = sum(shard.shape[2] for shard in shards) // 2
    shape = jax.ShapeDtypeStruct((LAYERS, rows, columns), jnp.bfloat16)
    out = pl.BlockSpec((1, rows, columns), lambda layer, where: (layer, 0, 0))
    own, other = pl.pallas_call(
        functools.partial(columns_kernel, blocks),
        out_shape=[shape, shape],
        grid_spec=pltpu.PrefetchScalarGridSpec(
            num_scalar_prefetch=1,
            grid=(LAYERS,),
            in_specs=[
                pl.BlockSpec((1, rows, shard.shape[2]), lambda layer, where: (layer, where[0], 0))
                for shard in shards
            ],
            out_specs=[out, out],
        ),
        cost_estimate=estimate(0, 4 * LAYERS * rows * columns * 2),
    )(scalars(member, core), *shards)
    both = by_core(own, swap(other, "fsdp", 1), 1)
    split = shards[0].shape[2] // 2
    both = both.reshape(LAYERS, 2 * rows, columns)
    return both[..., :split], both[..., split:]


def place_kernel(half_rows, blocks, parts, where_ref, *refs):
    count = len(parts)
    pieces, outs, (in_sems, out_sems) = refs[:count], refs[count : -count - 2], refs[-2:]
    held = refs[-count - 2 : -2]
    plane, member = where_ref[0], where_ref[1]
    arrivals = []
    for i in range(count):
        arrivals.append(pltpu.make_async_copy(pieces[i], held[i], in_sems.at[i]))
        arrivals[-1].start()
    copies = []
    for i, (k, halves) in enumerate(parts):
        arrivals[i].wait()
        for j in range(pieces[0].shape[0]):
            for b, (row, rows, column, columns, put) in enumerate(blocks):
                if row // half_rows not in halves:
                    continue
                first = row - halves[0] * half_rows
                copy = pltpu.make_async_copy(
                    held[i].at[j, first : first + rows, column : column + columns],
                    put(outs, j ^ plane, k ^ member),
                    out_sems.at[b, i, j],
                )
                copy.start()
                copies.append(copy)
    for copy in copies:
        copy.wait()


def place(pieces, parts, shapes, blocks):
    plane, core, member = position()
    planes = pieces[0].shape[0]
    outs = pl.pallas_call(
        functools.partial(place_kernel, pieces[0].shape[1] // 2, blocks, parts),
        out_shape=[jax.ShapeDtypeStruct(shape, pieces[0].dtype) for shape in shapes],
        in_specs=[pl.BlockSpec(memory_space=pltpu.SMEM)]
        + [pl.BlockSpec(memory_space=pl.ANY)] * len(pieces),
        out_specs=[pl.BlockSpec(memory_space=pl.ANY)] * len(shapes),
        scratch_shapes=[pltpu.VMEM(piece.shape, piece.dtype) for piece in pieces]
        + [
            pltpu.SemaphoreType.DMA((len(pieces),)),
            pltpu.SemaphoreType.DMA((len(blocks), len(pieces), planes)),
        ],
        compiler_params=params(20),
        cost_estimate=estimate(0, 4 * sum(piece.size for piece in pieces)),
    )(scalars(plane, member), *pieces)
    return [out.reshape(-1, out.shape[-1]) for out in outs]


def put_pair(side):
    return lambda outs, plane, member: outs[0].at[plane, side, member]


def place_first(pieces, parts, count, split):
    planes, rows, columns = pieces[0].shape
    half, rest = rows // 2, columns - split

    def put(side):
        return lambda outs, plane, member: outs[1].at[
            plane, member, :, side * rest : (side + 1) * rest
        ]

    shapes = [(planes, 2, count, half, split), (planes, count, half, 2 * rest)]
    blocks = [(side * half, half, 0, split, put_pair(side)) for side in range(2)]
    blocks += [(side * half, half, split, rest, put(side)) for side in range(2)]
    return place(pieces, parts, shapes, blocks)


def place_second(pieces, parts, count):
    planes, rows, columns = pieces[0].shape
    half, fine, width = rows // 2, rows // 4, columns // 2

    def put(side):
        return lambda outs, plane, member: outs[1].at[plane, member, side]

    shapes = [(planes, 2, count, fine, columns), (planes, count, 2, half, width)]
    blocks = [(side * fine, fine, 0, columns, put_pair(side)) for side in range(2)]
    blocks += [(half, half, side * width, width, put(side)) for side in range(2)]
    return place(pieces, parts, shapes, blocks)


def gather_planes(piece, *earlier, beside=()):
    column, sent, step = piece[None], list(earlier), lax.axis_size("fsdp") // 4
    while step:
        got = swap(after(column, *sent[-1:], *(beside if len(sent) > len(earlier) else ())), "fsdp", 2 * step)
        sent.append(got)
        column = jnp.stack([column, got], 1).reshape((-1,) + piece.shape)
        step //= 2
    return column, sent[len(earlier) :]


def gather_neighbours(column, earlier):
    held = {0: [column]}
    for bit in range(lax.axis_size("rep").bit_length() - 1):
        held[1 << bit] = [swap(after(column, *earlier), "rep", 1 << bit)]
    return held, [held[k][0] for k in held if k]


def gather_members(held, beside):
    count, rows = lax.axis_size("rep"), held[0][0].shape[1] // 2
    earlier = [held[k][0] for k in held if k] + list(beside)
    for level in range(1, count.bit_length() - 1):
        sent = []
        for k in range(1, count):
            if bin(k).count("1") != level + 1:
                continue
            held[k] = []
            for half, last in ((0, k & -k), (1, 1 << (k.bit_length() - 1))):
                source = held[k ^ last]
                if len(source) == 1:
                    source = source[0][:, half * rows : (half + 1) * rows]
                else:
                    source = source[half]
                held[k].append(swap(after(source, *earlier), "rep", last))
            sent += held[k]
        earlier = sent
    arrays, parts = [], []
    for k in range(count):
        for half, array in enumerate(held[k]):
            arrays.append(array)
            parts.append((k, (0, 1) if len(held[k]) == 1 else (half,)))
    return arrays, parts, earlier


def message_pieces(shards):
    heads, expand = column_pieces((shards[2], shards[10]))
    pieces = []
    for layer in range(LAYERS):
        output, shrink = quarter(shards[5][layer]), quarter(shards[12][layer])
        half = output.shape[1] // 2
        packed = jnp.concatenate([output[:, :half], output[:, half:]], 0)
        pieces.append(jnp.concatenate([heads[layer], packed], 1))
        half = shrink.shape[0] // 2
        packed = jnp.concatenate([shrink[:half], shrink[half:]], 1)
        pieces.append(jnp.concatenate([expand[layer], packed], 0))
    return pieces


def quarter(param):
    rows = param.shape[0] // lax.axis_size("rep")
    return lax.dynamic_slice_in_dim(param, lax.axis_index("rep") * rows, rows, 0)


def gather_small(all_params):
    packed = jnp.concatenate([all_params[i] for i in SMALL], 1)
    whole, owner, step = packed[None], lax.axis_index("fsdp"), 1
    while step < lax.axis_size("fsdp"):
        got = swap(whole, "fsdp", step)
        whole = jnp.where(
            (owner // step) % 2 == 0,
            jnp.concatenate([whole, got], 0),
            jnp.concatenate([got, whole], 0),
        )
        step *= 2
    vectors, start = [], 0
    for i in SMALL:
        size = all_params[i].shape[1]
        vectors.append(
            jnp.moveaxis(whole[:, :, start : start + size], 0, 1).reshape(LAYERS, -1)
        )
        start += size
    return vectors, got


def link_orders():
    bits = list(range(lax.axis_size("rep").bit_length() - 1))
    return [bits, bits[::-1]]


def divide(blocks, shapes, bits, outs):
    for side in range(len(shapes)):
        high, later = shapes[side]
        for i in range(high):
            for j in range(later):
                base = 2 * i * later + j
                for out_ref, index in (
                    (outs[2 * side], base + bits[side] * later),
                    (outs[2 * side + 1], base + (1 - bits[side]) * later),
                ):
                    for row, column, block in blocks(side, index):
                        out_ref[
                            0, i, j, row : row + block.shape[0], column : column + block.shape[1]
                        ] = block


def block_grad_kernel(shapes, where_ref, left_ref, grad_ref, more_ref, other_ref, *refs):
    outs, held, extra = refs[:-2], refs[-2], refs[-1]
    held[...] = low(weight_dot(left_ref[...], grad_ref[...])).reshape(held.shape)
    extra[...] = low(weight_dot(more_ref[...], other_ref[...])).reshape(extra.shape)
    rows, half, tall = held.shape[2], held.shape[3] // 2, extra.shape[1] // 2

    def blocks(side, index):
        return [
            (p * rows, 0, held[p, index, :, side * half : (side + 1) * half]) for p in range(2)
        ] + [(2 * rows, 0, extra[index, side * tall : (side + 1) * tall])]

    divide(blocks, shapes, (where_ref[0], where_ref[1]), outs)


def mixed_grad_kernel(shapes, where_ref, left_ref, grad_ref, more_ref, other_ref, *refs):
    outs, held, extra = refs[:4], refs[4], refs[5]
    held[...] = low(weight_dot(left_ref[...], grad_ref[...])).reshape(held.shape)
    extra[...] = low(weight_dot(more_ref[...], other_ref[...])).reshape(extra.shape)
    rows, rest = held.shape[2], extra.shape[2] // 2
    half = (held.shape[3] + rest) // 2

    def blocks(side, index):
        if side == 0:
            return [(p * rows, 0, held[p, index, :, :half]) for p in range(2)]
        return [(p * rows, 0, held[p, index, :, half:]) for p in range(2)] + [
            (p * rows, half - rest, extra[index, :, p * rest : (p + 1) * rest]) for p in range(2)
        ]

    divide(blocks, shapes, (where_ref[0], where_ref[1]), outs)


def grad_call(kernel, arrays, widths, rows, columns, scratch, orders):
    planes, count = lax.axis_size("fsdp") // 2, lax.axis_size("rep")
    member = lax.axis_index("rep")
    shapes = tuple((count >> (order[0] + 1), 1 << order[0]) for order in orders)
    tokens = arrays[0].shape[0]
    specs = []
    for array, width in zip(arrays, widths):
        if width is None:
            specs.append(pl.BlockSpec(array.shape, lambda z, where: (0, 0)))
        else:
            specs.append(pl.BlockSpec((tokens, width), lambda z, where: (0, z)))
    out_shapes, out_specs = [], []
    for high, later in shapes:
        block = (high, later, rows, columns // len(orders))
        out_specs += [pl.BlockSpec((1,) + block, lambda z, where: (z, 0, 0, 0, 0))] * 2
        out_shapes += [jax.ShapeDtypeStruct((planes,) + block, jnp.bfloat16)] * 2
    return pl.pallas_call(
        functools.partial(kernel, shapes),
        out_shape=out_shapes,
        grid_spec=pltpu.PrefetchScalarGridSpec(
            num_scalar_prefetch=1,
            grid=(planes,),
            in_specs=specs,
            out_specs=out_specs,
            scratch_shapes=[pltpu.VMEM(size, jnp.bfloat16) for size in scratch],
        ),
        compiler_params=params(40),
        cost_estimate=estimate(5, 0),
    )(scalars(*[(member >> order[0]) & 1 for order in orders]), *arrays)


def block_grad(left, grad, more, other, orders):
    planes, count = lax.axis_size("fsdp") // 2, lax.axis_size("rep")
    widths = left.shape[1] // planes, more.shape[1] // planes
    columns = grad.shape[1]
    rows, tall = widths[0] // (2 * count), widths[1] // count
    return grad_call(
        block_grad_kernel, (left, grad, more, other), (widths[0], None, widths[1], None),
        2 * rows + tall // 2, columns,
        [(2, count, rows, columns), (count, tall, other.shape[1])], orders,
    )


def mixed_grad(left, grad, more, other, orders):
    planes, count = lax.axis_size("fsdp") // 2, lax.axis_size("rep")
    widths = left.shape[1] // planes, more.shape[1] // planes
    columns, rest = grad.shape[1], other.shape[1]
    rows = widths[1] // count
    if widths[1] % 128:
        first = low(weight_dot(left, grad)).reshape(planes, 2, count, rows, columns)
        second = low(weight_dot(more, other)).reshape(planes, count, rows, 2, rest // 2)
        total = jnp.concatenate([jnp.swapaxes(first, 1, 2), jnp.swapaxes(second, 2, 3)], 4)
        total = total.reshape(planes, count, 2 * rows, -1)
        half, member = total.shape[3] // 2, lax.axis_index("rep")
        top = count // 2
        left_part = total[..., :half].reshape(planes, top, 2, 1, 2 * rows, half)
        right_part = total[..., half:].reshape(planes, 1, 2, top, 2 * rows, half)
        sides = member % 2, member // top
        return [
            pick(part, side if kept else 1 - side, 2)
            for part, side in zip((left_part, right_part), sides)
            for kept in (True, False)
        ]
    return grad_call(
        mixed_grad_kernel, (left, grad, more, other), (widths[0], None, widths[1], None),
        2 * rows, columns + rest // 2,
        [(2, count, rows, columns), (count, rows, rest)], orders,
    )


def split_kernel(where_ref, *refs):
    count = len(refs) // 4
    for n in range(count):
        bit = where_ref[n]
        keep_in, got_ref = refs[2 * n], refs[2 * n + 1]
        keep_ref, send_ref = refs[2 * (count + n)], refs[2 * (count + n) + 1]
        keep_ref[0] = low(widen(keep_in[0, bit]) + widen(got_ref[0, bit]))
        send_ref[0] = low(widen(keep_in[0, 1 - bit]) + widen(got_ref[0, 1 - bit]))


def add_split(pairs, later, sides, rows):
    if len({pair[0].size // n for pair, n in zip(pairs, later)}) > 1:
        return [
            out
            for pair, n, side in zip(pairs, later, sides)
            for out in add_split([pair], [n], [side], rows)
        ]
    arrays, in_specs, out_specs, out_shapes = [], [], [], []
    for pair, n in zip(pairs, later):
        columns = pair[0].shape[-1]
        for array in pair:
            arrays.append(array.reshape(-1, 2, n, rows, columns))
            in_specs.append(
                pl.BlockSpec((1, 2, n, rows, columns), lambda i, where: (i, 0, 0, 0, 0))
            )
            out_specs.append(pl.BlockSpec((1, n, rows, columns), lambda i, where: (i, 0, 0, 0)))
            out_shapes.append(
                jax.ShapeDtypeStruct((arrays[-1].shape[0], n, rows, columns), jnp.bfloat16)
            )
    return pl.pallas_call(
        split_kernel,
        out_shape=out_shapes,
        grid_spec=pltpu.PrefetchScalarGridSpec(
            num_scalar_prefetch=1,
            grid=(arrays[0].shape[0],),
            in_specs=in_specs,
            out_specs=out_specs,
        ),
        compiler_params=params(24),
        cost_estimate=estimate(0, sum(array.size for array in arrays) * 3),
    )(scalars(*sides), *arrays)


def merge_kernel(where_ref, *refs):
    arrays, (keep_ref, send_ref) = refs[:-2], refs[-2:]
    half = arrays[0].shape[-1]
    for out_ref, bit in ((keep_ref, where_ref[0]), (send_ref, 1 - where_ref[0])):
        start = 0
        for n in range(0, len(arrays), 4):
            left_ref, left_got, right_ref, right_got = arrays[n : n + 4]
            rows = slice(start, start + left_ref.shape[2])
            out_ref[0, rows, :half] = low(widen(left_ref[0, bit]) + widen(left_got[0, bit]))
            out_ref[0, rows, half:] = low(widen(right_ref[0, bit]) + widen(right_got[0, bit]))
            start += left_ref.shape[2]


def add_merge(messages, side):
    half = messages[0][0].shape[-1]
    arrays, specs, total = [], [], 0
    for message in messages:
        rows = message[0].shape[-2]
        arrays += [array.reshape(-1, 2, rows, half) for array in message]
        specs += [pl.BlockSpec((1, 2, rows, half), lambda i, where: (i, 0, 0, 0))] * 4
        total += rows
    high = arrays[0].shape[0]
    given = pl.BlockSpec((1, total, 2 * half), lambda i, where: (i, 0, 0))
    shape = jax.ShapeDtypeStruct((high, total, 2 * half), jnp.bfloat16)
    return pl.pallas_call(
        merge_kernel,
        out_shape=[shape, shape],
        grid_spec=pltpu.PrefetchScalarGridSpec(
            num_scalar_prefetch=1,
            grid=(high,),
            in_specs=specs,
            out_specs=[given, given],
        ),
        compiler_params=params(24),
        cost_estimate=estimate(0, sum(array.size for array in arrays) * 3),
    )(scalars(side), *arrays)


def reduce_members(arrays):
    member, lanes = lax.axis_index("rep"), range(2)
    rows, orders = arrays[0].shape[-2], link_orders()
    bits = [sorted(order) for order in orders]
    keeps, sends = list(arrays[::2]), list(arrays[1::2])
    for n in range(len(orders[0])):
        gots = [swap(sends[i], "rep", 1 << orders[i][n]) for i in lanes]
        for i in lanes:
            bits[i].remove(orders[i][n])
        token = yield sends, gots
        gots = [after(got, token) for got in gots]
        if n + 1 < len(orders[0]):
            later = [1 << bits[i].index(orders[i][n + 1]) for i in lanes]
            sides = [(member >> orders[i][n + 1]) & 1 for i in lanes]
            outs = add_split(list(zip(keeps, gots)), later, sides, rows)
            keeps, sends = list(outs[::2]), list(outs[1::2])
    return [keeps[0], gots[0], keeps[1], gots[1]]


def reduce_planes(messages):
    plane, planes = position()[0], lax.axis_size("fsdp") // 2
    rows = sum(message[0].shape[-2] for message in messages)
    keep, send = add_merge(messages, plane % 2)
    step = 1
    while True:
        got = swap(send, "fsdp", 2 * step)
        token = yield [send], [got]
        got = after(got, token)
        step *= 2
        if step == planes:
            return low(widen(keep) + widen(got)).reshape(rows, -1)
        keep, send = add_split([(keep, got)], [1], [(plane // step) % 2], rows)


def finish_columns(total, columns):
    core = position()[1]
    rows = total.shape[0] // 2
    part = total[:, :columns].reshape(2, rows, columns)
    got = swap(pick(part, 1 - core, 0), "fsdp", 1)
    part = jnp.concatenate([pick(part, core, 0), got], 0)
    return jnp.concatenate([part, total[:, columns:]], 1)


def spread(own, low_last):
    pieces = [own]
    for k in range(1, lax.axis_size("rep")):
        last = k & -k if low_last else 1 << (k.bit_length() - 1)
        pieces.append(swap(pieces[k ^ last], "rep", last))
    return pieces


def column_out(out_ref, block, side, ref, start):
    rows = out_ref.shape[2]
    for i in range(out_ref.shape[3] // block):
        first = start if i % 2 == side else start + rows
        out_ref[0, 0, :, i * block : (i + 1) * block] = widen(
            ref[first : first + rows, (i // 2) * block : (i // 2 + 1) * block]
        )


def early_out_kernel(block, where_ref, *refs):
    expand_out, shrink_out = refs[-2:]
    for k, ref in enumerate(refs[:-4]):
        for side in range(2):

            @pl.when((pl.program_id(0) == k) & (where_ref[1] == side))
            def _():
                column_out(expand_out, block, side, ref, 0)

        @pl.when(pl.program_id(0) == k)
        def _():
            rows, columns = shrink_out.shape[2] // 2, shrink_out.shape[3]
            start = ref.shape[0] - rows
            shrink_out[0, 0, :rows] = widen(ref[start:, :columns])
            shrink_out[0, 0, rows:] = widen(ref[start:, columns:])


def late_out_kernel(block, where_ref, *refs):
    heads_out, output_out = refs[-2:]
    for k, ref in enumerate(refs[:-4]):
        for side in range(2):

            @pl.when((pl.program_id(0) == k) & (where_ref[1] == side))
            def _():
                column_out(heads_out, block, side, ref, 0)

        @pl.when(pl.program_id(0) == k)
        def _():
            rows, half = output_out.shape[2], output_out.shape[3] // 2
            start = ref.shape[1] - half
            output_out[0, 0, :, :half] = widen(ref[:rows, start:])
            output_out[0, 0, :, half:] = widen(ref[rows:, start:])


def write_out(kernel, layer, pieces, sizes, earlier):
    plane, core, member = position()
    count = len(pieces)
    shapes = [(LAYERS, count) + size for size in sizes]
    if earlier is None:
        earlier = [jnp.zeros((8, 128), jnp.float32)] * len(sizes)
        aliases = {}
    else:
        earlier = [array.reshape(shape) for array, shape in zip(earlier, shapes)]
        aliases = {1 + count + i: i for i in range(len(sizes))}
    return pl.pallas_call(
        kernel,
        out_shape=[jax.ShapeDtypeStruct(shape, jnp.float32) for shape in shapes],
        grid_spec=pltpu.PrefetchScalarGridSpec(
            num_scalar_prefetch=1,
            grid=(count,),
            in_specs=[pl.BlockSpec(piece.shape, lambda k, where: (0, 0)) for piece in pieces]
            + [pl.BlockSpec(memory_space=pl.ANY)] * len(sizes),
            out_specs=[
                pl.BlockSpec((1, 1) + size, lambda k, where: (layer, k ^ where[0], 0, 0))
                for size in sizes
            ],
        ),
        input_output_aliases=aliases,
        compiler_params=params(24),
        cost_estimate=estimate(0, count * pieces[0].size * 6),
    )(scalars(member, core), *pieces, *earlier)


def reduce_small(grads, earlier):
    owners, count = lax.axis_size("fsdp"), lax.axis_size("rep")
    total = jnp.concatenate([g.reshape(LAYERS, owners, -1) for g in grads], 2)
    total = after(total, *earlier)
    owner = lax.axis_index("fsdp")
    step = owners // 2
    while step:
        total = total.reshape(LAYERS, 2, step, -1)
        mine = (owner // step) % 2
        total = pick(total, mine, 1) + swap(pick(total, 1 - mine, 1), "fsdp", step)
        step //= 2
    step = 1
    while step < count:
        total = total + swap(total, "rep", step)
        step *= 2
    total = total.reshape(LAYERS, -1)
    outs, start = [], 0
    for g in grads:
        size = g.shape[1] // owners
        outs.append(total[:, start : start + size])
        start += size
    return outs


def other_half(rows):
    return swap(rows, "fsdp", lax.axis_size("fsdp") // 2)


def image_side():
    return lax.axis_index("fsdp") // (lax.axis_size("fsdp") // 2)


def regroup(blocks):
    side = image_side()
    return pick(blocks, side, 0), other_half(pick(blocks, 1 - side, 0))


def ungroup(rows, got):
    own, got = rows[: rows.shape[0] // 2], got.astype(rows.dtype)
    return jnp.where(image_side() == 0, jnp.stack([own, got]), jnp.stack([got, own]))


def chips_per_image():
    return lax.axis_size("fsdp") // 4


def share_rows(local_kv):
    shared = [local_kv]
    for k in range(1, chips_per_image()):
        low_bit = k & -k
        shared.append(swap(shared[k ^ low_bit], "fsdp", 2 * low_bit))
    return shared


def collect_rows(own, others):
    chips = chips_per_image()
    if chips == 2:
        got = swap(others, "fsdp", 2)
        return low(widen(own) + widen(got)), got
    total = jnp.concatenate([own, others], 1)
    while chips > 1:
        rows = total.shape[1] // 2
        got = swap(total[:, rows:], "fsdp", chips)
        total = low(widen(total[:, :rows]) + widen(got))
        chips //= 2
    return total, got


def both_cores(rows):
    return jnp.concatenate([rows, swap(rows, "fsdp", 1)], 0)


def one_head(tensor, head):
    half = tensor.shape[1] // 2
    lane = lax.broadcasted_iota(jnp.int32, tensor.shape, 1)
    keep = lane < half if head == 0 else lane >= half
    return jnp.where(keep, tensor, jnp.zeros_like(tensor))


def join(refs, held):
    start = 0
    for ref in refs:
        held[start : start + ref.shape[0], :] = ref[...]
        start += ref.shape[0]
    return held[...]


def attend_kernel(factor, parts, query_ref, *refs):
    out_ref, log_ref, held_keys, held_values = refs[2 * parts :]
    keys, values = join(refs[:parts], held_keys), join(refs[parts : 2 * parts], held_values)
    results, logs = [], []
    for head in range(2):
        scores = input_dot(one_head(query_ref[...], head), keys)
        largest = jnp.max(scores, -1, keepdims=True)
        weights = jnp.exp2((scores - largest) * factor)
        total = jnp.sum(weights, -1, keepdims=True)
        results.append(forward_dot(low(weights), values) / total)
        logs.append(largest * factor + jnp.log2(total))
    out_ref[...] = low(one_head(results[0], 0) + one_head(results[1], 1))
    shape = log_ref.shape
    log_ref[...] = one_head(jnp.broadcast_to(logs[0], shape), 0) + one_head(
        jnp.broadcast_to(logs[1], shape), 1
    )


def pair_block(rows, start):
    return pl.BlockSpec((rows, 128), lambda i: (0, start + i))


def kv_parts(projected, others):
    pairs = projected.shape[1] // 384
    if projected.shape[0] % 16:
        others = [jnp.concatenate([projected[:, 128 * pairs :]] + others, 0)]
        parts = []
    else:
        parts = [(projected, pairs, 2 * pairs)]
    return parts + [(other, 0, pairs) for other in others]


def kv_specs(parts, first=0):
    keys = [pair_block(array.shape[0], first + start) for array, start, unused in parts]
    values = [pair_block(array.shape[0], first + start) for array, unused, start in parts]
    rows = sum(array.shape[0] for array, unused, more in parts)
    held = [pltpu.VMEM((rows, 128), jnp.bfloat16)] * 2
    return keys + values, [array for array, unused, more in parts] * 2, held


def attend(projected, others, head_size):
    tokens, width = projected.shape[0], projected.shape[1] // 3
    pairs = width // 128
    parts = kv_parts(projected, others)
    specs, arrays, held = kv_specs(parts)
    factor = head_size ** (-0.5) * math.log2(math.e)
    return pl.pallas_call(
        functools.partial(attend_kernel, factor, len(parts)),
        out_shape=[
            jax.ShapeDtypeStruct((tokens, width), jnp.bfloat16),
            jax.ShapeDtypeStruct((tokens, width), jnp.float32),
        ],
        grid=(pairs,),
        in_specs=[pair_block(tokens, 0)] + specs,
        out_specs=[pair_block(tokens, 0), pair_block(tokens, 0)],
        scratch_shapes=held,
        compiler_params=params(56),
        cost_estimate=estimate(18, 0),
    )(projected, *arrays)


def attend_back_kernel(factor, scale, parts, query_ref, *refs):
    log_ref, grad_ref, dq_ref, own_ref, others_ref, held_keys, held_values = refs[2 * parts :]
    keys, values = join(refs[:parts], held_keys), join(refs[parts : 2 * parts], held_values)
    d_query, d_key, d_value = [], 0.0, 0.0
    for head in range(2):
        query = one_head(query_ref[...], head)
        grad = one_head(grad_ref[...], head)
        half = query.shape[1] // 2
        log_total = log_ref[:, head * half : head * half + 1]
        probs = jnp.exp2(input_dot(query, keys) * factor - log_total)
        products = probs * input_dot(grad, values)
        d_scores = low(products - probs * jnp.sum(products, -1, keepdims=True))
        d_query.append(forward_dot(d_scores, keys))
        d_key = d_key + weight_dot(d_scores, query)
        d_value = d_value + weight_dot(low(probs), grad)
    dq_ref[...] = low((one_head(d_query[0], 0) + one_head(d_query[1], 1)) * scale)
    rows = own_ref.shape[1]
    for i, total in enumerate((low(d_key * scale), low(d_value))):
        own_ref[i] = total[:rows]
        others_ref[i] = total[rows:]


def attend_back(projected, others, log_total, d_attended, head_size, first, pairs):
    tokens, width = d_attended.shape[0], 128 * pairs
    parts = kv_parts(projected, others)
    specs, arrays, held = kv_specs(parts, first)
    rows = held[0].shape[0]
    scale = head_size ** (-0.5)
    own, taken = pair_block(tokens, 0), pair_block(tokens, first)
    return pl.pallas_call(
        functools.partial(attend_back_kernel, scale * math.log2(math.e), scale, len(parts)),
        out_shape=[
            jax.ShapeDtypeStruct((tokens, width), jnp.bfloat16),
            jax.ShapeDtypeStruct((2, tokens, width), jnp.bfloat16),
            jax.ShapeDtypeStruct((2, rows - tokens, width), jnp.bfloat16),
        ],
        grid=(pairs,),
        in_specs=[taken] + specs + [taken, taken],
        out_specs=[
            own,
            pl.BlockSpec((2, tokens, 128), lambda i: (0, 0, i)),
            pl.BlockSpec((2, rows - tokens, 128), lambda i: (0, 0, i)),
        ],
        scratch_shapes=held,
        compiler_params=params(60),
        cost_estimate=estimate(8 * pairs, 0),
    )(projected, *arrays, log_total, d_attended)


def add_tile(part, own_ref, other_ref, total_ref):
    @pl.when(pl.program_id(0) == 0)
    def _():
        total_ref[...] = part

    @pl.when(pl.program_id(0) > 0)
    def _():
        total_ref[...] += part

    @pl.when(pl.program_id(0) == pl.num_programs(0) - 1)
    def _():
        half = own_ref.shape[0]
        own_ref[...] = total_ref[:half]
        other_ref[...] = low(total_ref[half:])


def expand_kernel(
    rows_ref, expand_ref, bias_ref, shrink_ref, active_ref, slope_ref, own_ref, other_ref, total_ref
):
    hidden = forward_dot(rows_ref[...], expand_ref[...]) + bias_ref[...]
    normal = 0.5 + 0.5 * lax.erf(hidden * math.sqrt(0.5))
    density = jnp.exp2(hidden * hidden * (-0.5 * math.log2(math.e)))
    slope_ref[...] = low(normal + hidden * density * (1.0 / math.sqrt(2.0 * math.pi)))
    active = low(hidden * normal)
    active_ref[...] = active
    add_tile(forward_dot(active, shrink_ref[...]), own_ref, other_ref, total_ref)


def feed_forward(rows_in, expand, expand_bias, shrink):
    tokens, width = rows_in.shape
    units = expand.shape[1]
    tile = 512
    whole = pl.BlockSpec((tokens, width), lambda i: (0, 0))
    half = pl.BlockSpec((tokens // 2, width), lambda i: (0, 0))
    part = pl.BlockSpec((tokens, tile), lambda i: (0, i))
    return pl.pallas_call(
        expand_kernel,
        out_shape=[
            jax.ShapeDtypeStruct((tokens, units), jnp.bfloat16),
            jax.ShapeDtypeStruct((tokens, units), jnp.bfloat16),
            jax.ShapeDtypeStruct((tokens // 2, width), jnp.float32),
            jax.ShapeDtypeStruct((tokens // 2, width), jnp.bfloat16),
        ],
        grid=(units // tile,),
        in_specs=[
            whole,
            pl.BlockSpec((width, tile), lambda i: (0, i)),
            pl.BlockSpec((1, tile), lambda i: (0, i)),
            pl.BlockSpec((tile, width), lambda i: (i, 0)),
        ],
        out_specs=[part, part, half, half],
        scratch_shapes=[pltpu.VMEM((tokens, width), jnp.float32)],
        compiler_params=params(32),
        cost_estimate=estimate(14, 0),
    )(rows_in, expand, expand_bias[None], shrink)


def shrink_kernel(
    grad_ref, shrink_ref, slope_ref, expand_ref, hidden_ref, bias_ref, own_ref, other_ref, total_ref
):
    d_hidden = low(input_dot(grad_ref[...], shrink_ref[...]) * widen(slope_ref[...]))
    hidden_ref[...] = d_hidden
    bias_ref[...] = jnp.sum(widen(d_hidden), 0, keepdims=True)
    add_tile(input_dot(d_hidden, expand_ref[...]), own_ref, other_ref, total_ref)


def feed_back(d_mlp, shrink, slope, expand):
    tokens, width = d_mlp.shape
    units = expand.shape[1]
    tile = 512
    whole = pl.BlockSpec((tokens, width), lambda i: (0, 0))
    half = pl.BlockSpec((tokens // 2, width), lambda i: (0, 0))
    part = pl.BlockSpec((tokens, tile), lambda i: (0, i))
    return pl.pallas_call(
        shrink_kernel,
        out_shape=[
            jax.ShapeDtypeStruct((tokens, units), jnp.bfloat16),
            jax.ShapeDtypeStruct((1, units), jnp.float32),
            jax.ShapeDtypeStruct((tokens // 2, width), jnp.float32),
            jax.ShapeDtypeStruct((tokens // 2, width), jnp.bfloat16),
        ],
        grid=(units // tile,),
        in_specs=[
            whole,
            pl.BlockSpec((tile, width), lambda i: (i, 0)),
            part,
            pl.BlockSpec((width, tile), lambda i: (0, i)),
        ],
        out_specs=[part, pl.BlockSpec((1, tile), lambda i: (0, i)), half, half],
        scratch_shapes=[pltpu.VMEM((tokens, width), jnp.float32)],
        compiler_params=params(32),
        cost_estimate=estimate(9, 0),
    )(d_mlp, shrink, slope, expand)


def core_half(vector):
    core = position()[1]
    return pick(widen(vector).reshape(lax.axis_size("fsdp") // 2, 2, -1), core, 1).reshape(-1)


def core_fill(half):
    parts = half.reshape(lax.axis_size("fsdp") // 2, -1)
    return by_core(parts, jnp.zeros_like(parts), 1).reshape(-1)


def normed_rows(tok_rows, gathered):
    return both_cores(low(layer_norm(tok_rows, widen(gathered[0]), widen(gathered[1]))))


def project(normed, gathered, token):
    heads_weight, query_bias, value_bias = gathered[2], gathered[3], gathered[4]
    width = normed.shape[1]
    bias_row = jnp.concatenate(
        [core_half(query_bias), jnp.zeros((width // 2,), jnp.float32), core_half(value_bias)]
    )
    projected = low(forward_dot(normed, heads_weight) + bias_row)
    return projected, share_rows(after(projected[:, width // 2 :], token))[1:]


def forward_layer(
    tok_rows, normed, projected, others, gathered, beside, neighbours, following
):
    (
        attn_norm_gain,
        attn_norm_bias,
        heads_weight,
        query_bias,
        value_bias,
        output_weight,
        output_bias,
        attn_layerscale,
        mlp_norm_gain,
        mlp_norm_bias,
        expand_weight,
        expand_bias,
        shrink_weight,
        shrink_bias,
        mlp_layerscale,
    ) = gathered
    tokens, width = tok_rows.shape
    attended, log_total = attend(projected, others, width // HEADS)
    attended = after(attended, *beside)
    got = swap(low(forward_dot(attended[tokens:], output_weight)), "fsdp", 1)
    branch = forward_dot(attended[:tokens], output_weight) + widen(got) + widen(output_bias)
    middle = tok_rows + widen(attn_layerscale) * branch
    normed_two = low(layer_norm(middle, widen(mlp_norm_gain), widen(mlp_norm_bias)))
    normed_two = after(both_cores(normed_two), *neighbours)
    activated, slope, own_sum, other_sum = feed_forward(
        normed_two, expand_weight, core_half(expand_bias), shrink_weight
    )
    other_sum = after(other_sum, *following)
    mlp_out = own_sum + widen(swap(other_sum, "fsdp", 1)) + widen(shrink_bias)
    result = middle + widen(mlp_layerscale) * mlp_out
    saved = (
        tok_rows,
        normed,
        projected,
        others,
        log_total,
        attended,
        branch,
        middle,
        normed_two,
        slope,
        activated,
        mlp_out,
    )
    return (result, saved)


class Later:
    def __init__(self):
        self.running, self.done, self.sends, self.gots = {}, {}, {}, {}

    def begin(self, name, kernel, arrays):
        self.running[name] = reduce_members(kernel(*arrays, link_orders()))
        self.step(name, None)

    def join(self, name, parts, token):
        for part in parts:
            while part in self.running:
                self.step(part, token)
        self.running[name] = reduce_planes([self.done[part] for part in parts])
        self.step(name, None)

    def step(self, name, token):
        try:
            self.sends[name], self.gots[name] = self.running[name].send(token)
        except StopIteration as end:
            self.done[name] = end.value
            self.sends[name] = self.gots[name] = []
            del self.running[name]

    def sent(self, value, *names):
        return after(value, *[array for name in names for array in self.sends[name]])

    def came(self, value, *names):
        return after(value, *[array for name in names for array in self.gots[name]])


def backward_layer(d_result, saved, gathered, later, new, old, activation_got):
    (
        attn_norm_gain,
        attn_norm_bias,
        heads_weight,
        query_bias,
        value_bias,
        output_weight,
        output_bias,
        attn_layerscale,
        mlp_norm_gain,
        mlp_norm_bias,
        expand_weight,
        expand_bias,
        shrink_weight,
        shrink_bias,
        mlp_layerscale,
    ) = gathered
    (
        tok_rows,
        normed,
        projected,
        others,
        log_total,
        attended,
        branch,
        middle,
        normed_two,
        slope,
        activated,
        mlp_out,
    ) = saved
    tokens, width = tok_rows.shape
    d_mlp = low(d_result * widen(mlp_layerscale))
    d_mlp_both = both_cores(d_mlp)
    g_mlp_scale = jnp.sum(d_result * mlp_out, 0)
    g_shrink_bias = column_sum(d_mlp)
    d_hidden, g_expand_bias, own_sum, other_sum = feed_back(
        d_mlp_both, shrink_weight, slope, expand_weight
    )
    block, mixed, block_planes, mixed_planes = new
    if old:
        other_sum = later.came(other_sum, old[0])
        later.join(old[2], [old[0]], other_sum)
        d_hidden = later.sent(d_hidden, old[2])
    got = swap(other_sum, "fsdp", 1)
    later.begin(block, block_grad, (normed_two, d_hidden, activated, d_mlp_both))
    own_sum = later.sent(own_sum, block)
    if not old:
        own_sum = after(own_sum, activation_got)
    d_middle_norm, g_mlp_gain, g_mlp_shift = norm_back(
        middle, widen(mlp_norm_gain), widen(mlp_norm_bias), own_sum + widen(got)
    )
    d_middle = d_result + d_middle_norm
    d_branch = low(d_middle * widen(attn_layerscale))
    d_branch_both = both_cores(d_branch)
    g_attn_scale = jnp.sum(d_middle * branch, 0)
    g_output_bias = column_sum(d_branch)
    d_attended = low(input_dot(d_branch_both, output_weight))
    if old:
        later.step(old[1], d_attended)
        d_attended = later.sent(d_attended, old[1])
    pairs = d_attended.shape[1] // 128

    def back(first):
        return attend_back(
            projected, others, log_total, d_attended, width // HEADS, first, pairs // 2
        )

    first_query, d_own, d_others = back(0)
    first_kv, first_got = collect_rows(d_own, d_others)
    if old:
        d_attended = later.came(d_attended, old[2])
        later.step(old[2], first_query)
        d_attended = later.sent(d_attended, old[2])
    second_query, d_own, d_others = back(pairs // 2)
    d_others = after(d_others, first_got)
    second_kv, second_got = collect_rows(d_own, d_others)
    second_query = later.came(second_query, block)
    later.step(block, second_query)
    second_query = later.sent(second_query, block)
    d_query = jnp.concatenate([first_query, second_query], 1)
    d_key = jnp.concatenate([first_kv[0], second_kv[0]], 1)
    d_value = jnp.concatenate([first_kv[1], second_kv[1]], 1)
    d_projected = jnp.concatenate([d_query, d_key, d_value], 1)
    g_query_bias = column_sum(d_query)
    g_value_bias = column_sum(d_value)
    got = swap(low(input_dot(d_projected[tokens:], heads_weight)), "fsdp", 1)
    later.begin(mixed, mixed_grad, (normed, d_projected, attended, d_branch_both))
    d_projected = later.sent(d_projected, mixed)
    if old:
        later.join(old[3], [old[1]], d_projected)
        d_projected = later.sent(d_projected, old[3])
        later.join(block_planes, [block], d_projected)
        d_projected = later.sent(d_projected, block_planes)
    d_normed = input_dot(d_projected[:tokens], heads_weight) + widen(got)
    d_rows_norm, g_attn_gain, g_attn_shift = norm_back(
        tok_rows, widen(attn_norm_gain), widen(attn_norm_bias), d_normed
    )
    d_rows = d_middle + d_rows_norm
    small_grads = (
        g_attn_gain,
        g_attn_shift,
        core_fill(g_query_bias),
        core_fill(g_value_bias),
        g_output_bias,
        g_attn_scale,
        g_mlp_gain,
        g_mlp_shift,
        core_fill(g_expand_bias),
        g_shrink_bias,
        g_mlp_scale,
    )
    return (d_rows, small_grads)


def local(images, cotangent, *all_params):
    owners, count = lax.axis_size("fsdp"), lax.axis_size("rep")
    pieces = message_pieces(all_params)
    small, small_got = gather_small(all_params)
    column, planes = gather_planes(pieces[0], beside=[small_got])
    own, got = regroup(after(images, planes[0]))
    tok_rows = widen(jnp.concatenate([own, got], 0))
    column = after(column, got)
    next_column, next_planes = gather_planes(pieces[1], got)
    held, neighbours = gather_neighbours(column, [])
    members = gather_members(held, [])
    saved_layers, fetched = [], []
    for layer in range(LAYERS):
        gathered = [None] * len(all_params)
        for i, vector in zip(SMALL, small):
            gathered[i] = vector[layer]
        normed = normed_rows(tok_rows, gathered)
        arrays, parts, earlier = members
        arrays[0] = after(arrays[0], next_planes[-1])
        gathered[2], gathered[5] = place_first(
            arrays, parts, count, all_params[2].shape[2] // 2
        )
        projected, others = project(normed, gathered, next_planes[-1])
        held, neighbours = gather_neighbours(next_column, earlier)
        if layer + 1 < LAYERS:
            column, planes = gather_planes(pieces[2 * layer + 2], others[-1])
            beside = planes[:1]
        else:
            own, got = regroup(after(cotangent, others[-1]))
            d_rows = widen(jnp.concatenate([own, got], 0))
            beside, planes, neighbours, next_planes, members = [got], [], [], [], [[]] * 3
        arrays, parts, earlier = gather_members(held, [])
        if layer + 1 < LAYERS:
            next_column, next_planes = gather_planes(pieces[2 * layer + 3], planes[-1])
            held, neighbours = gather_neighbours(column, earlier)
            members = gather_members(held, [])
        arrays[0] = after(arrays[0], *planes[-1:], *next_planes[:1])
        gathered[10], gathered[12] = place_second(arrays, parts, count)
        fetched.append(tuple(gathered))
        tok_rows, saved = forward_layer(
            tok_rows,
            normed,
            projected,
            others,
            gathered,
            beside,
            neighbours,
            next_planes[1:] + members[2],
        )
        saved_layers.append(saved)
    activation_rows = low(tok_rows)
    small_grads = [None] * LAYERS
    outs = {}

    def size(i):
        return (all_params[i].shape[1] // count, all_params[i].shape[2])

    def block_piece(later, layer):
        total = later.done[layer, 2]
        half = total.shape[0] // 2
        return jnp.concatenate([finish_columns(total[:half], total.shape[1]), total[half:]], 0)

    def mixed_piece(later, layer):
        return finish_columns(later.done[layer, 3], size(2)[1] // 2)

    def write_block(layer, pieces):
        outs["block"] = write_out(
            functools.partial(early_out_kernel, size(10)[1] // owners),
            layer, pieces, [size(10), size(12)], outs.get("block"),
        )

    def write_mixed(layer, pieces):
        outs["mixed"] = write_out(
            functools.partial(late_out_kernel, size(2)[1] // 3 // owners),
            layer, pieces, [size(2), size(5)], outs.get("mixed"),
        )

    later = Later()
    for layer in reversed(range(LAYERS)):
        new = [(layer, n) for n in range(4)]
        old = [(layer + 1, n) for n in range(4)] if layer + 1 < LAYERS else None
        if not old:
            activation_got = other_half(activation_rows[activation_rows.shape[0] // 2 :])
        d_rows, small_grads[layer] = backward_layer(
            d_rows, saved_layers[layer], fetched[layer], later, new, old, activation_got
        )
    activations = ungroup(activation_rows, activation_got)
    image_got = other_half(low(d_rows[d_rows.shape[0] // 2 :]))
    d_images = ungroup(d_rows, image_got)
    for name in (old[2], old[3]):
        while name in later.running:
            later.step(name, d_rows)
    first = block_piece(later, layer + 1)
    rows = first.shape[0]
    first = after(jnp.concatenate([first, mixed_piece(later, layer + 1)], 0), d_rows)
    later.step(new[1], d_rows)
    pieces = spread(later.sent(first, new[1]), True)
    write_block(layer + 1, [piece[:rows] for piece in pieces])
    write_mixed(layer + 1, [piece[rows:] for piece in pieces])
    last_gots = later.gots[new[1]] + [image_got]
    later.join(new[3], [new[1]], d_rows)
    while new[3] in later.running:
        later.step(new[3], d_rows)
    while new[2] in later.running:
        later.step(new[2], d_rows)
    write_block(layer, spread(block_piece(later, layer), False))
    write_mixed(layer, spread(mixed_piece(later, layer), False))
    stacked = [None] * len(all_params)
    for i, out in zip((10, 12, 2, 5), list(outs["block"]) + list(outs["mixed"])):
        stacked[i] = out.reshape(all_params[i].shape)
    reduced = reduce_small(
        [jnp.stack([grads[n] for grads in small_grads]) for n in range(len(SMALL))], last_gots
    )
    for i, vector in zip(SMALL, reduced):
        stacked[i] = vector
    return (activations, d_images) + tuple(stacked)


def solution(mesh):
    in_specs = (
        P("rep", "fsdp", None),
        P("rep", "fsdp", None),
        P(None, "fsdp"),
        P(None, "fsdp"),
        P(None, "fsdp", None),
        P(None, "fsdp"),
        P(None, "fsdp"),
        P(None, "fsdp", None),
        P(None, "fsdp"),
        P(None, "fsdp"),
        P(None, "fsdp"),
        P(None, "fsdp"),
        P(None, "fsdp", None),
        P(None, "fsdp"),
        P(None, "fsdp", None),
        P(None, "fsdp"),
        P(None, "fsdp"),
    )
    out_specs = (
        P("rep", "fsdp", None),
        P("rep", "fsdp", None),
        P(None, "fsdp"),
        P(None, "fsdp"),
        P(None, "fsdp", None),
        P(None, "fsdp"),
        P(None, "fsdp"),
        P(None, "fsdp", None),
        P(None, "fsdp"),
        P(None, "fsdp"),
        P(None, "fsdp"),
        P(None, "fsdp"),
        P(None, "fsdp", None),
        P(None, "fsdp"),
        P(None, "fsdp", None),
        P(None, "fsdp"),
        P(None, "fsdp"),
    )
    return jax.shard_map(local, mesh=mesh, in_specs=in_specs, out_specs=out_specs, check_vma=False)
```

```python
import functools
import math

import jax
import jax.numpy as jnp
from jax import lax
from jax.experimental import pallas as pl
from jax.experimental.pallas import tpu as pltpu
from jax.sharding import PartitionSpec as P

HEADS = 16
LAYERS = 2
SMALL = (0, 1, 3, 4, 6, 7, 8, 9, 11, 13, 14)
MIB = 1 << 20

epsilon = 1e-06


def layer_norm(values_in, norm_gain, norm_shift):
    centre = jnp.mean(values_in, -1, keepdims=True)
    centered = values_in - centre
    spread = jnp.mean(centered * centered, -1, keepdims=True)
    return centered * lax.rsqrt(spread + epsilon) * norm_gain + norm_shift


def norm_back(values_in, norm_gain, norm_shift, grad):
    unused, pullback = jax.vjp(layer_norm, values_in, norm_gain, norm_shift)
    return pullback(grad)


def widen(tensor):
    return tensor.astype(jnp.float32)


def low(tensor):
    return tensor.astype(jnp.bfloat16)


def forward_dot(left, weight):
    return jnp.dot(left, weight, preferred_element_type=jnp.float32)


def weight_dot(left, grad):
    return lax.dot_general(left, grad, (((0,), (0,)), ((), ())), preferred_element_type=jnp.float32)


def input_dot(grad, weight):
    return lax.dot_general(
        grad, weight, (((1,), (1,)), ((), ())), preferred_element_type=jnp.float32
    )


def column_sum(grad):
    return jnp.sum(widen(grad), 0)


def pick(tensor, index, axis):
    return lax.dynamic_index_in_dim(tensor, index, axis, keepdims=False)


def swap(tensor, axis, offset):
    count = lax.axis_size(axis)
    return lax.ppermute(tensor, axis, [(i, i ^ offset) for i in range(count)])


def position():
    owner = lax.axis_index("fsdp")
    return owner // 2, owner % 2, lax.axis_index("rep")


def scalars(*values):
    return jnp.stack(values).astype(jnp.int32)


def estimate(microseconds, moved):
    return pl.CostEstimate(flops=1000, bytes_accessed=1000, transcendentals=0)


def params(mib):
    return pltpu.CompilerParams(vmem_limit_bytes=mib * MIB)


def after(tensor, *earlier):
    return lax.optimization_barrier((tensor,) + earlier)[0]


def by_core(own, got, axis):
    core = position()[1]
    return jnp.where(
        core == 0, jnp.stack([own, got], axis), jnp.stack([got, own], axis)
    )


def columns_kernel(blocks, where_ref, *refs):
    ins, (own_ref, other_ref) = refs[:-2], refs[-2:]
    for side in range(2):

        @pl.when(where_ref[1] == side)
        def _():
            for out_ref, parity in ((own_ref, side), (other_ref, 1 - side)):
                start = 0
                for ref, block in zip(ins, blocks):
                    for i in range(parity, ref.shape[2] // block, 2):
                        out_ref[0, :, start : start + block] = ref[0, :, i * block : (i + 1) * block]
                        start += block


def column_pieces(shards):
    plane, core, member = position()
    owners, count = lax.axis_size("fsdp"), lax.axis_size("rep")
    rows = shards[0].shape[1] // count
    blocks = tuple(
        size // owners for size in (shards[0].shape[2] // 3, shards[1].shape[2])
    )
    columns = sum(shard.shape[2] for shard in shards) // 2
    shape = jax.ShapeDtypeStruct((LAYERS, rows, columns), jnp.bfloat16)
    out = pl.BlockSpec((1, rows, columns), lambda layer, where: (layer, 0, 0))
    own, other = pl.pallas_call(
        functools.partial(columns_kernel, blocks),
        out_shape=[shape, shape],
        grid_spec=pltpu.PrefetchScalarGridSpec(
            num_scalar_prefetch=1,
            grid=(LAYERS,),
            in_specs=[
                pl.BlockSpec((1, rows, shard.shape[2]), lambda layer, where: (layer, where[0], 0))
                for shard in shards
            ],
            out_specs=[out, out],
        ),
        cost_estimate=estimate(0, 4 * LAYERS * rows * columns * 2),
    )(scalars(member, core), *shards)
    both = by_core(own, swap(other, "fsdp", 1), 1)
    split = shards[0].shape[2] // 2
    both = both.reshape(LAYERS, 2 * rows, columns)
    return both[..., :split], both[..., split:]


def place_kernel(half_rows, blocks, parts, where_ref, *refs):
    count = len(parts)
    pieces, outs, (in_sems, out_sems) = refs[:count], refs[count : -count - 2], refs[-2:]
    held = refs[-count - 2 : -2]
    plane, member = where_ref[0], where_ref[1]
    arrivals = []
    for i in range(count):
        arrivals.append(pltpu.make_async_copy(pieces[i], held[i], in_sems.at[i]))
        arrivals[-1].start()
    copies = []
    for i, (k, halves) in enumerate(parts):
        arrivals[i].wait()
        for j in range(pieces[0].shape[0]):
            for b, (row, rows, column, columns, put) in enumerate(blocks):
                if row // half_rows not in halves:
                    continue
                first = row - halves[0] * half_rows
                copy = pltpu.make_async_copy(
                    held[i].at[j, first : first + rows, column : column + columns],
                    put(outs, j ^ plane, k ^ member),
                    out_sems.at[b, i, j],
                )
                copy.start()
                copies.append(copy)
    for copy in copies:
        copy.wait()


def place(pieces, parts, shapes, blocks):
    plane, core, member = position()
    planes = pieces[0].shape[0]
    outs = pl.pallas_call(
        functools.partial(place_kernel, pieces[0].shape[1] // 2, blocks, parts),
        out_shape=[jax.ShapeDtypeStruct(shape, pieces[0].dtype) for shape in shapes],
        in_specs=[pl.BlockSpec(memory_space=pltpu.SMEM)]
        + [pl.BlockSpec(memory_space=pl.ANY)] * len(pieces),
        out_specs=[pl.BlockSpec(memory_space=pl.ANY)] * len(shapes),
        scratch_shapes=[pltpu.VMEM(piece.shape, piece.dtype) for piece in pieces]
        + [
            pltpu.SemaphoreType.DMA((len(pieces),)),
            pltpu.SemaphoreType.DMA((len(blocks), len(pieces), planes)),
        ],
        compiler_params=params(20),
        cost_estimate=estimate(0, 4 * sum(piece.size for piece in pieces)),
    )(scalars(plane, member), *pieces)
    return [out.reshape(-1, out.shape[-1]) for out in outs]


def put_pair(side):
    return lambda outs, plane, member: outs[0].at[plane, side, member]


def place_first(pieces, parts, count, split):
    planes, rows, columns = pieces[0].shape
    half, rest = rows // 2, columns - split

    def put(side):
        return lambda outs, plane, member: outs[1].at[
            plane, member, :, side * rest : (side + 1) * rest
        ]

    shapes = [(planes, 2, count, half, split), (planes, count, half, 2 * rest)]
    blocks = [(side * half, half, 0, split, put_pair(side)) for side in range(2)]
    blocks += [(side * half, half, split, rest, put(side)) for side in range(2)]
    return place(pieces, parts, shapes, blocks)


def place_second(pieces, parts, count):
    planes, rows, columns = pieces[0].shape
    half, fine, width = rows // 2, rows // 4, columns // 2

    def put(side):
        return lambda outs, plane, member: outs[1].at[plane, member, side]

    shapes = [(planes, 2, count, fine, columns), (planes, count, 2, half, width)]
    blocks = [(side * fine, fine, 0, columns, put_pair(side)) for side in range(2)]
    blocks += [(half, half, side * width, width, put(side)) for side in range(2)]
    return place(pieces, parts, shapes, blocks)


def gather_planes(piece, *earlier, beside=()):
    column, sent, step = piece[None], list(earlier), lax.axis_size("fsdp") // 4
    while step:
        got = swap(after(column, *sent[-1:], *(beside if len(sent) > len(earlier) else ())), "fsdp", 2 * step)
        sent.append(got)
        column = jnp.stack([column, got], 1).reshape((-1,) + piece.shape)
        step //= 2
    return column, sent[len(earlier) :]


def gather_neighbours(column, earlier):
    held = {0: [column]}
    for bit in range(lax.axis_size("rep").bit_length() - 1):
        held[1 << bit] = [swap(after(column, *earlier), "rep", 1 << bit)]
    return held, [held[k][0] for k in held if k]


def gather_members(held, beside):
    count, rows = lax.axis_size("rep"), held[0][0].shape[1] // 2
    earlier = [held[k][0] for k in held if k] + list(beside)
    for level in range(1, count.bit_length() - 1):
        sent = []
        for k in range(1, count):
            if bin(k).count("1") != level + 1:
                continue
            held[k] = []
            for half, last in ((0, k & -k), (1, 1 << (k.bit_length() - 1))):
                source = held[k ^ last]
                if len(source) == 1:
                    source = source[0][:, half * rows : (half + 1) * rows]
                else:
                    source = source[half]
                held[k].append(swap(after(source, *earlier), "rep", last))
            sent += held[k]
        earlier = sent
    arrays, parts = [], []
    for k in range(count):
        for half, array in enumerate(held[k]):
            arrays.append(array)
            parts.append((k, (0, 1) if len(held[k]) == 1 else (half,)))
    return arrays, parts, earlier


def message_pieces(shards):
    heads, expand = column_pieces((shards[2], shards[10]))
    pieces = []
    for layer in range(LAYERS):
        output, shrink = quarter(shards[5][layer]), quarter(shards[12][layer])
        half = output.shape[1] // 2
        packed = jnp.concatenate([output[:, :half], output[:, half:]], 0)
        pieces.append(jnp.concatenate([heads[layer], packed], 1))
        half = shrink.shape[0] // 2
        packed = jnp.concatenate([shrink[:half], shrink[half:]], 1)
        pieces.append(jnp.concatenate([expand[layer], packed], 0))
    return pieces


def quarter(param):
    rows = param.shape[0] // lax.axis_size("rep")
    return lax.dynamic_slice_in_dim(param, lax.axis_index("rep") * rows, rows, 0)


def gather_small(all_params):
    packed = jnp.concatenate([all_params[i] for i in SMALL], 1)
    whole, owner, step = packed[None], lax.axis_index("fsdp"), 1
    while step < lax.axis_size("fsdp"):
        got = swap(whole, "fsdp", step)
        whole = jnp.where(
            (owner // step) % 2 == 0,
            jnp.concatenate([whole, got], 0),
            jnp.concatenate([got, whole], 0),
        )
        step *= 2
    vectors, start = [], 0
    for i in SMALL:
        size = all_params[i].shape[1]
        vectors.append(
            jnp.moveaxis(whole[:, :, start : start + size], 0, 1).reshape(LAYERS, -1)
        )
        start += size
    return vectors, got


def link_orders():
    bits = list(range(lax.axis_size("rep").bit_length() - 1))
    return [bits, bits[::-1]]


def divide(blocks, shapes, bits, outs):
    for side in range(len(shapes)):
        high, later = shapes[side]
        for i in range(high):
            for j in range(later):
                base = 2 * i * later + j
                for out_ref, index in (
                    (outs[2 * side], base + bits[side] * later),
                    (outs[2 * side + 1], base + (1 - bits[side]) * later),
                ):
                    for row, column, block in blocks(side, index):
                        out_ref[
                            0, i, j, row : row + block.shape[0], column : column + block.shape[1]
                        ] = block


def block_grad_kernel(shapes, where_ref, left_ref, grad_ref, more_ref, other_ref, *refs):
    outs, held, extra = refs[:-2], refs[-2], refs[-1]
    held[...] = low(weight_dot(left_ref[...], grad_ref[...])).reshape(held.shape)
    extra[...] = low(weight_dot(more_ref[...], other_ref[...])).reshape(extra.shape)
    rows, half, tall = held.shape[2], held.shape[3] // 2, extra.shape[1] // 2

    def blocks(side, index):
        return [
            (p * rows, 0, held[p, index, :, side * half : (side + 1) * half]) for p in range(2)
        ] + [(2 * rows, 0, extra[index, side * tall : (side + 1) * tall])]

    divide(blocks, shapes, (where_ref[0], where_ref[1]), outs)


def mixed_grad_kernel(shapes, where_ref, left_ref, grad_ref, more_ref, other_ref, *refs):
    outs, held, extra = refs[:4], refs[4], refs[5]
    held[...] = low(weight_dot(left_ref[...], grad_ref[...])).reshape(held.shape)
    extra[...] = low(weight_dot(more_ref[...], other_ref[...])).reshape(extra.shape)
    rows, rest = held.shape[2], extra.shape[2] // 2
    half = (held.shape[3] + rest) // 2

    def blocks(side, index):
        if side == 0:
            return [(p * rows, 0, held[p, index, :, :half]) for p in range(2)]
        return [(p * rows, 0, held[p, index, :, half:]) for p in range(2)] + [
            (p * rows, half - rest, extra[index, :, p * rest : (p + 1) * rest]) for p in range(2)
        ]

    divide(blocks, shapes, (where_ref[0], where_ref[1]), outs)


def grad_call(kernel, arrays, widths, rows, columns, scratch, orders):
    planes, count = lax.axis_size("fsdp") // 2, lax.axis_size("rep")
    member = lax.axis_index("rep")
    shapes = tuple((count >> (order[0] + 1), 1 << order[0]) for order in orders)
    tokens = arrays[0].shape[0]
    specs = []
    for array, width in zip(arrays, widths):
        if width is None:
            specs.append(pl.BlockSpec(array.shape, lambda z, where: (0, 0)))
        else:
            specs.append(pl.BlockSpec((tokens, width), lambda z, where: (0, z)))
    out_shapes, out_specs = [], []
    for high, later in shapes:
        block = (high, later, rows, columns // len(orders))
        out_specs += [pl.BlockSpec((1,) + block, lambda z, where: (z, 0, 0, 0, 0))] * 2
        out_shapes += [jax.ShapeDtypeStruct((planes,) + block, jnp.bfloat16)] * 2
    return pl.pallas_call(
        functools.partial(kernel, shapes),
        out_shape=out_shapes,
        grid_spec=pltpu.PrefetchScalarGridSpec(
            num_scalar_prefetch=1,
            grid=(planes,),
            in_specs=specs,
            out_specs=out_specs,
            scratch_shapes=[pltpu.VMEM(size, jnp.bfloat16) for size in scratch],
        ),
        compiler_params=params(40),
        cost_estimate=estimate(5, 0),
    )(scalars(*[(member >> order[0]) & 1 for order in orders]), *arrays)


def block_grad(left, grad, more, other, orders):
    planes, count = lax.axis_size("fsdp") // 2, lax.axis_size("rep")
    widths = left.shape[1] // planes, more.shape[1] // planes
    columns = grad.shape[1]
    rows, tall = widths[0] // (2 * count), widths[1] // count
    return grad_call(
        block_grad_kernel, (left, grad, more, other), (widths[0], None, widths[1], None),
        2 * rows + tall // 2, columns,
        [(2, count, rows, columns), (count, tall, other.shape[1])], orders,
    )


def mixed_grad(left, grad, more, other, orders):
    planes, count = lax.axis_size("fsdp") // 2, lax.axis_size("rep")
    widths = left.shape[1] // planes, more.shape[1] // planes
    columns, rest = grad.shape[1], other.shape[1]
    rows = widths[1] // count
    if widths[1] % 128:
        first = low(weight_dot(left, grad)).reshape(planes, 2, count, rows, columns)
        second = low(weight_dot(more, other)).reshape(planes, count, rows, 2, rest // 2)
        total = jnp.concatenate([jnp.swapaxes(first, 1, 2), jnp.swapaxes(second, 2, 3)], 4)
        total = total.reshape(planes, count, 2 * rows, -1)
        half, member = total.shape[3] // 2, lax.axis_index("rep")
        top = count // 2
        left_part = total[..., :half].reshape(planes, top, 2, 1, 2 * rows, half)
        right_part = total[..., half:].reshape(planes, 1, 2, top, 2 * rows, half)
        sides = member % 2, member // top
        return [
            pick(part, side if kept else 1 - side, 2)
            for part, side in zip((left_part, right_part), sides)
            for kept in (True, False)
        ]
    return grad_call(
        mixed_grad_kernel, (left, grad, more, other), (widths[0], None, widths[1], None),
        2 * rows, columns + rest // 2,
        [(2, count, rows, columns), (count, rows, rest)], orders,
    )


def split_kernel(where_ref, *refs):
    count = len(refs) // 4
    for n in range(count):
        bit = where_ref[n]
        keep_in, got_ref = refs[2 * n], refs[2 * n + 1]
        keep_ref, send_ref = refs[2 * (count + n)], refs[2 * (count + n) + 1]
        keep_ref[0] = low(widen(keep_in[0, bit]) + widen(got_ref[0, bit]))
        send_ref[0] = low(widen(keep_in[0, 1 - bit]) + widen(got_ref[0, 1 - bit]))


def add_split(pairs, later, sides, rows):
    if len({pair[0].size // n for pair, n in zip(pairs, later)}) > 1:
        return [
            out
            for pair, n, side in zip(pairs, later, sides)
            for out in add_split([pair], [n], [side], rows)
        ]
    arrays, in_specs, out_specs, out_shapes = [], [], [], []
    for pair, n in zip(pairs, later):
        columns = pair[0].shape[-1]
        for array in pair:
            arrays.append(array.reshape(-1, 2, n, rows, columns))
            in_specs.append(
                pl.BlockSpec((1, 2, n, rows, columns), lambda i, where: (i, 0, 0, 0, 0))
            )
            out_specs.append(pl.BlockSpec((1, n, rows, columns), lambda i, where: (i, 0, 0, 0)))
            out_shapes.append(
                jax.ShapeDtypeStruct((arrays[-1].shape[0], n, rows, columns), jnp.bfloat16)
            )
    return pl.pallas_call(
        split_kernel,
        out_shape=out_shapes,
        grid_spec=pltpu.PrefetchScalarGridSpec(
            num_scalar_prefetch=1,
            grid=(arrays[0].shape[0],),
            in_specs=in_specs,
            out_specs=out_specs,
        ),
        compiler_params=params(24),
        cost_estimate=estimate(0, sum(array.size for array in arrays) * 3),
    )(scalars(*sides), *arrays)


def merge_kernel(where_ref, *refs):
    arrays, (keep_ref, send_ref) = refs[:-2], refs[-2:]
    half = arrays[0].shape[-1]
    for out_ref, bit in ((keep_ref, where_ref[0]), (send_ref, 1 - where_ref[0])):
        start = 0
        for n in range(0, len(arrays), 4):
            left_ref, left_got, right_ref, right_got = arrays[n : n + 4]
            rows = slice(start, start + left_ref.shape[2])
            out_ref[0, rows, :half] = low(widen(left_ref[0, bit]) + widen(left_got[0, bit]))
            out_ref[0, rows, half:] = low(widen(right_ref[0, bit]) + widen(right_got[0, bit]))
            start += left_ref.shape[2]


def add_merge(messages, side):
    half = messages[0][0].shape[-1]
    arrays, specs, total = [], [], 0
    for message in messages:
        rows = message[0].shape[-2]
        arrays += [array.reshape(-1, 2, rows, half) for array in message]
        specs += [pl.BlockSpec((1, 2, rows, half), lambda i, where: (i, 0, 0, 0))] * 4
        total += rows
    high = arrays[0].shape[0]
    given = pl.BlockSpec((1, total, 2 * half), lambda i, where: (i, 0, 0))
    shape = jax.ShapeDtypeStruct((high, total, 2 * half), jnp.bfloat16)
    return pl.pallas_call(
        merge_kernel,
        out_shape=[shape, shape],
        grid_spec=pltpu.PrefetchScalarGridSpec(
            num_scalar_prefetch=1,
            grid=(high,),
            in_specs=specs,
            out_specs=[given, given],
        ),
        compiler_params=params(24),
        cost_estimate=estimate(0, sum(array.size for array in arrays) * 3),
    )(scalars(side), *arrays)


def reduce_members(arrays):
    member, lanes = lax.axis_index("rep"), range(2)
    rows, orders = arrays[0].shape[-2], link_orders()
    bits = [sorted(order) for order in orders]
    keeps, sends = list(arrays[::2]), list(arrays[1::2])
    for n in range(len(orders[0])):
        gots = [swap(sends[i], "rep", 1 << orders[i][n]) for i in lanes]
        for i in lanes:
            bits[i].remove(orders[i][n])
        token = yield sends, gots
        gots = [after(got, token) for got in gots]
        if n + 1 < len(orders[0]):
            later = [1 << bits[i].index(orders[i][n + 1]) for i in lanes]
            sides = [(member >> orders[i][n + 1]) & 1 for i in lanes]
            outs = add_split(list(zip(keeps, gots)), later, sides, rows)
            keeps, sends = list(outs[::2]), list(outs[1::2])
    return [keeps[0], gots[0], keeps[1], gots[1]]


def reduce_planes(messages):
    plane, planes = position()[0], lax.axis_size("fsdp") // 2
    rows = sum(message[0].shape[-2] for message in messages)
    keep, send = add_merge(messages, plane % 2)
    step = 1
    while True:
        got = swap(send, "fsdp", 2 * step)
        token = yield [send], [got]
        got = after(got, token)
        step *= 2
        if step == planes:
            return low(widen(keep) + widen(got)).reshape(rows, -1)
        keep, send = add_split([(keep, got)], [1], [(plane // step) % 2], rows)


def finish_columns(total, columns):
    core = position()[1]
    rows = total.shape[0] // 2
    part = total[:, :columns].reshape(2, rows, columns)
    got = swap(pick(part, 1 - core, 0), "fsdp", 1)
    part = jnp.concatenate([pick(part, core, 0), got], 0)
    return jnp.concatenate([part, total[:, columns:]], 1)


def spread(own, low_last):
    pieces = [own]
    for k in range(1, lax.axis_size("rep")):
        last = k & -k if low_last else 1 << (k.bit_length() - 1)
        pieces.append(swap(pieces[k ^ last], "rep", last))
    return pieces


def column_out(out_ref, block, side, ref, start):
    rows = out_ref.shape[2]
    for i in range(out_ref.shape[3] // block):
        first = start if i % 2 == side else start + rows
        out_ref[0, 0, :, i * block : (i + 1) * block] = widen(
            ref[first : first + rows, (i // 2) * block : (i // 2 + 1) * block]
        )


def early_out_kernel(block, where_ref, *refs):
    expand_out, shrink_out = refs[-2:]
    for k, ref in enumerate(refs[:-4]):
        for side in range(2):

            @pl.when((pl.program_id(0) == k) & (where_ref[1] == side))
            def _():
                column_out(expand_out, block, side, ref, 0)

        @pl.when(pl.program_id(0) == k)
        def _():
            rows, columns = shrink_out.shape[2] // 2, shrink_out.shape[3]
            start = ref.shape[0] - rows
            shrink_out[0, 0, :rows] = widen(ref[start:, :columns])
            shrink_out[0, 0, rows:] = widen(ref[start:, columns:])


def late_out_kernel(block, where_ref, *refs):
    heads_out, output_out = refs[-2:]
    for k, ref in enumerate(refs[:-4]):
        for side in range(2):

            @pl.when((pl.program_id(0) == k) & (where_ref[1] == side))
            def _():
                column_out(heads_out, block, side, ref, 0)

        @pl.when(pl.program_id(0) == k)
        def _():
            rows, half = output_out.shape[2], output_out.shape[3] // 2
            start = ref.shape[1] - half
            output_out[0, 0, :, :half] = widen(ref[:rows, start:])
            output_out[0, 0, :, half:] = widen(ref[rows:, start:])


def write_out(kernel, layer, pieces, sizes, earlier):
    plane, core, member = position()
    count = len(pieces)
    shapes = [(LAYERS, count) + size for size in sizes]
    if earlier is None:
        earlier = [jnp.zeros((8, 128), jnp.float32)] * len(sizes)
        aliases = {}
    else:
        earlier = [array.reshape(shape) for array, shape in zip(earlier, shapes)]
        aliases = {1 + count + i: i for i in range(len(sizes))}
    return pl.pallas_call(
        kernel,
        out_shape=[jax.ShapeDtypeStruct(shape, jnp.float32) for shape in shapes],
        grid_spec=pltpu.PrefetchScalarGridSpec(
            num_scalar_prefetch=1,
            grid=(count,),
            in_specs=[pl.BlockSpec(piece.shape, lambda k, where: (0, 0)) for piece in pieces]
            + [pl.BlockSpec(memory_space=pl.ANY)] * len(sizes),
            out_specs=[
                pl.BlockSpec((1, 1) + size, lambda k, where: (layer, k ^ where[0], 0, 0))
                for size in sizes
            ],
        ),
        input_output_aliases=aliases,
        compiler_params=params(24),
        cost_estimate=estimate(0, count * pieces[0].size * 6),
    )(scalars(member, core), *pieces, *earlier)


def reduce_small(grads, earlier):
    owners, count = lax.axis_size("fsdp"), lax.axis_size("rep")
    total = jnp.concatenate([g.reshape(LAYERS, owners, -1) for g in grads], 2)
    total = after(total, *earlier)
    owner = lax.axis_index("fsdp")
    step = owners // 2
    while step:
        total = total.reshape(LAYERS, 2, step, -1)
        mine = (owner // step) % 2
        total = pick(total, mine, 1) + swap(pick(total, 1 - mine, 1), "fsdp", step)
        step //= 2
    step = 1
    while step < count:
        total = total + swap(total, "rep", step)
        step *= 2
    total = total.reshape(LAYERS, -1)
    outs, start = [], 0
    for g in grads:
        size = g.shape[1] // owners
        outs.append(total[:, start : start + size])
        start += size
    return outs


def other_half(rows):
    return swap(rows, "fsdp", lax.axis_size("fsdp") // 2)


def image_side():
    return lax.axis_index("fsdp") // (lax.axis_size("fsdp") // 2)


def regroup(blocks):
    side = image_side()
    return pick(blocks, side, 0), other_half(pick(blocks, 1 - side, 0))


def ungroup(rows, got):
    own, got = rows[: rows.shape[0] // 2], got.astype(rows.dtype)
    return jnp.where(image_side() == 0, jnp.stack([own, got]), jnp.stack([got, own]))


def chips_per_image():
    return lax.axis_size("fsdp") // 4


def share_rows(local_kv):
    shared = [local_kv]
    for k in range(1, chips_per_image()):
        low_bit = k & -k
        shared.append(swap(shared[k ^ low_bit], "fsdp", 2 * low_bit))
    return shared


def collect_rows(own, others):
    chips = chips_per_image()
    if chips == 2:
        got = swap(others, "fsdp", 2)
        return low(widen(own) + widen(got)), got
    total = jnp.concatenate([own, others], 1)
    while chips > 1:
        rows = total.shape[1] // 2
        got = swap(total[:, rows:], "fsdp", chips)
        total = low(widen(total[:, :rows]) + widen(got))
        chips //= 2
    return total, got


def both_cores(rows):
    return jnp.concatenate([rows, swap(rows, "fsdp", 1)], 0)


def one_head(tensor, head):
    half = tensor.shape[1] // 2
    lane = lax.broadcasted_iota(jnp.int32, tensor.shape, 1)
    keep = lane < half if head == 0 else lane >= half
    return jnp.where(keep, tensor, jnp.zeros_like(tensor))


def join(refs, held):
    start = 0
    for ref in refs:
        held[start : start + ref.shape[0], :] = ref[...]
        start += ref.shape[0]
    return held[...]


def attend_kernel(factor, parts, query_ref, *refs):
    out_ref, log_ref, held_keys, held_values = refs[2 * parts :]
    keys, values = join(refs[:parts], held_keys), join(refs[parts : 2 * parts], held_values)
    results, logs = [], []
    for head in range(2):
        scores = input_dot(one_head(query_ref[...], head), keys)
        largest = jnp.max(scores, -1, keepdims=True)
        weights = jnp.exp2((scores - largest) * factor)
        total = jnp.sum(weights, -1, keepdims=True)
        results.append(forward_dot(low(weights), values) / total)
        logs.append(largest * factor + jnp.log2(total))
    out_ref[...] = low(one_head(results[0], 0) + one_head(results[1], 1))
    shape = log_ref.shape
    log_ref[...] = one_head(jnp.broadcast_to(logs[0], shape), 0) + one_head(
        jnp.broadcast_to(logs[1], shape), 1
    )


def pair_block(rows, start):
    return pl.BlockSpec((rows, 128), lambda i: (0, start + i))


def kv_parts(projected, others):
    pairs = projected.shape[1] // 384
    if projected.shape[0] % 16:
        others = [jnp.concatenate([projected[:, 128 * pairs :]] + others, 0)]
        parts = []
    else:
        parts = [(projected, pairs, 2 * pairs)]
    return parts + [(other, 0, pairs) for other in others]


def kv_specs(parts, first=0):
    keys = [pair_block(array.shape[0], first + start) for array, start, unused in parts]
    values = [pair_block(array.shape[0], first + start) for array, unused, start in parts]
    rows = sum(array.shape[0] for array, unused, more in parts)
    held = [pltpu.VMEM((rows, 128), jnp.bfloat16)] * 2
    return keys + values, [array for array, unused, more in parts] * 2, held


def attend(projected, others, head_size):
    tokens, width = projected.shape[0], projected.shape[1] // 3
    pairs = width // 128
    parts = kv_parts(projected, others)
    specs, arrays, held = kv_specs(parts)
    factor = head_size ** (-0.5) * math.log2(math.e)
    return pl.pallas_call(
        functools.partial(attend_kernel, factor, len(parts)),
        out_shape=[
            jax.ShapeDtypeStruct((tokens, width), jnp.bfloat16),
            jax.ShapeDtypeStruct((tokens, width), jnp.float32),
        ],
        grid=(pairs,),
        in_specs=[pair_block(tokens, 0)] + specs,
        out_specs=[pair_block(tokens, 0), pair_block(tokens, 0)],
        scratch_shapes=held,
        compiler_params=params(56),
        cost_estimate=estimate(18, 0),
    )(projected, *arrays)


def attend_back_kernel(factor, scale, parts, query_ref, *refs):
    log_ref, grad_ref, dq_ref, own_ref, others_ref, held_keys, held_values = refs[2 * parts :]
    keys, values = join(refs[:parts], held_keys), join(refs[parts : 2 * parts], held_values)
    d_query, d_key, d_value = [], 0.0, 0.0
    for head in range(2):
        query = one_head(query_ref[...], head)
        grad = one_head(grad_ref[...], head)
        half = query.shape[1] // 2
        log_total = log_ref[:, head * half : head * half + 1]
        probs = jnp.exp2(input_dot(query, keys) * factor - log_total)
        products = probs * input_dot(grad, values)
        d_scores = low(products - probs * jnp.sum(products, -1, keepdims=True))
        d_query.append(forward_dot(d_scores, keys))
        d_key = d_key + weight_dot(d_scores, query)
        d_value = d_value + weight_dot(low(probs), grad)
    dq_ref[...] = low((one_head(d_query[0], 0) + one_head(d_query[1], 1)) * scale)
    rows = own_ref.shape[1]
    for i, total in enumerate((low(d_key * scale), low(d_value))):
        own_ref[i] = total[:rows]
        others_ref[i] = total[rows:]


def attend_back(projected, others, log_total, d_attended, head_size, first, pairs):
    tokens, width = d_attended.shape[0], 128 * pairs
    parts = kv_parts(projected, others)
    specs, arrays, held = kv_specs(parts, first)
    rows = held[0].shape[0]
    scale = head_size ** (-0.5)
    own, taken = pair_block(tokens, 0), pair_block(tokens, first)
    return pl.pallas_call(
        functools.partial(attend_back_kernel, scale * math.log2(math.e), scale, len(parts)),
        out_shape=[
            jax.ShapeDtypeStruct((tokens, width), jnp.bfloat16),
            jax.ShapeDtypeStruct((2, tokens, width), jnp.bfloat16),
            jax.ShapeDtypeStruct((2, rows - tokens, width), jnp.bfloat16),
        ],
        grid=(pairs,),
        in_specs=[taken] + specs + [taken, taken],
        out_specs=[
            own,
            pl.BlockSpec((2, tokens, 128), lambda i: (0, 0, i)),
            pl.BlockSpec((2, rows - tokens, 128), lambda i: (0, 0, i)),
        ],
        scratch_shapes=held,
        compiler_params=params(60),
        cost_estimate=estimate(8 * pairs, 0),
    )(projected, *arrays, log_total, d_attended)


def add_tile(part, own_ref, other_ref, total_ref):
    @pl.when(pl.program_id(0) == 0)
    def _():
        total_ref[...] = part

    @pl.when(pl.program_id(0) > 0)
    def _():
        total_ref[...] += part

    @pl.when(pl.program_id(0) == pl.num_programs(0) - 1)
    def _():
        half = own_ref.shape[0]
        own_ref[...] = total_ref[:half]
        other_ref[...] = low(total_ref[half:])


def expand_kernel(
    rows_ref, expand_ref, bias_ref, shrink_ref, active_ref, slope_ref, own_ref, other_ref, total_ref
):
    hidden = forward_dot(rows_ref[...], expand_ref[...]) + bias_ref[...]
    normal = 0.5 + 0.5 * lax.erf(hidden * math.sqrt(0.5))
    density = jnp.exp2(hidden * hidden * (-0.5 * math.log2(math.e)))
    slope_ref[...] = low(normal + hidden * density * (1.0 / math.sqrt(2.0 * math.pi)))
    active = low(hidden * normal)
    active_ref[...] = active
    add_tile(forward_dot(active, shrink_ref[...]), own_ref, other_ref, total_ref)


def feed_forward(rows_in, expand, expand_bias, shrink):
    tokens, width = rows_in.shape
    units = expand.shape[1]
    tile = 512
    whole = pl.BlockSpec((tokens, width), lambda i: (0, 0))
    half = pl.BlockSpec((tokens // 2, width), lambda i: (0, 0))
    part = pl.BlockSpec((tokens, tile), lambda i: (0, i))
    return pl.pallas_call(
        expand_kernel,
        out_shape=[
            jax.ShapeDtypeStruct((tokens, units), jnp.bfloat16),
            jax.ShapeDtypeStruct((tokens, units), jnp.bfloat16),
            jax.ShapeDtypeStruct((tokens // 2, width), jnp.float32),
            jax.ShapeDtypeStruct((tokens // 2, width), jnp.bfloat16),
        ],
        grid=(units // tile,),
        in_specs=[
            whole,
            pl.BlockSpec((width, tile), lambda i: (0, i)),
            pl.BlockSpec((1, tile), lambda i: (0, i)),
            pl.BlockSpec((tile, width), lambda i: (i, 0)),
        ],
        out_specs=[part, part, half, half],
        scratch_shapes=[pltpu.VMEM((tokens, width), jnp.float32)],
        compiler_params=params(32),
        cost_estimate=estimate(14, 0),
    )(rows_in, expand, expand_bias[None], shrink)


def shrink_kernel(
    grad_ref, shrink_ref, slope_ref, expand_ref, hidden_ref, bias_ref, own_ref, other_ref, total_ref
):
    d_hidden = low(input_dot(grad_ref[...], shrink_ref[...]) * widen(slope_ref[...]))
    hidden_ref[...] = d_hidden
    bias_ref[...] = jnp.sum(widen(d_hidden), 0, keepdims=True)
    add_tile(input_dot(d_hidden, expand_ref[...]), own_ref, other_ref, total_ref)


def feed_back(d_mlp, shrink, slope, expand):
    tokens, width = d_mlp.shape
    units = expand.shape[1]
    tile = 512
    whole = pl.BlockSpec((tokens, width), lambda i: (0, 0))
    half = pl.BlockSpec((tokens // 2, width), lambda i: (0, 0))
    part = pl.BlockSpec((tokens, tile), lambda i: (0, i))
    return pl.pallas_call(
        shrink_kernel,
        out_shape=[
            jax.ShapeDtypeStruct((tokens, units), jnp.bfloat16),
            jax.ShapeDtypeStruct((1, units), jnp.float32),
            jax.ShapeDtypeStruct((tokens // 2, width), jnp.float32),
            jax.ShapeDtypeStruct((tokens // 2, width), jnp.bfloat16),
        ],
        grid=(units // tile,),
        in_specs=[
            whole,
            pl.BlockSpec((tile, width), lambda i: (i, 0)),
            part,
            pl.BlockSpec((width, tile), lambda i: (0, i)),
        ],
        out_specs=[part, pl.BlockSpec((1, tile), lambda i: (0, i)), half, half],
        scratch_shapes=[pltpu.VMEM((tokens, width), jnp.float32)],
        compiler_params=params(32),
        cost_estimate=estimate(9, 0),
    )(d_mlp, shrink, slope, expand)


def core_half(vector):
    core = position()[1]
    return pick(widen(vector).reshape(lax.axis_size("fsdp") // 2, 2, -1), core, 1).reshape(-1)


def core_fill(half):
    parts = half.reshape(lax.axis_size("fsdp") // 2, -1)
    return by_core(parts, jnp.zeros_like(parts), 1).reshape(-1)


def normed_rows(tok_rows, gathered):
    return both_cores(low(layer_norm(tok_rows, widen(gathered[0]), widen(gathered[1]))))


def project(normed, gathered, token):
    heads_weight, query_bias, value_bias = gathered[2], gathered[3], gathered[4]
    width = normed.shape[1]
    bias_row = jnp.concatenate(
        [core_half(query_bias), jnp.zeros((width // 2,), jnp.float32), core_half(value_bias)]
    )
    projected = low(forward_dot(normed, heads_weight) + bias_row)
    return projected, share_rows(after(projected[:, width // 2 :], token))[1:]


def forward_layer(
    tok_rows, normed, projected, others, gathered, beside, following
):
    (
        attn_norm_gain,
        attn_norm_bias,
        heads_weight,
        query_bias,
        value_bias,
        output_weight,
        output_bias,
        attn_layerscale,
        mlp_norm_gain,
        mlp_norm_bias,
        expand_weight,
        expand_bias,
        shrink_weight,
        shrink_bias,
        mlp_layerscale,
    ) = gathered
    tokens, width = tok_rows.shape
    attended, log_total = attend(projected, others, width // HEADS)
    attended = after(attended, *beside)
    got = swap(low(forward_dot(attended[tokens:], output_weight)), "fsdp", 1)
    branch = forward_dot(attended[:tokens], output_weight) + widen(got) + widen(output_bias)
    middle = tok_rows + widen(attn_layerscale) * branch
    normed_two = low(layer_norm(middle, widen(mlp_norm_gain), widen(mlp_norm_bias)))
    normed_two = both_cores(normed_two)
    activated, slope, own_sum, other_sum = feed_forward(
        normed_two, expand_weight, core_half(expand_bias), shrink_weight
    )
    other_sum = after(other_sum, *following)
    mlp_out = own_sum + widen(swap(other_sum, "fsdp", 1)) + widen(shrink_bias)
    result = middle + widen(mlp_layerscale) * mlp_out
    saved = (
        tok_rows,
        normed,
        projected,
        others,
        log_total,
        attended,
        branch,
        middle,
        normed_two,
        slope,
        activated,
        mlp_out,
    )
    return (result, saved)


class Later:
    def __init__(self):
        self.running, self.done, self.sends, self.gots = {}, {}, {}, {}

    def begin(self, name, kernel, arrays):
        self.running[name] = reduce_members(kernel(*arrays, link_orders()))
        self.step(name, None)

    def join(self, name, parts, token):
        for part in parts:
            while part in self.running:
                self.step(part, token)
        self.running[name] = reduce_planes([self.done[part] for part in parts])
        self.step(name, None)

    def step(self, name, token):
        try:
            self.sends[name], self.gots[name] = self.running[name].send(token)
        except StopIteration as end:
            self.done[name] = end.value
            self.sends[name] = self.gots[name] = []
            del self.running[name]

    def sent(self, value, *names):
        return after(value, *[array for name in names for array in self.sends[name]])

    def came(self, value, *names):
        return after(value, *[array for name in names for array in self.gots[name]])


def backward_layer(d_result, saved, gathered, later, new, old, activation_got):
    (
        attn_norm_gain,
        attn_norm_bias,
        heads_weight,
        query_bias,
        value_bias,
        output_weight,
        output_bias,
        attn_layerscale,
        mlp_norm_gain,
        mlp_norm_bias,
        expand_weight,
        expand_bias,
        shrink_weight,
        shrink_bias,
        mlp_layerscale,
    ) = gathered
    (
        tok_rows,
        normed,
        projected,
        others,
        log_total,
        attended,
        branch,
        middle,
        normed_two,
        slope,
        activated,
        mlp_out,
    ) = saved
    tokens, width = tok_rows.shape
    d_mlp = low(d_result * widen(mlp_layerscale))
    d_mlp_both = both_cores(d_mlp)
    g_mlp_scale = jnp.sum(d_result * mlp_out, 0)
    g_shrink_bias = column_sum(d_mlp)
    d_hidden, g_expand_bias, own_sum, other_sum = feed_back(
        d_mlp_both, shrink_weight, slope, expand_weight
    )
    block, mixed, block_planes, mixed_planes = new
    if old:
        other_sum = later.came(other_sum, old[0])
        later.join(old[2], [old[0]], other_sum)
        d_hidden = later.sent(d_hidden, old[2])
    got = swap(other_sum, "fsdp", 1)
    later.begin(block, block_grad, (normed_two, d_hidden, activated, d_mlp_both))
    own_sum = later.sent(own_sum, block)
    if not old:
        own_sum = after(own_sum, activation_got)
    else:
        own_sum = later.came(own_sum, old[1])
        later.step(old[1], own_sum)
        own_sum = later.sent(own_sum, old[1])
    d_middle_norm, g_mlp_gain, g_mlp_shift = norm_back(
        middle, widen(mlp_norm_gain), widen(mlp_norm_bias), own_sum + widen(got)
    )
    d_middle = d_result + d_middle_norm
    d_branch = low(d_middle * widen(attn_layerscale))
    d_branch_both = both_cores(d_branch)
    g_attn_scale = jnp.sum(d_middle * branch, 0)
    g_output_bias = column_sum(d_branch)
    d_attended = low(input_dot(d_branch_both, output_weight))
    pairs = d_attended.shape[1] // 128

    def back(first):
        return attend_back(
            projected, others, log_total, d_attended, width // HEADS, first, pairs // 2
        )

    first_query, d_own, d_others = back(0)
    first_kv, first_got = collect_rows(d_own, d_others)
    if old:
        d_attended = later.came(d_attended, old[2])
        later.step(old[2], first_query)
        d_attended = later.sent(d_attended, old[2])
    second_query, d_own, d_others = back(pairs // 2)
    d_others = after(d_others, first_got)
    second_kv, second_got = collect_rows(d_own, d_others)
    second_query = later.came(second_query, block)
    later.step(block, second_query)
    second_query = later.sent(second_query, block)
    if old:
        second_query = later.came(second_query, old[1])
        later.join(old[3], [old[1]], second_query)
        second_query = later.sent(second_query, old[3])
    d_query = jnp.concatenate([first_query, second_query], 1)
    d_key = jnp.concatenate([first_kv[0], second_kv[0]], 1)
    d_value = jnp.concatenate([first_kv[1], second_kv[1]], 1)
    d_projected = jnp.concatenate([d_query, d_key, d_value], 1)
    g_query_bias = column_sum(d_query)
    g_value_bias = column_sum(d_value)
    got = swap(low(input_dot(d_projected[tokens:], heads_weight)), "fsdp", 1)
    later.begin(mixed, mixed_grad, (normed, d_projected, attended, d_branch_both))
    d_projected = later.sent(d_projected, mixed)
    if old:
        later.join(block_planes, [block], d_projected)
        d_projected = later.sent(d_projected, block_planes)
    d_normed = input_dot(d_projected[:tokens], heads_weight) + widen(got)
    d_rows_norm, g_attn_gain, g_attn_shift = norm_back(
        tok_rows, widen(attn_norm_gain), widen(attn_norm_bias), d_normed
    )
    d_rows = d_middle + d_rows_norm
    small_grads = (
        g_attn_gain,
        g_attn_shift,
        core_fill(g_query_bias),
        core_fill(g_value_bias),
        g_output_bias,
        g_attn_scale,
        g_mlp_gain,
        g_mlp_shift,
        core_fill(g_expand_bias),
        g_shrink_bias,
        g_mlp_scale,
    )
    return (d_rows, small_grads)


def local(images, cotangent, *all_params):
    owners, count = lax.axis_size("fsdp"), lax.axis_size("rep")
    pieces = message_pieces(all_params)
    small, small_got = gather_small(all_params)
    column, planes = gather_planes(pieces[0], beside=[small_got])
    own, got = regroup(after(images, planes[0]))
    tok_rows = widen(jnp.concatenate([own, got], 0))
    column = after(column, got)
    next_column, next_planes = gather_planes(pieces[1], got)
    held, neighbours = gather_neighbours(column, [])
    members = gather_members(held, [])
    saved_layers, fetched = [], []
    for layer in range(LAYERS):
        gathered = [None] * len(all_params)
        for i, vector in zip(SMALL, small):
            gathered[i] = vector[layer]
        normed = normed_rows(tok_rows, gathered)
        arrays, parts, earlier = members
        arrays[0] = after(arrays[0], next_planes[-1])
        gathered[2], gathered[5] = place_first(
            arrays, parts, count, all_params[2].shape[2] // 2
        )
        projected, others = project(normed, gathered, next_planes[-1])
        held, neighbours = gather_neighbours(next_column, earlier)
        if layer + 1 < LAYERS:
            column, planes = gather_planes(pieces[2 * layer + 2], others[-1])
            beside = planes[:1]
        else:
            own, got = regroup(after(cotangent, others[-1]))
            d_rows = widen(jnp.concatenate([own, got], 0))
            beside, planes, neighbours, next_planes, members = [got], [], [], [], [[]] * 3
        arrays, parts, earlier = gather_members(held, [])
        if layer + 1 < LAYERS:
            next_column, next_planes = gather_planes(pieces[2 * layer + 3], planes[-1])
            held, neighbours = gather_neighbours(column, earlier)
            members = gather_members(held, [])
        arrays[0] = after(arrays[0], *planes[-1:], *next_planes[:1])
        gathered[10], gathered[12] = place_second(arrays, parts, count)
        gathered[10] = after(gathered[10], *neighbours)
        fetched.append(tuple(gathered))
        tok_rows, saved = forward_layer(
            tok_rows,
            normed,
            projected,
            others,
            gathered,
            beside,
            next_planes[1:] + members[2],
        )
        saved_layers.append(saved)
    activation_rows = low(tok_rows)
    small_grads = [None] * LAYERS
    outs = {}

    def size(i):
        return (all_params[i].shape[1] // count, all_params[i].shape[2])

    def block_piece(later, layer):
        total = later.done[layer, 2]
        half = total.shape[0] // 2
        return jnp.concatenate([finish_columns(total[:half], total.shape[1]), total[half:]], 0)

    def mixed_piece(later, layer):
        return finish_columns(later.done[layer, 3], size(2)[1] // 2)

    def write_block(layer, pieces):
        outs["block"] = write_out(
            functools.partial(early_out_kernel, size(10)[1] // owners),
            layer, pieces, [size(10), size(12)], outs.get("block"),
        )

    def write_mixed(layer, pieces):
        outs["mixed"] = write_out(
            functools.partial(late_out_kernel, size(2)[1] // 3 // owners),
            layer, pieces, [size(2), size(5)], outs.get("mixed"),
        )

    later = Later()
    for layer in reversed(range(LAYERS)):
        new = [(layer, n) for n in range(4)]
        old = [(layer + 1, n) for n in range(4)] if layer + 1 < LAYERS else None
        if not old:
            activation_got = other_half(activation_rows[activation_rows.shape[0] // 2 :])
        d_rows, small_grads[layer] = backward_layer(
            d_rows, saved_layers[layer], fetched[layer], later, new, old, activation_got
        )
    activations = ungroup(activation_rows, activation_got)
    image_got = other_half(low(d_rows[d_rows.shape[0] // 2 :]))
    d_images = ungroup(d_rows, image_got)
    for name in (old[2], old[3]):
        while name in later.running:
            later.step(name, d_rows)
    first = block_piece(later, layer + 1)
    rows = first.shape[0]
    first = after(jnp.concatenate([first, mixed_piece(later, layer + 1)], 0), d_rows)
    later.step(new[1], d_rows)
    pieces = spread(later.sent(first, new[1]), True)
    write_block(layer + 1, [piece[:rows] for piece in pieces])
    write_mixed(layer + 1, [piece[rows:] for piece in pieces])
    last_gots = later.gots[new[1]] + [image_got]
    later.join(new[3], [new[1]], d_rows)
    while new[3] in later.running:
        later.step(new[3], d_rows)
    while new[2] in later.running:
        later.step(new[2], d_rows)
    write_block(layer, spread(block_piece(later, layer), False))
    write_mixed(layer, spread(mixed_piece(later, layer), False))
    stacked = [None] * len(all_params)
    for i, out in zip((10, 12, 2, 5), list(outs["block"]) + list(outs["mixed"])):
        stacked[i] = out.reshape(all_params[i].shape)
    reduced = reduce_small(
        [jnp.stack([grads[n] for grads in small_grads]) for n in range(len(SMALL))], last_gots
    )
    for i, vector in zip(SMALL, reduced):
        stacked[i] = vector
    return (activations, d_images) + tuple(stacked)


def solution(mesh):
    in_specs = (
        P("rep", "fsdp", None),
        P("rep", "fsdp", None),
        P(None, "fsdp"),
        P(None, "fsdp"),
        P(None, "fsdp", None),
        P(None, "fsdp"),
        P(None, "fsdp"),
        P(None, "fsdp", None),
        P(None, "fsdp"),
        P(None, "fsdp"),
        P(None, "fsdp"),
        P(None, "fsdp"),
        P(None, "fsdp", None),
        P(None, "fsdp"),
        P(None, "fsdp", None),
        P(None, "fsdp"),
        P(None, "fsdp"),
    )
    out_specs = (
        P("rep", "fsdp", None),
        P("rep", "fsdp", None),
        P(None, "fsdp"),
        P(None, "fsdp"),
        P(None, "fsdp", None),
        P(None, "fsdp"),
        P(None, "fsdp"),
        P(None, "fsdp", None),
        P(None, "fsdp"),
        P(None, "fsdp"),
        P(None, "fsdp"),
        P(None, "fsdp"),
        P(None, "fsdp", None),
        P(None, "fsdp"),
        P(None, "fsdp", None),
        P(None, "fsdp"),
        P(None, "fsdp"),
    )
    return jax.shard_map(local, mesh=mesh, in_specs=in_specs, out_specs=out_specs, check_vma=False)
```

```python
import functools
import math

import jax
import jax.numpy as jnp
from jax import lax
from jax.experimental import pallas as pl
from jax.experimental.pallas import tpu as pltpu
from jax.sharding import PartitionSpec as P

HEADS = 16
LAYERS = 2
SMALL = (0, 1, 3, 4, 6, 7, 8, 9, 11, 13, 14)
MIB = 1 << 20

epsilon = 1e-06


def layer_norm(values_in, norm_gain, norm_shift):
    centre = jnp.mean(values_in, -1, keepdims=True)
    centered = values_in - centre
    spread = jnp.mean(centered * centered, -1, keepdims=True)
    return centered * lax.rsqrt(spread + epsilon) * norm_gain + norm_shift


def norm_back(values_in, norm_gain, norm_shift, grad):
    unused, pullback = jax.vjp(layer_norm, values_in, norm_gain, norm_shift)
    return pullback(grad)


def widen(tensor):
    return tensor.astype(jnp.float32)


def low(tensor):
    return tensor.astype(jnp.bfloat16)


def forward_dot(left, weight):
    return jnp.dot(left, weight, preferred_element_type=jnp.float32)


def weight_dot(left, grad):
    return lax.dot_general(left, grad, (((0,), (0,)), ((), ())), preferred_element_type=jnp.float32)


def input_dot(grad, weight):
    return lax.dot_general(
        grad, weight, (((1,), (1,)), ((), ())), preferred_element_type=jnp.float32
    )


def column_sum(grad):
    return jnp.sum(widen(grad), 0)


def pick(tensor, index, axis):
    return lax.dynamic_index_in_dim(tensor, index, axis, keepdims=False)


def swap(tensor, axis, offset):
    count = lax.axis_size(axis)
    return lax.ppermute(tensor, axis, [(i, i ^ offset) for i in range(count)])


def position():
    owner = lax.axis_index("fsdp")
    return owner // 2, owner % 2, lax.axis_index("rep")


def scalars(*values):
    return jnp.stack(values).astype(jnp.int32)


def estimate(microseconds, moved):
    return pl.CostEstimate(flops=1000, bytes_accessed=1000, transcendentals=0)


def params(mib):
    return pltpu.CompilerParams(vmem_limit_bytes=mib * MIB)


def after(tensor, *earlier):
    return lax.optimization_barrier((tensor,) + earlier)[0]


def by_core(own, got, axis):
    core = position()[1]
    return jnp.where(
        core == 0, jnp.stack([own, got], axis), jnp.stack([got, own], axis)
    )


def columns_kernel(blocks, where_ref, *refs):
    ins, (own_ref, other_ref) = refs[:-2], refs[-2:]
    for side in range(2):

        @pl.when(where_ref[1] == side)
        def _():
            for out_ref, parity in ((own_ref, side), (other_ref, 1 - side)):
                start = 0
                for ref, block in zip(ins, blocks):
                    for i in range(parity, ref.shape[2] // block, 2):
                        out_ref[0, :, start : start + block] = ref[0, :, i * block : (i + 1) * block]
                        start += block


def column_pieces(shards):
    plane, core, member = position()
    owners, count = lax.axis_size("fsdp"), lax.axis_size("rep")
    rows = shards[0].shape[1] // count
    blocks = tuple(
        size // owners for size in (shards[0].shape[2] // 3, shards[1].shape[2])
    )
    columns = sum(shard.shape[2] for shard in shards) // 2
    shape = jax.ShapeDtypeStruct((LAYERS, rows, columns), jnp.bfloat16)
    out = pl.BlockSpec((1, rows, columns), lambda layer, where: (layer, 0, 0))
    own, other = pl.pallas_call(
        functools.partial(columns_kernel, blocks),
        out_shape=[shape, shape],
        grid_spec=pltpu.PrefetchScalarGridSpec(
            num_scalar_prefetch=1,
            grid=(LAYERS,),
            in_specs=[
                pl.BlockSpec((1, rows, shard.shape[2]), lambda layer, where: (layer, where[0], 0))
                for shard in shards
            ],
            out_specs=[out, out],
        ),
        cost_estimate=estimate(0, 4 * LAYERS * rows * columns * 2),
    )(scalars(member, core), *shards)
    both = by_core(own, swap(other, "fsdp", 1), 1)
    split = shards[0].shape[2] // 2
    both = both.reshape(LAYERS, 2 * rows, columns)
    return both[..., :split], both[..., split:]


def place_kernel(half_rows, blocks, parts, where_ref, *refs):
    count = len(parts)
    pieces, outs, (in_sems, out_sems) = refs[:count], refs[count : -count - 2], refs[-2:]
    held = refs[-count - 2 : -2]
    plane, member = where_ref[0], where_ref[1]
    arrivals = []
    for i in range(count):
        arrivals.append(pltpu.make_async_copy(pieces[i], held[i], in_sems.at[i]))
        arrivals[-1].start()
    copies = []
    for i, (k, halves) in enumerate(parts):
        arrivals[i].wait()
        for j in range(pieces[0].shape[0]):
            for b, (row, rows, column, columns, put) in enumerate(blocks):
                if row // half_rows not in halves:
                    continue
                first = row - halves[0] * half_rows
                copy = pltpu.make_async_copy(
                    held[i].at[j, first : first + rows, column : column + columns],
                    put(outs, j ^ plane, k ^ member),
                    out_sems.at[b, i, j],
                )
                copy.start()
                copies.append(copy)
    for copy in copies:
        copy.wait()


def place(pieces, parts, shapes, blocks):
    plane, core, member = position()
    planes = pieces[0].shape[0]
    outs = pl.pallas_call(
        functools.partial(place_kernel, pieces[0].shape[1] // 2, blocks, parts),
        out_shape=[jax.ShapeDtypeStruct(shape, pieces[0].dtype) for shape in shapes],
        in_specs=[pl.BlockSpec(memory_space=pltpu.SMEM)]
        + [pl.BlockSpec(memory_space=pl.ANY)] * len(pieces),
        out_specs=[pl.BlockSpec(memory_space=pl.ANY)] * len(shapes),
        scratch_shapes=[pltpu.VMEM(piece.shape, piece.dtype) for piece in pieces]
        + [
            pltpu.SemaphoreType.DMA((len(pieces),)),
            pltpu.SemaphoreType.DMA((len(blocks), len(pieces), planes)),
        ],
        compiler_params=params(20),
        cost_estimate=estimate(0, 4 * sum(piece.size for piece in pieces)),
    )(scalars(plane, member), *pieces)
    return [out.reshape(-1, out.shape[-1]) for out in outs]


def put_pair(side):
    return lambda outs, plane, member: outs[0].at[plane, side, member]


def place_first(pieces, parts, count, split):
    planes, rows, columns = pieces[0].shape
    half, rest = rows // 2, columns - split

    def put(side):
        return lambda outs, plane, member: outs[1].at[
            plane, member, :, side * rest : (side + 1) * rest
        ]

    shapes = [(planes, 2, count, half, split), (planes, count, half, 2 * rest)]
    blocks = [(side * half, half, 0, split, put_pair(side)) for side in range(2)]
    blocks += [(side * half, half, split, rest, put(side)) for side in range(2)]
    return place(pieces, parts, shapes, blocks)


def place_second(pieces, parts, count):
    planes, rows, columns = pieces[0].shape
    half, fine, width = rows // 2, rows // 4, columns // 2

    def put(side):
        return lambda outs, plane, member: outs[1].at[plane, member, side]

    shapes = [(planes, 2, count, fine, columns), (planes, count, 2, half, width)]
    blocks = [(side * fine, fine, 0, columns, put_pair(side)) for side in range(2)]
    blocks += [(half, half, side * width, width, put(side)) for side in range(2)]
    return place(pieces, parts, shapes, blocks)


def gather_planes(piece, *earlier, beside=()):
    column, sent, step = piece[None], list(earlier), lax.axis_size("fsdp") // 4
    while step:
        got = swap(after(column, *sent[-1:], *(beside if len(sent) > len(earlier) else ())), "fsdp", 2 * step)
        sent.append(got)
        column = jnp.stack([column, got], 1).reshape((-1,) + piece.shape)
        step //= 2
    return column, sent[len(earlier) :]


def gather_neighbours(column, earlier):
    held = {0: [column]}
    for bit in range(lax.axis_size("rep").bit_length() - 1):
        held[1 << bit] = [swap(after(column, *earlier), "rep", 1 << bit)]
    return held, [held[k][0] for k in held if k]


def gather_members(held, beside):
    count, rows = lax.axis_size("rep"), held[0][0].shape[1] // 2
    earlier = [held[k][0] for k in held if k] + list(beside)
    for level in range(1, count.bit_length() - 1):
        sent = []
        for k in range(1, count):
            if bin(k).count("1") != level + 1:
                continue
            held[k] = []
            for half, last in ((0, k & -k), (1, 1 << (k.bit_length() - 1))):
                source = held[k ^ last]
                if len(source) == 1:
                    source = source[0][:, half * rows : (half + 1) * rows]
                else:
                    source = source[half]
                held[k].append(swap(after(source, *earlier), "rep", last))
            sent += held[k]
        earlier = sent
    arrays, parts = [], []
    for k in range(count):
        for half, array in enumerate(held[k]):
            arrays.append(array)
            parts.append((k, (0, 1) if len(held[k]) == 1 else (half,)))
    return arrays, parts, earlier


def message_pieces(shards):
    heads, expand = column_pieces((shards[2], shards[10]))
    pieces = []
    for layer in range(LAYERS):
        output, shrink = quarter(shards[5][layer]), quarter(shards[12][layer])
        half = output.shape[1] // 2
        packed = jnp.concatenate([output[:, :half], output[:, half:]], 0)
        pieces.append(jnp.concatenate([heads[layer], packed], 1))
        half = shrink.shape[0] // 2
        packed = jnp.concatenate([shrink[:half], shrink[half:]], 1)
        pieces.append(jnp.concatenate([expand[layer], packed], 0))
    return pieces


def quarter(param):
    rows = param.shape[0] // lax.axis_size("rep")
    return lax.dynamic_slice_in_dim(param, lax.axis_index("rep") * rows, rows, 0)


def gather_small(all_params):
    packed = jnp.concatenate([all_params[i] for i in SMALL], 1)
    whole, owner, step = packed[None], lax.axis_index("fsdp"), 1
    while step < lax.axis_size("fsdp"):
        got = swap(whole, "fsdp", step)
        whole = jnp.where(
            (owner // step) % 2 == 0,
            jnp.concatenate([whole, got], 0),
            jnp.concatenate([got, whole], 0),
        )
        step *= 2
    vectors, start = [], 0
    for i in SMALL:
        size = all_params[i].shape[1]
        vectors.append(
            jnp.moveaxis(whole[:, :, start : start + size], 0, 1).reshape(LAYERS, -1)
        )
        start += size
    return vectors, got


def link_orders():
    bits = list(range(lax.axis_size("rep").bit_length() - 1))
    return [bits, bits[::-1]]


def divide(blocks, shapes, bits, outs):
    for side in range(len(shapes)):
        high, later = shapes[side]
        for i in range(high):
            for j in range(later):
                base = 2 * i * later + j
                for out_ref, index in (
                    (outs[2 * side], base + bits[side] * later),
                    (outs[2 * side + 1], base + (1 - bits[side]) * later),
                ):
                    for row, column, block in blocks(side, index):
                        out_ref[
                            0, i, j, row : row + block.shape[0], column : column + block.shape[1]
                        ] = block


def block_grad_kernel(shapes, where_ref, left_ref, grad_ref, more_ref, other_ref, *refs):
    outs, held, extra = refs[:-2], refs[-2], refs[-1]
    held[...] = low(weight_dot(left_ref[...], grad_ref[...])).reshape(held.shape)
    extra[...] = low(weight_dot(more_ref[...], other_ref[...])).reshape(extra.shape)
    rows, half, tall = held.shape[2], held.shape[3] // 2, extra.shape[1] // 2

    def blocks(side, index):
        return [
            (p * rows, 0, held[p, index, :, side * half : (side + 1) * half]) for p in range(2)
        ] + [(2 * rows, 0, extra[index, side * tall : (side + 1) * tall])]

    divide(blocks, shapes, (where_ref[0], where_ref[1]), outs)


def mixed_grad_kernel(shapes, where_ref, left_ref, grad_ref, more_ref, other_ref, *refs):
    outs, held, extra = refs[:4], refs[4], refs[5]
    held[...] = low(weight_dot(left_ref[...], grad_ref[...])).reshape(held.shape)
    extra[...] = low(weight_dot(more_ref[...], other_ref[...])).reshape(extra.shape)
    rows, rest = held.shape[2], extra.shape[2] // 2
    half = (held.shape[3] + rest) // 2

    def blocks(side, index):
        if side == 0:
            return [(p * rows, 0, held[p, index, :, :half]) for p in range(2)]
        return [(p * rows, 0, held[p, index, :, half:]) for p in range(2)] + [
            (p * rows, half - rest, extra[index, :, p * rest : (p + 1) * rest]) for p in range(2)
        ]

    divide(blocks, shapes, (where_ref[0], where_ref[1]), outs)


def grad_call(kernel, arrays, widths, rows, columns, scratch, orders):
    planes, count = lax.axis_size("fsdp") // 2, lax.axis_size("rep")
    member = lax.axis_index("rep")
    shapes = tuple((count >> (order[0] + 1), 1 << order[0]) for order in orders)
    tokens = arrays[0].shape[0]
    specs = []
    for array, width in zip(arrays, widths):
        if width is None:
            specs.append(pl.BlockSpec(array.shape, lambda z, where: (0, 0)))
        else:
            specs.append(pl.BlockSpec((tokens, width), lambda z, where: (0, z)))
    out_shapes, out_specs = [], []
    for high, later in shapes:
        block = (high, later, rows, columns // len(orders))
        out_specs += [pl.BlockSpec((1,) + block, lambda z, where: (z, 0, 0, 0, 0))] * 2
        out_shapes += [jax.ShapeDtypeStruct((planes,) + block, jnp.bfloat16)] * 2
    return pl.pallas_call(
        functools.partial(kernel, shapes),
        out_shape=out_shapes,
        grid_spec=pltpu.PrefetchScalarGridSpec(
            num_scalar_prefetch=1,
            grid=(planes,),
            in_specs=specs,
            out_specs=out_specs,
            scratch_shapes=[pltpu.VMEM(size, jnp.bfloat16) for size in scratch],
        ),
        compiler_params=params(40),
        cost_estimate=estimate(5, 0),
    )(scalars(*[(member >> order[0]) & 1 for order in orders]), *arrays)


def block_grad(left, grad, more, other, orders):
    planes, count = lax.axis_size("fsdp") // 2, lax.axis_size("rep")
    widths = left.shape[1] // planes, more.shape[1] // planes
    columns = grad.shape[1]
    rows, tall = widths[0] // (2 * count), widths[1] // count
    return grad_call(
        block_grad_kernel, (left, grad, more, other), (widths[0], None, widths[1], None),
        2 * rows + tall // 2, columns,
        [(2, count, rows, columns), (count, tall, other.shape[1])], orders,
    )


def mixed_grad(left, grad, more, other, orders):
    planes, count = lax.axis_size("fsdp") // 2, lax.axis_size("rep")
    widths = left.shape[1] // planes, more.shape[1] // planes
    columns, rest = grad.shape[1], other.shape[1]
    rows = widths[1] // count
    if widths[1] % 128:
        first = low(weight_dot(left, grad)).reshape(planes, 2, count, rows, columns)
        second = low(weight_dot(more, other)).reshape(planes, count, rows, 2, rest // 2)
        total = jnp.concatenate([jnp.swapaxes(first, 1, 2), jnp.swapaxes(second, 2, 3)], 4)
        total = total.reshape(planes, count, 2 * rows, -1)
        half, member = total.shape[3] // 2, lax.axis_index("rep")
        top = count // 2
        left_part = total[..., :half].reshape(planes, top, 2, 1, 2 * rows, half)
        right_part = total[..., half:].reshape(planes, 1, 2, top, 2 * rows, half)
        sides = member % 2, member // top
        return [
            pick(part, side if kept else 1 - side, 2)
            for part, side in zip((left_part, right_part), sides)
            for kept in (True, False)
        ]
    return grad_call(
        mixed_grad_kernel, (left, grad, more, other), (widths[0], None, widths[1], None),
        2 * rows, columns + rest // 2,
        [(2, count, rows, columns), (count, rows, rest)], orders,
    )


def split_kernel(where_ref, *refs):
    count = len(refs) // 4
    for n in range(count):
        bit = where_ref[n]
        keep_in, got_ref = refs[2 * n], refs[2 * n + 1]
        keep_ref, send_ref = refs[2 * (count + n)], refs[2 * (count + n) + 1]
        keep_ref[0] = low(widen(keep_in[0, bit]) + widen(got_ref[0, bit]))
        send_ref[0] = low(widen(keep_in[0, 1 - bit]) + widen(got_ref[0, 1 - bit]))


def add_split(pairs, later, sides, rows):
    if len({pair[0].size // n for pair, n in zip(pairs, later)}) > 1:
        return [
            out
            for pair, n, side in zip(pairs, later, sides)
            for out in add_split([pair], [n], [side], rows)
        ]
    arrays, in_specs, out_specs, out_shapes = [], [], [], []
    for pair, n in zip(pairs, later):
        columns = pair[0].shape[-1]
        for array in pair:
            arrays.append(array.reshape(-1, 2, n, rows, columns))
            in_specs.append(
                pl.BlockSpec((1, 2, n, rows, columns), lambda i, where: (i, 0, 0, 0, 0))
            )
            out_specs.append(pl.BlockSpec((1, n, rows, columns), lambda i, where: (i, 0, 0, 0)))
            out_shapes.append(
                jax.ShapeDtypeStruct((arrays[-1].shape[0], n, rows, columns), jnp.bfloat16)
            )
    return pl.pallas_call(
        split_kernel,
        out_shape=out_shapes,
        grid_spec=pltpu.PrefetchScalarGridSpec(
            num_scalar_prefetch=1,
            grid=(arrays[0].shape[0],),
            in_specs=in_specs,
            out_specs=out_specs,
        ),
        compiler_params=params(24),
        cost_estimate=estimate(0, sum(array.size for array in arrays) * 3),
    )(scalars(*sides), *arrays)


def merge_kernel(where_ref, *refs):
    arrays, (keep_ref, send_ref) = refs[:-2], refs[-2:]
    half = arrays[0].shape[-1]
    for out_ref, bit in ((keep_ref, where_ref[0]), (send_ref, 1 - where_ref[0])):
        start = 0
        for n in range(0, len(arrays), 4):
            left_ref, left_got, right_ref, right_got = arrays[n : n + 4]
            rows = slice(start, start + left_ref.shape[2])
            out_ref[0, rows, :half] = low(widen(left_ref[0, bit]) + widen(left_got[0, bit]))
            out_ref[0, rows, half:] = low(widen(right_ref[0, bit]) + widen(right_got[0, bit]))
            start += left_ref.shape[2]


def add_merge(messages, side):
    half = messages[0][0].shape[-1]
    arrays, specs, total = [], [], 0
    for message in messages:
        rows = message[0].shape[-2]
        arrays += [array.reshape(-1, 2, rows, half) for array in message]
        specs += [pl.BlockSpec((1, 2, rows, half), lambda i, where: (i, 0, 0, 0))] * 4
        total += rows
    high = arrays[0].shape[0]
    given = pl.BlockSpec((1, total, 2 * half), lambda i, where: (i, 0, 0))
    shape = jax.ShapeDtypeStruct((high, total, 2 * half), jnp.bfloat16)
    return pl.pallas_call(
        merge_kernel,
        out_shape=[shape, shape],
        grid_spec=pltpu.PrefetchScalarGridSpec(
            num_scalar_prefetch=1,
            grid=(high,),
            in_specs=specs,
            out_specs=[given, given],
        ),
        compiler_params=params(24),
        cost_estimate=estimate(0, sum(array.size for array in arrays) * 3),
    )(scalars(side), *arrays)


def reduce_members(arrays):
    member, lanes = lax.axis_index("rep"), range(2)
    rows, orders = arrays[0].shape[-2], link_orders()
    bits = [sorted(order) for order in orders]
    keeps, sends = list(arrays[::2]), list(arrays[1::2])
    for n in range(len(orders[0])):
        gots = [swap(sends[i], "rep", 1 << orders[i][n]) for i in lanes]
        for i in lanes:
            bits[i].remove(orders[i][n])
        token = yield sends, gots
        gots = [after(got, token) for got in gots]
        if n + 1 < len(orders[0]):
            later = [1 << bits[i].index(orders[i][n + 1]) for i in lanes]
            sides = [(member >> orders[i][n + 1]) & 1 for i in lanes]
            outs = add_split(list(zip(keeps, gots)), later, sides, rows)
            keeps, sends = list(outs[::2]), list(outs[1::2])
    return [keeps[0], gots[0], keeps[1], gots[1]]


def reduce_planes(messages):
    plane, planes = position()[0], lax.axis_size("fsdp") // 2
    rows = sum(message[0].shape[-2] for message in messages)
    keep, send = add_merge(messages, plane % 2)
    step = 1
    while True:
        got = swap(send, "fsdp", 2 * step)
        token = yield [send], [got]
        got = after(got, token)
        step *= 2
        if step == planes:
            return low(widen(keep) + widen(got)).reshape(rows, -1)
        keep, send = add_split([(keep, got)], [1], [(plane // step) % 2], rows)


def finish_columns(total, columns):
    core = position()[1]
    rows = total.shape[0] // 2
    part = total[:, :columns].reshape(2, rows, columns)
    got = swap(pick(part, 1 - core, 0), "fsdp", 1)
    part = jnp.concatenate([pick(part, core, 0), got], 0)
    return jnp.concatenate([part, total[:, columns:]], 1)


def spread(own, low_last):
    pieces = [own]
    for k in range(1, lax.axis_size("rep")):
        last = k & -k if low_last else 1 << (k.bit_length() - 1)
        pieces.append(swap(pieces[k ^ last], "rep", last))
    return pieces


def column_out(out_ref, block, side, ref, start):
    rows = out_ref.shape[2]
    for i in range(out_ref.shape[3] // block):
        first = start if i % 2 == side else start + rows
        out_ref[0, 0, :, i * block : (i + 1) * block] = widen(
            ref[first : first + rows, (i // 2) * block : (i // 2 + 1) * block]
        )


def early_out_kernel(block, where_ref, *refs):
    expand_out, shrink_out = refs[-2:]
    for k, ref in enumerate(refs[:-4]):
        for side in range(2):

            @pl.when((pl.program_id(0) == k) & (where_ref[1] == side))
            def _():
                column_out(expand_out, block, side, ref, 0)

        @pl.when(pl.program_id(0) == k)
        def _():
            rows, columns = shrink_out.shape[2] // 2, shrink_out.shape[3]
            start = ref.shape[0] - rows
            shrink_out[0, 0, :rows] = widen(ref[start:, :columns])
            shrink_out[0, 0, rows:] = widen(ref[start:, columns:])


def late_out_kernel(block, where_ref, *refs):
    heads_out, output_out = refs[-2:]
    for k, ref in enumerate(refs[:-4]):
        for side in range(2):

            @pl.when((pl.program_id(0) == k) & (where_ref[1] == side))
            def _():
                column_out(heads_out, block, side, ref, 0)

        @pl.when(pl.program_id(0) == k)
        def _():
            rows, half = output_out.shape[2], output_out.shape[3] // 2
            start = ref.shape[1] - half
            output_out[0, 0, :, :half] = widen(ref[:rows, start:])
            output_out[0, 0, :, half:] = widen(ref[rows:, start:])


def write_out(kernel, layer, pieces, sizes, earlier):
    plane, core, member = position()
    count = len(pieces)
    shapes = [(LAYERS, count) + size for size in sizes]
    if earlier is None:
        earlier = [jnp.zeros((8, 128), jnp.float32)] * len(sizes)
        aliases = {}
    else:
        earlier = [array.reshape(shape) for array, shape in zip(earlier, shapes)]
        aliases = {1 + count + i: i for i in range(len(sizes))}
    return pl.pallas_call(
        kernel,
        out_shape=[jax.ShapeDtypeStruct(shape, jnp.float32) for shape in shapes],
        grid_spec=pltpu.PrefetchScalarGridSpec(
            num_scalar_prefetch=1,
            grid=(count,),
            in_specs=[pl.BlockSpec(piece.shape, lambda k, where: (0, 0)) for piece in pieces]
            + [pl.BlockSpec(memory_space=pl.ANY)] * len(sizes),
            out_specs=[
                pl.BlockSpec((1, 1) + size, lambda k, where: (layer, k ^ where[0], 0, 0))
                for size in sizes
            ],
        ),
        input_output_aliases=aliases,
        compiler_params=params(24),
        cost_estimate=estimate(0, count * pieces[0].size * 6),
    )(scalars(member, core), *pieces, *earlier)


def reduce_small(grads, earlier):
    owners, count = lax.axis_size("fsdp"), lax.axis_size("rep")
    total = jnp.concatenate([g.reshape(LAYERS, owners, -1) for g in grads], 2)
    total = after(total, *earlier)
    owner = lax.axis_index("fsdp")
    step = owners // 2
    while step:
        total = total.reshape(LAYERS, 2, step, -1)
        mine = (owner // step) % 2
        total = pick(total, mine, 1) + swap(pick(total, 1 - mine, 1), "fsdp", step)
        step //= 2
    step = 1
    while step < count:
        total = total + swap(total, "rep", step)
        step *= 2
    total = total.reshape(LAYERS, -1)
    outs, start = [], 0
    for g in grads:
        size = g.shape[1] // owners
        outs.append(total[:, start : start + size])
        start += size
    return outs


def other_half(rows):
    return swap(rows, "fsdp", lax.axis_size("fsdp") // 2)


def image_side():
    return lax.axis_index("fsdp") // (lax.axis_size("fsdp") // 2)


def regroup(blocks):
    side = image_side()
    return pick(blocks, side, 0), other_half(pick(blocks, 1 - side, 0))


def ungroup(rows, got):
    own, got = rows[: rows.shape[0] // 2], got.astype(rows.dtype)
    return jnp.where(image_side() == 0, jnp.stack([own, got]), jnp.stack([got, own]))


def chips_per_image():
    return lax.axis_size("fsdp") // 4


def share_rows(local_kv):
    shared = [local_kv]
    for k in range(1, chips_per_image()):
        low_bit = k & -k
        shared.append(swap(shared[k ^ low_bit], "fsdp", 2 * low_bit))
    return shared


def collect_rows(own, others):
    chips = chips_per_image()
    if chips == 2:
        got = swap(others, "fsdp", 2)
        return low(widen(own) + widen(got)), got
    total = jnp.concatenate([own, others], 1)
    while chips > 1:
        rows = total.shape[1] // 2
        got = swap(total[:, rows:], "fsdp", chips)
        total = low(widen(total[:, :rows]) + widen(got))
        chips //= 2
    return total, got


def both_cores(rows):
    return jnp.concatenate([rows, swap(rows, "fsdp", 1)], 0)


def one_head(tensor, head):
    half = tensor.shape[1] // 2
    lane = lax.broadcasted_iota(jnp.int32, tensor.shape, 1)
    keep = lane < half if head == 0 else lane >= half
    return jnp.where(keep, tensor, jnp.zeros_like(tensor))


def join(refs, held):
    start = 0
    for ref in refs:
        held[start : start + ref.shape[0], :] = ref[...]
        start += ref.shape[0]
    return held[...]


def attend_kernel(factor, parts, query_ref, *refs):
    out_ref, log_ref, held_keys, held_values = refs[2 * parts :]
    keys, values = join(refs[:parts], held_keys), join(refs[parts : 2 * parts], held_values)
    results, logs = [], []
    for head in range(2):
        scores = input_dot(one_head(query_ref[...], head), keys)
        largest = jnp.max(scores, -1, keepdims=True)
        weights = jnp.exp2((scores - largest) * factor)
        total = jnp.sum(weights, -1, keepdims=True)
        results.append(forward_dot(low(weights), values) / total)
        logs.append(largest * factor + jnp.log2(total))
    out_ref[...] = low(one_head(results[0], 0) + one_head(results[1], 1))
    shape = log_ref.shape
    log_ref[...] = one_head(jnp.broadcast_to(logs[0], shape), 0) + one_head(
        jnp.broadcast_to(logs[1], shape), 1
    )


def pair_block(rows, start):
    return pl.BlockSpec((rows, 128), lambda i: (0, start + i))


def kv_parts(projected, others):
    pairs = projected.shape[1] // 384
    if projected.shape[0] % 16:
        others = [jnp.concatenate([projected[:, 128 * pairs :]] + others, 0)]
        parts = []
    else:
        parts = [(projected, pairs, 2 * pairs)]
    return parts + [(other, 0, pairs) for other in others]


def kv_specs(parts, first=0):
    keys = [pair_block(array.shape[0], first + start) for array, start, unused in parts]
    values = [pair_block(array.shape[0], first + start) for array, unused, start in parts]
    rows = sum(array.shape[0] for array, unused, more in parts)
    held = [pltpu.VMEM((rows, 128), jnp.bfloat16)] * 2
    return keys + values, [array for array, unused, more in parts] * 2, held


def attend(projected, others, head_size):
    tokens, width = projected.shape[0], projected.shape[1] // 3
    pairs = width // 128
    parts = kv_parts(projected, others)
    specs, arrays, held = kv_specs(parts)
    factor = head_size ** (-0.5) * math.log2(math.e)
    return pl.pallas_call(
        functools.partial(attend_kernel, factor, len(parts)),
        out_shape=[
            jax.ShapeDtypeStruct((tokens, width), jnp.bfloat16),
            jax.ShapeDtypeStruct((tokens, width), jnp.float32),
        ],
        grid=(pairs,),
        in_specs=[pair_block(tokens, 0)] + specs,
        out_specs=[pair_block(tokens, 0), pair_block(tokens, 0)],
        scratch_shapes=held,
        compiler_params=params(56),
        cost_estimate=estimate(18, 0),
    )(projected, *arrays)


def attend_back_kernel(factor, scale, parts, query_ref, *refs):
    log_ref, grad_ref, dq_ref, own_ref, others_ref, held_keys, held_values = refs[2 * parts :]
    keys, values = join(refs[:parts], held_keys), join(refs[parts : 2 * parts], held_values)
    d_query, d_key, d_value = [], 0.0, 0.0
    for head in range(2):
        query = one_head(query_ref[...], head)
        grad = one_head(grad_ref[...], head)
        half = query.shape[1] // 2
        log_total = log_ref[:, head * half : head * half + 1]
        probs = jnp.exp2(input_dot(query, keys) * factor - log_total)
        products = probs * input_dot(grad, values)
        d_scores = low(products - probs * jnp.sum(products, -1, keepdims=True))
        d_query.append(forward_dot(d_scores, keys))
        d_key = d_key + weight_dot(d_scores, query)
        d_value = d_value + weight_dot(low(probs), grad)
    dq_ref[...] = low((one_head(d_query[0], 0) + one_head(d_query[1], 1)) * scale)
    rows = own_ref.shape[1]
    for i, total in enumerate((low(d_key * scale), low(d_value))):
        own_ref[i] = total[:rows]
        others_ref[i] = total[rows:]


def attend_back(projected, others, log_total, d_attended, head_size, first, pairs):
    tokens, width = d_attended.shape[0], 128 * pairs
    parts = kv_parts(projected, others)
    specs, arrays, held = kv_specs(parts, first)
    rows = held[0].shape[0]
    scale = head_size ** (-0.5)
    own, taken = pair_block(tokens, 0), pair_block(tokens, first)
    return pl.pallas_call(
        functools.partial(attend_back_kernel, scale * math.log2(math.e), scale, len(parts)),
        out_shape=[
            jax.ShapeDtypeStruct((tokens, width), jnp.bfloat16),
            jax.ShapeDtypeStruct((2, tokens, width), jnp.bfloat16),
            jax.ShapeDtypeStruct((2, rows - tokens, width), jnp.bfloat16),
        ],
        grid=(pairs,),
        in_specs=[taken] + specs + [taken, taken],
        out_specs=[
            own,
            pl.BlockSpec((2, tokens, 128), lambda i: (0, 0, i)),
            pl.BlockSpec((2, rows - tokens, 128), lambda i: (0, 0, i)),
        ],
        scratch_shapes=held,
        compiler_params=params(60),
        cost_estimate=estimate(8 * pairs, 0),
    )(projected, *arrays, log_total, d_attended)


def add_tile(part, own_ref, other_ref, total_ref):
    @pl.when(pl.program_id(0) == 0)
    def _():
        total_ref[...] = part

    @pl.when(pl.program_id(0) > 0)
    def _():
        total_ref[...] += part

    @pl.when(pl.program_id(0) == pl.num_programs(0) - 1)
    def _():
        half = own_ref.shape[0]
        own_ref[...] = total_ref[:half]
        other_ref[...] = low(total_ref[half:])


def expand_kernel(
    rows_ref, expand_ref, bias_ref, shrink_ref, active_ref, slope_ref, own_ref, other_ref, total_ref
):
    hidden = forward_dot(rows_ref[...], expand_ref[...]) + bias_ref[...]
    normal = 0.5 + 0.5 * lax.erf(hidden * math.sqrt(0.5))
    density = jnp.exp2(hidden * hidden * (-0.5 * math.log2(math.e)))
    slope_ref[...] = low(normal + hidden * density * (1.0 / math.sqrt(2.0 * math.pi)))
    active = low(hidden * normal)
    active_ref[...] = active
    add_tile(forward_dot(active, shrink_ref[...]), own_ref, other_ref, total_ref)


def feed_forward(rows_in, expand, expand_bias, shrink):
    tokens, width = rows_in.shape
    units = expand.shape[1]
    tile = 512
    whole = pl.BlockSpec((tokens, width), lambda i: (0, 0))
    half = pl.BlockSpec((tokens // 2, width), lambda i: (0, 0))
    part = pl.BlockSpec((tokens, tile), lambda i: (0, i))
    return pl.pallas_call(
        expand_kernel,
        out_shape=[
            jax.ShapeDtypeStruct((tokens, units), jnp.bfloat16),
            jax.ShapeDtypeStruct((tokens, units), jnp.bfloat16),
            jax.ShapeDtypeStruct((tokens // 2, width), jnp.float32),
            jax.ShapeDtypeStruct((tokens // 2, width), jnp.bfloat16),
        ],
        grid=(units // tile,),
        in_specs=[
            whole,
            pl.BlockSpec((width, tile), lambda i: (0, i)),
            pl.BlockSpec((1, tile), lambda i: (0, i)),
            pl.BlockSpec((tile, width), lambda i: (i, 0)),
        ],
        out_specs=[part, part, half, half],
        scratch_shapes=[pltpu.VMEM((tokens, width), jnp.float32)],
        compiler_params=params(32),
        cost_estimate=estimate(14, 0),
    )(rows_in, expand, expand_bias[None], shrink)


def shrink_kernel(
    grad_ref, shrink_ref, slope_ref, expand_ref, hidden_ref, bias_ref, own_ref, other_ref, total_ref
):
    d_hidden = low(input_dot(grad_ref[...], shrink_ref[...]) * widen(slope_ref[...]))
    hidden_ref[...] = d_hidden
    bias_ref[...] = jnp.sum(widen(d_hidden), 0, keepdims=True)
    add_tile(input_dot(d_hidden, expand_ref[...]), own_ref, other_ref, total_ref)


def feed_back(d_mlp, shrink, slope, expand):
    tokens, width = d_mlp.shape
    units = expand.shape[1]
    tile = 512
    whole = pl.BlockSpec((tokens, width), lambda i: (0, 0))
    half = pl.BlockSpec((tokens // 2, width), lambda i: (0, 0))
    part = pl.BlockSpec((tokens, tile), lambda i: (0, i))
    return pl.pallas_call(
        shrink_kernel,
        out_shape=[
            jax.ShapeDtypeStruct((tokens, units), jnp.bfloat16),
            jax.ShapeDtypeStruct((1, units), jnp.float32),
            jax.ShapeDtypeStruct((tokens // 2, width), jnp.float32),
            jax.ShapeDtypeStruct((tokens // 2, width), jnp.bfloat16),
        ],
        grid=(units // tile,),
        in_specs=[
            whole,
            pl.BlockSpec((tile, width), lambda i: (i, 0)),
            part,
            pl.BlockSpec((width, tile), lambda i: (0, i)),
        ],
        out_specs=[part, pl.BlockSpec((1, tile), lambda i: (0, i)), half, half],
        scratch_shapes=[pltpu.VMEM((tokens, width), jnp.float32)],
        compiler_params=params(32),
        cost_estimate=estimate(9, 0),
    )(d_mlp, shrink, slope, expand)


def core_half(vector):
    core = position()[1]
    return pick(widen(vector).reshape(lax.axis_size("fsdp") // 2, 2, -1), core, 1).reshape(-1)


def core_fill(half):
    parts = half.reshape(lax.axis_size("fsdp") // 2, -1)
    return by_core(parts, jnp.zeros_like(parts), 1).reshape(-1)


def normed_rows(tok_rows, gathered):
    return both_cores(low(layer_norm(tok_rows, widen(gathered[0]), widen(gathered[1]))))


def project(normed, gathered, token):
    heads_weight, query_bias, value_bias = gathered[2], gathered[3], gathered[4]
    width = normed.shape[1]
    bias_row = jnp.concatenate(
        [core_half(query_bias), jnp.zeros((width // 2,), jnp.float32), core_half(value_bias)]
    )
    projected = low(forward_dot(normed, heads_weight) + bias_row)
    return projected, share_rows(after(projected[:, width // 2 :], token))[1:]


def forward_layer(
    tok_rows, normed, projected, others, gathered, beside, following
):
    (
        attn_norm_gain,
        attn_norm_bias,
        heads_weight,
        query_bias,
        value_bias,
        output_weight,
        output_bias,
        attn_layerscale,
        mlp_norm_gain,
        mlp_norm_bias,
        expand_weight,
        expand_bias,
        shrink_weight,
        shrink_bias,
        mlp_layerscale,
    ) = gathered
    tokens, width = tok_rows.shape
    attended, log_total = attend(projected, others, width // HEADS)
    attended = after(attended, *beside)
    got = swap(low(forward_dot(attended[tokens:], output_weight)), "fsdp", 1)
    branch = forward_dot(attended[:tokens], output_weight) + widen(got) + widen(output_bias)
    middle = tok_rows + widen(attn_layerscale) * branch
    normed_two = low(layer_norm(middle, widen(mlp_norm_gain), widen(mlp_norm_bias)))
    normed_two = both_cores(normed_two)
    activated, slope, own_sum, other_sum = feed_forward(
        normed_two, expand_weight, core_half(expand_bias), shrink_weight
    )
    other_sum = after(other_sum, *following)
    mlp_out = own_sum + widen(swap(other_sum, "fsdp", 1)) + widen(shrink_bias)
    result = middle + widen(mlp_layerscale) * mlp_out
    saved = (
        tok_rows,
        normed,
        projected,
        others,
        log_total,
        attended,
        branch,
        middle,
        normed_two,
        slope,
        activated,
        mlp_out,
    )
    return (result, saved)


class Later:
    def __init__(self):
        self.running, self.done, self.sends, self.gots = {}, {}, {}, {}

    def begin(self, name, kernel, arrays):
        self.running[name] = reduce_members(kernel(*arrays, link_orders()))
        self.step(name, None)

    def join(self, name, parts, token):
        for part in parts:
            while part in self.running:
                self.step(part, token)
        self.running[name] = reduce_planes([self.done[part] for part in parts])
        self.step(name, None)

    def step(self, name, token):
        try:
            self.sends[name], self.gots[name] = self.running[name].send(token)
        except StopIteration as end:
            self.done[name] = end.value
            self.sends[name] = self.gots[name] = []
            del self.running[name]

    def sent(self, value, *names):
        return after(value, *[array for name in names for array in self.sends[name]])

    def came(self, value, *names):
        return after(value, *[array for name in names for array in self.gots[name]])


def backward_layer(d_result, saved, gathered, later, new, old, activation_got):
    (
        attn_norm_gain,
        attn_norm_bias,
        heads_weight,
        query_bias,
        value_bias,
        output_weight,
        output_bias,
        attn_layerscale,
        mlp_norm_gain,
        mlp_norm_bias,
        expand_weight,
        expand_bias,
        shrink_weight,
        shrink_bias,
        mlp_layerscale,
    ) = gathered
    (
        tok_rows,
        normed,
        projected,
        others,
        log_total,
        attended,
        branch,
        middle,
        normed_two,
        slope,
        activated,
        mlp_out,
    ) = saved
    tokens, width = tok_rows.shape
    d_mlp = low(d_result * widen(mlp_layerscale))
    d_mlp_both = both_cores(d_mlp)
    g_mlp_scale = jnp.sum(d_result * mlp_out, 0)
    g_shrink_bias = column_sum(d_mlp)
    d_hidden, g_expand_bias, own_sum, other_sum = feed_back(
        d_mlp_both, shrink_weight, slope, expand_weight
    )
    block, mixed, block_planes, mixed_planes = new
    if old:
        other_sum = later.came(other_sum, old[0])
        later.join(old[2], [old[0]], other_sum)
        d_hidden = later.sent(d_hidden, old[2])
    got = swap(other_sum, "fsdp", 1)
    later.begin(block, block_grad, (normed_two, d_hidden, activated, d_mlp_both))
    own_sum = later.sent(own_sum, block)
    if not old:
        own_sum = after(own_sum, activation_got)
    else:
        own_sum = later.came(own_sum, old[1])
        later.step(old[1], own_sum)
        own_sum = later.sent(own_sum, old[1])
    d_middle_norm, g_mlp_gain, g_mlp_shift = norm_back(
        middle, widen(mlp_norm_gain), widen(mlp_norm_bias), own_sum + widen(got)
    )
    d_middle = d_result + d_middle_norm
    d_branch = low(d_middle * widen(attn_layerscale))
    d_branch_both = both_cores(d_branch)
    g_attn_scale = jnp.sum(d_middle * branch, 0)
    g_output_bias = column_sum(d_branch)
    d_attended = low(input_dot(d_branch_both, output_weight))
    pairs = d_attended.shape[1] // 128

    def back(first):
        return attend_back(
            projected, others, log_total, d_attended, width // HEADS, first, pairs // 2
        )

    first_query, d_own, d_others = back(0)
    first_kv, first_got = collect_rows(d_own, d_others)
    if old:
        d_attended = later.came(d_attended, old[2])
        later.step(old[2], first_query)
        d_attended = later.sent(d_attended, old[2])
    second_query, d_own, d_others = back(pairs // 2)
    d_others = after(d_others, first_got)
    second_kv, second_got = collect_rows(d_own, d_others)
    second_query = later.came(second_query, block)
    later.step(block, second_query)
    second_query = later.sent(second_query, block)
    if old:
        second_query = later.came(second_query, old[1])
        later.join(old[3], [old[1]], second_query)
        second_query = later.sent(second_query, old[3])
    d_query = jnp.concatenate([first_query, second_query], 1)
    d_key = jnp.concatenate([first_kv[0], second_kv[0]], 1)
    d_value = jnp.concatenate([first_kv[1], second_kv[1]], 1)
    d_projected = jnp.concatenate([d_query, d_key, d_value], 1)
    g_query_bias = column_sum(d_query)
    g_value_bias = column_sum(d_value)
    got = swap(low(input_dot(d_projected[tokens:], heads_weight)), "fsdp", 1)
    later.begin(mixed, mixed_grad, (normed, d_projected, attended, d_branch_both))
    d_projected = later.sent(d_projected, mixed)
    if old:
        later.join(block_planes, [block], d_projected)
        d_projected = later.sent(d_projected, block_planes)
    d_normed = input_dot(d_projected[:tokens], heads_weight) + widen(got)
    d_rows_norm, g_attn_gain, g_attn_shift = norm_back(
        tok_rows, widen(attn_norm_gain), widen(attn_norm_bias), d_normed
    )
    d_rows = d_middle + d_rows_norm
    small_grads = (
        g_attn_gain,
        g_attn_shift,
        core_fill(g_query_bias),
        core_fill(g_value_bias),
        g_output_bias,
        g_attn_scale,
        g_mlp_gain,
        g_mlp_shift,
        core_fill(g_expand_bias),
        g_shrink_bias,
        g_mlp_scale,
    )
    return (d_rows, small_grads)


def local(images, cotangent, *all_params):
    owners, count = lax.axis_size("fsdp"), lax.axis_size("rep")
    pieces = message_pieces(all_params)
    small, small_got = gather_small(all_params)
    column, planes = gather_planes(pieces[0], beside=[small_got])
    own, got = regroup(after(images, planes[0]))
    tok_rows = widen(jnp.concatenate([own, got], 0))
    column = after(column, got)
    next_column, next_planes = gather_planes(pieces[1], got)
    held, neighbours = gather_neighbours(column, [])
    members = gather_members(held, [])
    saved_layers, fetched = [], []
    for layer in range(LAYERS):
        gathered = [None] * len(all_params)
        for i, vector in zip(SMALL, small):
            gathered[i] = vector[layer]
        normed = normed_rows(tok_rows, gathered)
        arrays, parts, earlier = members
        arrays[0] = after(arrays[0], next_planes[-1])
        gathered[2], gathered[5] = place_first(
            arrays, parts, count, all_params[2].shape[2] // 2
        )
        projected, others = project(normed, gathered, next_planes[-1])
        held, neighbours = gather_neighbours(next_column, earlier)
        if layer + 1 < LAYERS:
            column, planes = gather_planes(pieces[2 * layer + 2], others[-1])
            beside = planes[:1]
        else:
            own, got = regroup(after(cotangent, others[-1]))
            d_rows = widen(jnp.concatenate([own, got], 0))
            beside, planes, neighbours, next_planes = [got], [], [], []
        arrays, parts, earlier = gather_members(held, [])
        if layer + 1 < LAYERS:
            next_column, next_planes = gather_planes(pieces[2 * layer + 3], planes[-1])
            held, neighbours = gather_neighbours(column, earlier)
            members = gather_members(held, [])
        arrays[0] = after(arrays[0], *planes[-1:], *next_planes[:1])
        gathered[10], gathered[12] = place_second(arrays, parts, count)
        fetched.append(tuple(gathered))
        tok_rows, saved = forward_layer(
            tok_rows,
            normed,
            projected,
            others,
            gathered,
            beside,
            next_planes[1:] + neighbours,
        )
        saved_layers.append(saved)
    activation_rows = low(tok_rows)
    small_grads = [None] * LAYERS
    outs = {}

    def size(i):
        return (all_params[i].shape[1] // count, all_params[i].shape[2])

    def block_piece(later, layer):
        total = later.done[layer, 2]
        half = total.shape[0] // 2
        return jnp.concatenate([finish_columns(total[:half], total.shape[1]), total[half:]], 0)

    def mixed_piece(later, layer):
        return finish_columns(later.done[layer, 3], size(2)[1] // 2)

    def write_block(layer, pieces):
        outs["block"] = write_out(
            functools.partial(early_out_kernel, size(10)[1] // owners),
            layer, pieces, [size(10), size(12)], outs.get("block"),
        )

    def write_mixed(layer, pieces):
        outs["mixed"] = write_out(
            functools.partial(late_out_kernel, size(2)[1] // 3 // owners),
            layer, pieces, [size(2), size(5)], outs.get("mixed"),
        )

    later = Later()
    for layer in reversed(range(LAYERS)):
        new = [(layer, n) for n in range(4)]
        old = [(layer + 1, n) for n in range(4)] if layer + 1 < LAYERS else None
        if not old:
            activation_got = other_half(activation_rows[activation_rows.shape[0] // 2 :])
        d_rows, small_grads[layer] = backward_layer(
            d_rows, saved_layers[layer], fetched[layer], later, new, old, activation_got
        )
    activations = ungroup(activation_rows, activation_got)
    image_got = other_half(low(d_rows[d_rows.shape[0] // 2 :]))
    d_images = ungroup(d_rows, image_got)
    for name in (old[2], old[3]):
        while name in later.running:
            later.step(name, d_rows)
    first = block_piece(later, layer + 1)
    rows = first.shape[0]
    first = after(jnp.concatenate([first, mixed_piece(later, layer + 1)], 0), d_rows)
    later.step(new[1], d_rows)
    pieces = spread(later.sent(first, new[1]), True)
    last_gots = later.gots[new[1]] + [image_got]
    later.step(new[2], later.sends[new[1]][0])
    later.join(new[3], [new[1]], later.gots[new[2]][0])
    while new[2] in later.running:
        later.step(new[2], d_rows)
    while new[3] in later.running:
        later.step(new[3], pieces[1])
    write_block(layer + 1, [piece[:rows] for piece in pieces])
    write_mixed(layer + 1, [piece[rows:] for piece in pieces])
    write_block(layer, spread(block_piece(later, layer), False))
    write_mixed(layer, spread(mixed_piece(later, layer), False))
    stacked = [None] * len(all_params)
    for i, out in zip((10, 12, 2, 5), list(outs["block"]) + list(outs["mixed"])):
        stacked[i] = out.reshape(all_params[i].shape)
    reduced = reduce_small(
        [jnp.stack([grads[n] for grads in small_grads]) for n in range(len(SMALL))], last_gots
    )
    for i, vector in zip(SMALL, reduced):
        stacked[i] = vector
    return (activations, d_images) + tuple(stacked)


def solution(mesh):
    in_specs = (
        P("rep", "fsdp", None),
        P("rep", "fsdp", None),
        P(None, "fsdp"),
        P(None, "fsdp"),
        P(None, "fsdp", None),
        P(None, "fsdp"),
        P(None, "fsdp"),
        P(None, "fsdp", None),
        P(None, "fsdp"),
        P(None, "fsdp"),
        P(None, "fsdp"),
        P(None, "fsdp"),
        P(None, "fsdp", None),
        P(None, "fsdp"),
        P(None, "fsdp", None),
        P(None, "fsdp"),
        P(None, "fsdp"),
    )
    out_specs = (
        P("rep", "fsdp", None),
        P("rep", "fsdp", None),
        P(None, "fsdp"),
        P(None, "fsdp"),
        P(None, "fsdp", None),
        P(None, "fsdp"),
        P(None, "fsdp"),
        P(None, "fsdp", None),
        P(None, "fsdp"),
        P(None, "fsdp"),
        P(None, "fsdp"),
        P(None, "fsdp"),
        P(None, "fsdp", None),
        P(None, "fsdp"),
        P(None, "fsdp", None),
        P(None, "fsdp"),
        P(None, "fsdp"),
    )
    return jax.shard_map(local, mesh=mesh, in_specs=in_specs, out_specs=out_specs, check_vma=False)
```

```python
import functools
import math

import jax
import jax.numpy as jnp
from jax import lax
from jax.experimental import pallas as pl
from jax.experimental.pallas import tpu as pltpu
from jax.sharding import PartitionSpec as P

HEADS = 16
LAYERS = 2
SMALL = (0, 1, 3, 4, 6, 7, 8, 9, 11, 13, 14)
MIB = 1 << 20

epsilon = 1e-06


def layer_norm(values_in, norm_gain, norm_shift):
    centre = jnp.mean(values_in, -1, keepdims=True)
    centered = values_in - centre
    spread = jnp.mean(centered * centered, -1, keepdims=True)
    return centered * lax.rsqrt(spread + epsilon) * norm_gain + norm_shift


def norm_back(values_in, norm_gain, norm_shift, grad):
    unused, pullback = jax.vjp(layer_norm, values_in, norm_gain, norm_shift)
    return pullback(grad)


def widen(tensor):
    return tensor.astype(jnp.float32)


def low(tensor):
    return tensor.astype(jnp.bfloat16)


def forward_dot(left, weight):
    return jnp.dot(left, weight, preferred_element_type=jnp.float32)


def weight_dot(left, grad):
    return lax.dot_general(left, grad, (((0,), (0,)), ((), ())), preferred_element_type=jnp.float32)


def input_dot(grad, weight):
    return lax.dot_general(
        grad, weight, (((1,), (1,)), ((), ())), preferred_element_type=jnp.float32
    )


def column_sum(grad):
    return jnp.sum(widen(grad), 0)


def pick(tensor, index, axis):
    return lax.dynamic_index_in_dim(tensor, index, axis, keepdims=False)


def swap(tensor, axis, offset):
    count = lax.axis_size(axis)
    return lax.ppermute(tensor, axis, [(i, i ^ offset) for i in range(count)])


def position():
    owner = lax.axis_index("fsdp")
    return owner // 2, owner % 2, lax.axis_index("rep")


def scalars(*values):
    return jnp.stack(values).astype(jnp.int32)


def estimate(microseconds, moved):
    return pl.CostEstimate(flops=1000, bytes_accessed=1000, transcendentals=0)


def params(mib):
    return pltpu.CompilerParams(vmem_limit_bytes=mib * MIB)


def after(tensor, *earlier):
    return lax.optimization_barrier((tensor,) + earlier)[0]


def by_core(own, got, axis):
    core = position()[1]
    return jnp.where(
        core == 0, jnp.stack([own, got], axis), jnp.stack([got, own], axis)
    )


def columns_kernel(blocks, where_ref, *refs):
    ins, (own_ref, other_ref) = refs[:-2], refs[-2:]
    for side in range(2):

        @pl.when(where_ref[1] == side)
        def _():
            for out_ref, parity in ((own_ref, side), (other_ref, 1 - side)):
                start = 0
                for ref, block in zip(ins, blocks):
                    for i in range(parity, ref.shape[2] // block, 2):
                        out_ref[0, :, start : start + block] = ref[0, :, i * block : (i + 1) * block]
                        start += block


def column_pieces(shards):
    plane, core, member = position()
    owners, count = lax.axis_size("fsdp"), lax.axis_size("rep")
    rows = shards[0].shape[1] // count
    blocks = tuple(
        size // owners for size in (shards[0].shape[2] // 3, shards[1].shape[2])
    )
    columns = sum(shard.shape[2] for shard in shards) // 2
    shape = jax.ShapeDtypeStruct((LAYERS, rows, columns), jnp.bfloat16)
    out = pl.BlockSpec((1, rows, columns), lambda layer, where: (layer, 0, 0))
    own, other = pl.pallas_call(
        functools.partial(columns_kernel, blocks),
        out_shape=[shape, shape],
        grid_spec=pltpu.PrefetchScalarGridSpec(
            num_scalar_prefetch=1,
            grid=(LAYERS,),
            in_specs=[
                pl.BlockSpec((1, rows, shard.shape[2]), lambda layer, where: (layer, where[0], 0))
                for shard in shards
            ],
            out_specs=[out, out],
        ),
        cost_estimate=estimate(0, 4 * LAYERS * rows * columns * 2),
    )(scalars(member, core), *shards)
    both = by_core(own, swap(other, "fsdp", 1), 1)
    split = shards[0].shape[2] // 2
    both = both.reshape(LAYERS, 2 * rows, columns)
    return both[..., :split], both[..., split:]


def place_kernel(half_rows, blocks, parts, where_ref, *refs):
    count = len(parts)
    pieces, outs, (in_sems, out_sems) = refs[:count], refs[count : -count - 2], refs[-2:]
    held = refs[-count - 2 : -2]
    plane, member = where_ref[0], where_ref[1]
    arrivals = []
    for i in range(count):
        arrivals.append(pltpu.make_async_copy(pieces[i], held[i], in_sems.at[i]))
        arrivals[-1].start()
    copies = []
    for i, (k, halves) in enumerate(parts):
        arrivals[i].wait()
        for j in range(pieces[0].shape[0]):
            for b, (row, rows, column, columns, put) in enumerate(blocks):
                if row // half_rows not in halves:
                    continue
                first = row - halves[0] * half_rows
                copy = pltpu.make_async_copy(
                    held[i].at[j, first : first + rows, column : column + columns],
                    put(outs, j ^ plane, k ^ member),
                    out_sems.at[b, i, j],
                )
                copy.start()
                copies.append(copy)
    for copy in copies:
        copy.wait()


def place(pieces, parts, shapes, blocks):
    plane, core, member = position()
    planes = pieces[0].shape[0]
    outs = pl.pallas_call(
        functools.partial(place_kernel, pieces[0].shape[1] // 2, blocks, parts),
        out_shape=[jax.ShapeDtypeStruct(shape, pieces[0].dtype) for shape in shapes],
        in_specs=[pl.BlockSpec(memory_space=pltpu.SMEM)]
        + [pl.BlockSpec(memory_space=pl.ANY)] * len(pieces),
        out_specs=[pl.BlockSpec(memory_space=pl.ANY)] * len(shapes),
        scratch_shapes=[pltpu.VMEM(piece.shape, piece.dtype) for piece in pieces]
        + [
            pltpu.SemaphoreType.DMA((len(pieces),)),
            pltpu.SemaphoreType.DMA((len(blocks), len(pieces), planes)),
        ],
        compiler_params=params(60),
        cost_estimate=estimate(0, 4 * sum(piece.size for piece in pieces)),
    )(scalars(plane, member), *pieces)
    return [out.reshape(-1, out.shape[-1]) for out in outs]


def put_pair(side):
    return lambda outs, plane, member: outs[0].at[plane, side, member]


def place_first(pieces, parts, count, split):
    planes, rows, columns = pieces[0].shape
    half, rest = rows // 2, columns - split

    def put(side):
        return lambda outs, plane, member: outs[1].at[
            plane, member, :, side * rest : (side + 1) * rest
        ]

    shapes = [(planes, 2, count, half, split), (planes, count, half, 2 * rest)]
    blocks = [(side * half, half, 0, split, put_pair(side)) for side in range(2)]
    blocks += [(side * half, half, split, rest, put(side)) for side in range(2)]
    return place(pieces, parts, shapes, blocks)


def place_second(pieces, parts, count):
    planes, rows, columns = pieces[0].shape
    half, fine, width = rows // 2, rows // 4, columns // 2

    def put(side):
        return lambda outs, plane, member: outs[1].at[plane, member, side]

    shapes = [(planes, 2, count, fine, columns), (planes, count, 2, half, width)]
    blocks = [(side * fine, fine, 0, columns, put_pair(side)) for side in range(2)]
    blocks += [(half, half, side * width, width, put(side)) for side in range(2)]
    return place(pieces, parts, shapes, blocks)


def gather_planes(piece, *earlier, beside=()):
    column, sent, step = piece[None], list(earlier), lax.axis_size("fsdp") // 4
    while step:
        got = swap(after(column, *sent[-1:], *(beside if len(sent) > len(earlier) else ())), "fsdp", 2 * step)
        sent.append(got)
        column = jnp.stack([column, got], 1).reshape((-1,) + piece.shape)
        step //= 2
    return column, sent[len(earlier) :]


def gather_neighbours(column, earlier):
    held = {0: [column]}
    for bit in range(lax.axis_size("rep").bit_length() - 1):
        held[1 << bit] = [swap(after(column, *earlier), "rep", 1 << bit)]
    return held, [held[k][0] for k in held if k]


def gather_members(held, beside):
    count, rows = lax.axis_size("rep"), held[0][0].shape[1] // 2
    earlier = [held[k][0] for k in held if k] + list(beside)
    for level in range(1, count.bit_length() - 1):
        sent = []
        for k in range(1, count):
            if bin(k).count("1") != level + 1:
                continue
            held[k] = []
            for half, last in ((0, k & -k), (1, 1 << (k.bit_length() - 1))):
                source = held[k ^ last]
                if len(source) == 1:
                    source = source[0][:, half * rows : (half + 1) * rows]
                else:
                    source = source[half]
                held[k].append(swap(after(source, *earlier), "rep", last))
            sent += held[k]
        earlier = sent
    arrays, parts = [], []
    for k in range(count):
        for half, array in enumerate(held[k]):
            arrays.append(array)
            parts.append((k, (0, 1) if len(held[k]) == 1 else (half,)))
    return arrays, parts, earlier


def message_pieces(shards):
    heads, expand = column_pieces((shards[2], shards[10]))
    pieces = []
    for layer in range(LAYERS):
        output, shrink = quarter(shards[5][layer]), quarter(shards[12][layer])
        half = output.shape[1] // 2
        packed = jnp.concatenate([output[:, :half], output[:, half:]], 0)
        pieces.append(jnp.concatenate([heads[layer], packed], 1))
        half = shrink.shape[0] // 2
        packed = jnp.concatenate([shrink[:half], shrink[half:]], 1)
        pieces.append(jnp.concatenate([expand[layer], packed], 0))
    return pieces


def quarter(param):
    rows = param.shape[0] // lax.axis_size("rep")
    return lax.dynamic_slice_in_dim(param, lax.axis_index("rep") * rows, rows, 0)


def gather_small(all_params, token):
    packed = after(jnp.concatenate([all_params[i] for i in SMALL], 1), token)
    whole, owner, step = packed[None], lax.axis_index("fsdp"), 1
    while step < lax.axis_size("fsdp"):
        got = swap(whole, "fsdp", step)
        whole = jnp.where(
            (owner // step) % 2 == 0,
            jnp.concatenate([whole, got], 0),
            jnp.concatenate([got, whole], 0),
        )
        step *= 2
    vectors, start = [], 0
    for i in SMALL:
        size = all_params[i].shape[1]
        vectors.append(
            jnp.moveaxis(whole[:, :, start : start + size], 0, 1).reshape(LAYERS, -1)
        )
        start += size
    return vectors


def link_orders():
    bits = list(range(lax.axis_size("rep").bit_length() - 1))
    return [bits, bits[::-1]]


def divide(blocks, shapes, bits, outs):
    for side in range(len(shapes)):
        high, later = shapes[side]
        for i in range(high):
            for j in range(later):
                base = 2 * i * later + j
                for out_ref, index in (
                    (outs[2 * side], base + bits[side] * later),
                    (outs[2 * side + 1], base + (1 - bits[side]) * later),
                ):
                    for row, column, block in blocks(side, index):
                        out_ref[
                            0, i, j, row : row + block.shape[0], column : column + block.shape[1]
                        ] = block


def block_grad_kernel(shapes, where_ref, left_ref, grad_ref, more_ref, other_ref, *refs):
    outs, held, extra = refs[:-2], refs[-2], refs[-1]
    held[...] = low(weight_dot(left_ref[...], grad_ref[...])).reshape(held.shape)
    extra[...] = low(weight_dot(more_ref[...], other_ref[...])).reshape(extra.shape)
    rows, half, tall = held.shape[2], held.shape[3] // 2, extra.shape[1] // 2

    def blocks(side, index):
        return [
            (p * rows, 0, held[p, index, :, side * half : (side + 1) * half]) for p in range(2)
        ] + [(2 * rows, 0, extra[index, side * tall : (side + 1) * tall])]

    divide(blocks, shapes, (where_ref[0], where_ref[1]), outs)


def mixed_grad_kernel(shapes, where_ref, left_ref, grad_ref, more_ref, other_ref, *refs):
    outs, held, extra = refs[:4], refs[4], refs[5]
    held[...] = low(weight_dot(left_ref[...], grad_ref[...])).reshape(held.shape)
    extra[...] = low(weight_dot(more_ref[...], other_ref[...])).reshape(extra.shape)
    rows, rest = held.shape[2], extra.shape[2] // 2
    half = (held.shape[3] + rest) // 2

    def blocks(side, index):
        if side == 0:
            return [(p * rows, 0, held[p, index, :, :half]) for p in range(2)]
        return [(p * rows, 0, held[p, index, :, half:]) for p in range(2)] + [
            (p * rows, half - rest, extra[index, :, p * rest : (p + 1) * rest]) for p in range(2)
        ]

    divide(blocks, shapes, (where_ref[0], where_ref[1]), outs)


def grad_call(kernel, arrays, widths, rows, columns, scratch, orders):
    planes, count = lax.axis_size("fsdp") // 2, lax.axis_size("rep")
    member = lax.axis_index("rep")
    shapes = tuple((count >> (order[0] + 1), 1 << order[0]) for order in orders)
    tokens = arrays[0].shape[0]
    specs = []
    for array, width in zip(arrays, widths):
        if width is None:
            specs.append(pl.BlockSpec(array.shape, lambda z, where: (0, 0)))
        else:
            specs.append(pl.BlockSpec((tokens, width), lambda z, where: (0, z)))
    out_shapes, out_specs = [], []
    for high, later in shapes:
        block = (high, later, rows, columns // len(orders))
        out_specs += [pl.BlockSpec((1,) + block, lambda z, where: (z, 0, 0, 0, 0))] * 2
        out_shapes += [jax.ShapeDtypeStruct((planes,) + block, jnp.bfloat16)] * 2
    return pl.pallas_call(
        functools.partial(kernel, shapes),
        out_shape=out_shapes,
        grid_spec=pltpu.PrefetchScalarGridSpec(
            num_scalar_prefetch=1,
            grid=(planes,),
            in_specs=specs,
            out_specs=out_specs,
            scratch_shapes=[pltpu.VMEM(size, jnp.bfloat16) for size in scratch],
        ),
        compiler_params=params(40),
        cost_estimate=estimate(5, 0),
    )(scalars(*[(member >> order[0]) & 1 for order in orders]), *arrays)


def block_grad(left, grad, more, other, orders):
    planes, count = lax.axis_size("fsdp") // 2, lax.axis_size("rep")
    widths = left.shape[1] // planes, more.shape[1] // planes
    columns = grad.shape[1]
    rows, tall = widths[0] // (2 * count), widths[1] // count
    return grad_call(
        block_grad_kernel, (left, grad, more, other), (widths[0], None, widths[1], None),
        2 * rows + tall // 2, columns,
        [(2, count, rows, columns), (count, tall, other.shape[1])], orders,
    )


def mixed_grad(left, grad, more, other, orders):
    planes, count = lax.axis_size("fsdp") // 2, lax.axis_size("rep")
    widths = left.shape[1] // planes, more.shape[1] // planes
    columns, rest = grad.shape[1], other.shape[1]
    rows = widths[1] // count
    if widths[1] % 128:
        first = low(weight_dot(left, grad)).reshape(planes, 2, count, rows, columns)
        second = low(weight_dot(more, other)).reshape(planes, count, rows, 2, rest // 2)
        total = jnp.concatenate([jnp.swapaxes(first, 1, 2), jnp.swapaxes(second, 2, 3)], 4)
        total = total.reshape(planes, count, 2 * rows, -1)
        half, member = total.shape[3] // 2, lax.axis_index("rep")
        top = count // 2
        left_part = total[..., :half].reshape(planes, top, 2, 1, 2 * rows, half)
        right_part = total[..., half:].reshape(planes, 1, 2, top, 2 * rows, half)
        sides = member % 2, member // top
        return [
            pick(part, side if kept else 1 - side, 2)
            for part, side in zip((left_part, right_part), sides)
            for kept in (True, False)
        ]
    return grad_call(
        mixed_grad_kernel, (left, grad, more, other), (widths[0], None, widths[1], None),
        2 * rows, columns + rest // 2,
        [(2, count, rows, columns), (count, rows, rest)], orders,
    )


def split_kernel(where_ref, *refs):
    count = len(refs) // 4
    for n in range(count):
        bit = where_ref[n]
        keep_in, got_ref = refs[2 * n], refs[2 * n + 1]
        keep_ref, send_ref = refs[2 * (count + n)], refs[2 * (count + n) + 1]
        keep_ref[0] = low(widen(keep_in[0, bit]) + widen(got_ref[0, bit]))
        send_ref[0] = low(widen(keep_in[0, 1 - bit]) + widen(got_ref[0, 1 - bit]))


def add_split(pairs, later, sides, rows):
    if len({pair[0].size // n for pair, n in zip(pairs, later)}) > 1:
        return [
            out
            for pair, n, side in zip(pairs, later, sides)
            for out in add_split([pair], [n], [side], rows)
        ]
    arrays, in_specs, out_specs, out_shapes = [], [], [], []
    for pair, n in zip(pairs, later):
        columns = pair[0].shape[-1]
        for array in pair:
            arrays.append(array.reshape(-1, 2, n, rows, columns))
            in_specs.append(
                pl.BlockSpec((1, 2, n, rows, columns), lambda i, where: (i, 0, 0, 0, 0))
            )
            out_specs.append(pl.BlockSpec((1, n, rows, columns), lambda i, where: (i, 0, 0, 0)))
            out_shapes.append(
                jax.ShapeDtypeStruct((arrays[-1].shape[0], n, rows, columns), jnp.bfloat16)
            )
    return pl.pallas_call(
        split_kernel,
        out_shape=out_shapes,
        grid_spec=pltpu.PrefetchScalarGridSpec(
            num_scalar_prefetch=1,
            grid=(arrays[0].shape[0],),
            in_specs=in_specs,
            out_specs=out_specs,
        ),
        compiler_params=params(24),
        cost_estimate=estimate(0, sum(array.size for array in arrays) * 3),
    )(scalars(*sides), *arrays)


def merge_kernel(where_ref, *refs):
    arrays, (keep_ref, send_ref) = refs[:-2], refs[-2:]
    half = arrays[0].shape[-1]
    for out_ref, bit in ((keep_ref, where_ref[0]), (send_ref, 1 - where_ref[0])):
        start = 0
        for n in range(0, len(arrays), 4):
            left_ref, left_got, right_ref, right_got = arrays[n : n + 4]
            rows = slice(start, start + left_ref.shape[2])
            out_ref[0, rows, :half] = low(widen(left_ref[0, bit]) + widen(left_got[0, bit]))
            out_ref[0, rows, half:] = low(widen(right_ref[0, bit]) + widen(right_got[0, bit]))
            start += left_ref.shape[2]


def add_merge(messages, side):
    half = messages[0][0].shape[-1]
    arrays, specs, total = [], [], 0
    for message in messages:
        rows = message[0].shape[-2]
        arrays += [array.reshape(-1, 2, rows, half) for array in message]
        specs += [pl.BlockSpec((1, 2, rows, half), lambda i, where: (i, 0, 0, 0))] * 4
        total += rows
    high = arrays[0].shape[0]
    given = pl.BlockSpec((1, total, 2 * half), lambda i, where: (i, 0, 0))
    shape = jax.ShapeDtypeStruct((high, total, 2 * half), jnp.bfloat16)
    return pl.pallas_call(
        merge_kernel,
        out_shape=[shape, shape],
        grid_spec=pltpu.PrefetchScalarGridSpec(
            num_scalar_prefetch=1,
            grid=(high,),
            in_specs=specs,
            out_specs=[given, given],
        ),
        compiler_params=params(24),
        cost_estimate=estimate(0, sum(array.size for array in arrays) * 3),
    )(scalars(side), *arrays)


def reduce_members(arrays):
    member, lanes = lax.axis_index("rep"), range(2)
    rows, orders = arrays[0].shape[-2], link_orders()
    bits = [sorted(order) for order in orders]
    keeps, sends = list(arrays[::2]), list(arrays[1::2])
    for n in range(len(orders[0])):
        gots = [swap(sends[i], "rep", 1 << orders[i][n]) for i in lanes]
        for i in lanes:
            bits[i].remove(orders[i][n])
        token = yield sends, gots
        gots = [after(got, token) for got in gots]
        if n + 1 < len(orders[0]):
            later = [1 << bits[i].index(orders[i][n + 1]) for i in lanes]
            sides = [(member >> orders[i][n + 1]) & 1 for i in lanes]
            outs = add_split(list(zip(keeps, gots)), later, sides, rows)
            keeps, sends = list(outs[::2]), list(outs[1::2])
    return [keeps[0], gots[0], keeps[1], gots[1]]


def reduce_planes(messages):
    plane, planes = position()[0], lax.axis_size("fsdp") // 2
    rows = sum(message[0].shape[-2] for message in messages)
    keep, send = add_merge(messages, plane % 2)
    step = 1
    while True:
        got = swap(send, "fsdp", 2 * step)
        token = yield [send], [got]
        got = after(got, token)
        step *= 2
        if step == planes:
            return low(widen(keep) + widen(got)).reshape(rows, -1)
        keep, send = add_split([(keep, got)], [1], [(plane // step) % 2], rows)


def finish_columns(total, columns):
    core = position()[1]
    rows = total.shape[0] // 2
    part = total[:, :columns].reshape(2, rows, columns)
    got = swap(pick(part, 1 - core, 0), "fsdp", 1)
    part = jnp.concatenate([pick(part, core, 0), got], 0)
    return jnp.concatenate([part, total[:, columns:]], 1)


def spread(own, low_last):
    pieces = [own]
    for k in range(1, lax.axis_size("rep")):
        last = k & -k if low_last else 1 << (k.bit_length() - 1)
        pieces.append(swap(pieces[k ^ last], "rep", last))
    return pieces


def column_out(out_ref, block, side, ref, start):
    rows = out_ref.shape[2]
    for i in range(out_ref.shape[3] // block):
        first = start if i % 2 == side else start + rows
        out_ref[0, 0, :, i * block : (i + 1) * block] = widen(
            ref[first : first + rows, (i // 2) * block : (i // 2 + 1) * block]
        )


def early_out_kernel(block, where_ref, *refs):
    expand_out, shrink_out = refs[-2:]
    for k, ref in enumerate(refs[:-4]):
        for side in range(2):

            @pl.when((pl.program_id(0) == k) & (where_ref[1] == side))
            def _():
                column_out(expand_out, block, side, ref, 0)

        @pl.when(pl.program_id(0) == k)
        def _():
            rows, columns = shrink_out.shape[2] // 2, shrink_out.shape[3]
            start = ref.shape[0] - rows
            shrink_out[0, 0, :rows] = widen(ref[start:, :columns])
            shrink_out[0, 0, rows:] = widen(ref[start:, columns:])


def late_out_kernel(block, where_ref, *refs):
    heads_out, output_out = refs[-2:]
    for k, ref in enumerate(refs[:-4]):
        for side in range(2):

            @pl.when((pl.program_id(0) == k) & (where_ref[1] == side))
            def _():
                column_out(heads_out, block, side, ref, 0)

        @pl.when(pl.program_id(0) == k)
        def _():
            rows, half = output_out.shape[2], output_out.shape[3] // 2
            start = ref.shape[1] - half
            output_out[0, 0, :, :half] = widen(ref[:rows, start:])
            output_out[0, 0, :, half:] = widen(ref[rows:, start:])


def write_out(kernel, layer, pieces, sizes, earlier):
    plane, core, member = position()
    count = len(pieces)
    shapes = [(LAYERS, count) + size for size in sizes]
    if earlier is None:
        earlier = [jnp.zeros((8, 128), jnp.float32)] * len(sizes)
        aliases = {}
    else:
        earlier = [array.reshape(shape) for array, shape in zip(earlier, shapes)]
        aliases = {1 + count + i: i for i in range(len(sizes))}
    return pl.pallas_call(
        kernel,
        out_shape=[jax.ShapeDtypeStruct(shape, jnp.float32) for shape in shapes],
        grid_spec=pltpu.PrefetchScalarGridSpec(
            num_scalar_prefetch=1,
            grid=(count,),
            in_specs=[pl.BlockSpec(piece.shape, lambda k, where: (0, 0)) for piece in pieces]
            + [pl.BlockSpec(memory_space=pl.ANY)] * len(sizes),
            out_specs=[
                pl.BlockSpec((1, 1) + size, lambda k, where: (layer, k ^ where[0], 0, 0))
                for size in sizes
            ],
        ),
        input_output_aliases=aliases,
        compiler_params=params(24),
        cost_estimate=estimate(0, count * pieces[0].size * 6),
    )(scalars(member, core), *pieces, *earlier)


def reduce_small(grads, earlier):
    owners, count = lax.axis_size("fsdp"), lax.axis_size("rep")
    total = jnp.concatenate([g.reshape(LAYERS, owners, -1) for g in grads], 2)
    total = after(total, *earlier)
    owner = lax.axis_index("fsdp")
    step = owners // 2
    while step:
        total = total.reshape(LAYERS, 2, step, -1)
        mine = (owner // step) % 2
        total = pick(total, mine, 1) + swap(pick(total, 1 - mine, 1), "fsdp", step)
        step //= 2
    step = 1
    while step < count:
        total = total + swap(total, "rep", step)
        step *= 2
    total = total.reshape(LAYERS, -1)
    outs, start = [], 0
    for g in grads:
        size = g.shape[1] // owners
        outs.append(total[:, start : start + size])
        start += size
    return outs


def other_half(rows):
    return swap(rows, "fsdp", lax.axis_size("fsdp") // 2)


def image_side():
    return lax.axis_index("fsdp") // (lax.axis_size("fsdp") // 2)


def regroup(blocks):
    side = image_side()
    return pick(blocks, side, 0), other_half(pick(blocks, 1 - side, 0))


def ungroup(rows, got):
    own, got = rows[: rows.shape[0] // 2], got.astype(rows.dtype)
    return jnp.where(image_side() == 0, jnp.stack([own, got]), jnp.stack([got, own]))


def chips_per_image():
    return lax.axis_size("fsdp") // 4


def share_rows(local_kv):
    shared = [local_kv]
    for k in range(1, chips_per_image()):
        low_bit = k & -k
        shared.append(swap(shared[k ^ low_bit], "fsdp", 2 * low_bit))
    return shared


def collect_rows(own, others):
    chips = chips_per_image()
    if chips == 2:
        got = swap(others, "fsdp", 2)
        return low(widen(own) + widen(got)), got
    total = jnp.concatenate([own, others], 1)
    while chips > 1:
        rows = total.shape[1] // 2
        got = swap(total[:, rows:], "fsdp", chips)
        total = low(widen(total[:, :rows]) + widen(got))
        chips //= 2
    return total, got


def both_cores(rows):
    return jnp.concatenate([rows, swap(rows, "fsdp", 1)], 0)


def one_head(tensor, head):
    half = tensor.shape[1] // 2
    lane = lax.broadcasted_iota(jnp.int32, tensor.shape, 1)
    keep = lane < half if head == 0 else lane >= half
    return jnp.where(keep, tensor, jnp.zeros_like(tensor))


def join(refs, held):
    start = 0
    for ref in refs:
        held[start : start + ref.shape[0], :] = ref[...]
        start += ref.shape[0]
    return held[...]


def attend_kernel(factor, parts, query_ref, *refs):
    out_ref, log_ref, held_keys, held_values = refs[2 * parts :]
    keys, values = join(refs[:parts], held_keys), join(refs[parts : 2 * parts], held_values)
    results, logs = [], []
    for head in range(2):
        scores = input_dot(one_head(query_ref[...], head), keys)
        largest = jnp.max(scores, -1, keepdims=True)
        weights = jnp.exp2((scores - largest) * factor)
        total = jnp.sum(weights, -1, keepdims=True)
        results.append(forward_dot(low(weights), values) / total)
        logs.append(largest * factor + jnp.log2(total))
    out_ref[...] = low(one_head(results[0], 0) + one_head(results[1], 1))
    shape = log_ref.shape
    log_ref[...] = one_head(jnp.broadcast_to(logs[0], shape), 0) + one_head(
        jnp.broadcast_to(logs[1], shape), 1
    )


def pair_block(rows, start):
    return pl.BlockSpec((rows, 128), lambda i: (0, start + i))


def kv_parts(projected, others):
    pairs = projected.shape[1] // 384
    if projected.shape[0] % 16:
        others = [jnp.concatenate([projected[:, 128 * pairs :]] + others, 0)]
        parts = []
    else:
        parts = [(projected, pairs, 2 * pairs)]
    return parts + [(other, 0, pairs) for other in others]


def kv_specs(parts, first=0):
    keys = [pair_block(array.shape[0], first + start) for array, start, unused in parts]
    values = [pair_block(array.shape[0], first + start) for array, unused, start in parts]
    rows = sum(array.shape[0] for array, unused, more in parts)
    held = [pltpu.VMEM((rows, 128), jnp.bfloat16)] * 2
    return keys + values, [array for array, unused, more in parts] * 2, held


def attend(projected, others, head_size):
    tokens, width = projected.shape[0], projected.shape[1] // 3
    pairs = width // 128
    parts = kv_parts(projected, others)
    specs, arrays, held = kv_specs(parts)
    factor = head_size ** (-0.5) * math.log2(math.e)
    return pl.pallas_call(
        functools.partial(attend_kernel, factor, len(parts)),
        out_shape=[
            jax.ShapeDtypeStruct((tokens, width), jnp.bfloat16),
            jax.ShapeDtypeStruct((tokens, width), jnp.float32),
        ],
        grid=(pairs,),
        in_specs=[pair_block(tokens, 0)] + specs,
        out_specs=[pair_block(tokens, 0), pair_block(tokens, 0)],
        scratch_shapes=held,
        compiler_params=params(56),
        cost_estimate=estimate(18, 0),
    )(projected, *arrays)


def attend_back_kernel(factor, scale, parts, query_ref, *refs):
    log_ref, grad_ref, dq_ref, own_ref, others_ref, held_keys, held_values = refs[2 * parts :]
    keys, values = join(refs[:parts], held_keys), join(refs[parts : 2 * parts], held_values)
    d_query, d_key, d_value = [], 0.0, 0.0
    for head in range(2):
        query = one_head(query_ref[...], head)
        grad = one_head(grad_ref[...], head)
        half = query.shape[1] // 2
        log_total = log_ref[:, head * half : head * half + 1]
        probs = jnp.exp2(input_dot(query, keys) * factor - log_total)
        products = probs * input_dot(grad, values)
        d_scores = low(products - probs * jnp.sum(products, -1, keepdims=True))
        d_query.append(forward_dot(d_scores, keys))
        d_key = d_key + weight_dot(d_scores, query)
        d_value = d_value + weight_dot(low(probs), grad)
    dq_ref[...] = low((one_head(d_query[0], 0) + one_head(d_query[1], 1)) * scale)
    rows = own_ref.shape[1]
    for i, total in enumerate((low(d_key * scale), low(d_value))):
        own_ref[i] = total[:rows]
        others_ref[i] = total[rows:]


def attend_back(projected, others, log_total, d_attended, head_size, first, pairs):
    tokens, width = d_attended.shape[0], 128 * pairs
    parts = kv_parts(projected, others)
    specs, arrays, held = kv_specs(parts, first)
    rows = held[0].shape[0]
    scale = head_size ** (-0.5)
    own, taken = pair_block(tokens, 0), pair_block(tokens, first)
    return pl.pallas_call(
        functools.partial(attend_back_kernel, scale * math.log2(math.e), scale, len(parts)),
        out_shape=[
            jax.ShapeDtypeStruct((tokens, width), jnp.bfloat16),
            jax.ShapeDtypeStruct((2, tokens, width), jnp.bfloat16),
            jax.ShapeDtypeStruct((2, rows - tokens, width), jnp.bfloat16),
        ],
        grid=(pairs,),
        in_specs=[taken] + specs + [taken, taken],
        out_specs=[
            own,
            pl.BlockSpec((2, tokens, 128), lambda i: (0, 0, i)),
            pl.BlockSpec((2, rows - tokens, 128), lambda i: (0, 0, i)),
        ],
        scratch_shapes=held,
        compiler_params=params(60),
        cost_estimate=estimate(8 * pairs, 0),
    )(projected, *arrays, log_total, d_attended)


def add_tile(part, own_ref, other_ref, total_ref):
    @pl.when(pl.program_id(0) == 0)
    def _():
        total_ref[...] = part

    @pl.when(pl.program_id(0) > 0)
    def _():
        total_ref[...] += part

    @pl.when(pl.program_id(0) == pl.num_programs(0) - 1)
    def _():
        half = own_ref.shape[0]
        own_ref[...] = total_ref[:half]
        other_ref[...] = low(total_ref[half:])


def expand_kernel(
    rows_ref, expand_ref, bias_ref, shrink_ref, active_ref, slope_ref, own_ref, other_ref, total_ref
):
    hidden = forward_dot(rows_ref[...], expand_ref[...]) + bias_ref[...]
    normal = 0.5 + 0.5 * lax.erf(hidden * math.sqrt(0.5))
    density = jnp.exp2(hidden * hidden * (-0.5 * math.log2(math.e)))
    slope_ref[...] = low(normal + hidden * density * (1.0 / math.sqrt(2.0 * math.pi)))
    active = low(hidden * normal)
    active_ref[...] = active
    add_tile(forward_dot(active, shrink_ref[...]), own_ref, other_ref, total_ref)


def feed_forward(rows_in, expand, expand_bias, shrink):
    tokens, width = rows_in.shape
    units = expand.shape[1]
    tile = 512
    whole = pl.BlockSpec((tokens, width), lambda i: (0, 0))
    half = pl.BlockSpec((tokens // 2, width), lambda i: (0, 0))
    part = pl.BlockSpec((tokens, tile), lambda i: (0, i))
    return pl.pallas_call(
        expand_kernel,
        out_shape=[
            jax.ShapeDtypeStruct((tokens, units), jnp.bfloat16),
            jax.ShapeDtypeStruct((tokens, units), jnp.bfloat16),
            jax.ShapeDtypeStruct((tokens // 2, width), jnp.float32),
            jax.ShapeDtypeStruct((tokens // 2, width), jnp.bfloat16),
        ],
        grid=(units // tile,),
        in_specs=[
            whole,
            pl.BlockSpec((width, tile), lambda i: (0, i)),
            pl.BlockSpec((1, tile), lambda i: (0, i)),
            pl.BlockSpec((tile, width), lambda i: (i, 0)),
        ],
        out_specs=[part, part, half, half],
        scratch_shapes=[pltpu.VMEM((tokens, width), jnp.float32)],
        compiler_params=params(32),
        cost_estimate=estimate(14, 0),
    )(rows_in, expand, expand_bias[None], shrink)


def shrink_kernel(
    grad_ref, shrink_ref, slope_ref, expand_ref, hidden_ref, bias_ref, own_ref, other_ref, total_ref
):
    d_hidden = low(input_dot(grad_ref[...], shrink_ref[...]) * widen(slope_ref[...]))
    hidden_ref[...] = d_hidden
    bias_ref[...] = jnp.sum(widen(d_hidden), 0, keepdims=True)
    add_tile(input_dot(d_hidden, expand_ref[...]), own_ref, other_ref, total_ref)


def feed_back(d_mlp, shrink, slope, expand):
    tokens, width = d_mlp.shape
    units = expand.shape[1]
    tile = 512
    whole = pl.BlockSpec((tokens, width), lambda i: (0, 0))
    half = pl.BlockSpec((tokens // 2, width), lambda i: (0, 0))
    part = pl.BlockSpec((tokens, tile), lambda i: (0, i))
    return pl.pallas_call(
        shrink_kernel,
        out_shape=[
            jax.ShapeDtypeStruct((tokens, units), jnp.bfloat16),
            jax.ShapeDtypeStruct((1, units), jnp.float32),
            jax.ShapeDtypeStruct((tokens // 2, width), jnp.float32),
            jax.ShapeDtypeStruct((tokens // 2, width), jnp.bfloat16),
        ],
        grid=(units // tile,),
        in_specs=[
            whole,
            pl.BlockSpec((tile, width), lambda i: (i, 0)),
            part,
            pl.BlockSpec((width, tile), lambda i: (0, i)),
        ],
        out_specs=[part, pl.BlockSpec((1, tile), lambda i: (0, i)), half, half],
        scratch_shapes=[pltpu.VMEM((tokens, width), jnp.float32)],
        compiler_params=params(32),
        cost_estimate=estimate(9, 0),
    )(d_mlp, shrink, slope, expand)


def core_half(vector):
    core = position()[1]
    return pick(widen(vector).reshape(lax.axis_size("fsdp") // 2, 2, -1), core, 1).reshape(-1)


def core_fill(half):
    parts = half.reshape(lax.axis_size("fsdp") // 2, -1)
    return by_core(parts, jnp.zeros_like(parts), 1).reshape(-1)


def normed_rows(tok_rows, gathered):
    return both_cores(low(layer_norm(tok_rows, widen(gathered[0]), widen(gathered[1]))))


def project(normed, gathered, token):
    heads_weight, query_bias, value_bias = gathered[2], gathered[3], gathered[4]
    width = normed.shape[1]
    bias_row = jnp.concatenate(
        [core_half(query_bias), jnp.zeros((width // 2,), jnp.float32), core_half(value_bias)]
    )
    projected = low(forward_dot(normed, heads_weight) + bias_row)
    return projected, share_rows(after(projected[:, width // 2 :], token))[1:]


def forward_layer(tok_rows, normed, projected, others, gathered, beside, neighbours, planes):
    (
        attn_norm_gain,
        attn_norm_bias,
        heads_weight,
        query_bias,
        value_bias,
        output_weight,
        output_bias,
        attn_layerscale,
        mlp_norm_gain,
        mlp_norm_bias,
        expand_weight,
        expand_bias,
        shrink_weight,
        shrink_bias,
        mlp_layerscale,
    ) = gathered
    tokens, width = tok_rows.shape
    attended, log_total = attend(projected, others, width // HEADS)
    attended = after(attended, *beside)
    got = swap(low(forward_dot(attended[tokens:], output_weight)), "fsdp", 1)
    branch = forward_dot(attended[:tokens], output_weight) + widen(got) + widen(output_bias)
    middle = tok_rows + widen(attn_layerscale) * branch
    normed_two = low(layer_norm(middle, widen(mlp_norm_gain), widen(mlp_norm_bias)))
    normed_two = both_cores(after(normed_two, *planes[:1]))
    activated, slope, own_sum, other_sum = feed_forward(
        normed_two, expand_weight, core_half(expand_bias), shrink_weight
    )
    other_sum = after(other_sum, *neighbours, *planes[1:])
    mlp_out = own_sum + widen(swap(other_sum, "fsdp", 1)) + widen(shrink_bias)
    result = middle + widen(mlp_layerscale) * mlp_out
    saved = (
        tok_rows,
        normed,
        projected,
        others,
        log_total,
        attended,
        branch,
        middle,
        normed_two,
        slope,
        activated,
        mlp_out,
    )
    return (result, saved)


class Later:
    def __init__(self):
        self.running, self.done, self.sends, self.gots = {}, {}, {}, {}

    def begin(self, name, kernel, arrays):
        self.running[name] = reduce_members(kernel(*arrays, link_orders()))
        self.step(name, None)

    def join(self, name, parts, token):
        for part in parts:
            while part in self.running:
                self.step(part, token)
        self.running[name] = reduce_planes([self.done[part] for part in parts])
        self.step(name, None)

    def step(self, name, token):
        try:
            self.sends[name], self.gots[name] = self.running[name].send(token)
        except StopIteration as end:
            self.done[name] = end.value
            self.sends[name] = self.gots[name] = []
            del self.running[name]

    def sent(self, value, *names):
        return after(value, *[array for name in names for array in self.sends[name]])

    def came(self, value, *names):
        return after(value, *[array for name in names for array in self.gots[name]])


def backward_layer(d_result, saved, gathered, later, new, old, activation_got):
    (
        attn_norm_gain,
        attn_norm_bias,
        heads_weight,
        query_bias,
        value_bias,
        output_weight,
        output_bias,
        attn_layerscale,
        mlp_norm_gain,
        mlp_norm_bias,
        expand_weight,
        expand_bias,
        shrink_weight,
        shrink_bias,
        mlp_layerscale,
    ) = gathered
    (
        tok_rows,
        normed,
        projected,
        others,
        log_total,
        attended,
        branch,
        middle,
        normed_two,
        slope,
        activated,
        mlp_out,
    ) = saved
    tokens, width = tok_rows.shape
    d_mlp = low(d_result * widen(mlp_layerscale))
    d_mlp_both = both_cores(d_mlp)
    g_mlp_scale = jnp.sum(d_result * mlp_out, 0)
    g_shrink_bias = column_sum(d_mlp)
    d_hidden, g_expand_bias, own_sum, other_sum = feed_back(
        d_mlp_both, shrink_weight, slope, expand_weight
    )
    block, mixed, block_planes, mixed_planes = new
    if old:
        other_sum = later.came(other_sum, old[0])
        later.join(old[2], [old[0]], other_sum)
        d_hidden = later.sent(d_hidden, old[2])
    got = swap(other_sum, "fsdp", 1)
    later.begin(block, block_grad, (normed_two, d_hidden, activated, d_mlp_both))
    own_sum = later.sent(own_sum, block)
    if not old:
        own_sum = after(own_sum, activation_got)
    if old:
        own_sum = later.came(own_sum, old[1])
        later.step(old[1], own_sum)
        own_sum = later.sent(own_sum, old[1])
    d_middle_norm, g_mlp_gain, g_mlp_shift = norm_back(
        middle, widen(mlp_norm_gain), widen(mlp_norm_bias), own_sum + widen(got)
    )
    d_middle = d_result + d_middle_norm
    d_branch = low(d_middle * widen(attn_layerscale))
    d_branch_both = both_cores(d_branch)
    g_attn_scale = jnp.sum(d_middle * branch, 0)
    g_output_bias = column_sum(d_branch)
    d_attended = low(input_dot(d_branch_both, output_weight))
    pairs = d_attended.shape[1] // 128

    def back(first):
        return attend_back(
            projected, others, log_total, d_attended, width // HEADS, first, pairs // 2
        )

    first_query, d_own, d_others = back(0)
    first_kv, first_got = collect_rows(d_own, d_others)
    if old:
        d_attended = later.came(d_attended, old[2])
        later.step(old[2], first_query)
        d_attended = later.sent(d_attended, old[2])
    second_query, d_own, d_others = back(pairs // 2)
    d_others = after(d_others, first_got)
    second_kv, second_got = collect_rows(d_own, d_others)
    second_query = later.came(second_query, block)
    later.step(block, second_query)
    second_query = later.sent(second_query, block)
    if old:
        second_query = later.came(second_query, old[1])
        later.join(old[3], [old[1]], second_query)
        second_query = later.sent(second_query, old[3])
    d_query = jnp.concatenate([first_query, second_query], 1)
    d_key = jnp.concatenate([first_kv[0], second_kv[0]], 1)
    d_value = jnp.concatenate([first_kv[1], second_kv[1]], 1)
    d_projected = jnp.concatenate([d_query, d_key, d_value], 1)
    g_query_bias = column_sum(d_query)
    g_value_bias = column_sum(d_value)
    got = swap(low(input_dot(d_projected[tokens:], heads_weight)), "fsdp", 1)
    later.begin(mixed, mixed_grad, (normed, d_projected, attended, d_branch_both))
    d_projected = later.sent(d_projected, mixed)
    if old:
        later.join(block_planes, [block], d_projected)
        d_projected = later.sent(d_projected, block_planes)
    d_normed = input_dot(d_projected[:tokens], heads_weight) + widen(got)
    d_rows_norm, g_attn_gain, g_attn_shift = norm_back(
        tok_rows, widen(attn_norm_gain), widen(attn_norm_bias), d_normed
    )
    d_rows = d_middle + d_rows_norm
    small_grads = (
        g_attn_gain,
        g_attn_shift,
        core_fill(g_query_bias),
        core_fill(g_value_bias),
        g_output_bias,
        g_attn_scale,
        g_mlp_gain,
        g_mlp_shift,
        core_fill(g_expand_bias),
        g_shrink_bias,
        g_mlp_scale,
    )
    return (d_rows, small_grads)


def local(images, cotangent, *all_params):
    owners, count = lax.axis_size("fsdp"), lax.axis_size("rep")
    pieces = message_pieces(all_params)
    column, planes = gather_planes(pieces[0])
    own, got = regroup(after(images, planes[0]))
    tok_rows = widen(jnp.concatenate([own, got], 0))
    column = after(column, got)
    next_column, next_planes = gather_planes(pieces[1], got)
    small = gather_small(all_params, got)
    held, neighbours = gather_neighbours(column, [])
    saved_layers, fetched = [], []
    for layer in range(LAYERS):
        gathered = [None] * len(all_params)
        for i, vector in zip(SMALL, small):
            gathered[i] = vector[layer]
        normed = normed_rows(tok_rows, gathered)
        arrays, parts, earlier = gather_members(held, [])
        arrays[0] = after(arrays[0], next_planes[-1])
        gathered[2], gathered[5] = place_first(
            arrays, parts, count, all_params[2].shape[2] // 2
        )
        projected, others = project(normed, gathered, next_planes[-1])
        held, neighbours = gather_neighbours(next_column, earlier)
        if layer + 1 < LAYERS:
            column, planes = gather_planes(pieces[2 * layer + 2], others[-1])
            beside = planes[:1]
        else:
            own, got = regroup(after(cotangent, others[-1]))
            d_rows = widen(jnp.concatenate([own, got], 0))
            beside, planes, neighbours, next_planes = [got], [], [], []
        arrays, parts, earlier = gather_members(held, [])
        arrays[0] = after(arrays[0], *planes[-1:])
        if layer + 1 < LAYERS:
            next_column, next_planes = gather_planes(pieces[2 * layer + 3], planes[-1])
            held, neighbours = gather_neighbours(column, earlier)
        gathered[10], gathered[12] = place_second(arrays, parts, count)
        fetched.append(tuple(gathered))
        tok_rows, saved = forward_layer(
            tok_rows, normed, projected, others, gathered, beside, neighbours, next_planes
        )
        saved_layers.append(saved)
    activation_rows = low(tok_rows)
    small_grads = [None] * LAYERS
    outs = {}

    def size(i):
        return (all_params[i].shape[1] // count, all_params[i].shape[2])

    def block_piece(later, layer):
        total = later.done[layer, 2]
        half = total.shape[0] // 2
        return jnp.concatenate([finish_columns(total[:half], total.shape[1]), total[half:]], 0)

    def mixed_piece(later, layer):
        return finish_columns(later.done[layer, 3], size(2)[1] // 2)

    def write_block(layer, pieces):
        outs["block"] = write_out(
            functools.partial(early_out_kernel, size(10)[1] // owners),
            layer, pieces, [size(10), size(12)], outs.get("block"),
        )

    def write_mixed(layer, pieces):
        outs["mixed"] = write_out(
            functools.partial(late_out_kernel, size(2)[1] // 3 // owners),
            layer, pieces, [size(2), size(5)], outs.get("mixed"),
        )

    later = Later()
    for layer in reversed(range(LAYERS)):
        new = [(layer, n) for n in range(4)]
        old = [(layer + 1, n) for n in range(4)] if layer + 1 < LAYERS else None
        if not old:
            activation_got = other_half(activation_rows[activation_rows.shape[0] // 2 :])
        d_rows, small_grads[layer] = backward_layer(
            d_rows, saved_layers[layer], fetched[layer], later, new, old, activation_got
        )
    activations = ungroup(activation_rows, activation_got)
    image_got = other_half(low(d_rows[d_rows.shape[0] // 2 :]))
    d_images = ungroup(d_rows, image_got)
    for name in (old[2], old[3]):
        while name in later.running:
            later.step(name, d_rows)
    first = block_piece(later, layer + 1)
    rows = first.shape[0]
    first = after(jnp.concatenate([first, mixed_piece(later, layer + 1)], 0), d_rows)
    later.step(new[1], d_rows)
    pieces = spread(later.sent(first, new[1]), True)
    write_block(layer + 1, [piece[:rows] for piece in pieces])
    write_mixed(layer + 1, [piece[rows:] for piece in pieces])
    last_gots = later.gots[new[1]] + [image_got]
    later.join(new[3], [new[1]], d_rows)
    while new[3] in later.running:
        later.step(new[3], d_rows)
    while new[2] in later.running:
        later.step(new[2], d_rows)
    write_block(layer, spread(block_piece(later, layer), False))
    write_mixed(layer, spread(mixed_piece(later, layer), False))
    stacked = [None] * len(all_params)
    for i, out in zip((10, 12, 2, 5), list(outs["block"]) + list(outs["mixed"])):
        stacked[i] = out.reshape(all_params[i].shape)
    reduced = reduce_small(
        [jnp.stack([grads[n] for grads in small_grads]) for n in range(len(SMALL))], last_gots
    )
    for i, vector in zip(SMALL, reduced):
        stacked[i] = vector
    return (activations, d_images) + tuple(stacked)


def solution(mesh):
    in_specs = (
        P("rep", "fsdp", None),
        P("rep", "fsdp", None),
        P(None, "fsdp"),
        P(None, "fsdp"),
        P(None, "fsdp", None),
        P(None, "fsdp"),
        P(None, "fsdp"),
        P(None, "fsdp", None),
        P(None, "fsdp"),
        P(None, "fsdp"),
        P(None, "fsdp"),
        P(None, "fsdp"),
        P(None, "fsdp", None),
        P(None, "fsdp"),
        P(None, "fsdp", None),
        P(None, "fsdp"),
        P(None, "fsdp"),
    )
    out_specs = (
        P("rep", "fsdp", None),
        P("rep", "fsdp", None),
        P(None, "fsdp"),
        P(None, "fsdp"),
        P(None, "fsdp", None),
        P(None, "fsdp"),
        P(None, "fsdp"),
        P(None, "fsdp", None),
        P(None, "fsdp"),
        P(None, "fsdp"),
        P(None, "fsdp"),
        P(None, "fsdp"),
        P(None, "fsdp", None),
        P(None, "fsdp"),
        P(None, "fsdp", None),
        P(None, "fsdp"),
        P(None, "fsdp"),
    )
    return jax.shard_map(local, mesh=mesh, in_specs=in_specs, out_specs=out_specs, check_vma=False)
```

```python
import functools
import math

import jax
import jax.numpy as jnp
from jax import lax
from jax.experimental import pallas as pl
from jax.experimental.pallas import tpu as pltpu
from jax.sharding import PartitionSpec as P

HEADS = 16
LAYERS = 2
SMALL = (0, 1, 3, 4, 6, 7, 8, 9, 11, 13, 14)
MIB = 1 << 20

epsilon = 1e-06


def layer_norm(values_in, norm_gain, norm_shift):
    centre = jnp.mean(values_in, -1, keepdims=True)
    centered = values_in - centre
    spread = jnp.mean(centered * centered, -1, keepdims=True)
    return centered * lax.rsqrt(spread + epsilon) * norm_gain + norm_shift


def norm_back(values_in, norm_gain, norm_shift, grad):
    unused, pullback = jax.vjp(layer_norm, values_in, norm_gain, norm_shift)
    return pullback(grad)


def widen(tensor):
    return tensor.astype(jnp.float32)


def low(tensor):
    return tensor.astype(jnp.bfloat16)


def forward_dot(left, weight):
    return jnp.dot(left, weight, preferred_element_type=jnp.float32)


def weight_dot(left, grad):
    return lax.dot_general(left, grad, (((0,), (0,)), ((), ())), preferred_element_type=jnp.float32)


def input_dot(grad, weight):
    return lax.dot_general(
        grad, weight, (((1,), (1,)), ((), ())), preferred_element_type=jnp.float32
    )


def column_sum(grad):
    return jnp.sum(widen(grad), 0)


def pick(tensor, index, axis):
    return lax.dynamic_index_in_dim(tensor, index, axis, keepdims=False)


def swap(tensor, axis, offset):
    count = lax.axis_size(axis)
    return lax.ppermute(tensor, axis, [(i, i ^ offset) for i in range(count)])


def position():
    owner = lax.axis_index("fsdp")
    return owner // 2, owner % 2, lax.axis_index("rep")


def scalars(*values):
    return jnp.stack(values).astype(jnp.int32)


def estimate(microseconds, moved):
    return pl.CostEstimate(flops=1000, bytes_accessed=1000, transcendentals=0)


def params(mib):
    return pltpu.CompilerParams(vmem_limit_bytes=mib * MIB)


def after(tensor, *earlier):
    return lax.optimization_barrier((tensor,) + earlier)[0]


def by_core(own, got, axis):
    core = position()[1]
    return jnp.where(
        core == 0, jnp.stack([own, got], axis), jnp.stack([got, own], axis)
    )


def columns_kernel(blocks, where_ref, *refs):
    ins, (own_ref, other_ref) = refs[:-2], refs[-2:]
    for side in range(2):

        @pl.when(where_ref[1] == side)
        def _():
            for out_ref, parity in ((own_ref, side), (other_ref, 1 - side)):
                start = 0
                for ref, block in zip(ins, blocks):
                    for i in range(parity, ref.shape[2] // block, 2):
                        out_ref[0, :, start : start + block] = ref[0, :, i * block : (i + 1) * block]
                        start += block


def column_pieces(shards):
    plane, core, member = position()
    owners, count = lax.axis_size("fsdp"), lax.axis_size("rep")
    rows = shards[0].shape[1] // count
    blocks = tuple(
        size // owners for size in (shards[0].shape[2] // 3, shards[1].shape[2])
    )
    columns = sum(shard.shape[2] for shard in shards) // 2
    shape = jax.ShapeDtypeStruct((LAYERS, rows, columns), jnp.bfloat16)
    out = pl.BlockSpec((1, rows, columns), lambda layer, where: (layer, 0, 0))
    own, other = pl.pallas_call(
        functools.partial(columns_kernel, blocks),
        out_shape=[shape, shape],
        grid_spec=pltpu.PrefetchScalarGridSpec(
            num_scalar_prefetch=1,
            grid=(LAYERS,),
            in_specs=[
                pl.BlockSpec((1, rows, shard.shape[2]), lambda layer, where: (layer, where[0], 0))
                for shard in shards
            ],
            out_specs=[out, out],
        ),
        cost_estimate=estimate(0, 4 * LAYERS * rows * columns * 2),
    )(scalars(member, core), *shards)
    both = by_core(own, swap(other, "fsdp", 1), 1)
    split = shards[0].shape[2] // 2
    both = both.reshape(LAYERS, 2 * rows, columns)
    return both[..., :split], both[..., split:]


def place_kernel(half_rows, blocks, parts, where_ref, *refs):
    count = len(parts)
    pieces, outs, (in_sems, out_sems) = refs[:count], refs[count : -count - 2], refs[-2:]
    held = refs[-count - 2 : -2]
    plane, member = where_ref[0], where_ref[1]
    arrivals = []
    for i in range(count):
        arrivals.append(pltpu.make_async_copy(pieces[i], held[i], in_sems.at[i]))
        arrivals[-1].start()
    copies = []
    for i, (k, halves) in enumerate(parts):
        arrivals[i].wait()
        for j in range(pieces[0].shape[0]):
            for b, (row, rows, column, columns, put) in enumerate(blocks):
                if row // half_rows not in halves:
                    continue
                first = row - halves[0] * half_rows
                copy = pltpu.make_async_copy(
                    held[i].at[j, first : first + rows, column : column + columns],
                    put(outs, j ^ plane, k ^ member),
                    out_sems.at[b, i, j],
                )
                copy.start()
                copies.append(copy)
    for copy in copies:
        copy.wait()


def place(pieces, parts, shapes, blocks):
    plane, core, member = position()
    planes = pieces[0].shape[0]
    outs = pl.pallas_call(
        functools.partial(place_kernel, pieces[0].shape[1] // 2, blocks, parts),
        out_shape=[jax.ShapeDtypeStruct(shape, pieces[0].dtype) for shape in shapes],
        in_specs=[pl.BlockSpec(memory_space=pltpu.SMEM)]
        + [pl.BlockSpec(memory_space=pl.ANY)] * len(pieces),
        out_specs=[pl.BlockSpec(memory_space=pl.ANY)] * len(shapes),
        scratch_shapes=[pltpu.VMEM(piece.shape, piece.dtype) for piece in pieces]
        + [
            pltpu.SemaphoreType.DMA((len(pieces),)),
            pltpu.SemaphoreType.DMA((len(blocks), len(pieces), planes)),
        ],
        compiler_params=params(20),
        cost_estimate=estimate(0, 4 * sum(piece.size for piece in pieces)),
    )(scalars(plane, member), *pieces)
    return [out.reshape(-1, out.shape[-1]) for out in outs]


def put_pair(side):
    return lambda outs, plane, member: outs[0].at[plane, side, member]


def place_first(pieces, parts, count, split):
    planes, rows, columns = pieces[0].shape
    half, rest = rows // 2, columns - split

    def put(side):
        return lambda outs, plane, member: outs[1].at[
            plane, member, :, side * rest : (side + 1) * rest
        ]

    shapes = [(planes, 2, count, half, split), (planes, count, half, 2 * rest)]
    blocks = [(side * half, half, 0, split, put_pair(side)) for side in range(2)]
    blocks += [(side * half, half, split, rest, put(side)) for side in range(2)]
    return place(pieces, parts, shapes, blocks)


def place_second(pieces, parts, count):
    planes, rows, columns = pieces[0].shape
    half, fine, width = rows // 2, rows // 4, columns // 2

    def put(side):
        return lambda outs, plane, member: outs[1].at[plane, member, side]

    shapes = [(planes, 2, count, fine, columns), (planes, count, 2, half, width)]
    blocks = [(side * fine, fine, 0, columns, put_pair(side)) for side in range(2)]
    blocks += [(half, half, side * width, width, put(side)) for side in range(2)]
    return place(pieces, parts, shapes, blocks)


def gather_planes(piece, *earlier, beside=()):
    column, sent, step = piece[None], list(earlier), lax.axis_size("fsdp") // 4
    while step:
        got = swap(after(column, *sent[-1:], *(beside if len(sent) > len(earlier) else ())), "fsdp", 2 * step)
        sent.append(got)
        column = jnp.stack([column, got], 1).reshape((-1,) + piece.shape)
        step //= 2
    return column, sent[len(earlier) :]


def gather_neighbours(column, earlier):
    held = {0: [column]}
    for bit in range(lax.axis_size("rep").bit_length() - 1):
        held[1 << bit] = [swap(after(column, *earlier), "rep", 1 << bit)]
    return held, [held[k][0] for k in held if k]


def gather_members(held, beside):
    count, rows = lax.axis_size("rep"), held[0][0].shape[1] // 2
    earlier = [held[k][0] for k in held if k] + list(beside)
    for level in range(1, count.bit_length() - 1):
        sent = []
        for k in range(1, count):
            if bin(k).count("1") != level + 1:
                continue
            held[k] = []
            for half, last in ((0, k & -k), (1, 1 << (k.bit_length() - 1))):
                source = held[k ^ last]
                if len(source) == 1:
                    source = source[0][:, half * rows : (half + 1) * rows]
                else:
                    source = source[half]
                held[k].append(swap(after(source, *earlier), "rep", last))
            sent += held[k]
        earlier = sent
    arrays, parts = [], []
    for k in range(count):
        for half, array in enumerate(held[k]):
            arrays.append(array)
            parts.append((k, (0, 1) if len(held[k]) == 1 else (half,)))
    return arrays, parts, earlier


def message_pieces(shards):
    heads, expand = column_pieces((shards[2], shards[10]))
    pieces = []
    for layer in range(LAYERS):
        output, shrink = quarter(shards[5][layer]), quarter(shards[12][layer])
        half = output.shape[1] // 2
        packed = jnp.concatenate([output[:, :half], output[:, half:]], 0)
        pieces.append(jnp.concatenate([heads[layer], packed], 1))
        half = shrink.shape[0] // 2
        packed = jnp.concatenate([shrink[:half], shrink[half:]], 1)
        pieces.append(jnp.concatenate([expand[layer], packed], 0))
    return pieces


def quarter(param):
    rows = param.shape[0] // lax.axis_size("rep")
    return lax.dynamic_slice_in_dim(param, lax.axis_index("rep") * rows, rows, 0)


def gather_small(all_params, token):
    packed = after(jnp.concatenate([all_params[i] for i in SMALL], 1), token)
    whole, owner, step = packed[None], lax.axis_index("fsdp"), 1
    while step < lax.axis_size("fsdp"):
        got = swap(whole, "fsdp", step)
        whole = jnp.where(
            (owner // step) % 2 == 0,
            jnp.concatenate([whole, got], 0),
            jnp.concatenate([got, whole], 0),
        )
        step *= 2
    vectors, start = [], 0
    for i in SMALL:
        size = all_params[i].shape[1]
        vectors.append(
            jnp.moveaxis(whole[:, :, start : start + size], 0, 1).reshape(LAYERS, -1)
        )
        start += size
    return vectors, got


def link_orders():
    bits = list(range(lax.axis_size("rep").bit_length() - 1))
    return [bits, bits[::-1]]


def divide(blocks, shapes, bits, outs):
    for side in range(len(shapes)):
        high, later = shapes[side]
        for i in range(high):
            for j in range(later):
                base = 2 * i * later + j
                for out_ref, index in (
                    (outs[2 * side], base + bits[side] * later),
                    (outs[2 * side + 1], base + (1 - bits[side]) * later),
                ):
                    for row, column, block in blocks(side, index):
                        out_ref[
                            0, i, j, row : row + block.shape[0], column : column + block.shape[1]
                        ] = block


def block_grad_kernel(shapes, where_ref, left_ref, grad_ref, more_ref, other_ref, *refs):
    outs, held, extra = refs[:-2], refs[-2], refs[-1]
    held[...] = low(weight_dot(left_ref[...], grad_ref[...])).reshape(held.shape)
    extra[...] = low(weight_dot(more_ref[...], other_ref[...])).reshape(extra.shape)
    rows, half, tall = held.shape[2], held.shape[3] // 2, extra.shape[1] // 2

    def blocks(side, index):
        return [
            (p * rows, 0, held[p, index, :, side * half : (side + 1) * half]) for p in range(2)
        ] + [(2 * rows, 0, extra[index, side * tall : (side + 1) * tall])]

    divide(blocks, shapes, (where_ref[0], where_ref[1]), outs)


def mixed_grad_kernel(shapes, where_ref, left_ref, grad_ref, more_ref, other_ref, *refs):
    outs, held, extra = refs[:4], refs[4], refs[5]
    held[...] = low(weight_dot(left_ref[...], grad_ref[...])).reshape(held.shape)
    extra[...] = low(weight_dot(more_ref[...], other_ref[...])).reshape(extra.shape)
    rows, rest = held.shape[2], extra.shape[2] // 2
    half = (held.shape[3] + rest) // 2

    def blocks(side, index):
        if side == 0:
            return [(p * rows, 0, held[p, index, :, :half]) for p in range(2)]
        return [(p * rows, 0, held[p, index, :, half:]) for p in range(2)] + [
            (p * rows, half - rest, extra[index, :, p * rest : (p + 1) * rest]) for p in range(2)
        ]

    divide(blocks, shapes, (where_ref[0], where_ref[1]), outs)


def grad_call(kernel, arrays, widths, rows, columns, scratch, orders):
    planes, count = lax.axis_size("fsdp") // 2, lax.axis_size("rep")
    member = lax.axis_index("rep")
    shapes = tuple((count >> (order[0] + 1), 1 << order[0]) for order in orders)
    tokens = arrays[0].shape[0]
    specs = []
    for array, width in zip(arrays, widths):
        if width is None:
            specs.append(pl.BlockSpec(array.shape, lambda z, where: (0, 0)))
        else:
            specs.append(pl.BlockSpec((tokens, width), lambda z, where: (0, z)))
    out_shapes, out_specs = [], []
    for high, later in shapes:
        block = (high, later, rows, columns // len(orders))
        out_specs += [pl.BlockSpec((1,) + block, lambda z, where: (z, 0, 0, 0, 0))] * 2
        out_shapes += [jax.ShapeDtypeStruct((planes,) + block, jnp.bfloat16)] * 2
    return pl.pallas_call(
        functools.partial(kernel, shapes),
        out_shape=out_shapes,
        grid_spec=pltpu.PrefetchScalarGridSpec(
            num_scalar_prefetch=1,
            grid=(planes,),
            in_specs=specs,
            out_specs=out_specs,
            scratch_shapes=[pltpu.VMEM(size, jnp.bfloat16) for size in scratch],
        ),
        compiler_params=params(40),
        cost_estimate=estimate(5, 0),
    )(scalars(*[(member >> order[0]) & 1 for order in orders]), *arrays)


def block_grad(left, grad, more, other, orders):
    planes, count = lax.axis_size("fsdp") // 2, lax.axis_size("rep")
    widths = left.shape[1] // planes, more.shape[1] // planes
    columns = grad.shape[1]
    rows, tall = widths[0] // (2 * count), widths[1] // count
    return grad_call(
        block_grad_kernel, (left, grad, more, other), (widths[0], None, widths[1], None),
        2 * rows + tall // 2, columns,
        [(2, count, rows, columns), (count, tall, other.shape[1])], orders,
    )


def mixed_grad(left, grad, more, other, orders):
    planes, count = lax.axis_size("fsdp") // 2, lax.axis_size("rep")
    widths = left.shape[1] // planes, more.shape[1] // planes
    columns, rest = grad.shape[1], other.shape[1]
    rows = widths[1] // count
    if widths[1] % 128:
        first = low(weight_dot(left, grad)).reshape(planes, 2, count, rows, columns)
        second = low(weight_dot(more, other)).reshape(planes, count, rows, 2, rest // 2)
        total = jnp.concatenate([jnp.swapaxes(first, 1, 2), jnp.swapaxes(second, 2, 3)], 4)
        total = total.reshape(planes, count, 2 * rows, -1)
        half, member = total.shape[3] // 2, lax.axis_index("rep")
        top = count // 2
        left_part = total[..., :half].reshape(planes, top, 2, 1, 2 * rows, half)
        right_part = total[..., half:].reshape(planes, 1, 2, top, 2 * rows, half)
        sides = member % 2, member // top
        return [
            pick(part, side if kept else 1 - side, 2)
            for part, side in zip((left_part, right_part), sides)
            for kept in (True, False)
        ]
    return grad_call(
        mixed_grad_kernel, (left, grad, more, other), (widths[0], None, widths[1], None),
        2 * rows, columns + rest // 2,
        [(2, count, rows, columns), (count, rows, rest)], orders,
    )


def split_kernel(where_ref, *refs):
    count = len(refs) // 4
    for n in range(count):
        bit = where_ref[n]
        keep_in, got_ref = refs[2 * n], refs[2 * n + 1]
        keep_ref, send_ref = refs[2 * (count + n)], refs[2 * (count + n) + 1]
        keep_ref[0] = low(widen(keep_in[0, bit]) + widen(got_ref[0, bit]))
        send_ref[0] = low(widen(keep_in[0, 1 - bit]) + widen(got_ref[0, 1 - bit]))


def add_split(pairs, later, sides, rows):
    if len({pair[0].size // n for pair, n in zip(pairs, later)}) > 1:
        return [
            out
            for pair, n, side in zip(pairs, later, sides)
            for out in add_split([pair], [n], [side], rows)
        ]
    arrays, in_specs, out_specs, out_shapes = [], [], [], []
    for pair, n in zip(pairs, later):
        columns = pair[0].shape[-1]
        for array in pair:
            arrays.append(array.reshape(-1, 2, n, rows, columns))
            in_specs.append(
                pl.BlockSpec((1, 2, n, rows, columns), lambda i, where: (i, 0, 0, 0, 0))
            )
            out_specs.append(pl.BlockSpec((1, n, rows, columns), lambda i, where: (i, 0, 0, 0)))
            out_shapes.append(
                jax.ShapeDtypeStruct((arrays[-1].shape[0], n, rows, columns), jnp.bfloat16)
            )
    return pl.pallas_call(
        split_kernel,
        out_shape=out_shapes,
        grid_spec=pltpu.PrefetchScalarGridSpec(
            num_scalar_prefetch=1,
            grid=(arrays[0].shape[0],),
            in_specs=in_specs,
            out_specs=out_specs,
        ),
        compiler_params=params(24),
        cost_estimate=estimate(0, sum(array.size for array in arrays) * 3),
    )(scalars(*sides), *arrays)


def merge_kernel(where_ref, *refs):
    arrays, (keep_ref, send_ref) = refs[:-2], refs[-2:]
    half = arrays[0].shape[-1]
    for out_ref, bit in ((keep_ref, where_ref[0]), (send_ref, 1 - where_ref[0])):
        start = 0
        for n in range(0, len(arrays), 4):
            left_ref, left_got, right_ref, right_got = arrays[n : n + 4]
            rows = slice(start, start + left_ref.shape[2])
            out_ref[0, rows, :half] = low(widen(left_ref[0, bit]) + widen(left_got[0, bit]))
            out_ref[0, rows, half:] = low(widen(right_ref[0, bit]) + widen(right_got[0, bit]))
            start += left_ref.shape[2]


def add_merge(messages, side):
    half = messages[0][0].shape[-1]
    arrays, specs, total = [], [], 0
    for message in messages:
        rows = message[0].shape[-2]
        arrays += [array.reshape(-1, 2, rows, half) for array in message]
        specs += [pl.BlockSpec((1, 2, rows, half), lambda i, where: (i, 0, 0, 0))] * 4
        total += rows
    high = arrays[0].shape[0]
    given = pl.BlockSpec((1, total, 2 * half), lambda i, where: (i, 0, 0))
    shape = jax.ShapeDtypeStruct((high, total, 2 * half), jnp.bfloat16)
    return pl.pallas_call(
        merge_kernel,
        out_shape=[shape, shape],
        grid_spec=pltpu.PrefetchScalarGridSpec(
            num_scalar_prefetch=1,
            grid=(high,),
            in_specs=specs,
            out_specs=[given, given],
        ),
        compiler_params=params(24),
        cost_estimate=estimate(0, sum(array.size for array in arrays) * 3),
    )(scalars(side), *arrays)


def reduce_members(arrays):
    member, lanes = lax.axis_index("rep"), range(2)
    rows, orders = arrays[0].shape[-2], link_orders()
    bits = [sorted(order) for order in orders]
    keeps, sends = list(arrays[::2]), list(arrays[1::2])
    for n in range(len(orders[0])):
        gots = [swap(sends[i], "rep", 1 << orders[i][n]) for i in lanes]
        for i in lanes:
            bits[i].remove(orders[i][n])
        token = yield sends, gots
        gots = [after(got, token) for got in gots]
        if n + 1 < len(orders[0]):
            later = [1 << bits[i].index(orders[i][n + 1]) for i in lanes]
            sides = [(member >> orders[i][n + 1]) & 1 for i in lanes]
            outs = add_split(list(zip(keeps, gots)), later, sides, rows)
            keeps, sends = list(outs[::2]), list(outs[1::2])
    return [keeps[0], gots[0], keeps[1], gots[1]]


def reduce_planes(messages):
    plane, planes = position()[0], lax.axis_size("fsdp") // 2
    rows = sum(message[0].shape[-2] for message in messages)
    keep, send = add_merge(messages, plane % 2)
    step = 1
    while True:
        got = swap(send, "fsdp", 2 * step)
        token = yield [send], [got]
        got = after(got, token)
        step *= 2
        if step == planes:
            return low(widen(keep) + widen(got)).reshape(rows, -1)
        keep, send = add_split([(keep, got)], [1], [(plane // step) % 2], rows)


def finish_columns(total, columns):
    core = position()[1]
    rows = total.shape[0] // 2
    part = total[:, :columns].reshape(2, rows, columns)
    got = swap(pick(part, 1 - core, 0), "fsdp", 1)
    part = jnp.concatenate([pick(part, core, 0), got], 0)
    return jnp.concatenate([part, total[:, columns:]], 1)


def spread(own, low_last):
    pieces = [own]
    for k in range(1, lax.axis_size("rep")):
        last = k & -k if low_last else 1 << (k.bit_length() - 1)
        pieces.append(swap(pieces[k ^ last], "rep", last))
    return pieces


def column_out(out_ref, block, side, ref, start):
    rows = out_ref.shape[2]
    for i in range(out_ref.shape[3] // block):
        first = start if i % 2 == side else start + rows
        out_ref[0, 0, :, i * block : (i + 1) * block] = widen(
            ref[first : first + rows, (i // 2) * block : (i // 2 + 1) * block]
        )


def early_out_kernel(block, where_ref, *refs):
    expand_out, shrink_out = refs[-2:]
    for k, ref in enumerate(refs[:-4]):
        for side in range(2):

            @pl.when((pl.program_id(0) == k) & (where_ref[1] == side))
            def _():
                column_out(expand_out, block, side, ref, 0)

        @pl.when(pl.program_id(0) == k)
        def _():
            rows, columns = shrink_out.shape[2] // 2, shrink_out.shape[3]
            start = ref.shape[0] - rows
            shrink_out[0, 0, :rows] = widen(ref[start:, :columns])
            shrink_out[0, 0, rows:] = widen(ref[start:, columns:])


def late_out_kernel(block, where_ref, *refs):
    heads_out, output_out = refs[-2:]
    for k, ref in enumerate(refs[:-4]):
        for side in range(2):

            @pl.when((pl.program_id(0) == k) & (where_ref[1] == side))
            def _():
                column_out(heads_out, block, side, ref, 0)

        @pl.when(pl.program_id(0) == k)
        def _():
            rows, half = output_out.shape[2], output_out.shape[3] // 2
            start = ref.shape[1] - half
            output_out[0, 0, :, :half] = widen(ref[:rows, start:])
            output_out[0, 0, :, half:] = widen(ref[rows:, start:])


def write_out(kernel, layer, pieces, sizes, earlier):
    plane, core, member = position()
    count = len(pieces)
    shapes = [(LAYERS, count) + size for size in sizes]
    if earlier is None:
        earlier = [jnp.zeros((8, 128), jnp.float32)] * len(sizes)
        aliases = {}
    else:
        earlier = [array.reshape(shape) for array, shape in zip(earlier, shapes)]
        aliases = {1 + count + i: i for i in range(len(sizes))}
    return pl.pallas_call(
        kernel,
        out_shape=[jax.ShapeDtypeStruct(shape, jnp.float32) for shape in shapes],
        grid_spec=pltpu.PrefetchScalarGridSpec(
            num_scalar_prefetch=1,
            grid=(count,),
            in_specs=[pl.BlockSpec(piece.shape, lambda k, where: (0, 0)) for piece in pieces]
            + [pl.BlockSpec(memory_space=pl.ANY)] * len(sizes),
            out_specs=[
                pl.BlockSpec((1, 1) + size, lambda k, where: (layer, k ^ where[0], 0, 0))
                for size in sizes
            ],
        ),
        input_output_aliases=aliases,
        compiler_params=params(24),
        cost_estimate=estimate(0, count * pieces[0].size * 6),
    )(scalars(member, core), *pieces, *earlier)


def reduce_small(grads, earlier):
    owners, count = lax.axis_size("fsdp"), lax.axis_size("rep")
    total = jnp.concatenate([g.reshape(LAYERS, owners, -1) for g in grads], 2)
    total = after(total, *earlier)
    owner = lax.axis_index("fsdp")
    step = owners // 2
    while step:
        total = total.reshape(LAYERS, 2, step, -1)
        mine = (owner // step) % 2
        total = pick(total, mine, 1) + swap(pick(total, 1 - mine, 1), "fsdp", step)
        step //= 2
    step = 1
    while step < count:
        total = total + swap(total, "rep", step)
        step *= 2
    total = total.reshape(LAYERS, -1)
    outs, start = [], 0
    for g in grads:
        size = g.shape[1] // owners
        outs.append(total[:, start : start + size])
        start += size
    return outs


def other_half(rows):
    return swap(rows, "fsdp", lax.axis_size("fsdp") // 2)


def image_side():
    return lax.axis_index("fsdp") // (lax.axis_size("fsdp") // 2)


def regroup(blocks):
    side = image_side()
    return pick(blocks, side, 0), other_half(pick(blocks, 1 - side, 0))


def ungroup(rows, got):
    own, got = rows[: rows.shape[0] // 2], got.astype(rows.dtype)
    return jnp.where(image_side() == 0, jnp.stack([own, got]), jnp.stack([got, own]))


def chips_per_image():
    return lax.axis_size("fsdp") // 4


def share_rows(local_kv):
    shared = [local_kv]
    for k in range(1, chips_per_image()):
        low_bit = k & -k
        shared.append(swap(shared[k ^ low_bit], "fsdp", 2 * low_bit))
    return shared


def collect_rows(own, others):
    chips = chips_per_image()
    if chips == 2:
        got = swap(others, "fsdp", 2)
        return low(widen(own) + widen(got)), got
    total = jnp.concatenate([own, others], 1)
    while chips > 1:
        rows = total.shape[1] // 2
        got = swap(total[:, rows:], "fsdp", chips)
        total = low(widen(total[:, :rows]) + widen(got))
        chips //= 2
    return total, got


def both_cores(rows):
    return jnp.concatenate([rows, swap(rows, "fsdp", 1)], 0)


def one_head(tensor, head):
    half = tensor.shape[1] // 2
    lane = lax.broadcasted_iota(jnp.int32, tensor.shape, 1)
    keep = lane < half if head == 0 else lane >= half
    return jnp.where(keep, tensor, jnp.zeros_like(tensor))


def join(refs, held):
    start = 0
    for ref in refs:
        held[start : start + ref.shape[0], :] = ref[...]
        start += ref.shape[0]
    return held[...]


def attend_kernel(factor, parts, query_ref, *refs):
    out_ref, log_ref, held_keys, held_values = refs[2 * parts :]
    keys, values = join(refs[:parts], held_keys), join(refs[parts : 2 * parts], held_values)
    results, logs = [], []
    for head in range(2):
        scores = input_dot(one_head(query_ref[...], head), keys)
        largest = jnp.max(scores, -1, keepdims=True)
        weights = jnp.exp2((scores - largest) * factor)
        total = jnp.sum(weights, -1, keepdims=True)
        results.append(forward_dot(low(weights), values) / total)
        logs.append(largest * factor + jnp.log2(total))
    out_ref[...] = low(one_head(results[0], 0) + one_head(results[1], 1))
    shape = log_ref.shape
    log_ref[...] = one_head(jnp.broadcast_to(logs[0], shape), 0) + one_head(
        jnp.broadcast_to(logs[1], shape), 1
    )


def pair_block(rows, start):
    return pl.BlockSpec((rows, 128), lambda i: (0, start + i))


def kv_parts(projected, others):
    pairs = projected.shape[1] // 384
    if projected.shape[0] % 16:
        others = [jnp.concatenate([projected[:, 128 * pairs :]] + others, 0)]
        parts = []
    else:
        parts = [(projected, pairs, 2 * pairs)]
    return parts + [(other, 0, pairs) for other in others]


def kv_specs(parts, first=0):
    keys = [pair_block(array.shape[0], first + start) for array, start, unused in parts]
    values = [pair_block(array.shape[0], first + start) for array, unused, start in parts]
    rows = sum(array.shape[0] for array, unused, more in parts)
    held = [pltpu.VMEM((rows, 128), jnp.bfloat16)] * 2
    return keys + values, [array for array, unused, more in parts] * 2, held


def attend(projected, others, head_size):
    tokens, width = projected.shape[0], projected.shape[1] // 3
    pairs = width // 128
    parts = kv_parts(projected, others)
    specs, arrays, held = kv_specs(parts)
    factor = head_size ** (-0.5) * math.log2(math.e)
    return pl.pallas_call(
        functools.partial(attend_kernel, factor, len(parts)),
        out_shape=[
            jax.ShapeDtypeStruct((tokens, width), jnp.bfloat16),
            jax.ShapeDtypeStruct((tokens, width), jnp.float32),
        ],
        grid=(pairs,),
        in_specs=[pair_block(tokens, 0)] + specs,
        out_specs=[pair_block(tokens, 0), pair_block(tokens, 0)],
        scratch_shapes=held,
        compiler_params=params(56),
        cost_estimate=estimate(18, 0),
    )(projected, *arrays)


def attend_back_kernel(factor, scale, parts, query_ref, *refs):
    log_ref, grad_ref, dq_ref, own_ref, others_ref, held_keys, held_values = refs[2 * parts :]
    keys, values = join(refs[:parts], held_keys), join(refs[parts : 2 * parts], held_values)
    d_query, d_key, d_value = [], 0.0, 0.0
    for head in range(2):
        query = one_head(query_ref[...], head)
        grad = one_head(grad_ref[...], head)
        half = query.shape[1] // 2
        log_total = log_ref[:, head * half : head * half + 1]
        probs = jnp.exp2(input_dot(query, keys) * factor - log_total)
        products = probs * input_dot(grad, values)
        d_scores = low(products - probs * jnp.sum(products, -1, keepdims=True))
        d_query.append(forward_dot(d_scores, keys))
        d_key = d_key + weight_dot(d_scores, query)
        d_value = d_value + weight_dot(low(probs), grad)
    dq_ref[...] = low((one_head(d_query[0], 0) + one_head(d_query[1], 1)) * scale)
    rows = own_ref.shape[1]
    for i, total in enumerate((low(d_key * scale), low(d_value))):
        own_ref[i] = total[:rows]
        others_ref[i] = total[rows:]


def attend_back(projected, others, log_total, d_attended, head_size, first, pairs):
    tokens, width = d_attended.shape[0], 128 * pairs
    parts = kv_parts(projected, others)
    specs, arrays, held = kv_specs(parts, first)
    rows = held[0].shape[0]
    scale = head_size ** (-0.5)
    own, taken = pair_block(tokens, 0), pair_block(tokens, first)
    return pl.pallas_call(
        functools.partial(attend_back_kernel, scale * math.log2(math.e), scale, len(parts)),
        out_shape=[
            jax.ShapeDtypeStruct((tokens, width), jnp.bfloat16),
            jax.ShapeDtypeStruct((2, tokens, width), jnp.bfloat16),
            jax.ShapeDtypeStruct((2, rows - tokens, width), jnp.bfloat16),
        ],
        grid=(pairs,),
        in_specs=[taken] + specs + [taken, taken],
        out_specs=[
            own,
            pl.BlockSpec((2, tokens, 128), lambda i: (0, 0, i)),
            pl.BlockSpec((2, rows - tokens, 128), lambda i: (0, 0, i)),
        ],
        scratch_shapes=held,
        compiler_params=params(60),
        cost_estimate=estimate(8 * pairs, 0),
    )(projected, *arrays, log_total, d_attended)


def add_tile(part, own_ref, other_ref, total_ref):
    @pl.when(pl.program_id(0) == 0)
    def _():
        total_ref[...] = part

    @pl.when(pl.program_id(0) > 0)
    def _():
        total_ref[...] += part

    @pl.when(pl.program_id(0) == pl.num_programs(0) - 1)
    def _():
        half = own_ref.shape[0]
        own_ref[...] = total_ref[:half]
        other_ref[...] = low(total_ref[half:])


def expand_kernel(
    rows_ref, expand_ref, bias_ref, shrink_ref, active_ref, slope_ref, own_ref, other_ref, total_ref
):
    hidden = forward_dot(rows_ref[...], expand_ref[...]) + bias_ref[...]
    normal = 0.5 + 0.5 * lax.erf(hidden * math.sqrt(0.5))
    density = jnp.exp2(hidden * hidden * (-0.5 * math.log2(math.e)))
    slope_ref[...] = low(normal + hidden * density * (1.0 / math.sqrt(2.0 * math.pi)))
    active = low(hidden * normal)
    active_ref[...] = active
    add_tile(forward_dot(active, shrink_ref[...]), own_ref, other_ref, total_ref)


def feed_forward(rows_in, expand, expand_bias, shrink):
    tokens, width = rows_in.shape
    units = expand.shape[1]
    tile = 512
    whole = pl.BlockSpec((tokens, width), lambda i: (0, 0))
    half = pl.BlockSpec((tokens // 2, width), lambda i: (0, 0))
    part = pl.BlockSpec((tokens, tile), lambda i: (0, i))
    return pl.pallas_call(
        expand_kernel,
        out_shape=[
            jax.ShapeDtypeStruct((tokens, units), jnp.bfloat16),
            jax.ShapeDtypeStruct((tokens, units), jnp.bfloat16),
            jax.ShapeDtypeStruct((tokens // 2, width), jnp.float32),
            jax.ShapeDtypeStruct((tokens // 2, width), jnp.bfloat16),
        ],
        grid=(units // tile,),
        in_specs=[
            whole,
            pl.BlockSpec((width, tile), lambda i: (0, i)),
            pl.BlockSpec((1, tile), lambda i: (0, i)),
            pl.BlockSpec((tile, width), lambda i: (i, 0)),
        ],
        out_specs=[part, part, half, half],
        scratch_shapes=[pltpu.VMEM((tokens, width), jnp.float32)],
        compiler_params=params(32),
        cost_estimate=estimate(14, 0),
    )(rows_in, expand, expand_bias[None], shrink)


def shrink_kernel(
    grad_ref, shrink_ref, slope_ref, expand_ref, hidden_ref, bias_ref, own_ref, other_ref, total_ref
):
    d_hidden = low(input_dot(grad_ref[...], shrink_ref[...]) * widen(slope_ref[...]))
    hidden_ref[...] = d_hidden
    bias_ref[...] = jnp.sum(widen(d_hidden), 0, keepdims=True)
    add_tile(input_dot(d_hidden, expand_ref[...]), own_ref, other_ref, total_ref)


def feed_back(d_mlp, shrink, slope, expand):
    tokens, width = d_mlp.shape
    units = expand.shape[1]
    tile = 512
    whole = pl.BlockSpec((tokens, width), lambda i: (0, 0))
    half = pl.BlockSpec((tokens // 2, width), lambda i: (0, 0))
    part = pl.BlockSpec((tokens, tile), lambda i: (0, i))
    return pl.pallas_call(
        shrink_kernel,
        out_shape=[
            jax.ShapeDtypeStruct((tokens, units), jnp.bfloat16),
            jax.ShapeDtypeStruct((1, units), jnp.float32),
            jax.ShapeDtypeStruct((tokens // 2, width), jnp.float32),
            jax.ShapeDtypeStruct((tokens // 2, width), jnp.bfloat16),
        ],
        grid=(units // tile,),
        in_specs=[
            whole,
            pl.BlockSpec((tile, width), lambda i: (i, 0)),
            part,
            pl.BlockSpec((width, tile), lambda i: (0, i)),
        ],
        out_specs=[part, pl.BlockSpec((1, tile), lambda i: (0, i)), half, half],
        scratch_shapes=[pltpu.VMEM((tokens, width), jnp.float32)],
        compiler_params=params(32),
        cost_estimate=estimate(9, 0),
    )(d_mlp, shrink, slope, expand)


def core_half(vector):
    core = position()[1]
    return pick(widen(vector).reshape(lax.axis_size("fsdp") // 2, 2, -1), core, 1).reshape(-1)


def core_fill(half):
    parts = half.reshape(lax.axis_size("fsdp") // 2, -1)
    return by_core(parts, jnp.zeros_like(parts), 1).reshape(-1)


def normed_rows(tok_rows, gathered):
    return both_cores(low(layer_norm(tok_rows, widen(gathered[0]), widen(gathered[1]))))


def project(normed, gathered, token):
    heads_weight, query_bias, value_bias = gathered[2], gathered[3], gathered[4]
    width = normed.shape[1]
    bias_row = jnp.concatenate(
        [core_half(query_bias), jnp.zeros((width // 2,), jnp.float32), core_half(value_bias)]
    )
    projected = low(forward_dot(normed, heads_weight) + bias_row)
    return projected, share_rows(after(projected[:, width // 2 :], token))[1:]


def forward_layer(tok_rows, normed, projected, others, gathered, beside, neighbours, planes):
    (
        attn_norm_gain,
        attn_norm_bias,
        heads_weight,
        query_bias,
        value_bias,
        output_weight,
        output_bias,
        attn_layerscale,
        mlp_norm_gain,
        mlp_norm_bias,
        expand_weight,
        expand_bias,
        shrink_weight,
        shrink_bias,
        mlp_layerscale,
    ) = gathered
    tokens, width = tok_rows.shape
    attended, log_total = attend(projected, others, width // HEADS)
    attended = after(attended, *beside)
    got = swap(low(forward_dot(attended[tokens:], output_weight)), "fsdp", 1)
    branch = forward_dot(attended[:tokens], output_weight) + widen(got) + widen(output_bias)
    middle = tok_rows + widen(attn_layerscale) * branch
    normed_two = low(layer_norm(middle, widen(mlp_norm_gain), widen(mlp_norm_bias)))
    normed_two = both_cores(after(normed_two, *planes[:1]))
    activated, slope, own_sum, other_sum = feed_forward(
        normed_two, expand_weight, core_half(expand_bias), shrink_weight
    )
    other_sum = after(other_sum, *neighbours, *planes[1:])
    mlp_out = own_sum + widen(swap(other_sum, "fsdp", 1)) + widen(shrink_bias)
    result = middle + widen(mlp_layerscale) * mlp_out
    saved = (
        tok_rows,
        normed,
        projected,
        others,
        log_total,
        attended,
        branch,
        middle,
        normed_two,
        slope,
        activated,
        mlp_out,
    )
    return (result, saved)


class Later:
    def __init__(self):
        self.running, self.done, self.sends, self.gots = {}, {}, {}, {}

    def begin(self, name, kernel, arrays):
        self.running[name] = reduce_members(kernel(*arrays, link_orders()))
        self.step(name, None)

    def join(self, name, parts, token):
        for part in parts:
            while part in self.running:
                self.step(part, token)
        self.running[name] = reduce_planes([self.done[part] for part in parts])
        self.step(name, None)

    def step(self, name, token):
        try:
            self.sends[name], self.gots[name] = self.running[name].send(token)
        except StopIteration as end:
            self.done[name] = end.value
            self.sends[name] = self.gots[name] = []
            del self.running[name]

    def sent(self, value, *names):
        return after(value, *[array for name in names for array in self.sends[name]])

    def came(self, value, *names):
        return after(value, *[array for name in names for array in self.gots[name]])


def backward_layer(d_result, saved, gathered, later, new, old, activation_got):
    (
        attn_norm_gain,
        attn_norm_bias,
        heads_weight,
        query_bias,
        value_bias,
        output_weight,
        output_bias,
        attn_layerscale,
        mlp_norm_gain,
        mlp_norm_bias,
        expand_weight,
        expand_bias,
        shrink_weight,
        shrink_bias,
        mlp_layerscale,
    ) = gathered
    (
        tok_rows,
        normed,
        projected,
        others,
        log_total,
        attended,
        branch,
        middle,
        normed_two,
        slope,
        activated,
        mlp_out,
    ) = saved
    tokens, width = tok_rows.shape
    d_mlp = low(d_result * widen(mlp_layerscale))
    d_mlp_both = both_cores(d_mlp)
    g_mlp_scale = jnp.sum(d_result * mlp_out, 0)
    g_shrink_bias = column_sum(d_mlp)
    d_hidden, g_expand_bias, own_sum, other_sum = feed_back(
        d_mlp_both, shrink_weight, slope, expand_weight
    )
    block, mixed, block_planes, mixed_planes = new
    if old:
        other_sum = later.came(other_sum, old[0])
        later.join(old[2], [old[0]], other_sum)
        d_hidden = later.sent(d_hidden, old[2])
    got = swap(other_sum, "fsdp", 1)
    later.begin(block, block_grad, (normed_two, d_hidden, activated, d_mlp_both))
    own_sum = later.sent(own_sum, block)
    if not old:
        own_sum = after(own_sum, activation_got)
    if old:
        own_sum = later.came(own_sum, old[1])
        later.step(old[1], own_sum)
        own_sum = later.sent(own_sum, old[1])
    d_middle_norm, g_mlp_gain, g_mlp_shift = norm_back(
        middle, widen(mlp_norm_gain), widen(mlp_norm_bias), own_sum + widen(got)
    )
    d_middle = d_result + d_middle_norm
    d_branch = low(d_middle * widen(attn_layerscale))
    d_branch_both = both_cores(d_branch)
    g_attn_scale = jnp.sum(d_middle * branch, 0)
    g_output_bias = column_sum(d_branch)
    d_attended = low(input_dot(d_branch_both, output_weight))
    pairs = d_attended.shape[1] // 128

    def back(first):
        return attend_back(
            projected, others, log_total, d_attended, width // HEADS, first, pairs // 2
        )

    first_query, d_own, d_others = back(0)
    first_kv, first_got = collect_rows(d_own, d_others)
    if old:
        d_attended = later.came(d_attended, old[2])
        later.step(old[2], first_query)
        d_attended = later.sent(d_attended, old[2])
    second_query, d_own, d_others = back(pairs // 2)
    d_others = after(d_others, first_got)
    second_kv, second_got = collect_rows(d_own, d_others)
    second_query = later.came(second_query, block)
    later.step(block, second_query)
    second_query = later.sent(second_query, block)
    if old:
        second_query = later.came(second_query, old[1])
    d_query = jnp.concatenate([first_query, second_query], 1)
    d_key = jnp.concatenate([first_kv[0], second_kv[0]], 1)
    d_value = jnp.concatenate([first_kv[1], second_kv[1]], 1)
    d_projected = jnp.concatenate([d_query, d_key, d_value], 1)
    g_query_bias = column_sum(d_query)
    g_value_bias = column_sum(d_value)
    got = swap(low(input_dot(d_projected[tokens:], heads_weight)), "fsdp", 1)
    later.begin(mixed, mixed_grad, (normed, d_projected, attended, d_branch_both))
    d_projected = later.sent(d_projected, mixed)
    if old:
        later.join(old[3], [old[1]], d_projected)
        later.join(block_planes, [block], d_projected)
        d_projected = later.sent(d_projected, block_planes)
    d_normed = input_dot(d_projected[:tokens], heads_weight) + widen(got)
    d_rows_norm, g_attn_gain, g_attn_shift = norm_back(
        tok_rows, widen(attn_norm_gain), widen(attn_norm_bias), d_normed
    )
    d_rows = d_middle + d_rows_norm
    small_grads = (
        g_attn_gain,
        g_attn_shift,
        core_fill(g_query_bias),
        core_fill(g_value_bias),
        g_output_bias,
        g_attn_scale,
        g_mlp_gain,
        g_mlp_shift,
        core_fill(g_expand_bias),
        g_shrink_bias,
        g_mlp_scale,
    )
    return (d_rows, small_grads)


def local(images, cotangent, *all_params):
    owners, count = lax.axis_size("fsdp"), lax.axis_size("rep")
    pieces = message_pieces(all_params)
    small, small_got = gather_small(all_params, pieces[0])
    column, planes = gather_planes(pieces[0], beside=[small_got])
    own, got = regroup(after(images, planes[0]))
    tok_rows = widen(jnp.concatenate([own, got], 0))
    column = after(column, got)
    next_column, next_planes = gather_planes(pieces[1], got)
    held, neighbours = gather_neighbours(column, [])
    saved_layers, fetched = [], []
    for layer in range(LAYERS):
        gathered = [None] * len(all_params)
        for i, vector in zip(SMALL, small):
            gathered[i] = vector[layer]
        normed = normed_rows(tok_rows, gathered)
        arrays, parts, earlier = gather_members(held, [])
        arrays[0] = after(arrays[0], next_planes[-1])
        gathered[2], gathered[5] = place_first(
            arrays, parts, count, all_params[2].shape[2] // 2
        )
        projected, others = project(normed, gathered, next_planes[-1])
        held, neighbours = gather_neighbours(next_column, earlier)
        if layer + 1 < LAYERS:
            column, planes = gather_planes(pieces[2 * layer + 2], others[-1])
            beside = planes[:1]
        else:
            own, got = regroup(after(cotangent, others[-1]))
            d_rows = widen(jnp.concatenate([own, got], 0))
            beside, planes, neighbours, next_planes = [got], [], [], []
        arrays, parts, earlier = gather_members(held, [])
        arrays[0] = after(arrays[0], *planes[-1:])
        if layer + 1 < LAYERS:
            next_column, next_planes = gather_planes(pieces[2 * layer + 3], planes[-1])
            held, neighbours = gather_neighbours(column, earlier)
        gathered[10], gathered[12] = place_second(arrays, parts, count)
        fetched.append(tuple(gathered))
        tok_rows, saved = forward_layer(
            tok_rows, normed, projected, others, gathered, beside, neighbours, next_planes
        )
        saved_layers.append(saved)
    activation_rows = low(tok_rows)
    small_grads = [None] * LAYERS
    outs = {}

    def size(i):
        return (all_params[i].shape[1] // count, all_params[i].shape[2])

    def block_piece(later, layer):
        total = later.done[layer, 2]
        half = total.shape[0] // 2
        return jnp.concatenate([finish_columns(total[:half], total.shape[1]), total[half:]], 0)

    def mixed_piece(later, layer):
        return finish_columns(later.done[layer, 3], size(2)[1] // 2)

    def write_block(layer, pieces):
        outs["block"] = write_out(
            functools.partial(early_out_kernel, size(10)[1] // owners),
            layer, pieces, [size(10), size(12)], outs.get("block"),
        )

    def write_mixed(layer, pieces):
        outs["mixed"] = write_out(
            functools.partial(late_out_kernel, size(2)[1] // 3 // owners),
            layer, pieces, [size(2), size(5)], outs.get("mixed"),
        )

    later = Later()
    for layer in reversed(range(LAYERS)):
        new = [(layer, n) for n in range(4)]
        old = [(layer + 1, n) for n in range(4)] if layer + 1 < LAYERS else None
        if not old:
            activation_got = other_half(activation_rows[activation_rows.shape[0] // 2 :])
        d_rows, small_grads[layer] = backward_layer(
            d_rows, saved_layers[layer], fetched[layer], later, new, old, activation_got
        )
    activations = ungroup(activation_rows, activation_got)
    image_got = other_half(low(d_rows[d_rows.shape[0] // 2 :]))
    d_images = ungroup(d_rows, image_got)
    while old[2] in later.running:
        later.step(old[2], d_rows)
    first = after(block_piece(later, layer + 1), d_rows)
    later.step(new[1], d_rows)
    write_block(layer + 1, spread(later.sent(first, new[1]), True))
    last_gots = later.gots[new[1]] + [image_got]
    later.join(new[3], [new[1]], d_rows)
    for name in (new[3], new[2], old[3]):
        while name in later.running:
            later.step(name, d_rows)
    write_block(layer, spread(block_piece(later, layer), False))
    both = [mixed_piece(later, n) for n in (layer + 1, layer)]
    rows = both[0].shape[0]
    pieces = spread(jnp.concatenate(both, 0), True)
    write_mixed(layer + 1, [piece[:rows] for piece in pieces])
    write_mixed(layer, [piece[rows:] for piece in pieces])
    stacked = [None] * len(all_params)
    for i, out in zip((10, 12, 2, 5), list(outs["block"]) + list(outs["mixed"])):
        stacked[i] = out.reshape(all_params[i].shape)
    reduced = reduce_small(
        [jnp.stack([grads[n] for grads in small_grads]) for n in range(len(SMALL))], last_gots
    )
    for i, vector in zip(SMALL, reduced):
        stacked[i] = vector
    return (activations, d_images) + tuple(stacked)


def solution(mesh):
    in_specs = (
        P("rep", "fsdp", None),
        P("rep", "fsdp", None),
        P(None, "fsdp"),
        P(None, "fsdp"),
        P(None, "fsdp", None),
        P(None, "fsdp"),
        P(None, "fsdp"),
        P(None, "fsdp", None),
        P(None, "fsdp"),
        P(None, "fsdp"),
        P(None, "fsdp"),
        P(None, "fsdp"),
        P(None, "fsdp", None),
        P(None, "fsdp"),
        P(None, "fsdp", None),
        P(None, "fsdp"),
        P(None, "fsdp"),
    )
    out_specs = (
        P("rep", "fsdp", None),
        P("rep", "fsdp", None),
        P(None, "fsdp"),
        P(None, "fsdp"),
        P(None, "fsdp", None),
        P(None, "fsdp"),
        P(None, "fsdp"),
        P(None, "fsdp", None),
        P(None, "fsdp"),
        P(None, "fsdp"),
        P(None, "fsdp"),
        P(None, "fsdp"),
        P(None, "fsdp", None),
        P(None, "fsdp"),
        P(None, "fsdp", None),
        P(None, "fsdp"),
        P(None, "fsdp"),
    )
    return jax.shard_map(local, mesh=mesh, in_specs=in_specs, out_specs=out_specs, check_vma=False)
```

```python
import functools
import math

import jax
import jax.numpy as jnp
from jax import lax
from jax.experimental import pallas as pl
from jax.experimental.pallas import tpu as pltpu
from jax.sharding import PartitionSpec as P

HEADS = 16
LAYERS = 2
SMALL = (0, 1, 3, 4, 6, 7, 8, 9, 11, 13, 14)
MIB = 1 << 20

epsilon = 1e-06


def layer_norm(values_in, norm_gain, norm_shift):
    centre = jnp.mean(values_in, -1, keepdims=True)
    centered = values_in - centre
    spread = jnp.mean(centered * centered, -1, keepdims=True)
    return centered * lax.rsqrt(spread + epsilon) * norm_gain + norm_shift


def norm_back(values_in, norm_gain, norm_shift, grad):
    unused, pullback = jax.vjp(layer_norm, values_in, norm_gain, norm_shift)
    return pullback(grad)


def widen(tensor):
    return tensor.astype(jnp.float32)


def low(tensor):
    return tensor.astype(jnp.bfloat16)


def forward_dot(left, weight):
    return jnp.dot(left, weight, preferred_element_type=jnp.float32)


def weight_dot(left, grad):
    return lax.dot_general(left, grad, (((0,), (0,)), ((), ())), preferred_element_type=jnp.float32)


def input_dot(grad, weight):
    return lax.dot_general(
        grad, weight, (((1,), (1,)), ((), ())), preferred_element_type=jnp.float32
    )


def column_sum(grad):
    return jnp.sum(widen(grad), 0)


def pick(tensor, index, axis):
    return lax.dynamic_index_in_dim(tensor, index, axis, keepdims=False)


def swap(tensor, axis, offset):
    count = lax.axis_size(axis)
    return lax.ppermute(tensor, axis, [(i, i ^ offset) for i in range(count)])


def position():
    owner = lax.axis_index("fsdp")
    return owner // 2, owner % 2, lax.axis_index("rep")


def scalars(*values):
    return jnp.stack(values).astype(jnp.int32)


def estimate(microseconds, moved):
    return pl.CostEstimate(flops=1000, bytes_accessed=1000, transcendentals=0)


def params(mib):
    return pltpu.CompilerParams(vmem_limit_bytes=mib * MIB)


def after(tensor, *earlier):
    return lax.optimization_barrier((tensor,) + earlier)[0]


def by_core(own, got, axis):
    core = position()[1]
    return jnp.where(
        core == 0, jnp.stack([own, got], axis), jnp.stack([got, own], axis)
    )


def columns_kernel(blocks, where_ref, *refs):
    ins, (own_ref, other_ref) = refs[:-2], refs[-2:]
    for side in range(2):

        @pl.when(where_ref[1] == side)
        def _():
            for out_ref, parity in ((own_ref, side), (other_ref, 1 - side)):
                start = 0
                for ref, block in zip(ins, blocks):
                    for i in range(parity, ref.shape[2] // block, 2):
                        out_ref[0, :, start : start + block] = ref[0, :, i * block : (i + 1) * block]
                        start += block


def column_pieces(shards):
    plane, core, member = position()
    owners, count = lax.axis_size("fsdp"), lax.axis_size("rep")
    rows = shards[0].shape[1] // count
    blocks = tuple(
        size // owners for size in (shards[0].shape[2] // 3, shards[1].shape[2])
    )
    columns = sum(shard.shape[2] for shard in shards) // 2
    shape = jax.ShapeDtypeStruct((LAYERS, rows, columns), jnp.bfloat16)
    out = pl.BlockSpec((1, rows, columns), lambda layer, where: (layer, 0, 0))
    own, other = pl.pallas_call(
        functools.partial(columns_kernel, blocks),
        out_shape=[shape, shape],
        grid_spec=pltpu.PrefetchScalarGridSpec(
            num_scalar_prefetch=1,
            grid=(LAYERS,),
            in_specs=[
                pl.BlockSpec((1, rows, shard.shape[2]), lambda layer, where: (layer, where[0], 0))
                for shard in shards
            ],
            out_specs=[out, out],
        ),
        cost_estimate=estimate(0, 4 * LAYERS * rows * columns * 2),
    )(scalars(member, core), *shards)
    both = by_core(own, swap(other, "fsdp", 1), 1)
    split = shards[0].shape[2] // 2
    both = both.reshape(LAYERS, 2 * rows, columns)
    return both[..., :split], both[..., split:]


def place_kernel(half_rows, blocks, parts, where_ref, *refs):
    count = len(parts)
    pieces, outs, (in_sems, out_sems) = refs[:count], refs[count : -count - 2], refs[-2:]
    held = refs[-count - 2 : -2]
    plane, member = where_ref[0], where_ref[1]
    arrivals = []
    for i in range(count):
        arrivals.append(pltpu.make_async_copy(pieces[i], held[i], in_sems.at[i]))
        arrivals[-1].start()
    copies = []
    for i, (k, halves) in enumerate(parts):
        arrivals[i].wait()
        for j in range(pieces[0].shape[0]):
            for b, (row, rows, column, columns, put) in enumerate(blocks):
                if row // half_rows not in halves:
                    continue
                first = row - halves[0] * half_rows
                copy = pltpu.make_async_copy(
                    held[i].at[j, first : first + rows, column : column + columns],
                    put(outs, j ^ plane, k ^ member),
                    out_sems.at[b, i, j],
                )
                copy.start()
                copies.append(copy)
    for copy in copies:
        copy.wait()


def place(pieces, parts, shapes, blocks):
    plane, core, member = position()
    planes = pieces[0].shape[0]
    outs = pl.pallas_call(
        functools.partial(place_kernel, pieces[0].shape[1] // 2, blocks, parts),
        out_shape=[jax.ShapeDtypeStruct(shape, pieces[0].dtype) for shape in shapes],
        in_specs=[pl.BlockSpec(memory_space=pltpu.SMEM)]
        + [pl.BlockSpec(memory_space=pl.ANY)] * len(pieces),
        out_specs=[pl.BlockSpec(memory_space=pl.ANY)] * len(shapes),
        scratch_shapes=[pltpu.VMEM(piece.shape, piece.dtype) for piece in pieces]
        + [
            pltpu.SemaphoreType.DMA((len(pieces),)),
            pltpu.SemaphoreType.DMA((len(blocks), len(pieces), planes)),
        ],
        compiler_params=params(20),
        cost_estimate=estimate(0, 4 * sum(piece.size for piece in pieces)),
    )(scalars(plane, member), *pieces)
    return [out.reshape(-1, out.shape[-1]) for out in outs]


def put_pair(side):
    return lambda outs, plane, member: outs[0].at[plane, side, member]


def place_first(pieces, parts, count, split):
    planes, rows, columns = pieces[0].shape
    half, rest = rows // 2, columns - split

    def put(side):
        return lambda outs, plane, member: outs[1].at[
            plane, member, :, side * rest : (side + 1) * rest
        ]

    shapes = [(planes, 2, count, half, split), (planes, count, half, 2 * rest)]
    blocks = [(side * half, half, 0, split, put_pair(side)) for side in range(2)]
    blocks += [(side * half, half, split, rest, put(side)) for side in range(2)]
    return place(pieces, parts, shapes, blocks)


def place_second(pieces, parts, count):
    planes, rows, columns = pieces[0].shape
    half, fine, width = rows // 2, rows // 4, columns // 2

    def put(side):
        return lambda outs, plane, member: outs[1].at[plane, member, side]

    shapes = [(planes, 2, count, fine, columns), (planes, count, 2, half, width)]
    blocks = [(side * fine, fine, 0, columns, put_pair(side)) for side in range(2)]
    blocks += [(half, half, side * width, width, put(side)) for side in range(2)]
    return place(pieces, parts, shapes, blocks)


def gather_planes(piece, *earlier, beside=()):
    column, sent, step = piece[None], list(earlier), lax.axis_size("fsdp") // 4
    while step:
        got = swap(after(column, *sent[-1:], *(beside if len(sent) > len(earlier) else ())), "fsdp", 2 * step)
        sent.append(got)
        column = jnp.stack([column, got], 1).reshape((-1,) + piece.shape)
        step //= 2
    return column, sent[len(earlier) :]


def gather_neighbours(column, earlier):
    held = {0: [column]}
    for bit in range(lax.axis_size("rep").bit_length() - 1):
        held[1 << bit] = [swap(after(column, *earlier), "rep", 1 << bit)]
    return held, [held[k][0] for k in held if k]


def gather_members(held, beside):
    count, rows = lax.axis_size("rep"), held[0][0].shape[1] // 2
    earlier = [held[k][0] for k in held if k] + list(beside)
    for level in range(1, count.bit_length() - 1):
        sent = []
        for k in range(1, count):
            if bin(k).count("1") != level + 1:
                continue
            held[k] = []
            for half, last in ((0, k & -k), (1, 1 << (k.bit_length() - 1))):
                source = held[k ^ last]
                if len(source) == 1:
                    source = source[0][:, half * rows : (half + 1) * rows]
                else:
                    source = source[half]
                held[k].append(swap(after(source, *earlier), "rep", last))
            sent += held[k]
        earlier = sent
    arrays, parts = [], []
    for k in range(count):
        for half, array in enumerate(held[k]):
            arrays.append(array)
            parts.append((k, (0, 1) if len(held[k]) == 1 else (half,)))
    return arrays, parts, earlier


def message_pieces(shards):
    heads, expand = column_pieces((shards[2], shards[10]))
    pieces = []
    for layer in range(LAYERS):
        output, shrink = quarter(shards[5][layer]), quarter(shards[12][layer])
        half = output.shape[1] // 2
        packed = jnp.concatenate([output[:, :half], output[:, half:]], 0)
        pieces.append(jnp.concatenate([heads[layer], packed], 1))
        half = shrink.shape[0] // 2
        packed = jnp.concatenate([shrink[:half], shrink[half:]], 1)
        pieces.append(jnp.concatenate([expand[layer], packed], 0))
    return pieces


def quarter(param):
    rows = param.shape[0] // lax.axis_size("rep")
    return lax.dynamic_slice_in_dim(param, lax.axis_index("rep") * rows, rows, 0)


def gather_small(all_params, token):
    packed = after(jnp.concatenate([all_params[i] for i in SMALL], 1), token)
    whole, owner, step = packed[None], lax.axis_index("fsdp"), 1
    while step < lax.axis_size("fsdp"):
        got = swap(whole, "fsdp", step)
        whole = jnp.where(
            (owner // step) % 2 == 0,
            jnp.concatenate([whole, got], 0),
            jnp.concatenate([got, whole], 0),
        )
        step *= 2
    vectors, start = [], 0
    for i in SMALL:
        size = all_params[i].shape[1]
        vectors.append(
            jnp.moveaxis(whole[:, :, start : start + size], 0, 1).reshape(LAYERS, -1)
        )
        start += size
    return vectors


def link_orders():
    bits = list(range(lax.axis_size("rep").bit_length() - 1))
    return [bits, bits[::-1]]


def divide(blocks, shapes, bits, outs):
    for side in range(len(shapes)):
        high, later = shapes[side]
        for i in range(high):
            for j in range(later):
                base = 2 * i * later + j
                for out_ref, index in (
                    (outs[2 * side], base + bits[side] * later),
                    (outs[2 * side + 1], base + (1 - bits[side]) * later),
                ):
                    for row, column, block in blocks(side, index):
                        out_ref[
                            0, i, j, row : row + block.shape[0], column : column + block.shape[1]
                        ] = block


def block_grad_kernel(shapes, where_ref, left_ref, grad_ref, more_ref, other_ref, *refs):
    outs, held, extra = refs[:-2], refs[-2], refs[-1]
    held[...] = low(weight_dot(left_ref[...], grad_ref[...])).reshape(held.shape)
    extra[...] = low(weight_dot(more_ref[...], other_ref[...])).reshape(extra.shape)
    rows, half, tall = held.shape[2], held.shape[3] // 2, extra.shape[1] // 2

    def blocks(side, index):
        return [
            (p * rows, 0, held[p, index, :, side * half : (side + 1) * half]) for p in range(2)
        ] + [(2 * rows, 0, extra[index, side * tall : (side + 1) * tall])]

    divide(blocks, shapes, (where_ref[0], where_ref[1]), outs)


def mixed_grad_kernel(shapes, where_ref, left_ref, grad_ref, more_ref, other_ref, *refs):
    outs, held, extra = refs[:4], refs[4], refs[5]
    held[...] = low(weight_dot(left_ref[...], grad_ref[...])).reshape(held.shape)
    extra[...] = low(weight_dot(more_ref[...], other_ref[...])).reshape(extra.shape)
    rows, rest = held.shape[2], extra.shape[2] // 2
    half = (held.shape[3] + rest) // 2

    def blocks(side, index):
        if side == 0:
            return [(p * rows, 0, held[p, index, :, :half]) for p in range(2)]
        return [(p * rows, 0, held[p, index, :, half:]) for p in range(2)] + [
            (p * rows, half - rest, extra[index, :, p * rest : (p + 1) * rest]) for p in range(2)
        ]

    divide(blocks, shapes, (where_ref[0], where_ref[1]), outs)


def grad_call(kernel, arrays, widths, rows, columns, scratch, orders):
    planes, count = lax.axis_size("fsdp") // 2, lax.axis_size("rep")
    member = lax.axis_index("rep")
    shapes = tuple((count >> (order[0] + 1), 1 << order[0]) for order in orders)
    tokens = arrays[0].shape[0]
    specs = []
    for array, width in zip(arrays, widths):
        if width is None:
            specs.append(pl.BlockSpec(array.shape, lambda z, where: (0, 0)))
        else:
            specs.append(pl.BlockSpec((tokens, width), lambda z, where: (0, z)))
    out_shapes, out_specs = [], []
    for high, later in shapes:
        block = (high, later, rows, columns // len(orders))
        out_specs += [pl.BlockSpec((1,) + block, lambda z, where: (z, 0, 0, 0, 0))] * 2
        out_shapes += [jax.ShapeDtypeStruct((planes,) + block, jnp.bfloat16)] * 2
    return pl.pallas_call(
        functools.partial(kernel, shapes),
        out_shape=out_shapes,
        grid_spec=pltpu.PrefetchScalarGridSpec(
            num_scalar_prefetch=1,
            grid=(planes,),
            in_specs=specs,
            out_specs=out_specs,
            scratch_shapes=[pltpu.VMEM(size, jnp.bfloat16) for size in scratch],
        ),
        compiler_params=params(40),
        cost_estimate=estimate(5, 0),
    )(scalars(*[(member >> order[0]) & 1 for order in orders]), *arrays)


def block_grad(left, grad, more, other, orders):
    planes, count = lax.axis_size("fsdp") // 2, lax.axis_size("rep")
    widths = left.shape[1] // planes, more.shape[1] // planes
    columns = grad.shape[1]
    rows, tall = widths[0] // (2 * count), widths[1] // count
    return grad_call(
        block_grad_kernel, (left, grad, more, other), (widths[0], None, widths[1], None),
        2 * rows + tall // 2, columns,
        [(2, count, rows, columns), (count, tall, other.shape[1])], orders,
    )


def mixed_grad(left, grad, more, other, orders):
    planes, count = lax.axis_size("fsdp") // 2, lax.axis_size("rep")
    widths = left.shape[1] // planes, more.shape[1] // planes
    columns, rest = grad.shape[1], other.shape[1]
    rows = widths[1] // count
    if widths[1] % 128:
        first = low(weight_dot(left, grad)).reshape(planes, 2, count, rows, columns)
        second = low(weight_dot(more, other)).reshape(planes, count, rows, 2, rest // 2)
        total = jnp.concatenate([jnp.swapaxes(first, 1, 2), jnp.swapaxes(second, 2, 3)], 4)
        total = total.reshape(planes, count, 2 * rows, -1)
        half, member = total.shape[3] // 2, lax.axis_index("rep")
        top = count // 2
        left_part = total[..., :half].reshape(planes, top, 2, 1, 2 * rows, half)
        right_part = total[..., half:].reshape(planes, 1, 2, top, 2 * rows, half)
        sides = member % 2, member // top
        return [
            pick(part, side if kept else 1 - side, 2)
            for part, side in zip((left_part, right_part), sides)
            for kept in (True, False)
        ]
    return grad_call(
        mixed_grad_kernel, (left, grad, more, other), (widths[0], None, widths[1], None),
        2 * rows, columns + rest // 2,
        [(2, count, rows, columns), (count, rows, rest)], orders,
    )


def split_kernel(where_ref, *refs):
    count = len(refs) // 4
    for n in range(count):
        bit = where_ref[n]
        keep_in, got_ref = refs[2 * n], refs[2 * n + 1]
        keep_ref, send_ref = refs[2 * (count + n)], refs[2 * (count + n) + 1]
        keep_ref[0] = low(widen(keep_in[0, bit]) + widen(got_ref[0, bit]))
        send_ref[0] = low(widen(keep_in[0, 1 - bit]) + widen(got_ref[0, 1 - bit]))


def add_split(pairs, later, sides, rows):
    if len({pair[0].size // n for pair, n in zip(pairs, later)}) > 1:
        return [
            out
            for pair, n, side in zip(pairs, later, sides)
            for out in add_split([pair], [n], [side], rows)
        ]
    arrays, in_specs, out_specs, out_shapes = [], [], [], []
    for pair, n in zip(pairs, later):
        columns = pair[0].shape[-1]
        for array in pair:
            arrays.append(array.reshape(-1, 2, n, rows, columns))
            in_specs.append(
                pl.BlockSpec((1, 2, n, rows, columns), lambda i, where: (i, 0, 0, 0, 0))
            )
            out_specs.append(pl.BlockSpec((1, n, rows, columns), lambda i, where: (i, 0, 0, 0)))
            out_shapes.append(
                jax.ShapeDtypeStruct((arrays[-1].shape[0], n, rows, columns), jnp.bfloat16)
            )
    return pl.pallas_call(
        split_kernel,
        out_shape=out_shapes,
        grid_spec=pltpu.PrefetchScalarGridSpec(
            num_scalar_prefetch=1,
            grid=(arrays[0].shape[0],),
            in_specs=in_specs,
            out_specs=out_specs,
        ),
        compiler_params=params(24),
        cost_estimate=estimate(0, sum(array.size for array in arrays) * 3),
    )(scalars(*sides), *arrays)


def merge_kernel(where_ref, *refs):
    arrays, (keep_ref, send_ref) = refs[:-2], refs[-2:]
    half = arrays[0].shape[-1]
    for out_ref, bit in ((keep_ref, where_ref[0]), (send_ref, 1 - where_ref[0])):
        start = 0
        for n in range(0, len(arrays), 4):
            left_ref, left_got, right_ref, right_got = arrays[n : n + 4]
            rows = slice(start, start + left_ref.shape[2])
            out_ref[0, rows, :half] = low(widen(left_ref[0, bit]) + widen(left_got[0, bit]))
            out_ref[0, rows, half:] = low(widen(right_ref[0, bit]) + widen(right_got[0, bit]))
            start += left_ref.shape[2]


def add_merge(messages, side):
    half = messages[0][0].shape[-1]
    arrays, specs, total = [], [], 0
    for message in messages:
        rows = message[0].shape[-2]
        arrays += [array.reshape(-1, 2, rows, half) for array in message]
        specs += [pl.BlockSpec((1, 2, rows, half), lambda i, where: (i, 0, 0, 0))] * 4
        total += rows
    high = arrays[0].shape[0]
    given = pl.BlockSpec((1, total, 2 * half), lambda i, where: (i, 0, 0))
    shape = jax.ShapeDtypeStruct((high, total, 2 * half), jnp.bfloat16)
    return pl.pallas_call(
        merge_kernel,
        out_shape=[shape, shape],
        grid_spec=pltpu.PrefetchScalarGridSpec(
            num_scalar_prefetch=1,
            grid=(high,),
            in_specs=specs,
            out_specs=[given, given],
        ),
        compiler_params=params(24),
        cost_estimate=estimate(0, sum(array.size for array in arrays) * 3),
    )(scalars(side), *arrays)


def reduce_members(arrays):
    member, lanes = lax.axis_index("rep"), range(2)
    rows, orders = arrays[0].shape[-2], link_orders()
    bits = [sorted(order) for order in orders]
    keeps, sends = list(arrays[::2]), list(arrays[1::2])
    for n in range(len(orders[0])):
        gots = [swap(sends[i], "rep", 1 << orders[i][n]) for i in lanes]
        for i in lanes:
            bits[i].remove(orders[i][n])
        token = yield sends, gots
        gots = [after(got, token) for got in gots]
        if n + 1 < len(orders[0]):
            later = [1 << bits[i].index(orders[i][n + 1]) for i in lanes]
            sides = [(member >> orders[i][n + 1]) & 1 for i in lanes]
            outs = add_split(list(zip(keeps, gots)), later, sides, rows)
            keeps, sends = list(outs[::2]), list(outs[1::2])
    return [keeps[0], gots[0], keeps[1], gots[1]]


def reduce_planes(messages):
    plane, planes = position()[0], lax.axis_size("fsdp") // 2
    rows = sum(message[0].shape[-2] for message in messages)
    keep, send = add_merge(messages, plane % 2)
    step = 1
    while True:
        got = swap(send, "fsdp", 2 * step)
        token = yield [send], [got]
        got = after(got, token)
        step *= 2
        if step == planes:
            return low(widen(keep) + widen(got)).reshape(rows, -1)
        keep, send = add_split([(keep, got)], [1], [(plane // step) % 2], rows)


def finish_columns(total, columns):
    core = position()[1]
    rows = total.shape[0] // 2
    part = total[:, :columns].reshape(2, rows, columns)
    got = swap(pick(part, 1 - core, 0), "fsdp", 1)
    part = jnp.concatenate([pick(part, core, 0), got], 0)
    return jnp.concatenate([part, total[:, columns:]], 1)


def spread(own, low_last):
    pieces = [own]
    for k in range(1, lax.axis_size("rep")):
        last = k & -k if low_last else 1 << (k.bit_length() - 1)
        pieces.append(swap(pieces[k ^ last], "rep", last))
    return pieces


def column_out(out_ref, block, side, ref, start):
    rows = out_ref.shape[2]
    for i in range(out_ref.shape[3] // block):
        first = start if i % 2 == side else start + rows
        out_ref[0, 0, :, i * block : (i + 1) * block] = widen(
            ref[first : first + rows, (i // 2) * block : (i // 2 + 1) * block]
        )


def early_out_kernel(block, where_ref, *refs):
    expand_out, shrink_out = refs[-2:]
    for k, ref in enumerate(refs[:-4]):
        for side in range(2):

            @pl.when((pl.program_id(0) == k) & (where_ref[1] == side))
            def _():
                column_out(expand_out, block, side, ref, 0)

        @pl.when(pl.program_id(0) == k)
        def _():
            rows, columns = shrink_out.shape[2] // 2, shrink_out.shape[3]
            start = ref.shape[0] - rows
            shrink_out[0, 0, :rows] = widen(ref[start:, :columns])
            shrink_out[0, 0, rows:] = widen(ref[start:, columns:])


def late_out_kernel(block, where_ref, *refs):
    heads_out, output_out = refs[-2:]
    for k, ref in enumerate(refs[:-4]):
        for side in range(2):

            @pl.when((pl.program_id(0) == k) & (where_ref[1] == side))
            def _():
                column_out(heads_out, block, side, ref, 0)

        @pl.when(pl.program_id(0) == k)
        def _():
            rows, half = output_out.shape[2], output_out.shape[3] // 2
            start = ref.shape[1] - half
            output_out[0, 0, :, :half] = widen(ref[:rows, start:])
            output_out[0, 0, :, half:] = widen(ref[rows:, start:])


def write_out(kernel, layer, pieces, sizes, earlier):
    plane, core, member = position()
    count = len(pieces)
    shapes = [(LAYERS, count) + size for size in sizes]
    if earlier is None:
        earlier = [jnp.zeros((8, 128), jnp.float32)] * len(sizes)
        aliases = {}
    else:
        earlier = [array.reshape(shape) for array, shape in zip(earlier, shapes)]
        aliases = {1 + count + i: i for i in range(len(sizes))}
    return pl.pallas_call(
        kernel,
        out_shape=[jax.ShapeDtypeStruct(shape, jnp.float32) for shape in shapes],
        grid_spec=pltpu.PrefetchScalarGridSpec(
            num_scalar_prefetch=1,
            grid=(count,),
            in_specs=[pl.BlockSpec(piece.shape, lambda k, where: (0, 0)) for piece in pieces]
            + [pl.BlockSpec(memory_space=pl.ANY)] * len(sizes),
            out_specs=[
                pl.BlockSpec((1, 1) + size, lambda k, where: (layer, k ^ where[0], 0, 0))
                for size in sizes
            ],
        ),
        input_output_aliases=aliases,
        compiler_params=params(24),
        cost_estimate=estimate(0, count * pieces[0].size * 6),
    )(scalars(member, core), *pieces, *earlier)


def reduce_small(grads, earlier):
    owners, count = lax.axis_size("fsdp"), lax.axis_size("rep")
    total = jnp.concatenate([g.reshape(LAYERS, owners, -1) for g in grads], 2)
    total = after(total, *earlier)
    owner = lax.axis_index("fsdp")
    step = owners // 2
    while step:
        total = total.reshape(LAYERS, 2, step, -1)
        mine = (owner // step) % 2
        total = pick(total, mine, 1) + swap(pick(total, 1 - mine, 1), "fsdp", step)
        step //= 2
    step = 1
    while step < count:
        total = total + swap(total, "rep", step)
        step *= 2
    total = total.reshape(LAYERS, -1)
    outs, start = [], 0
    for g in grads:
        size = g.shape[1] // owners
        outs.append(total[:, start : start + size])
        start += size
    return outs


def other_half(rows):
    return swap(rows, "fsdp", lax.axis_size("fsdp") // 2)


def image_side():
    return lax.axis_index("fsdp") // (lax.axis_size("fsdp") // 2)


def regroup(blocks):
    side = image_side()
    return pick(blocks, side, 0), other_half(pick(blocks, 1 - side, 0))


def ungroup(rows, got):
    own, got = rows[: rows.shape[0] // 2], got.astype(rows.dtype)
    return jnp.where(image_side() == 0, jnp.stack([own, got]), jnp.stack([got, own]))


def chips_per_image():
    return lax.axis_size("fsdp") // 4


def share_rows(local_kv):
    shared = [local_kv]
    for k in range(1, chips_per_image()):
        low_bit = k & -k
        shared.append(swap(shared[k ^ low_bit], "fsdp", 2 * low_bit))
    return shared


def collect_rows(own, others):
    chips = chips_per_image()
    if chips == 2:
        got = swap(others, "fsdp", 2)
        return low(widen(own) + widen(got)), got
    total = jnp.concatenate([own, others], 1)
    while chips > 1:
        rows = total.shape[1] // 2
        got = swap(total[:, rows:], "fsdp", chips)
        total = low(widen(total[:, :rows]) + widen(got))
        chips //= 2
    return total, got


def both_cores(rows):
    return jnp.concatenate([rows, swap(rows, "fsdp", 1)], 0)


def one_head(tensor, head):
    half = tensor.shape[1] // 2
    lane = lax.broadcasted_iota(jnp.int32, tensor.shape, 1)
    keep = lane < half if head == 0 else lane >= half
    return jnp.where(keep, tensor, jnp.zeros_like(tensor))


def join(refs, held):
    start = 0
    for ref in refs:
        held[start : start + ref.shape[0], :] = ref[...]
        start += ref.shape[0]
    return held[...]


def attend_kernel(factor, parts, query_ref, *refs):
    out_ref, log_ref, held_keys, held_values = refs[2 * parts :]
    keys, values = join(refs[:parts], held_keys), join(refs[parts : 2 * parts], held_values)
    results, logs = [], []
    for head in range(2):
        scores = input_dot(one_head(query_ref[...], head), keys)
        largest = jnp.max(scores, -1, keepdims=True)
        weights = jnp.exp2((scores - largest) * factor)
        total = jnp.sum(weights, -1, keepdims=True)
        results.append(forward_dot(low(weights), values) / total)
        logs.append(largest * factor + jnp.log2(total))
    out_ref[...] = low(one_head(results[0], 0) + one_head(results[1], 1))
    shape = log_ref.shape
    log_ref[...] = one_head(jnp.broadcast_to(logs[0], shape), 0) + one_head(
        jnp.broadcast_to(logs[1], shape), 1
    )


def pair_block(rows, start):
    return pl.BlockSpec((rows, 128), lambda i: (0, start + i))


def kv_parts(projected, others):
    pairs = projected.shape[1] // 384
    if projected.shape[0] % 16:
        others = [jnp.concatenate([projected[:, 128 * pairs :]] + others, 0)]
        parts = []
    else:
        parts = [(projected, pairs, 2 * pairs)]
    return parts + [(other, 0, pairs) for other in others]


def kv_specs(parts, first=0):
    keys = [pair_block(array.shape[0], first + start) for array, start, unused in parts]
    values = [pair_block(array.shape[0], first + start) for array, unused, start in parts]
    rows = sum(array.shape[0] for array, unused, more in parts)
    held = [pltpu.VMEM((rows, 128), jnp.bfloat16)] * 2
    return keys + values, [array for array, unused, more in parts] * 2, held


def attend(projected, others, head_size):
    tokens, width = projected.shape[0], projected.shape[1] // 3
    pairs = width // 128
    parts = kv_parts(projected, others)
    specs, arrays, held = kv_specs(parts)
    factor = head_size ** (-0.5) * math.log2(math.e)
    return pl.pallas_call(
        functools.partial(attend_kernel, factor, len(parts)),
        out_shape=[
            jax.ShapeDtypeStruct((tokens, width), jnp.bfloat16),
            jax.ShapeDtypeStruct((tokens, width), jnp.float32),
        ],
        grid=(pairs,),
        in_specs=[pair_block(tokens, 0)] + specs,
        out_specs=[pair_block(tokens, 0), pair_block(tokens, 0)],
        scratch_shapes=held,
        compiler_params=params(56),
        cost_estimate=estimate(18, 0),
    )(projected, *arrays)


def attend_back_kernel(factor, scale, parts, query_ref, *refs):
    log_ref, grad_ref, dq_ref, own_ref, others_ref, held_keys, held_values = refs[2 * parts :]
    keys, values = join(refs[:parts], held_keys), join(refs[parts : 2 * parts], held_values)
    d_query, d_key, d_value = [], 0.0, 0.0
    for head in range(2):
        query = one_head(query_ref[...], head)
        grad = one_head(grad_ref[...], head)
        half = query.shape[1] // 2
        log_total = log_ref[:, head * half : head * half + 1]
        probs = jnp.exp2(input_dot(query, keys) * factor - log_total)
        products = probs * input_dot(grad, values)
        d_scores = low(products - probs * jnp.sum(products, -1, keepdims=True))
        d_query.append(forward_dot(d_scores, keys))
        d_key = d_key + weight_dot(d_scores, query)
        d_value = d_value + weight_dot(low(probs), grad)
    dq_ref[...] = low((one_head(d_query[0], 0) + one_head(d_query[1], 1)) * scale)
    rows = own_ref.shape[1]
    for i, total in enumerate((low(d_key * scale), low(d_value))):
        own_ref[i] = total[:rows]
        others_ref[i] = total[rows:]


def attend_back(projected, others, log_total, d_attended, head_size, first, pairs):
    tokens, width = d_attended.shape[0], 128 * pairs
    parts = kv_parts(projected, others)
    specs, arrays, held = kv_specs(parts, first)
    rows = held[0].shape[0]
    scale = head_size ** (-0.5)
    own, taken = pair_block(tokens, 0), pair_block(tokens, first)
    return pl.pallas_call(
        functools.partial(attend_back_kernel, scale * math.log2(math.e), scale, len(parts)),
        out_shape=[
            jax.ShapeDtypeStruct((tokens, width), jnp.bfloat16),
            jax.ShapeDtypeStruct((2, tokens, width), jnp.bfloat16),
            jax.ShapeDtypeStruct((2, rows - tokens, width), jnp.bfloat16),
        ],
        grid=(pairs,),
        in_specs=[taken] + specs + [taken, taken],
        out_specs=[
            own,
            pl.BlockSpec((2, tokens, 128), lambda i: (0, 0, i)),
            pl.BlockSpec((2, rows - tokens, 128), lambda i: (0, 0, i)),
        ],
        scratch_shapes=held,
        compiler_params=params(60),
        cost_estimate=estimate(8 * pairs, 0),
    )(projected, *arrays, log_total, d_attended)


def add_tile(part, own_ref, other_ref, total_ref):
    @pl.when(pl.program_id(0) == 0)
    def _():
        total_ref[...] = part

    @pl.when(pl.program_id(0) > 0)
    def _():
        total_ref[...] += part

    @pl.when(pl.program_id(0) == pl.num_programs(0) - 1)
    def _():
        half = own_ref.shape[0]
        own_ref[...] = total_ref[:half]
        other_ref[...] = low(total_ref[half:])


def expand_kernel(
    rows_ref, expand_ref, bias_ref, shrink_ref, active_ref, slope_ref, own_ref, other_ref, total_ref
):
    hidden = forward_dot(rows_ref[...], expand_ref[...]) + bias_ref[...]
    normal = 0.5 + 0.5 * lax.erf(hidden * math.sqrt(0.5))
    density = jnp.exp2(hidden * hidden * (-0.5 * math.log2(math.e)))
    slope_ref[...] = low(normal + hidden * density * (1.0 / math.sqrt(2.0 * math.pi)))
    active = low(hidden * normal)
    active_ref[...] = active
    add_tile(forward_dot(active, shrink_ref[...]), own_ref, other_ref, total_ref)


def feed_forward(rows_in, expand, expand_bias, shrink):
    tokens, width = rows_in.shape
    units = expand.shape[1]
    tile = 512
    whole = pl.BlockSpec((tokens, width), lambda i: (0, 0))
    half = pl.BlockSpec((tokens // 2, width), lambda i: (0, 0))
    part = pl.BlockSpec((tokens, tile), lambda i: (0, i))
    return pl.pallas_call(
        expand_kernel,
        out_shape=[
            jax.ShapeDtypeStruct((tokens, units), jnp.bfloat16),
            jax.ShapeDtypeStruct((tokens, units), jnp.bfloat16),
            jax.ShapeDtypeStruct((tokens // 2, width), jnp.float32),
            jax.ShapeDtypeStruct((tokens // 2, width), jnp.bfloat16),
        ],
        grid=(units // tile,),
        in_specs=[
            whole,
            pl.BlockSpec((width, tile), lambda i: (0, i)),
            pl.BlockSpec((1, tile), lambda i: (0, i)),
            pl.BlockSpec((tile, width), lambda i: (i, 0)),
        ],
        out_specs=[part, part, half, half],
        scratch_shapes=[pltpu.VMEM((tokens, width), jnp.float32)],
        compiler_params=params(32),
        cost_estimate=estimate(14, 0),
    )(rows_in, expand, expand_bias[None], shrink)


def shrink_kernel(
    grad_ref, shrink_ref, slope_ref, expand_ref, hidden_ref, bias_ref, own_ref, other_ref, total_ref
):
    d_hidden = low(input_dot(grad_ref[...], shrink_ref[...]) * widen(slope_ref[...]))
    hidden_ref[...] = d_hidden
    bias_ref[...] = jnp.sum(widen(d_hidden), 0, keepdims=True)
    add_tile(input_dot(d_hidden, expand_ref[...]), own_ref, other_ref, total_ref)


def feed_back(d_mlp, shrink, slope, expand):
    tokens, width = d_mlp.shape
    units = expand.shape[1]
    tile = 512
    whole = pl.BlockSpec((tokens, width), lambda i: (0, 0))
    half = pl.BlockSpec((tokens // 2, width), lambda i: (0, 0))
    part = pl.BlockSpec((tokens, tile), lambda i: (0, i))
    return pl.pallas_call(
        shrink_kernel,
        out_shape=[
            jax.ShapeDtypeStruct((tokens, units), jnp.bfloat16),
            jax.ShapeDtypeStruct((1, units), jnp.float32),
            jax.ShapeDtypeStruct((tokens // 2, width), jnp.float32),
            jax.ShapeDtypeStruct((tokens // 2, width), jnp.bfloat16),
        ],
        grid=(units // tile,),
        in_specs=[
            whole,
            pl.BlockSpec((tile, width), lambda i: (i, 0)),
            part,
            pl.BlockSpec((width, tile), lambda i: (0, i)),
        ],
        out_specs=[part, pl.BlockSpec((1, tile), lambda i: (0, i)), half, half],
        scratch_shapes=[pltpu.VMEM((tokens, width), jnp.float32)],
        compiler_params=params(32),
        cost_estimate=estimate(9, 0),
    )(d_mlp, shrink, slope, expand)


def core_half(vector):
    core = position()[1]
    return pick(widen(vector).reshape(lax.axis_size("fsdp") // 2, 2, -1), core, 1).reshape(-1)


def core_fill(half):
    parts = half.reshape(lax.axis_size("fsdp") // 2, -1)
    return by_core(parts, jnp.zeros_like(parts), 1).reshape(-1)


def normed_rows(tok_rows, gathered):
    return both_cores(low(layer_norm(tok_rows, widen(gathered[0]), widen(gathered[1]))))


def project(normed, gathered, token):
    heads_weight, query_bias, value_bias = gathered[2], gathered[3], gathered[4]
    width = normed.shape[1]
    bias_row = jnp.concatenate(
        [core_half(query_bias), jnp.zeros((width // 2,), jnp.float32), core_half(value_bias)]
    )
    projected = low(forward_dot(normed, heads_weight) + bias_row)
    return projected, share_rows(after(projected[:, width // 2 :], token))[1:]


def forward_layer(tok_rows, normed, projected, others, gathered, beside, neighbours, planes):
    (
        attn_norm_gain,
        attn_norm_bias,
        heads_weight,
        query_bias,
        value_bias,
        output_weight,
        output_bias,
        attn_layerscale,
        mlp_norm_gain,
        mlp_norm_bias,
        expand_weight,
        expand_bias,
        shrink_weight,
        shrink_bias,
        mlp_layerscale,
    ) = gathered
    tokens, width = tok_rows.shape
    attended, log_total = attend(projected, others, width // HEADS)
    attended = after(attended, *beside)
    got = swap(low(forward_dot(attended[tokens:], output_weight)), "fsdp", 1)
    branch = forward_dot(attended[:tokens], output_weight) + widen(got) + widen(output_bias)
    middle = tok_rows + widen(attn_layerscale) * branch
    normed_two = low(layer_norm(middle, widen(mlp_norm_gain), widen(mlp_norm_bias)))
    normed_two = both_cores(after(normed_two, *planes[:1]))
    activated, slope, own_sum, other_sum = feed_forward(
        normed_two, expand_weight, core_half(expand_bias), shrink_weight
    )
    other_sum = after(other_sum, *neighbours, *planes[1:])
    mlp_out = own_sum + widen(swap(other_sum, "fsdp", 1)) + widen(shrink_bias)
    result = middle + widen(mlp_layerscale) * mlp_out
    saved = (
        tok_rows,
        normed,
        projected,
        others,
        log_total,
        attended,
        branch,
        middle,
        normed_two,
        slope,
        activated,
        mlp_out,
    )
    return (result, saved)


class Later:
    def __init__(self):
        self.running, self.done, self.sends, self.gots = {}, {}, {}, {}

    def begin(self, name, kernel, arrays):
        self.running[name] = reduce_members(kernel(*arrays, link_orders()))
        self.step(name, None)

    def join(self, name, parts, token):
        for part in parts:
            while part in self.running:
                self.step(part, token)
        self.running[name] = reduce_planes([self.done[part] for part in parts])
        self.step(name, None)

    def step(self, name, token):
        try:
            self.sends[name], self.gots[name] = self.running[name].send(token)
        except StopIteration as end:
            self.done[name] = end.value
            self.sends[name] = self.gots[name] = []
            del self.running[name]

    def sent(self, value, *names):
        return after(value, *[array for name in names for array in self.sends[name]])

    def came(self, value, *names):
        return after(value, *[array for name in names for array in self.gots[name]])


def backward_layer(d_result, saved, gathered, later, new, old, activation_got):
    (
        attn_norm_gain,
        attn_norm_bias,
        heads_weight,
        query_bias,
        value_bias,
        output_weight,
        output_bias,
        attn_layerscale,
        mlp_norm_gain,
        mlp_norm_bias,
        expand_weight,
        expand_bias,
        shrink_weight,
        shrink_bias,
        mlp_layerscale,
    ) = gathered
    (
        tok_rows,
        normed,
        projected,
        others,
        log_total,
        attended,
        branch,
        middle,
        normed_two,
        slope,
        activated,
        mlp_out,
    ) = saved
    tokens, width = tok_rows.shape
    d_mlp = low(d_result * widen(mlp_layerscale))
    d_mlp_both = both_cores(d_mlp)
    g_mlp_scale = jnp.sum(d_result * mlp_out, 0)
    g_shrink_bias = column_sum(d_mlp)
    d_hidden, g_expand_bias, own_sum, other_sum = feed_back(
        d_mlp_both, shrink_weight, slope, expand_weight
    )
    block, mixed, block_planes, mixed_planes = new
    if old:
        other_sum = later.came(other_sum, old[0])
        later.join(old[2], [old[0]], other_sum)
        d_hidden = later.sent(d_hidden, old[2])
    got = swap(other_sum, "fsdp", 1)
    later.begin(block, block_grad, (normed_two, d_hidden, activated, d_mlp_both))
    own_sum = later.sent(own_sum, block)
    if not old:
        own_sum = after(own_sum, activation_got)
    if old:
        own_sum = later.came(own_sum, old[1])
        later.step(old[1], own_sum)
        own_sum = later.sent(own_sum, old[1])
    d_middle_norm, g_mlp_gain, g_mlp_shift = norm_back(
        middle, widen(mlp_norm_gain), widen(mlp_norm_bias), own_sum + widen(got)
    )
    d_middle = d_result + d_middle_norm
    d_branch = low(d_middle * widen(attn_layerscale))
    d_branch_both = both_cores(d_branch)
    g_attn_scale = jnp.sum(d_middle * branch, 0)
    g_output_bias = column_sum(d_branch)
    d_attended = low(input_dot(d_branch_both, output_weight))
    pairs = d_attended.shape[1] // 128

    def back(first):
        return attend_back(
            projected, others, log_total, d_attended, width // HEADS, first, pairs // 2
        )

    first_query, d_own, d_others = back(0)
    first_kv, first_got = collect_rows(d_own, d_others)
    if old:
        d_attended = later.came(d_attended, old[2])
        later.step(old[2], first_query)
        d_attended = later.sent(d_attended, old[2])
    second_query, d_own, d_others = back(pairs // 2)
    d_others = after(d_others, first_got)
    if old:
        d_others = later.came(d_others, old[2])
    second_kv, second_got = collect_rows(d_own, d_others)
    second_query = later.came(second_query, block)
    later.step(block, second_query)
    second_query = later.sent(second_query, block)
    d_query = jnp.concatenate([first_query, second_query], 1)
    d_key = jnp.concatenate([first_kv[0], second_kv[0]], 1)
    d_value = jnp.concatenate([first_kv[1], second_kv[1]], 1)
    d_projected = jnp.concatenate([d_query, d_key, d_value], 1)
    g_query_bias = column_sum(d_query)
    g_value_bias = column_sum(d_value)
    got = swap(low(input_dot(d_projected[tokens:], heads_weight)), "fsdp", 1)
    later.begin(mixed, mixed_grad, (normed, d_projected, attended, d_branch_both))
    d_projected = later.sent(d_projected, mixed)
    if old:
        later.join(old[3], [old[1]], d_projected)
        d_projected = later.sent(d_projected, old[3])
        later.join(block_planes, [block], d_projected)
        d_projected = later.sent(d_projected, block_planes)
    d_normed = input_dot(d_projected[:tokens], heads_weight) + widen(got)
    d_rows_norm, g_attn_gain, g_attn_shift = norm_back(
        tok_rows, widen(attn_norm_gain), widen(attn_norm_bias), d_normed
    )
    d_rows = d_middle + d_rows_norm
    small_grads = (
        g_attn_gain,
        g_attn_shift,
        core_fill(g_query_bias),
        core_fill(g_value_bias),
        g_output_bias,
        g_attn_scale,
        g_mlp_gain,
        g_mlp_shift,
        core_fill(g_expand_bias),
        g_shrink_bias,
        g_mlp_scale,
    )
    return (d_rows, small_grads)


def local(images, cotangent, *all_params):
    owners, count = lax.axis_size("fsdp"), lax.axis_size("rep")
    pieces = message_pieces(all_params)
    column, planes = gather_planes(pieces[0])
    own, got = regroup(after(images, planes[0]))
    tok_rows = widen(jnp.concatenate([own, got], 0))
    column = after(column, got)
    next_column, next_planes = gather_planes(pieces[1], got)
    small = gather_small(all_params, got)
    held, neighbours = gather_neighbours(column, [])
    saved_layers, fetched = [], []
    for layer in range(LAYERS):
        gathered = [None] * len(all_params)
        for i, vector in zip(SMALL, small):
            gathered[i] = vector[layer]
        normed = normed_rows(tok_rows, gathered)
        arrays, parts, earlier = gather_members(held, [])
        arrays[0] = after(arrays[0], next_planes[-1])
        gathered[2], gathered[5] = place_first(
            arrays, parts, count, all_params[2].shape[2] // 2
        )
        projected, others = project(normed, gathered, next_planes[-1])
        held, neighbours = gather_neighbours(next_column, earlier)
        if layer + 1 < LAYERS:
            column, planes = gather_planes(pieces[2 * layer + 2], others[-1])
            beside = planes[:1]
        else:
            own, got = regroup(after(cotangent, others[-1]))
            d_rows = widen(jnp.concatenate([own, got], 0))
            beside, planes, neighbours, next_planes = [got], [], [], []
        arrays, parts, earlier = gather_members(held, [])
        arrays[0] = after(arrays[0], *planes[-1:])
        if layer + 1 < LAYERS:
            next_column, next_planes = gather_planes(pieces[2 * layer + 3], planes[-1])
            held, neighbours = gather_neighbours(column, earlier)
        gathered[10], gathered[12] = place_second(arrays, parts, count)
        fetched.append(tuple(gathered))
        tok_rows, saved = forward_layer(
            tok_rows, normed, projected, others, gathered, beside, neighbours, next_planes
        )
        saved_layers.append(saved)
    activation_rows = low(tok_rows)
    small_grads = [None] * LAYERS
    outs = {}

    def size(i):
        return (all_params[i].shape[1] // count, all_params[i].shape[2])

    def block_piece(later, layer):
        total = later.done[layer, 2]
        half = total.shape[0] // 2
        return jnp.concatenate([finish_columns(total[:half], total.shape[1]), total[half:]], 0)

    def mixed_piece(later, layer):
        return finish_columns(later.done[layer, 3], size(2)[1] // 2)

    def write_block(layer, pieces):
        outs["block"] = write_out(
            functools.partial(early_out_kernel, size(10)[1] // owners),
            layer, pieces, [size(10), size(12)], outs.get("block"),
        )

    def write_mixed(layer, pieces):
        outs["mixed"] = write_out(
            functools.partial(late_out_kernel, size(2)[1] // 3 // owners),
            layer, pieces, [size(2), size(5)], outs.get("mixed"),
        )

    later = Later()
    for layer in reversed(range(LAYERS)):
        new = [(layer, n) for n in range(4)]
        old = [(layer + 1, n) for n in range(4)] if layer + 1 < LAYERS else None
        if not old:
            activation_got = other_half(activation_rows[activation_rows.shape[0] // 2 :])
        d_rows, small_grads[layer] = backward_layer(
            d_rows, saved_layers[layer], fetched[layer], later, new, old, activation_got
        )
    activations = ungroup(activation_rows, activation_got)
    image_got = other_half(low(d_rows[d_rows.shape[0] // 2 :]))
    d_images = ungroup(d_rows, image_got)
    for name in (old[2], old[3]):
        while name in later.running:
            later.step(name, d_rows)
    first = block_piece(later, layer + 1)
    rows = first.shape[0]
    first = after(jnp.concatenate([first, mixed_piece(later, layer + 1)], 0), d_rows)
    later.step(new[1], d_rows)
    pieces = spread(later.sent(first, new[1]), True)
    write_block(layer + 1, [piece[:rows] for piece in pieces])
    write_mixed(layer + 1, [piece[rows:] for piece in pieces])
    last_gots = later.gots[new[1]] + [image_got]
    later.join(new[3], [new[1]], d_rows)
    while new[3] in later.running:
        later.step(new[3], d_rows)
    while new[2] in later.running:
        later.step(new[2], d_rows)
    write_block(layer, spread(block_piece(later, layer), False))
    write_mixed(layer, spread(mixed_piece(later, layer), False))
    stacked = [None] * len(all_params)
    for i, out in zip((10, 12, 2, 5), list(outs["block"]) + list(outs["mixed"])):
        stacked[i] = out.reshape(all_params[i].shape)
    reduced = reduce_small(
        [jnp.stack([grads[n] for grads in small_grads]) for n in range(len(SMALL))], last_gots
    )
    for i, vector in zip(SMALL, reduced):
        stacked[i] = vector
    return (activations, d_images) + tuple(stacked)


def solution(mesh):
    in_specs = (
        P("rep", "fsdp", None),
        P("rep", "fsdp", None),
        P(None, "fsdp"),
        P(None, "fsdp"),
        P(None, "fsdp", None),
        P(None, "fsdp"),
        P(None, "fsdp"),
        P(None, "fsdp", None),
        P(None, "fsdp"),
        P(None, "fsdp"),
        P(None, "fsdp"),
        P(None, "fsdp"),
        P(None, "fsdp", None),
        P(None, "fsdp"),
        P(None, "fsdp", None),
        P(None, "fsdp"),
        P(None, "fsdp"),
    )
    out_specs = (
        P("rep", "fsdp", None),
        P("rep", "fsdp", None),
        P(None, "fsdp"),
        P(None, "fsdp"),
        P(None, "fsdp", None),
        P(None, "fsdp"),
        P(None, "fsdp"),
        P(None, "fsdp", None),
        P(None, "fsdp"),
        P(None, "fsdp"),
        P(None, "fsdp"),
        P(None, "fsdp"),
        P(None, "fsdp", None),
        P(None, "fsdp"),
        P(None, "fsdp", None),
        P(None, "fsdp"),
        P(None, "fsdp"),
    )
    return jax.shard_map(local, mesh=mesh, in_specs=in_specs, out_specs=out_specs, check_vma=False)
```

```python
import functools
import math

import jax
import jax.numpy as jnp
from jax import lax
from jax.experimental import pallas as pl
from jax.experimental.pallas import tpu as pltpu
from jax.sharding import PartitionSpec as P

HEADS = 16
LAYERS = 2
SMALL = (0, 1, 3, 4, 6, 7, 8, 9, 11, 13, 14)
MIB = 1 << 20

epsilon = 1e-06


def layer_norm(values_in, norm_gain, norm_shift):
    centre = jnp.mean(values_in, -1, keepdims=True)
    centered = values_in - centre
    spread = jnp.mean(centered * centered, -1, keepdims=True)
    return centered * lax.rsqrt(spread + epsilon) * norm_gain + norm_shift


def norm_back(values_in, norm_gain, norm_shift, grad):
    unused, pullback = jax.vjp(layer_norm, values_in, norm_gain, norm_shift)
    return pullback(grad)


def widen(tensor):
    return tensor.astype(jnp.float32)


def low(tensor):
    return tensor.astype(jnp.bfloat16)


def forward_dot(left, weight):
    return jnp.dot(left, weight, preferred_element_type=jnp.float32)


def weight_dot(left, grad):
    return lax.dot_general(left, grad, (((0,), (0,)), ((), ())), preferred_element_type=jnp.float32)


def input_dot(grad, weight):
    return lax.dot_general(
        grad, weight, (((1,), (1,)), ((), ())), preferred_element_type=jnp.float32
    )


def column_sum(grad):
    return jnp.sum(widen(grad), 0)


def pick(tensor, index, axis):
    return lax.dynamic_index_in_dim(tensor, index, axis, keepdims=False)


def swap(tensor, axis, offset):
    count = lax.axis_size(axis)
    return lax.ppermute(tensor, axis, [(i, i ^ offset) for i in range(count)])


def position():
    owner = lax.axis_index("fsdp")
    return owner // 2, owner % 2, lax.axis_index("rep")


def scalars(*values):
    return jnp.stack(values).astype(jnp.int32)


def estimate(microseconds, moved):
    return pl.CostEstimate(flops=1000, bytes_accessed=1000, transcendentals=0)


def params(mib):
    return pltpu.CompilerParams(vmem_limit_bytes=mib * MIB)


def after(tensor, *earlier):
    return lax.optimization_barrier((tensor,) + earlier)[0]


def by_core(own, got, axis):
    core = position()[1]
    return jnp.where(
        core == 0, jnp.stack([own, got], axis), jnp.stack([got, own], axis)
    )


def columns_kernel(blocks, where_ref, *refs):
    ins, (own_ref, other_ref) = refs[:-2], refs[-2:]
    for side in range(2):

        @pl.when(where_ref[1] == side)
        def _():
            for out_ref, parity in ((own_ref, side), (other_ref, 1 - side)):
                start = 0
                for ref, block in zip(ins, blocks):
                    for i in range(parity, ref.shape[2] // block, 2):
                        out_ref[0, :, start : start + block] = ref[0, :, i * block : (i + 1) * block]
                        start += block


def column_pieces(shards):
    plane, core, member = position()
    owners, count = lax.axis_size("fsdp"), lax.axis_size("rep")
    rows = shards[0].shape[1] // count
    blocks = tuple(
        size // owners for size in (shards[0].shape[2] // 3, shards[1].shape[2])
    )
    columns = sum(shard.shape[2] for shard in shards) // 2
    shape = jax.ShapeDtypeStruct((LAYERS, rows, columns), jnp.bfloat16)
    out = pl.BlockSpec((1, rows, columns), lambda layer, where: (layer, 0, 0))
    own, other = pl.pallas_call(
        functools.partial(columns_kernel, blocks),
        out_shape=[shape, shape],
        grid_spec=pltpu.PrefetchScalarGridSpec(
            num_scalar_prefetch=1,
            grid=(LAYERS,),
            in_specs=[
                pl.BlockSpec((1, rows, shard.shape[2]), lambda layer, where: (layer, where[0], 0))
                for shard in shards
            ],
            out_specs=[out, out],
        ),
        cost_estimate=estimate(0, 4 * LAYERS * rows * columns * 2),
    )(scalars(member, core), *shards)
    both = by_core(own, swap(other, "fsdp", 1), 1)
    split = shards[0].shape[2] // 2
    both = both.reshape(LAYERS, 2 * rows, columns)
    return both[..., :split], both[..., split:]


def place_kernel(half_rows, blocks, parts, where_ref, *refs):
    count = len(parts)
    pieces, outs, (in_sems, out_sems) = refs[:count], refs[count : -count - 2], refs[-2:]
    held = refs[-count - 2 : -2]
    plane, member = where_ref[0], where_ref[1]
    arrivals = []
    for i in range(count):
        arrivals.append(pltpu.make_async_copy(pieces[i], held[i], in_sems.at[i]))
        arrivals[-1].start()
    copies = []
    for i, (k, halves) in enumerate(parts):
        arrivals[i].wait()
        for j in range(pieces[0].shape[0]):
            for b, (row, rows, column, columns, put) in enumerate(blocks):
                if row // half_rows not in halves:
                    continue
                first = row - halves[0] * half_rows
                copy = pltpu.make_async_copy(
                    held[i].at[j, first : first + rows, column : column + columns],
                    put(outs, j ^ plane, k ^ member),
                    out_sems.at[b, i, j],
                )
                copy.start()
                copies.append(copy)
    for copy in copies:
        copy.wait()


def place(pieces, parts, shapes, blocks):
    plane, core, member = position()
    planes = pieces[0].shape[0]
    outs = pl.pallas_call(
        functools.partial(place_kernel, pieces[0].shape[1] // 2, blocks, parts),
        out_shape=[jax.ShapeDtypeStruct(shape, pieces[0].dtype) for shape in shapes],
        in_specs=[pl.BlockSpec(memory_space=pltpu.SMEM)]
        + [pl.BlockSpec(memory_space=pl.ANY)] * len(pieces),
        out_specs=[pl.BlockSpec(memory_space=pl.ANY)] * len(shapes),
        scratch_shapes=[pltpu.VMEM(piece.shape, piece.dtype) for piece in pieces]
        + [
            pltpu.SemaphoreType.DMA((len(pieces),)),
            pltpu.SemaphoreType.DMA((len(blocks), len(pieces), planes)),
        ],
        compiler_params=params(20),
        cost_estimate=estimate(0, 4 * sum(piece.size for piece in pieces)),
    )(scalars(plane, member), *pieces)
    return [out.reshape(-1, out.shape[-1]) for out in outs]


def put_pair(side):
    return lambda outs, plane, member: outs[0].at[plane, side, member]


def place_first(pieces, parts, count, split):
    planes, rows, columns = pieces[0].shape
    half, rest = rows // 2, columns - split

    def put(side):
        return lambda outs, plane, member: outs[1].at[
            plane, member, :, side * rest : (side + 1) * rest
        ]

    shapes = [(planes, 2, count, half, split), (planes, count, half, 2 * rest)]
    blocks = [(side * half, half, 0, split, put_pair(side)) for side in range(2)]
    blocks += [(side * half, half, split, rest, put(side)) for side in range(2)]
    return place(pieces, parts, shapes, blocks)


def place_second(pieces, parts, count):
    planes, rows, columns = pieces[0].shape
    half, fine, width = rows // 2, rows // 4, columns // 2

    def put(side):
        return lambda outs, plane, member: outs[1].at[plane, member, side]

    shapes = [(planes, 2, count, fine, columns), (planes, count, 2, half, width)]
    blocks = [(side * fine, fine, 0, columns, put_pair(side)) for side in range(2)]
    blocks += [(half, half, side * width, width, put(side)) for side in range(2)]
    return place(pieces, parts, shapes, blocks)


def gather_planes(piece, *earlier, beside=()):
    column, sent, step = piece[None], list(earlier), lax.axis_size("fsdp") // 4
    while step:
        got = swap(after(column, *sent[-1:], *(beside if len(sent) > len(earlier) else ())), "fsdp", 2 * step)
        sent.append(got)
        column = jnp.stack([column, got], 1).reshape((-1,) + piece.shape)
        step //= 2
    return column, sent[len(earlier) :]


def gather_neighbours(column, earlier):
    held = {0: [column]}
    for bit in range(lax.axis_size("rep").bit_length() - 1):
        held[1 << bit] = [swap(after(column, *earlier), "rep", 1 << bit)]
    return held, [held[k][0] for k in held if k]


def gather_members(held, beside):
    count, rows = lax.axis_size("rep"), held[0][0].shape[1] // 2
    earlier = [held[k][0] for k in held if k] + list(beside)
    for level in range(1, count.bit_length() - 1):
        sent = []
        for k in range(1, count):
            if bin(k).count("1") != level + 1:
                continue
            held[k] = []
            for half, last in ((0, k & -k), (1, 1 << (k.bit_length() - 1))):
                source = held[k ^ last]
                if len(source) == 1:
                    source = source[0][:, half * rows : (half + 1) * rows]
                else:
                    source = source[half]
                held[k].append(swap(after(source, *earlier), "rep", last))
            sent += held[k]
        earlier = sent
    arrays, parts = [], []
    for k in range(count):
        for half, array in enumerate(held[k]):
            arrays.append(array)
            parts.append((k, (0, 1) if len(held[k]) == 1 else (half,)))
    return arrays, parts, earlier


def message_pieces(shards):
    heads, expand = column_pieces((shards[2], shards[10]))
    pieces = []
    for layer in range(LAYERS):
        output, shrink = quarter(shards[5][layer]), quarter(shards[12][layer])
        half = output.shape[1] // 2
        packed = jnp.concatenate([output[:, :half], output[:, half:]], 0)
        pieces.append(jnp.concatenate([heads[layer], packed], 1))
        half = shrink.shape[0] // 2
        packed = jnp.concatenate([shrink[:half], shrink[half:]], 1)
        pieces.append(jnp.concatenate([expand[layer], packed], 0))
    return pieces


def quarter(param):
    rows = param.shape[0] // lax.axis_size("rep")
    return lax.dynamic_slice_in_dim(param, lax.axis_index("rep") * rows, rows, 0)


def gather_small(all_params, token):
    packed = after(jnp.concatenate([all_params[i] for i in SMALL], 1), token)
    whole, owner, step = packed[None], lax.axis_index("fsdp"), 1
    while step < lax.axis_size("fsdp"):
        got = swap(whole, "fsdp", step)
        whole = jnp.where(
            (owner // step) % 2 == 0,
            jnp.concatenate([whole, got], 0),
            jnp.concatenate([got, whole], 0),
        )
        step *= 2
    vectors, start = [], 0
    for i in SMALL:
        size = all_params[i].shape[1]
        vectors.append(
            jnp.moveaxis(whole[:, :, start : start + size], 0, 1).reshape(LAYERS, -1)
        )
        start += size
    return vectors


def link_orders():
    bits = list(range(lax.axis_size("rep").bit_length() - 1))
    return [bits, bits[::-1]]


def divide(blocks, shapes, bits, outs):
    for side in range(len(shapes)):
        high, later = shapes[side]
        for i in range(high):
            for j in range(later):
                base = 2 * i * later + j
                for out_ref, index in (
                    (outs[2 * side], base + bits[side] * later),
                    (outs[2 * side + 1], base + (1 - bits[side]) * later),
                ):
                    for row, column, block in blocks(side, index):
                        out_ref[
                            0, i, j, row : row + block.shape[0], column : column + block.shape[1]
                        ] = block


def block_grad_kernel(shapes, where_ref, left_ref, grad_ref, more_ref, other_ref, *refs):
    outs, held, extra = refs[:-2], refs[-2], refs[-1]
    held[...] = low(weight_dot(left_ref[...], grad_ref[...])).reshape(held.shape)
    extra[...] = low(weight_dot(more_ref[...], other_ref[...])).reshape(extra.shape)
    rows, half, tall = held.shape[2], held.shape[3] // 2, extra.shape[1] // 2

    def blocks(side, index):
        return [
            (p * rows, 0, held[p, index, :, side * half : (side + 1) * half]) for p in range(2)
        ] + [(2 * rows, 0, extra[index, side * tall : (side + 1) * tall])]

    divide(blocks, shapes, (where_ref[0], where_ref[1]), outs)


def mixed_grad_kernel(shapes, where_ref, left_ref, grad_ref, more_ref, other_ref, *refs):
    outs, held, extra = refs[:4], refs[4], refs[5]
    held[...] = low(weight_dot(left_ref[...], grad_ref[...])).reshape(held.shape)
    extra[...] = low(weight_dot(more_ref[...], other_ref[...])).reshape(extra.shape)
    rows, rest = held.shape[2], extra.shape[2] // 2
    half = (held.shape[3] + rest) // 2

    def blocks(side, index):
        if side == 0:
            return [(p * rows, 0, held[p, index, :, :half]) for p in range(2)]
        return [(p * rows, 0, held[p, index, :, half:]) for p in range(2)] + [
            (p * rows, half - rest, extra[index, :, p * rest : (p + 1) * rest]) for p in range(2)
        ]

    divide(blocks, shapes, (where_ref[0], where_ref[1]), outs)


def grad_call(kernel, arrays, widths, rows, columns, scratch, orders):
    planes, count = lax.axis_size("fsdp") // 2, lax.axis_size("rep")
    member = lax.axis_index("rep")
    shapes = tuple((count >> (order[0] + 1), 1 << order[0]) for order in orders)
    tokens = arrays[0].shape[0]
    specs = []
    for array, width in zip(arrays, widths):
        if width is None:
            specs.append(pl.BlockSpec(array.shape, lambda z, where: (0, 0)))
        else:
            specs.append(pl.BlockSpec((tokens, width), lambda z, where: (0, z)))
    out_shapes, out_specs = [], []
    for high, later in shapes:
        block = (high, later, rows, columns // len(orders))
        out_specs += [pl.BlockSpec((1,) + block, lambda z, where: (z, 0, 0, 0, 0))] * 2
        out_shapes += [jax.ShapeDtypeStruct((planes,) + block, jnp.bfloat16)] * 2
    return pl.pallas_call(
        functools.partial(kernel, shapes),
        out_shape=out_shapes,
        grid_spec=pltpu.PrefetchScalarGridSpec(
            num_scalar_prefetch=1,
            grid=(planes,),
            in_specs=specs,
            out_specs=out_specs,
            scratch_shapes=[pltpu.VMEM(size, jnp.bfloat16) for size in scratch],
        ),
        compiler_params=params(40),
        cost_estimate=estimate(5, 0),
    )(scalars(*[(member >> order[0]) & 1 for order in orders]), *arrays)


def block_grad(left, grad, more, other, orders):
    planes, count = lax.axis_size("fsdp") // 2, lax.axis_size("rep")
    widths = left.shape[1] // planes, more.shape[1] // planes
    columns = grad.shape[1]
    rows, tall = widths[0] // (2 * count), widths[1] // count
    return grad_call(
        block_grad_kernel, (left, grad, more, other), (widths[0], None, widths[1], None),
        2 * rows + tall // 2, columns,
        [(2, count, rows, columns), (count, tall, other.shape[1])], orders,
    )


def mixed_grad(left, grad, more, other, orders):
    planes, count = lax.axis_size("fsdp") // 2, lax.axis_size("rep")
    widths = left.shape[1] // planes, more.shape[1] // planes
    columns, rest = grad.shape[1], other.shape[1]
    rows = widths[1] // count
    if widths[1] % 128:
        first = low(weight_dot(left, grad)).reshape(planes, 2, count, rows, columns)
        second = low(weight_dot(more, other)).reshape(planes, count, rows, 2, rest // 2)
        total = jnp.concatenate([jnp.swapaxes(first, 1, 2), jnp.swapaxes(second, 2, 3)], 4)
        total = total.reshape(planes, count, 2 * rows, -1)
        half, member = total.shape[3] // 2, lax.axis_index("rep")
        top = count // 2
        left_part = total[..., :half].reshape(planes, top, 2, 1, 2 * rows, half)
        right_part = total[..., half:].reshape(planes, 1, 2, top, 2 * rows, half)
        sides = member % 2, member // top
        return [
            pick(part, side if kept else 1 - side, 2)
            for part, side in zip((left_part, right_part), sides)
            for kept in (True, False)
        ]
    return grad_call(
        mixed_grad_kernel, (left, grad, more, other), (widths[0], None, widths[1], None),
        2 * rows, columns + rest // 2,
        [(2, count, rows, columns), (count, rows, rest)], orders,
    )


def split_kernel(where_ref, *refs):
    count = len(refs) // 4
    for n in range(count):
        bit = where_ref[n]
        keep_in, got_ref = refs[2 * n], refs[2 * n + 1]
        keep_ref, send_ref = refs[2 * (count + n)], refs[2 * (count + n) + 1]
        keep_ref[0] = low(widen(keep_in[0, bit]) + widen(got_ref[0, bit]))
        send_ref[0] = low(widen(keep_in[0, 1 - bit]) + widen(got_ref[0, 1 - bit]))


def add_split(pairs, later, sides, rows):
    if len({pair[0].size // n for pair, n in zip(pairs, later)}) > 1:
        return [
            out
            for pair, n, side in zip(pairs, later, sides)
            for out in add_split([pair], [n], [side], rows)
        ]
    arrays, in_specs, out_specs, out_shapes = [], [], [], []
    for pair, n in zip(pairs, later):
        columns = pair[0].shape[-1]
        for array in pair:
            arrays.append(array.reshape(-1, 2, n, rows, columns))
            in_specs.append(
                pl.BlockSpec((1, 2, n, rows, columns), lambda i, where: (i, 0, 0, 0, 0))
            )
            out_specs.append(pl.BlockSpec((1, n, rows, columns), lambda i, where: (i, 0, 0, 0)))
            out_shapes.append(
                jax.ShapeDtypeStruct((arrays[-1].shape[0], n, rows, columns), jnp.bfloat16)
            )
    return pl.pallas_call(
        split_kernel,
        out_shape=out_shapes,
        grid_spec=pltpu.PrefetchScalarGridSpec(
            num_scalar_prefetch=1,
            grid=(arrays[0].shape[0],),
            in_specs=in_specs,
            out_specs=out_specs,
        ),
        compiler_params=params(24),
        cost_estimate=estimate(0, sum(array.size for array in arrays) * 3),
    )(scalars(*sides), *arrays)


def merge_kernel(where_ref, *refs):
    arrays, (keep_ref, send_ref) = refs[:-2], refs[-2:]
    half = arrays[0].shape[-1]
    for out_ref, bit in ((keep_ref, where_ref[0]), (send_ref, 1 - where_ref[0])):
        start = 0
        for n in range(0, len(arrays), 4):
            left_ref, left_got, right_ref, right_got = arrays[n : n + 4]
            rows = slice(start, start + left_ref.shape[2])
            out_ref[0, rows, :half] = low(widen(left_ref[0, bit]) + widen(left_got[0, bit]))
            out_ref[0, rows, half:] = low(widen(right_ref[0, bit]) + widen(right_got[0, bit]))
            start += left_ref.shape[2]


def add_merge(messages, side):
    half = messages[0][0].shape[-1]
    arrays, specs, total = [], [], 0
    for message in messages:
        rows = message[0].shape[-2]
        arrays += [array.reshape(-1, 2, rows, half) for array in message]
        specs += [pl.BlockSpec((1, 2, rows, half), lambda i, where: (i, 0, 0, 0))] * 4
        total += rows
    high = arrays[0].shape[0]
    given = pl.BlockSpec((1, total, 2 * half), lambda i, where: (i, 0, 0))
    shape = jax.ShapeDtypeStruct((high, total, 2 * half), jnp.bfloat16)
    return pl.pallas_call(
        merge_kernel,
        out_shape=[shape, shape],
        grid_spec=pltpu.PrefetchScalarGridSpec(
            num_scalar_prefetch=1,
            grid=(high,),
            in_specs=specs,
            out_specs=[given, given],
        ),
        compiler_params=params(24),
        cost_estimate=estimate(0, sum(array.size for array in arrays) * 3),
    )(scalars(side), *arrays)


def reduce_members(arrays):
    member, lanes = lax.axis_index("rep"), range(2)
    rows, orders = arrays[0].shape[-2], link_orders()
    bits = [sorted(order) for order in orders]
    keeps, sends = list(arrays[::2]), list(arrays[1::2])
    for n in range(len(orders[0])):
        gots = [swap(sends[i], "rep", 1 << orders[i][n]) for i in lanes]
        for i in lanes:
            bits[i].remove(orders[i][n])
        token = yield sends, gots
        gots = [after(got, token) for got in gots]
        if n + 1 < len(orders[0]):
            later = [1 << bits[i].index(orders[i][n + 1]) for i in lanes]
            sides = [(member >> orders[i][n + 1]) & 1 for i in lanes]
            outs = add_split(list(zip(keeps, gots)), later, sides, rows)
            keeps, sends = list(outs[::2]), list(outs[1::2])
    return [keeps[0], gots[0], keeps[1], gots[1]]


def reduce_planes(messages):
    plane, planes = position()[0], lax.axis_size("fsdp") // 2
    rows = sum(message[0].shape[-2] for message in messages)
    keep, send = add_merge(messages, plane % 2)
    step = 1
    while True:
        got = swap(send, "fsdp", 2 * step)
        token = yield [send], [got]
        got = after(got, token)
        step *= 2
        if step == planes:
            return low(widen(keep) + widen(got)).reshape(rows, -1)
        keep, send = add_split([(keep, got)], [1], [(plane // step) % 2], rows)


def finish_columns(total, columns):
    core = position()[1]
    rows = total.shape[0] // 2
    part = total[:, :columns].reshape(2, rows, columns)
    got = swap(pick(part, 1 - core, 0), "fsdp", 1)
    part = jnp.concatenate([pick(part, core, 0), got], 0)
    return jnp.concatenate([part, total[:, columns:]], 1)


def spread(own, low_last):
    pieces = [own]
    for k in range(1, lax.axis_size("rep")):
        last = k & -k if low_last else 1 << (k.bit_length() - 1)
        pieces.append(swap(pieces[k ^ last], "rep", last))
    return pieces


def column_out(out_ref, block, side, ref, start):
    rows = out_ref.shape[2]
    for i in range(out_ref.shape[3] // block):
        first = start if i % 2 == side else start + rows
        out_ref[0, 0, :, i * block : (i + 1) * block] = widen(
            ref[first : first + rows, (i // 2) * block : (i // 2 + 1) * block]
        )


def early_out_kernel(block, where_ref, *refs):
    expand_out, shrink_out = refs[-2:]
    for k, ref in enumerate(refs[:-4]):
        for side in range(2):

            @pl.when((pl.program_id(0) == k) & (where_ref[1] == side))
            def _():
                column_out(expand_out, block, side, ref, 0)

        @pl.when(pl.program_id(0) == k)
        def _():
            rows, columns = shrink_out.shape[2] // 2, shrink_out.shape[3]
            start = ref.shape[0] - rows
            shrink_out[0, 0, :rows] = widen(ref[start:, :columns])
            shrink_out[0, 0, rows:] = widen(ref[start:, columns:])


def late_out_kernel(block, where_ref, *refs):
    heads_out, output_out = refs[-2:]
    for k, ref in enumerate(refs[:-4]):
        for side in range(2):

            @pl.when((pl.program_id(0) == k) & (where_ref[1] == side))
            def _():
                column_out(heads_out, block, side, ref, 0)

        @pl.when(pl.program_id(0) == k)
        def _():
            rows, half = output_out.shape[2], output_out.shape[3] // 2
            start = ref.shape[1] - half
            output_out[0, 0, :, :half] = widen(ref[:rows, start:])
            output_out[0, 0, :, half:] = widen(ref[rows:, start:])


def write_out(kernel, layer, pieces, sizes, earlier):
    plane, core, member = position()
    count = len(pieces)
    shapes = [(LAYERS, count) + size for size in sizes]
    if earlier is None:
        earlier = [jnp.zeros((8, 128), jnp.float32)] * len(sizes)
        aliases = {}
    else:
        earlier = [array.reshape(shape) for array, shape in zip(earlier, shapes)]
        aliases = {1 + count + i: i for i in range(len(sizes))}
    return pl.pallas_call(
        kernel,
        out_shape=[jax.ShapeDtypeStruct(shape, jnp.float32) for shape in shapes],
        grid_spec=pltpu.PrefetchScalarGridSpec(
            num_scalar_prefetch=1,
            grid=(count,),
            in_specs=[pl.BlockSpec(piece.shape, lambda k, where: (0, 0)) for piece in pieces]
            + [pl.BlockSpec(memory_space=pl.ANY)] * len(sizes),
            out_specs=[
                pl.BlockSpec((1, 1) + size, lambda k, where: (layer, k ^ where[0], 0, 0))
                for size in sizes
            ],
        ),
        input_output_aliases=aliases,
        compiler_params=params(24),
        cost_estimate=estimate(0, count * pieces[0].size * 6),
    )(scalars(member, core), *pieces, *earlier)


def reduce_small(grads, earlier):
    owners, count = lax.axis_size("fsdp"), lax.axis_size("rep")
    total = jnp.concatenate([g.reshape(LAYERS, owners, -1) for g in grads], 2)
    total = after(total, *earlier)
    owner = lax.axis_index("fsdp")
    step = owners // 2
    while step:
        total = total.reshape(LAYERS, 2, step, -1)
        mine = (owner // step) % 2
        total = pick(total, mine, 1) + swap(pick(total, 1 - mine, 1), "fsdp", step)
        step //= 2
    step = 1
    while step < count:
        total = total + swap(total, "rep", step)
        step *= 2
    total = total.reshape(LAYERS, -1)
    outs, start = [], 0
    for g in grads:
        size = g.shape[1] // owners
        outs.append(total[:, start : start + size])
        start += size
    return outs


def other_half(rows):
    return swap(rows, "fsdp", lax.axis_size("fsdp") // 2)


def image_side():
    return lax.axis_index("fsdp") // (lax.axis_size("fsdp") // 2)


def regroup(blocks):
    side = image_side()
    return pick(blocks, side, 0), other_half(pick(blocks, 1 - side, 0))


def ungroup(rows, got):
    own, got = rows[: rows.shape[0] // 2], got.astype(rows.dtype)
    return jnp.where(image_side() == 0, jnp.stack([own, got]), jnp.stack([got, own]))


def chips_per_image():
    return lax.axis_size("fsdp") // 4


def share_rows(local_kv):
    shared = [local_kv]
    for k in range(1, chips_per_image()):
        low_bit = k & -k
        shared.append(swap(shared[k ^ low_bit], "fsdp", 2 * low_bit))
    return shared


def collect_rows(own, others):
    chips = chips_per_image()
    if chips == 2:
        got = swap(others, "fsdp", 2)
        return low(widen(own) + widen(got)), got
    total = jnp.concatenate([own, others], 1)
    while chips > 1:
        rows = total.shape[1] // 2
        got = swap(total[:, rows:], "fsdp", chips)
        total = low(widen(total[:, :rows]) + widen(got))
        chips //= 2
    return total, got


def both_cores(rows):
    return jnp.concatenate([rows, swap(rows, "fsdp", 1)], 0)


def one_head(tensor, head):
    half = tensor.shape[1] // 2
    lane = lax.broadcasted_iota(jnp.int32, tensor.shape, 1)
    keep = lane < half if head == 0 else lane >= half
    return jnp.where(keep, tensor, jnp.zeros_like(tensor))


def join(refs, held):
    start = 0
    for ref in refs:
        held[start : start + ref.shape[0], :] = ref[...]
        start += ref.shape[0]
    return held[...]


def attend_kernel(factor, parts, query_ref, *refs):
    out_ref, log_ref, held_keys, held_values = refs[2 * parts :]
    keys, values = join(refs[:parts], held_keys), join(refs[parts : 2 * parts], held_values)
    results, logs = [], []
    for head in range(2):
        scores = input_dot(one_head(query_ref[...], head), keys)
        largest = jnp.max(scores, -1, keepdims=True)
        weights = jnp.exp2((scores - largest) * factor)
        total = jnp.sum(weights, -1, keepdims=True)
        results.append(forward_dot(low(weights), values) / total)
        logs.append(largest * factor + jnp.log2(total))
    out_ref[...] = low(one_head(results[0], 0) + one_head(results[1], 1))
    shape = log_ref.shape
    log_ref[...] = one_head(jnp.broadcast_to(logs[0], shape), 0) + one_head(
        jnp.broadcast_to(logs[1], shape), 1
    )


def pair_block(rows, start):
    return pl.BlockSpec((rows, 128), lambda i: (0, start + i))


def kv_parts(projected, others):
    pairs = projected.shape[1] // 384
    if projected.shape[0] % 16:
        others = [jnp.concatenate([projected[:, 128 * pairs :]] + others, 0)]
        parts = []
    else:
        parts = [(projected, pairs, 2 * pairs)]
    return parts + [(other, 0, pairs) for other in others]


def kv_specs(parts, first=0):
    keys = [pair_block(array.shape[0], first + start) for array, start, unused in parts]
    values = [pair_block(array.shape[0], first + start) for array, unused, start in parts]
    rows = sum(array.shape[0] for array, unused, more in parts)
    held = [pltpu.VMEM((rows, 128), jnp.bfloat16)] * 2
    return keys + values, [array for array, unused, more in parts] * 2, held


def attend(projected, others, head_size):
    tokens, width = projected.shape[0], projected.shape[1] // 3
    pairs = width // 128
    parts = kv_parts(projected, others)
    specs, arrays, held = kv_specs(parts)
    factor = head_size ** (-0.5) * math.log2(math.e)
    return pl.pallas_call(
        functools.partial(attend_kernel, factor, len(parts)),
        out_shape=[
            jax.ShapeDtypeStruct((tokens, width), jnp.bfloat16),
            jax.ShapeDtypeStruct((tokens, width), jnp.float32),
        ],
        grid=(pairs,),
        in_specs=[pair_block(tokens, 0)] + specs,
        out_specs=[pair_block(tokens, 0), pair_block(tokens, 0)],
        scratch_shapes=held,
        compiler_params=params(56),
        cost_estimate=estimate(18, 0),
    )(projected, *arrays)


def attend_back_kernel(factor, scale, parts, query_ref, *refs):
    log_ref, grad_ref, dq_ref, own_ref, others_ref, held_keys, held_values = refs[2 * parts :]
    keys, values = join(refs[:parts], held_keys), join(refs[parts : 2 * parts], held_values)
    d_query, d_key, d_value = [], 0.0, 0.0
    for head in range(2):
        query = one_head(query_ref[...], head)
        grad = one_head(grad_ref[...], head)
        half = query.shape[1] // 2
        log_total = log_ref[:, head * half : head * half + 1]
        probs = jnp.exp2(input_dot(query, keys) * factor - log_total)
        products = probs * input_dot(grad, values)
        d_scores = low(products - probs * jnp.sum(products, -1, keepdims=True))
        d_query.append(forward_dot(d_scores, keys))
        d_key = d_key + weight_dot(d_scores, query)
        d_value = d_value + weight_dot(low(probs), grad)
    dq_ref[...] = low((one_head(d_query[0], 0) + one_head(d_query[1], 1)) * scale)
    rows = own_ref.shape[1]
    for i, total in enumerate((low(d_key * scale), low(d_value))):
        own_ref[i] = total[:rows]
        others_ref[i] = total[rows:]


def attend_back(projected, others, log_total, d_attended, head_size, first, pairs):
    tokens, width = d_attended.shape[0], 128 * pairs
    parts = kv_parts(projected, others)
    specs, arrays, held = kv_specs(parts, first)
    rows = held[0].shape[0]
    scale = head_size ** (-0.5)
    own, taken = pair_block(tokens, 0), pair_block(tokens, first)
    return pl.pallas_call(
        functools.partial(attend_back_kernel, scale * math.log2(math.e), scale, len(parts)),
        out_shape=[
            jax.ShapeDtypeStruct((tokens, width), jnp.bfloat16),
            jax.ShapeDtypeStruct((2, tokens, width), jnp.bfloat16),
            jax.ShapeDtypeStruct((2, rows - tokens, width), jnp.bfloat16),
        ],
        grid=(pairs,),
        in_specs=[taken] + specs + [taken, taken],
        out_specs=[
            own,
            pl.BlockSpec((2, tokens, 128), lambda i: (0, 0, i)),
            pl.BlockSpec((2, rows - tokens, 128), lambda i: (0, 0, i)),
        ],
        scratch_shapes=held,
        compiler_params=params(60),
        cost_estimate=estimate(8 * pairs, 0),
    )(projected, *arrays, log_total, d_attended)


def add_tile(part, own_ref, other_ref, total_ref):
    @pl.when(pl.program_id(0) == 0)
    def _():
        total_ref[...] = part

    @pl.when(pl.program_id(0) > 0)
    def _():
        total_ref[...] += part

    @pl.when(pl.program_id(0) == pl.num_programs(0) - 1)
    def _():
        half = own_ref.shape[0]
        own_ref[...] = total_ref[:half]
        other_ref[...] = low(total_ref[half:])


def expand_kernel(
    rows_ref, expand_ref, bias_ref, shrink_ref, active_ref, slope_ref, own_ref, other_ref, total_ref
):
    hidden = forward_dot(rows_ref[...], expand_ref[...]) + bias_ref[...]
    normal = 0.5 + 0.5 * lax.erf(hidden * math.sqrt(0.5))
    density = jnp.exp2(hidden * hidden * (-0.5 * math.log2(math.e)))
    slope_ref[...] = low(normal + hidden * density * (1.0 / math.sqrt(2.0 * math.pi)))
    active = low(hidden * normal)
    active_ref[...] = active
    add_tile(forward_dot(active, shrink_ref[...]), own_ref, other_ref, total_ref)


def feed_forward(rows_in, expand, expand_bias, shrink):
    tokens, width = rows_in.shape
    units = expand.shape[1]
    tile = 512
    whole = pl.BlockSpec((tokens, width), lambda i: (0, 0))
    half = pl.BlockSpec((tokens // 2, width), lambda i: (0, 0))
    part = pl.BlockSpec((tokens, tile), lambda i: (0, i))
    return pl.pallas_call(
        expand_kernel,
        out_shape=[
            jax.ShapeDtypeStruct((tokens, units), jnp.bfloat16),
            jax.ShapeDtypeStruct((tokens, units), jnp.bfloat16),
            jax.ShapeDtypeStruct((tokens // 2, width), jnp.float32),
            jax.ShapeDtypeStruct((tokens // 2, width), jnp.bfloat16),
        ],
        grid=(units // tile,),
        in_specs=[
            whole,
            pl.BlockSpec((width, tile), lambda i: (0, i)),
            pl.BlockSpec((1, tile), lambda i: (0, i)),
            pl.BlockSpec((tile, width), lambda i: (i, 0)),
        ],
        out_specs=[part, part, half, half],
        scratch_shapes=[pltpu.VMEM((tokens, width), jnp.float32)],
        compiler_params=params(32),
        cost_estimate=estimate(14, 0),
    )(rows_in, expand, expand_bias[None], shrink)


def shrink_kernel(
    grad_ref, shrink_ref, slope_ref, expand_ref, hidden_ref, bias_ref, own_ref, other_ref, total_ref
):
    d_hidden = low(input_dot(grad_ref[...], shrink_ref[...]) * widen(slope_ref[...]))
    hidden_ref[...] = d_hidden
    bias_ref[...] = jnp.sum(widen(d_hidden), 0, keepdims=True)
    add_tile(input_dot(d_hidden, expand_ref[...]), own_ref, other_ref, total_ref)


def feed_back(d_mlp, shrink, slope, expand):
    tokens, width = d_mlp.shape
    units = expand.shape[1]
    tile = 512
    whole = pl.BlockSpec((tokens, width), lambda i: (0, 0))
    half = pl.BlockSpec((tokens // 2, width), lambda i: (0, 0))
    part = pl.BlockSpec((tokens, tile), lambda i: (0, i))
    return pl.pallas_call(
        shrink_kernel,
        out_shape=[
            jax.ShapeDtypeStruct((tokens, units), jnp.bfloat16),
            jax.ShapeDtypeStruct((1, units), jnp.float32),
            jax.ShapeDtypeStruct((tokens // 2, width), jnp.float32),
            jax.ShapeDtypeStruct((tokens // 2, width), jnp.bfloat16),
        ],
        grid=(units // tile,),
        in_specs=[
            whole,
            pl.BlockSpec((tile, width), lambda i: (i, 0)),
            part,
            pl.BlockSpec((width, tile), lambda i: (0, i)),
        ],
        out_specs=[part, pl.BlockSpec((1, tile), lambda i: (0, i)), half, half],
        scratch_shapes=[pltpu.VMEM((tokens, width), jnp.float32)],
        compiler_params=params(32),
        cost_estimate=estimate(9, 0),
    )(d_mlp, shrink, slope, expand)


def core_half(vector):
    core = position()[1]
    return pick(widen(vector).reshape(lax.axis_size("fsdp") // 2, 2, -1), core, 1).reshape(-1)


def core_fill(half):
    parts = half.reshape(lax.axis_size("fsdp") // 2, -1)
    return by_core(parts, jnp.zeros_like(parts), 1).reshape(-1)


def normed_rows(tok_rows, gathered):
    return both_cores(low(layer_norm(tok_rows, widen(gathered[0]), widen(gathered[1]))))


def project(normed, gathered, token):
    heads_weight, query_bias, value_bias = gathered[2], gathered[3], gathered[4]
    width = normed.shape[1]
    bias_row = jnp.concatenate(
        [core_half(query_bias), jnp.zeros((width // 2,), jnp.float32), core_half(value_bias)]
    )
    projected = low(forward_dot(normed, heads_weight) + bias_row)
    return projected, share_rows(after(projected[:, width // 2 :], token))[1:]


def forward_layer(tok_rows, normed, projected, others, gathered, beside, neighbours, planes):
    (
        attn_norm_gain,
        attn_norm_bias,
        heads_weight,
        query_bias,
        value_bias,
        output_weight,
        output_bias,
        attn_layerscale,
        mlp_norm_gain,
        mlp_norm_bias,
        expand_weight,
        expand_bias,
        shrink_weight,
        shrink_bias,
        mlp_layerscale,
    ) = gathered
    tokens, width = tok_rows.shape
    attended, log_total = attend(projected, others, width // HEADS)
    attended = after(attended, *beside)
    got = swap(low(forward_dot(attended[tokens:], output_weight)), "fsdp", 1)
    branch = forward_dot(attended[:tokens], output_weight) + widen(got) + widen(output_bias)
    middle = tok_rows + widen(attn_layerscale) * branch
    normed_two = low(layer_norm(middle, widen(mlp_norm_gain), widen(mlp_norm_bias)))
    normed_two = both_cores(after(normed_two, *planes[:1]))
    activated, slope, own_sum, other_sum = feed_forward(
        normed_two, expand_weight, core_half(expand_bias), shrink_weight
    )
    other_sum = after(other_sum, *neighbours, *planes[1:])
    mlp_out = own_sum + widen(swap(other_sum, "fsdp", 1)) + widen(shrink_bias)
    result = middle + widen(mlp_layerscale) * mlp_out
    saved = (
        tok_rows,
        normed,
        projected,
        others,
        log_total,
        attended,
        branch,
        middle,
        normed_two,
        slope,
        activated,
        mlp_out,
    )
    return (result, saved)


class Later:
    def __init__(self):
        self.running, self.done, self.sends, self.gots = {}, {}, {}, {}

    def begin(self, name, kernel, arrays):
        self.running[name] = reduce_members(kernel(*arrays, link_orders()))
        self.step(name, None)

    def join(self, name, parts, token):
        for part in parts:
            while part in self.running:
                self.step(part, token)
        self.running[name] = reduce_planes([self.done[part] for part in parts])
        self.step(name, None)

    def step(self, name, token):
        try:
            self.sends[name], self.gots[name] = self.running[name].send(token)
        except StopIteration as end:
            self.done[name] = end.value
            self.sends[name] = self.gots[name] = []
            del self.running[name]

    def sent(self, value, *names):
        return after(value, *[array for name in names for array in self.sends[name]])

    def came(self, value, *names):
        return after(value, *[array for name in names for array in self.gots[name]])


def backward_layer(d_result, saved, gathered, later, new, old, activation_got):
    (
        attn_norm_gain,
        attn_norm_bias,
        heads_weight,
        query_bias,
        value_bias,
        output_weight,
        output_bias,
        attn_layerscale,
        mlp_norm_gain,
        mlp_norm_bias,
        expand_weight,
        expand_bias,
        shrink_weight,
        shrink_bias,
        mlp_layerscale,
    ) = gathered
    (
        tok_rows,
        normed,
        projected,
        others,
        log_total,
        attended,
        branch,
        middle,
        normed_two,
        slope,
        activated,
        mlp_out,
    ) = saved
    tokens, width = tok_rows.shape
    d_mlp = low(d_result * widen(mlp_layerscale))
    d_mlp_both = both_cores(d_mlp)
    g_mlp_scale = jnp.sum(d_result * mlp_out, 0)
    g_shrink_bias = column_sum(d_mlp)
    d_hidden, g_expand_bias, own_sum, other_sum = feed_back(
        d_mlp_both, shrink_weight, slope, expand_weight
    )
    block, mixed, block_planes, mixed_planes = new
    if old:
        other_sum = later.came(other_sum, old[0])
        later.join(old[2], [old[0]], other_sum)
        d_hidden = later.sent(d_hidden, old[2])
    got = swap(other_sum, "fsdp", 1)
    later.begin(block, block_grad, (normed_two, d_hidden, activated, d_mlp_both))
    own_sum = later.sent(own_sum, block)
    if not old:
        own_sum = after(own_sum, activation_got)
    if old:
        own_sum = later.came(own_sum, old[1])
        later.step(old[1], own_sum)
        own_sum = later.sent(own_sum, old[1])
    d_middle_norm, g_mlp_gain, g_mlp_shift = norm_back(
        middle, widen(mlp_norm_gain), widen(mlp_norm_bias), own_sum + widen(got)
    )
    d_middle = d_result + d_middle_norm
    d_branch = low(d_middle * widen(attn_layerscale))
    d_branch_both = both_cores(d_branch)
    g_attn_scale = jnp.sum(d_middle * branch, 0)
    g_output_bias = column_sum(d_branch)
    d_attended = low(input_dot(d_branch_both, output_weight))
    pairs = d_attended.shape[1] // 128

    def back(first):
        return attend_back(
            projected, others, log_total, d_attended, width // HEADS, first, pairs // 2
        )

    first_query, d_own, d_others = back(0)
    first_kv, first_got = collect_rows(d_own, d_others)
    if old:
        d_attended = later.came(d_attended, old[2])
        later.step(old[2], first_query)
        d_attended = later.sent(d_attended, old[2])
    second_query, d_own, d_others = back(pairs // 2)
    d_others = after(d_others, first_got)
    if old:
        d_others = later.came(d_others, old[2])
    second_kv, second_got = collect_rows(d_own, d_others)
    second_query = later.came(second_query, block)
    later.step(block, second_query)
    second_query = later.sent(second_query, block)
    d_query = jnp.concatenate([first_query, second_query], 1)
    d_key = jnp.concatenate([first_kv[0], second_kv[0]], 1)
    d_value = jnp.concatenate([first_kv[1], second_kv[1]], 1)
    d_projected = jnp.concatenate([d_query, d_key, d_value], 1)
    g_query_bias = column_sum(d_query)
    g_value_bias = column_sum(d_value)
    got = swap(low(input_dot(d_projected[tokens:], heads_weight)), "fsdp", 1)
    later.begin(mixed, mixed_grad, (normed, d_projected, attended, d_branch_both))
    d_projected = later.sent(d_projected, mixed)
    if old:
        later.join(old[3], [old[1]], d_projected)
        d_projected = later.sent(d_projected, old[3])
        later.join(block_planes, [block], d_projected)
        d_projected = later.sent(d_projected, block_planes)
    d_normed = input_dot(d_projected[:tokens], heads_weight) + widen(got)
    d_rows_norm, g_attn_gain, g_attn_shift = norm_back(
        tok_rows, widen(attn_norm_gain), widen(attn_norm_bias), d_normed
    )
    d_rows = d_middle + d_rows_norm
    small_grads = (
        g_attn_gain,
        g_attn_shift,
        core_fill(g_query_bias),
        core_fill(g_value_bias),
        g_output_bias,
        g_attn_scale,
        g_mlp_gain,
        g_mlp_shift,
        core_fill(g_expand_bias),
        g_shrink_bias,
        g_mlp_scale,
    )
    return (d_rows, small_grads)


def local(images, cotangent, *all_params):
    owners, count = lax.axis_size("fsdp"), lax.axis_size("rep")
    pieces = message_pieces(all_params)
    column, planes = gather_planes(pieces[0])
    own, got = regroup(after(images, planes[0]))
    tok_rows = widen(jnp.concatenate([own, got], 0))
    column = after(column, got)
    next_column, next_planes = gather_planes(pieces[1], got)
    small = gather_small(all_params, got)
    held, neighbours = gather_neighbours(column, [])
    saved_layers, fetched = [], []
    for layer in range(LAYERS):
        gathered = [None] * len(all_params)
        for i, vector in zip(SMALL, small):
            gathered[i] = vector[layer]
        normed = normed_rows(tok_rows, gathered)
        arrays, parts, earlier = gather_members(held, [])
        arrays[0] = after(arrays[0], next_planes[-1])
        gathered[2], gathered[5] = place_first(
            arrays, parts, count, all_params[2].shape[2] // 2
        )
        projected, others = project(normed, gathered, next_planes[-1])
        held, neighbours = gather_neighbours(next_column, earlier)
        if layer + 1 < LAYERS:
            column, planes = gather_planes(pieces[2 * layer + 2], others[-1])
            beside = planes[:1]
        else:
            own, got = regroup(after(cotangent, others[-1]))
            d_rows = widen(jnp.concatenate([own, got], 0))
            beside, planes, neighbours, next_planes = [got], [], [], []
        arrays, parts, earlier = gather_members(held, [])
        arrays[0] = after(arrays[0], *planes[-1:])
        if layer + 1 < LAYERS:
            next_column, next_planes = gather_planes(pieces[2 * layer + 3], planes[-1])
            held, neighbours = gather_neighbours(column, earlier)
        gathered[10], gathered[12] = place_second(arrays, parts, count)
        fetched.append(tuple(gathered))
        tok_rows, saved = forward_layer(
            tok_rows, normed, projected, others, gathered, beside, neighbours, next_planes
        )
        saved_layers.append(saved)
    activation_rows = low(tok_rows)
    small_grads = [None] * LAYERS
    outs = {}

    def size(i):
        return (all_params[i].shape[1] // count, all_params[i].shape[2])

    def block_piece(later, layer):
        total = later.done[layer, 2]
        half = total.shape[0] // 2
        return jnp.concatenate([finish_columns(total[:half], total.shape[1]), total[half:]], 0)

    def mixed_piece(later, layer):
        return finish_columns(later.done[layer, 3], size(2)[1] // 2)

    def write_block(layer, pieces):
        outs["block"] = write_out(
            functools.partial(early_out_kernel, size(10)[1] // owners),
            layer, pieces, [size(10), size(12)], outs.get("block"),
        )

    def write_mixed(layer, pieces):
        outs["mixed"] = write_out(
            functools.partial(late_out_kernel, size(2)[1] // 3 // owners),
            layer, pieces, [size(2), size(5)], outs.get("mixed"),
        )

    later = Later()
    for layer in reversed(range(LAYERS)):
        new = [(layer, n) for n in range(4)]
        old = [(layer + 1, n) for n in range(4)] if layer + 1 < LAYERS else None
        if not old:
            activation_got = other_half(activation_rows[activation_rows.shape[0] // 2 :])
        d_rows, small_grads[layer] = backward_layer(
            d_rows, saved_layers[layer], fetched[layer], later, new, old, activation_got
        )
    activations = ungroup(activation_rows, activation_got)
    image_got = other_half(low(d_rows[d_rows.shape[0] // 2 :]))
    d_images = ungroup(d_rows, image_got)
    while old[2] in later.running:
        later.step(old[2], d_rows)
    first = after(block_piece(later, layer + 1), d_rows)
    later.step(new[1], d_rows)
    write_block(layer + 1, spread(later.sent(first, new[1]), True))
    last_gots = later.gots[new[1]] + [image_got]
    later.join(new[3], [new[1]], d_rows)
    for name in (new[3], new[2], old[3]):
        while name in later.running:
            later.step(name, d_rows)
    write_block(layer, spread(block_piece(later, layer), False))
    both = [mixed_piece(later, n) for n in (layer + 1, layer)]
    rows = both[0].shape[0]
    pieces = spread(jnp.concatenate(both, 0), True)
    write_mixed(layer + 1, [piece[:rows] for piece in pieces])
    write_mixed(layer, [piece[rows:] for piece in pieces])
    stacked = [None] * len(all_params)
    for i, out in zip((10, 12, 2, 5), list(outs["block"]) + list(outs["mixed"])):
        stacked[i] = out.reshape(all_params[i].shape)
    reduced = reduce_small(
        [jnp.stack([grads[n] for grads in small_grads]) for n in range(len(SMALL))], last_gots
    )
    for i, vector in zip(SMALL, reduced):
        stacked[i] = vector
    return (activations, d_images) + tuple(stacked)


def solution(mesh):
    in_specs = (
        P("rep", "fsdp", None),
        P("rep", "fsdp", None),
        P(None, "fsdp"),
        P(None, "fsdp"),
        P(None, "fsdp", None),
        P(None, "fsdp"),
        P(None, "fsdp"),
        P(None, "fsdp", None),
        P(None, "fsdp"),
        P(None, "fsdp"),
        P(None, "fsdp"),
        P(None, "fsdp"),
        P(None, "fsdp", None),
        P(None, "fsdp"),
        P(None, "fsdp", None),
        P(None, "fsdp"),
        P(None, "fsdp"),
    )
    out_specs = (
        P("rep", "fsdp", None),
        P("rep", "fsdp", None),
        P(None, "fsdp"),
        P(None, "fsdp"),
        P(None, "fsdp", None),
        P(None, "fsdp"),
        P(None, "fsdp"),
        P(None, "fsdp", None),
        P(None, "fsdp"),
        P(None, "fsdp"),
        P(None, "fsdp"),
        P(None, "fsdp"),
        P(None, "fsdp", None),
        P(None, "fsdp"),
        P(None, "fsdp", None),
        P(None, "fsdp"),
        P(None, "fsdp"),
    )
    return jax.shard_map(local, mesh=mesh, in_specs=in_specs, out_specs=out_specs, check_vma=False)
```
